32 devices in a mesh: row: 8 (over y, x, core), col: 4 (over z).
Axes of the slice: x: 2, y: 2, z: 4, core: 2. Of those that a mesh axis runs over, the one named last changes fastest.
Arguments:
- volume_plane: bfloat16 [2, 4096, 4096], P(None, 'row', 'col'), may hold values from -4 to 4
- wave_a: bfloat16 [2, 4096, 4096], P(None, 'row', 'col'), may hold values from -4 to 4
- wave_b: bfloat16 [2, 4096, 4096], P(None, 'col', 'row'), may hold values from -4 to 4
- shift_rows: int32 [2, 2, 4096], P(None, None, 'row'), may hold values from -864 to 864, as said below
- fraction_rows: float32 [2, 2, 4096], P(None, None, 'row'), may hold values from -0.5 to 0.5
- shift_columns: int32 [2, 4096], P(None, 'col'), may hold values from -1728 to 1728, as said below
- fraction_columns: float32 [2, 4096], P(None, 'col'), may hold values from -0.5 to 0.5
- travel_distance: float32 [2], replicated, may hold values from 16 to 32
Outputs:
- exit_a: bfloat16 [2, 4096, 4096], P(None, 'row', 'col')
- exit_b: bfloat16 [2, 4096, 4096], P(None, 'col', 'row')
The draws below stay inside these ranges and needn't reach their ends.
Inputs may be any that keep to these rules, and one draw needn't show every extreme that they name: For view v, both shift_rows[v, 0] and shift_rows[v, 1] equal -s_v floor((2 r - 4095) m_v / 4095) for row r, with a sign s_v of 1 or -1 and a whole magnitude m_v from 432 to 864; m_0 = 864. shift_columns[v, c] = s_v floor((2 c - 4095) 2 m_v / 4095) with the s_v and m_v of shift_rows.
All inputs are finite; a program needn't handle non-finite values.
Results may differ from the reference program's by a relative error of at most 0.018.
Values may be sent and summed in bfloat16 or wider, within the bound.
No kernel may reach another device: no remote copies, remote signals or barrier semaphores. Data moves between devices by JAX's collectives and lax.ppermute only.
A program may use at most 64 MiB of HBM per device.

```python
import math
import jax
import jax.numpy as jnp
from jax import lax

BLOCK = 128
MARGIN = 32
SHIFT_X = 864
SHIFT_Y = 1728
PLANE = 4096


def shear_sizes(key):
    base = jax.random.fold_in(key, 4242)
    magnitudes = jax.random.randint(jax.random.fold_in(base, 1), (2,), SHIFT_X // 2, SHIFT_X + 1)
    magnitudes = jnp.where(jnp.arange(2) == 0, SHIFT_X, magnitudes).astype(jnp.int32)
    signs = (2 * jax.random.randint(jax.random.fold_in(base, 2), (2,), 0, 2) - 1).astype(jnp.int32)
    return (magnitudes, signs)


def linear_profile(magnitude, sign):
    position = jnp.arange(PLANE, dtype=jnp.int32)
    return sign * ((2 * position + 1 - PLANE) * magnitude // (PLANE - 1))


def draw_shift_rows(key, part):
    magnitudes, signs = shear_sizes(key)
    profiles = jnp.stack([linear_profile(magnitudes[member], -signs[member]) for member in range(2)])
    return jnp.stack([profiles, profiles], 1).astype(jnp.int32)


def draw_shift_columns(key, part):
    magnitudes, signs = shear_sizes(key)
    profiles = jnp.stack([linear_profile(2 * magnitudes[member], signs[member]) for member in range(2)])
    return profiles.astype(jnp.int32)


def block_levels(stream_key, shape, split, least, high):
    gain, own = 1.0, jax.random.fold_in(stream_key, 6)
    for dim, blocks in split:
        heights = jnp.exp(jax.random.uniform(jax.random.fold_in(own, dim), (blocks,), jnp.float32, least / len(split), high / len(split)))
        gain = gain * jnp.repeat(heights, shape[dim] // blocks).reshape([-1 if axis == dim else 1 for axis in range(len(shape))])
    return gain


def normal_values(stream_key, dims, spread, limit, pieces=(), held_as=jnp.bfloat16):
    values = jax.random.normal(stream_key, dims, jnp.float32) * spread
    if len(pieces) > 0:
        values = block_levels(stream_key, dims, pieces, -0.22, 0.18) * values
    return jnp.clip(values, min=-limit, max=limit).astype(held_as)


def setup_inputs(seed: int = 0) -> dict:
    seeds = jax.random.split(jax.random.key(seed), 9)
    volume_plane = normal_values(seeds[0], (2, PLANE, PLANE), 1.0, 4.0, ((1, 8), (2, 4)))
    wave_a = normal_values(seeds[1], (2, PLANE, PLANE), 0.7, 4.0, ((1, 8), (2, 4)))
    wave_b = normal_values(seeds[2], (2, PLANE, PLANE), 0.7, 4.0, ((1, 4), (2, 8)))
    shift_rows = draw_shift_rows(jax.random.fold_in(seeds[8], 71), 0)
    fraction_rows = jnp.clip(jax.random.uniform(seeds[4], (2, 2, PLANE), jnp.float32, -0.5, 0.5) * block_levels(seeds[4], (2, 2, PLANE), ((2, 8),), -0.4, 0.0), -0.5, 0.5)
    shift_columns = draw_shift_columns(jax.random.fold_in(seeds[8], 71), 0)
    fraction_columns = jnp.clip(jax.random.uniform(seeds[6], (2, PLANE), jnp.float32, -0.5, 0.5) * block_levels(seeds[6], (2, PLANE), ((1, 4),), -0.4, 0.0), -0.5, 0.5)
    travel_distance = jnp.clip(jax.random.uniform(seeds[7], (2,), jnp.float32, 16.0, 32.0), 16.0, 32.0)
    return dict(volume_plane=volume_plane, wave_a=wave_a, wave_b=wave_b, shift_rows=shift_rows, fraction_rows=fraction_rows, shift_columns=shift_columns, fraction_columns=fraction_columns, travel_distance=travel_distance)


ABSORB = 0.25


def fourier_tables(block_len, margin):
    window_len = block_len + 2 * margin
    frequency = jnp.arange(window_len, dtype=jnp.int32) - window_len // 2
    position = jnp.arange(window_len, dtype=jnp.int32)
    angles = 2.0 * jnp.pi * jnp.mod(position[:, None] * frequency[None, :], window_len).astype(jnp.float32) / window_len
    cosine = jnp.cos(angles)
    sines = jnp.sin(angles)
    forward = jnp.concatenate([jnp.concatenate([cosine, -sines], 1), jnp.concatenate([sines, cosine], 1)], 0).astype(jnp.bfloat16)
    target = jnp.arange(block_len, dtype=jnp.int32) + margin
    inverse_angle = 2.0 * jnp.pi * jnp.mod(frequency[:, None] * target[None, :], window_len).astype(jnp.float32) / window_len
    inverse_cosine = jnp.cos(inverse_angle) / window_len
    inverse_sine = jnp.sin(inverse_angle) / window_len
    inverse = jnp.concatenate([jnp.concatenate([inverse_cosine, inverse_sine], 1), jnp.concatenate([-inverse_sine, inverse_cosine], 1)], 0).astype(jnp.bfloat16)
    return forward, inverse, frequency.astype(jnp.float32)


def shear_ramp(fractions, frequency):
    window_len = frequency.shape[0]
    phases = (-2.0 * jnp.pi / window_len) * fractions[:, None] * frequency[None, :]
    nyquist = (jnp.arange(window_len) == 0)[None, :]
    ramp_real = jnp.where(nyquist, jnp.cos(jnp.pi * fractions)[:, None], jnp.cos(phases))
    ramp_imaginary = jnp.where(nyquist, 0.0, jnp.sin(phases))
    return ramp_real, ramp_imaginary


def travel_ramp(distance, frequency):
    window_len = frequency.shape[0]
    phases = (-2.0 * jnp.pi / (window_len * window_len)) * distance * frequency * frequency
    return jnp.cos(phases)[None, :], jnp.sin(phases)[None, :]


def line_pass(padded, extent, shifts, ramp_real, ramp_imaginary, tables):
    forward, inverse = tables[0], tables[1]
    window_len = BLOCK + 2 * MARGIN
    line_count = padded.shape[1]
    blocks = (padded.shape[2] - 2 * extent) // BLOCK
    reach_len = blocks * BLOCK + 2 * MARGIN
    starts = (extent - MARGIN - shifts).astype(jnp.int32)

    def pick(single, start):
        return lax.dynamic_slice_in_dim(single, start, reach_len, 1)

    shifted = jax.vmap(pick, in_axes=(1, 0), out_axes=1)(padded, starts)
    middle = shifted[:, :, MARGIN:MARGIN + blocks * BLOCK].reshape(2, line_count, blocks, BLOCK)
    left_rim = shifted[:, :, :blocks * BLOCK].reshape(2, line_count, blocks, BLOCK)[..., :MARGIN]
    right_rim = shifted[:, :, 2 * MARGIN:2 * MARGIN + blocks * BLOCK].reshape(2, line_count, blocks, BLOCK)[..., BLOCK - MARGIN:]
    windows = jnp.concatenate([left_rim, middle, right_rim], 3)
    spectrum = jnp.einsum("cpms,cst->pmt", windows.astype(jnp.float32), forward.astype(jnp.float32).reshape(2, window_len, 2 * window_len), precision=lax.Precision.HIGHEST)
    spec_real = spectrum[..., :window_len]
    spec_imaginary = spectrum[..., window_len:]
    factor_real = ramp_real[:, None, :]
    factor_imaginary = ramp_imaginary[:, None, :]
    ramped = jnp.concatenate([spec_real * factor_real - spec_imaginary * factor_imaginary, spec_real * factor_imaginary + spec_imaginary * factor_real], -1).astype(jnp.bfloat16)
    result = jnp.einsum("pms,scb->cpmb", ramped.astype(jnp.float32), inverse.astype(jnp.float32).reshape(2 * window_len, 2, BLOCK), precision=lax.Precision.HIGHEST)
    return result.reshape(2, line_count, blocks * BLOCK).astype(jnp.bfloat16)


def blockwise(padded, extent, shifts, ramp_real, ramp_imaginary, tables):
    line_count = padded.shape[1]
    groups = math.gcd(line_count, 512)
    group_count = line_count // groups
    window_len = ramp_real.shape[-1]
    grouped = padded.reshape(2, group_count, groups, padded.shape[2]).transpose(1, 0, 2, 3)
    group_shifts = shifts.reshape(group_count, groups)
    group_real = jnp.broadcast_to(ramp_real, (line_count, window_len)).reshape(group_count, groups, window_len)
    group_imaginary = jnp.broadcast_to(ramp_imaginary, (line_count, window_len)).reshape(group_count, groups, window_len)

    def run_block(payload):
        return line_pass(payload[0], extent, payload[1], payload[2], payload[3], tables)

    finished = lax.map(run_block, (grouped, group_shifts, group_real, group_imaginary))
    return finished.transpose(1, 0, 2, 3).reshape(2, line_count, -1)


def shift_last(plane_data, halo_depth, shifts, fractions, tables):
    padded = jnp.pad(plane_data, ((0, 0), (0, 0), (halo_depth, halo_depth)))
    ramp_real, ramp_imaginary = shear_ramp(fractions, tables[2])
    return blockwise(padded, halo_depth, shifts, ramp_real, ramp_imaginary, tables)


def shift_first(plane_data, halo_depth, shifts, fractions, tables):
    return jnp.swapaxes(shift_last(jnp.swapaxes(plane_data, 1, 2), halo_depth, shifts, fractions, tables), 1, 2)


def travel(wave, distance, tables):
    ramp_real, ramp_imaginary = travel_ramp(distance, tables[2])
    no_shift = jnp.zeros((wave.shape[1],), jnp.int32)
    halfway = blockwise(jnp.pad(wave, ((0, 0), (0, 0), (MARGIN, MARGIN))), MARGIN, no_shift, ramp_real, ramp_imaginary, tables)
    flipped = jnp.swapaxes(halfway, 1, 2)
    no_shift_two = jnp.zeros((flipped.shape[1],), jnp.int32)
    finished = blockwise(jnp.pad(flipped, ((0, 0), (0, 0), (MARGIN, MARGIN))), MARGIN, no_shift_two, ramp_real, ramp_imaginary, tables)
    return jnp.swapaxes(finished, 1, 2)


def transmit(rotated, wave):
    phase_part = rotated[0].astype(jnp.float32)
    absorb_part = rotated[1].astype(jnp.float32)
    amplitude = jnp.exp(-ABSORB * absorb_part)
    through_real = amplitude * jnp.cos(phase_part)
    through_imaginary = amplitude * jnp.sin(phase_part)
    wave_real = wave[0].astype(jnp.float32)
    wave_imaginary = wave[1].astype(jnp.float32)
    return jnp.stack([wave_real * through_real - wave_imaginary * through_imaginary, wave_real * through_imaginary + wave_imaginary * through_real]).astype(jnp.bfloat16)


def reference(volume_plane, wave_a, wave_b, shift_rows, fraction_rows, shift_columns, fraction_columns, travel_distance):
    tables = fourier_tables(BLOCK, MARGIN)
    results = []
    for member in range(2):
        section = shift_last(volume_plane, SHIFT_X + MARGIN, shift_rows[member, 0], fraction_rows[member, 0], tables)
        section = shift_first(section, SHIFT_Y + MARGIN, shift_columns[member], fraction_columns[member], tables)
        section = shift_last(section, SHIFT_X + MARGIN, shift_rows[member, 1], fraction_rows[member, 1], tables)
        results.append(section)
    turned = jnp.swapaxes(jnp.flip(results[1], 2), 1, 2)
    exit_a = travel(transmit(results[0], wave_a), travel_distance[0], tables)
    exit_b = travel(transmit(turned, wave_b), travel_distance[1], tables)
    return exit_a, exit_b
```

```python
import functools

import jax
import jax.numpy as jnp
import numpy as np
from jax import lax
from jax.experimental import pallas as pl
from jax.experimental.pallas import tpu as pltpu
from jax.sharding import PartitionSpec as P

BLOCK = 128
MARGIN = 32
SHIFT_X = 864
SHIFT_Y = 1728


ABSORB = 0.25

WINDOW = BLOCK + 2 * MARGIN
BINS = WINDOW // 2
GROUP = 16
VMEM_LIMIT = 56 * 1024 * 1024


def angle_table(rows, columns):
    return 2.0 * np.pi * (np.outer(rows, columns) % WINDOW) / WINDOW


def real_tables():
    position = np.arange(WINDOW)
    bins = np.arange(BINS + 1)
    target = np.arange(BLOCK) + MARGIN
    forward = np.zeros((2 * BLOCK, 2 * BLOCK), np.float32)
    forward[:WINDOW, : BINS + 1] = np.cos(angle_table(position, bins))
    forward[:WINDOW, BLOCK + 1 : BLOCK + BINS] = -np.sin(angle_table(position, bins[1:BINS]))
    weight = np.where((bins == 0) | (bins == BINS), 1.0, 2.0) / WINDOW
    inverse = np.zeros((2 * BLOCK, BLOCK), np.float32)
    inverse[: BINS + 1] = np.cos(angle_table(bins, target)) * weight[:, None]
    inverse[BLOCK + 1 : BLOCK + BINS] = (
        -np.sin(angle_table(bins[1:BINS], target)) * weight[1:BINS, None]
    )
    return forward, inverse


def shear_phase(fractions):
    frequency = jnp.arange(BLOCK, dtype=jnp.float32)
    phases = -2.0 * jnp.pi / WINDOW * fractions[:, None] * frequency[None, :]
    return jnp.cos(phases), jnp.sin(phases)


def travel_matrices(distance, forward, inverse):
    frequency = jnp.arange(BLOCK, dtype=jnp.float32)
    phases = -2.0 * jnp.pi / (WINDOW * WINDOW) * distance[:, None] * frequency * frequency
    ramps = jnp.stack([jnp.cos(phases), jnp.sin(phases)], 1)
    ramps = jnp.concatenate([ramps, ramps], 2)
    scaled = ramps[..., None] * jnp.asarray(inverse)
    matrices = jnp.einsum(
        "pq,vrqu->vrpu",
        jnp.asarray(forward[:WINDOW]),
        scaled,
        precision=lax.Precision.HIGHEST,
    )
    return matrices


def lane_iota(rows):
    return lax.broadcasted_iota(jnp.int32, (rows, BLOCK), 1)


def shift_lines(strip, shifted, base, base_offset, spare, windows, chunk_offset, rows):
    def one_group(group, carry):
        first = pl.multiple_of(group * GROUP, GROUP)
        lines = pl.ds(first, GROUP)
        start = base[base_offset + group] + chunk_offset
        offset = spare[lines, :]
        later = offset >= BLOCK
        lane = lane_iota(GROUP) + (offset & (BLOCK - 1))
        wraps = lane >= BLOCK
        index = lane & (BLOCK - 1)
        for part in range(2):
            here = strip[start, part, lines, :].astype(jnp.float32)
            before = None
            for i in range(windows + 2):
                following = strip[start + i + 1, part, lines, :].astype(jnp.float32)
                turned = jnp.take_along_axis(jnp.where(later, following, here), index, axis=1)
                if before is not None:
                    shifted[i - 1, part, lines, :] = jnp.where(wraps, turned, before).astype(
                        jnp.bfloat16
                    )
                before = turned
                here = following
        return carry

    lax.fori_loop(0, rows // GROUP, one_group, 0)


def ramped_lines(shifted, first, count, rows, cosine, sine, forward):
    lower = shifted[first : first + count].reshape(count * 2 * rows, BLOCK)
    upper = shifted[first + 1 : first + 1 + count].reshape(count * 2 * rows, BLOCK)
    spectrum = jnp.dot(
        jnp.concatenate([lower, upper], 1), forward[...], preferred_element_type=jnp.float32
    )
    real = spectrum[:, :BLOCK].reshape(count * 2, rows, BLOCK)
    imaginary = spectrum[:, BLOCK:].reshape(count * 2, rows, BLOCK)
    ramp_real = cosine[...][None]
    ramp_imaginary = sine[...][None]
    ramped = jnp.concatenate(
        [
            (real * ramp_real - imaginary * ramp_imaginary).astype(jnp.bfloat16),
            (real * ramp_imaginary + imaginary * ramp_real).astype(jnp.bfloat16),
        ],
        2,
    )
    return ramped.reshape(count * 2 * rows, 2 * BLOCK)


def shear_tile_kernel(
    views, halo, tiles, rows, batch, wide, left_chunks, right_chunks, base, *refs
):
    lefts, refs = refs[: len(left_chunks)], refs[len(left_chunks) :]
    rights, refs = refs[: len(right_chunks)], refs[len(right_chunks) :]
    own, spare, cosine, sine, forward, inverse = refs[:6]
    outs, (strip, shifted) = refs[6 : 6 + views], refs[6 + views :]
    step = pl.program_id(0)
    groups = rows // GROUP
    end = halo + tiles + halo

    @pl.when(step == 0)
    def _():
        strip[end : end + 2] = jnp.zeros((2, 2, rows, BLOCK), jnp.bfloat16)

    def fill(piece, first, count):
        for i in range(count):
            if wide:
                strip[first + i] = piece[:, :, i * BLOCK : (i + 1) * BLOCK]
            else:
                strip[first + i] = piece[i]

    for piece, (near, far) in zip(lefts, left_chunks):
        fill(piece, halo - far, far - near + 1)
    for piece, (near, far) in zip(rights, right_chunks):
        fill(piece, halo + tiles + near - 1, far - near + 1)
    fill(own, halo, tiles)
    for view in range(views):
        steps = base.shape[0] // (views * groups)
        offset = (view * steps + step) * groups
        shift_lines(strip, shifted, base, offset, spare.at[view], tiles, 0, rows)
        for first in range(0, tiles, batch):
            ramped = ramped_lines(
                shifted, first, batch, rows, cosine.at[view], sine.at[view], forward
            )
            result = jnp.dot(ramped, inverse[...], preferred_element_type=jnp.float32)
            outs[view][first : first + batch] = result.astype(jnp.bfloat16).reshape(
                batch, 2, rows, BLOCK
            )


def shear_tile(own, lefts, rights, left_chunks, right_chunks, halo, base, spare, ramps, tables):
    wide = own.ndim == 3
    line_count = own.shape[-2]
    tiles = own.shape[2] // BLOCK if wide else own.shape[0]
    views = spare.shape[0]
    rows = BLOCK
    forward, inverse = tables
    cosine, sine = ramps

    def piece_spec(piece):
        if wide:
            return pl.BlockSpec((2, rows, piece.shape[2]), lambda i, *_: (0, i, 0))
        return pl.BlockSpec((piece.shape[0], 2, rows, BLOCK), lambda i, *_: (0, 0, i, 0))

    line_spec = pl.BlockSpec((views, rows, BLOCK), lambda i, *_: (0, i, 0))
    out_shape = jax.ShapeDtypeStruct((tiles, 2, line_count, BLOCK), jnp.bfloat16)
    out_spec = pl.BlockSpec((tiles, 2, rows, BLOCK), lambda i, *_: (0, 0, i, 0))
    kernel = functools.partial(
        shear_tile_kernel,
        views,
        halo,
        tiles,
        rows,
        tiles // 2 if tiles % 2 == 0 else tiles,
        wide,
        left_chunks,
        right_chunks,
    )
    return pl.pallas_call(
        kernel,
        grid_spec=pltpu.PrefetchScalarGridSpec(
            num_scalar_prefetch=1,
            grid=(line_count // rows,),
            in_specs=[piece_spec(p) for p in (*lefts, *rights, own)]
            + [line_spec] * 3
            + [
                pl.BlockSpec(forward.shape, lambda i, *_: (0, 0)),
                pl.BlockSpec(inverse.shape, lambda i, *_: (0, 0)),
            ],
            out_specs=[out_spec] * views,
            scratch_shapes=[
                pltpu.VMEM((halo + tiles + halo + 2, 2, rows, BLOCK), jnp.bfloat16),
                pltpu.VMEM((tiles + 1, 2, rows, BLOCK), jnp.bfloat16),
            ],
        ),
        out_shape=[out_shape] * views,
        compiler_params=pltpu.CompilerParams(vmem_limit_bytes=VMEM_LIMIT),
        name="shear_tile",
    )(base.reshape(-1), *lefts, *rights, own, spare, cosine, sine, forward, inverse)


def shear_whole_kernel(
    halo, devices, tiles, rows, base, own, spare, cosine, sine, forward, flipped, out, strip, shifted
):
    step = pl.program_id(0)
    chunks = devices * tiles
    length = tiles * BLOCK

    @pl.when(step == 0)
    def _():
        strip[0:halo] = jnp.zeros((halo, 2, rows, BLOCK), jnp.bfloat16)
        strip[halo + chunks :] = jnp.zeros((halo + 2, 2, rows, BLOCK), jnp.bfloat16)
        for chunk in range(chunks):
            strip[halo + chunk] = own[chunk % tiles, chunk // tiles]
        out[0, :, 0:MARGIN, :] = jnp.zeros((2, MARGIN, rows), jnp.bfloat16)
        out[devices - 1, :, MARGIN + length :, :] = jnp.zeros((2, MARGIN, rows), jnp.bfloat16)

    shift_lines(strip, shifted, base, 0, spare, tiles, step * tiles, rows)
    ramped = ramped_lines(shifted, 0, tiles, rows, cosine, sine, forward)
    target = devices - 1 - step
    for window in range(tiles):
        lines = ramped[window * 2 * rows : (window + 1) * 2 * rows]
        result = lax.dot_general(
            flipped[...], lines, (((1,), (1,)), ((), ())), preferred_element_type=jnp.float32
        ).astype(jnp.bfloat16)
        block = tiles - 1 - window
        low = MARGIN + block * BLOCK
        for part in range(2):
            piece = result[:, part * rows : (part + 1) * rows]
            out[target, part, low : low + BLOCK, :] = piece
            if block == 0:

                @pl.when(target > 0)
                def _():
                    out[target - 1, part, MARGIN + length :, :] = piece[:MARGIN]

            if block == tiles - 1:

                @pl.when(target < devices - 1)
                def _():
                    out[target + 1, part, 0:MARGIN, :] = piece[BLOCK - MARGIN :]


def shear_whole(own, halo, base, spare, ramps, tables):
    tiles, devices, _, rows, _ = own.shape
    forward, flipped = tables
    cosine, sine = ramps
    full = lambda shape: pl.BlockSpec(shape, lambda i, *_: (0,) * len(shape))
    out = (devices, 2, tiles * BLOCK + 2 * MARGIN, rows)
    return pl.pallas_call(
        functools.partial(shear_whole_kernel, halo, devices, tiles, rows),
        grid_spec=pltpu.PrefetchScalarGridSpec(
            num_scalar_prefetch=1,
            grid=(devices,),
            in_specs=[
                full(x.shape) for x in (own, spare, cosine, sine, forward, flipped)
            ],
            out_specs=full(out),
            scratch_shapes=[
                pltpu.VMEM((2 * halo + devices * tiles + 2, 2, rows, BLOCK), jnp.bfloat16),
                pltpu.VMEM((tiles + 1, 2, rows, BLOCK), jnp.bfloat16),
            ],
        ),
        out_shape=jax.ShapeDtypeStruct(out, jnp.bfloat16),
        compiler_params=pltpu.CompilerParams(vmem_limit_bytes=VMEM_LIMIT),
        name="shear_whole",
    )(base, own, spare, cosine, sine, forward, flipped)


def shear_columns_kernel(
    front, blocks, length, rows_out, base, own, spare, cosine, sine, forward, inverse, out, strip, shifted
):
    step = pl.program_id(0)
    per_step = length // BLOCK
    total = strip.shape[1]

    @pl.when(step == 0)
    def _():
        strip[:, 0:front, :] = jnp.zeros((2, front, BLOCK), jnp.bfloat16)
        back = front + blocks * length
        strip[:, back:, :] = jnp.zeros((2, total - back, BLOCK), jnp.bfloat16)
        for block in range(blocks):
            for part in range(2):
                first = front + block * length
                strip[part, first : first + length, :] = own[block, part]

    offset = spare[...]
    row = lax.broadcasted_iota(jnp.int32, (8, BLOCK), 0) + (offset & 7)
    wraps = row >= 8
    index = row & 7

    def one_chunk(chunk):
        begin = pl.multiple_of(base[0] + chunk * BLOCK, GROUP)
        for part in range(2):
            value = strip[part, pl.ds(begin, 2 * BLOCK), :].astype(jnp.float32)
            value = value.reshape(2 * BLOCK // 8, 8, BLOCK)
            for bit in (64, 32, 16, 8):
                taken = ((offset & bit) != 0)[None]
                value = jnp.where(taken, value[bit // 8 :], value[: -(bit // 8)])
            pieces = [
                jnp.take_along_axis(value[i], index, axis=0) for i in range(BLOCK // 8 + 1)
            ]
            moved = [
                jnp.where(wraps, pieces[i + 1], pieces[i]) for i in range(BLOCK // 8)
            ]
            lanes = slice(part * BLOCK, (part + 1) * BLOCK)
            place = pl.ds(pl.multiple_of(chunk * BLOCK, BLOCK), BLOCK)
            shifted[place, lanes] = jnp.concatenate(moved, 0).astype(jnp.bfloat16)

    @pl.when(step == 0)
    def _():
        one_chunk(0)

    for window in range(per_step):
        one_chunk(step * per_step + window + 1)
    ramp_real = jnp.concatenate([cosine[...]] * 2, 1)
    ramp_imaginary = jnp.concatenate([sine[...]] * 2, 1)
    for window in range(per_step):
        first = pl.multiple_of((step * per_step + window) * BLOCK, BLOCK)
        spectrum = jnp.dot(
            forward[...], shifted[pl.ds(first, 2 * BLOCK), :], preferred_element_type=jnp.float32
        )
        real, imaginary = spectrum[:BLOCK], spectrum[BLOCK:]
        ramped = jnp.concatenate(
            [
                (real * ramp_real - imaginary * ramp_imaginary).astype(jnp.bfloat16),
                (real * ramp_imaginary + imaginary * ramp_real).astype(jnp.bfloat16),
            ],
            0,
        )
        result = jnp.dot(inverse[...], ramped, preferred_element_type=jnp.float32).astype(
            jnp.bfloat16
        )
        low = window * BLOCK
        block, within = low // rows_out, low % rows_out
        for part in range(2):
            out[block, part, within : within + BLOCK, :] = result[
                :, part * BLOCK : (part + 1) * BLOCK
            ]


def shear_columns(own, front, back, base, spare, ramps, tables, rows_out):
    blocks, _, length, _ = own.shape
    forward, inverse = tables
    cosine, sine = ramps
    full = lambda shape: pl.BlockSpec(shape, lambda i, *_: (0,) * len(shape))
    pieces = blocks * length // rows_out
    per_step = pieces // blocks
    return pl.pallas_call(
        functools.partial(shear_columns_kernel, front, blocks, length, rows_out),
        grid_spec=pltpu.PrefetchScalarGridSpec(
            num_scalar_prefetch=1,
            grid=(blocks,),
            in_specs=[full(x.shape) for x in (own, spare, cosine, sine, forward, inverse)],
            out_specs=pl.BlockSpec((per_step, 2, rows_out, BLOCK), lambda i, *_: (i, 0, 0, 0)),
            scratch_shapes=[
                pltpu.VMEM((2, front + blocks * length + back, BLOCK), jnp.bfloat16),
                pltpu.VMEM((blocks * length + BLOCK, 2 * BLOCK), jnp.bfloat16),
            ],
        ),
        out_shape=jax.ShapeDtypeStruct((pieces, 2, rows_out, BLOCK), jnp.bfloat16),
        compiler_params=pltpu.CompilerParams(vmem_limit_bytes=VMEM_LIMIT),
        name="shear_columns",
    )(base, own, spare, cosine, sine, forward, inverse)


def sine_cosine(angle):
    turns = jnp.round(angle * (2.0 / np.pi))
    rest = angle - turns * 1.5703125
    rest = rest - turns * 4.837512969970703125e-4
    rest = rest - turns * 7.549789954891882e-8
    square = rest * rest
    sine = rest + rest * square * (
        -1.6666654611e-1 + square * (8.3321608736e-3 - square * 1.9515295891e-4)
    )
    cosine = (
        1.0
        - 0.5 * square
        + square
        * square
        * (4.166664568298827e-2 + square * (-1.388731625493765e-3 + square * 2.443315711809948e-5))
    )
    quadrant = turns.astype(jnp.int32)
    odd = (quadrant & 1) != 0
    sine_out = jnp.where(odd, cosine, sine)
    cosine_out = jnp.where(odd, sine, cosine)
    sine_out = jnp.where((quadrant & 2) != 0, -sine_out, sine_out)
    cosine_out = jnp.where(((quadrant + 1) & 2) != 0, -cosine_out, cosine_out)
    return sine_out, cosine_out


def transmitted(rotated, wave):
    sine, cosine = sine_cosine(rotated[0].astype(jnp.float32))
    amplitude = jnp.exp(-ABSORB * rotated[1].astype(jnp.float32))
    through_real = amplitude * cosine
    through_imaginary = amplitude * sine
    wave_real = wave[0].astype(jnp.float32)
    wave_imaginary = wave[1].astype(jnp.float32)
    return (
        (wave_real * through_real - wave_imaginary * through_imaginary).astype(jnp.bfloat16),
        (wave_real * through_imaginary + wave_imaginary * through_real).astype(jnp.bfloat16),
    )


def travel_first_kernel(length, extended, *refs):
    if extended:
        body, wave, wave_top, wave_bottom, matrix, out, field = refs
        top = body.at[0, :, 0:MARGIN]
        middle = body.at[0, :, MARGIN : MARGIN + length]
        bottom = body.at[0, :, MARGIN + length :]
    else:
        body, top, bottom, wave, wave_top, wave_bottom, matrix, out, field = refs
        top, middle, bottom = top.at[0], body.at[0], bottom.at[0]
    pieces = [(0, MARGIN, top, wave_top, 0)]
    for first in range(0, length, BLOCK):
        pieces.append((MARGIN + first, BLOCK, middle, wave, first))
    pieces.append((MARGIN + length, MARGIN, bottom, wave_bottom, 0))
    for place, count, value, waves, first in pieces:
        lines = slice(first, first + count)
        parts = transmitted(
            [value[p, lines, :] for p in range(2)], [waves[p, lines, :] for p in range(2)]
        )
        for part in range(2):
            field[part, place : place + count, :] = parts[part]
    windows = [
        jnp.concatenate([field[0, m : m + WINDOW, :], field[1, m : m + WINDOW, :]], 0)
        for m in range(0, length, BLOCK)
    ]
    result = jnp.dot(
        matrix[...], jnp.concatenate(windows, 1), preferred_element_type=jnp.float32
    ).astype(jnp.bfloat16)
    for m in range(length // BLOCK):
        lanes = slice(m * BLOCK, (m + 1) * BLOCK)
        for part in range(2):
            out[0, part, lanes, :] = result[part * BLOCK : (part + 1) * BLOCK, lanes]


def travel_first(body, halos, wave, wave_halos, matrix):
    chunks = body.shape[0]
    length = wave.shape[1]
    chunk_spec = lambda x: pl.BlockSpec((1, 2, x.shape[2], BLOCK), lambda i: (i, 0, 0, 0))
    wide_spec = lambda x: pl.BlockSpec((2, x.shape[1], BLOCK), lambda i: (0, 0, i))
    return pl.pallas_call(
        functools.partial(travel_first_kernel, length, len(halos) == 0),
        grid=(chunks,),
        in_specs=[chunk_spec(body)]
        + [chunk_spec(x) for x in halos]
        + [wide_spec(x) for x in (wave, *wave_halos)]
        + [pl.BlockSpec(matrix.shape, lambda i: (0, 0))],
        out_specs=pl.BlockSpec((1, 2, length, BLOCK), lambda i: (i, 0, 0, 0)),
        out_shape=jax.ShapeDtypeStruct((chunks, 2, length, BLOCK), jnp.bfloat16),
        scratch_shapes=[pltpu.VMEM((2, length + 2 * MARGIN, BLOCK), jnp.bfloat16)],
        compiler_params=pltpu.CompilerParams(vmem_limit_bytes=VMEM_LIMIT),
        name="travel_first",
    )(body, *halos, wave, *wave_halos, matrix)


def travel_second_kernel(chunks, rows, left, body, right, matrix, out):
    parts = [[left[0, p]] + [body[m, p] for m in range(chunks)] + [right[0, p]] for p in range(2)]
    windows = [
        jnp.concatenate(parts[0][m : m + 3] + parts[1][m : m + 3], 1) for m in range(chunks)
    ]
    result = jnp.dot(
        jnp.concatenate(windows, 0), matrix[...], preferred_element_type=jnp.float32
    ).astype(jnp.bfloat16)
    for m in range(chunks):
        for part in range(2):
            out[part, :, m * BLOCK : (m + 1) * BLOCK] = result[
                m * rows : (m + 1) * rows, part * BLOCK : (part + 1) * BLOCK
            ]


def travel_second(left, body, right, matrix):
    chunks, _, length, _ = body.shape
    rows = BLOCK
    edge = pl.BlockSpec((1, 2, rows, BLOCK), lambda i: (0, 0, i, 0))
    return pl.pallas_call(
        functools.partial(travel_second_kernel, chunks, rows),
        grid=(length // rows,),
        in_specs=[
            edge,
            pl.BlockSpec((chunks, 2, rows, BLOCK), lambda i: (0, 0, i, 0)),
            edge,
            pl.BlockSpec(matrix.shape, lambda i: (0, 0)),
        ],
        out_specs=pl.BlockSpec((2, rows, chunks * BLOCK), lambda i: (0, i, 0)),
        out_shape=jax.ShapeDtypeStruct((2, length, chunks * BLOCK), jnp.bfloat16),
        compiler_params=pltpu.CompilerParams(vmem_limit_bytes=VMEM_LIMIT),
        name="travel_second",
    )(left, body, right, matrix)


def from_both_sides(first, last, axis):
    devices = lax.axis_size(axis)
    up = [(i, i + 1) for i in range(devices - 1)]
    down = [(j, i) for i, j in up]
    return lax.ppermute(last, axis, up), lax.ppermute(first, axis, down)


def halo_plan(line_count, row_devices, halo):
    share = line_count // row_devices
    reach = []
    for device in range(row_devices):
        ends = [device * share, (device + 1) * share - 1]
        most = max(
            -(-abs(2 * r + 1 - line_count) * SHIFT_X // (line_count - 1)) for r in ends
        )
        reach.append(-(-(min(most, SHIFT_X) + MARGIN) // BLOCK))
    plan = []
    for chunk in range(1, halo + 1):
        users = [d for d in range(row_devices) if reach[d] >= chunk]
        if plan and plan[-1][2] == users:
            plan[-1] = (plan[-1][0], chunk, users)
        else:
            plan.append((chunk, chunk, users))
    return plan


def exchange_chunks(piece, plan, tiles):
    columns = lax.axis_size("col")
    lefts, rights = [], []
    for near, far, users in plan:
        up = [
            (d * columns + c, d * columns + c + 1) for d in users for c in range(columns - 1)
        ]
        down = [(b, a) for a, b in up]
        lefts.append(lax.ppermute(piece(tiles - far, tiles - near + 1), ("row", "col"), up))
        rights.append(lax.ppermute(piece(near - 1, far), ("row", "col"), down))
    return lefts, rights


def group_starts(starts, group, unit):
    lines = starts.shape[-1]
    grouped = starts.reshape(*starts.shape[:-1], lines // group, group)
    base = jnp.min(grouped, -1) // unit
    spare = grouped - base[..., None] * unit
    return base.astype(jnp.int32), spare.reshape(starts.shape)


def over_lanes(spare):
    return jnp.broadcast_to(spare[..., None], (*spare.shape, BLOCK)).astype(jnp.int32)


def on_device(
    volume_plane,
    wave_a,
    wave_b,
    shift_rows,
    fraction_rows,
    shift_columns,
    fraction_columns,
    travel_distance,
):
    _, line_count, width = volume_plane.shape
    row_devices, column_devices = lax.axis_size("row"), lax.axis_size("col")
    row_index, column_index = lax.axis_index("row"), lax.axis_index("col")
    tiles = width // BLOCK
    halo = -(-(SHIFT_X + MARGIN) // BLOCK)
    plan = halo_plan(line_count * row_devices, row_devices, halo)
    chunks = [(near, far) for near, far, _ in plan]

    forward, inverse = real_tables()
    half = lambda x: jnp.asarray(x, jnp.bfloat16)
    row_tables = (half(forward), half(inverse))
    column_tables = (half(forward.T), half(inverse.T))
    turned_tables = (half(forward), half(inverse[:, ::-1].T))

    lefts, rights = exchange_chunks(
        lambda a, b: volume_plane[:, :, a * BLOCK : b * BLOCK], plan, tiles
    )
    wave_a_halos = from_both_sides(wave_a[:, :MARGIN], wave_a[:, -MARGIN:], "row")
    wave_b_halos = from_both_sides(wave_b[:, :MARGIN], wave_b[:, -MARGIN:], "col")

    base_rows, spare_rows = group_starts(halo * BLOCK - MARGIN - shift_rows, GROUP, BLOCK)
    first_ramps = shear_phase(fraction_rows[:, 0].reshape(-1))
    first_ramps = [x.reshape(2, line_count, BLOCK) for x in first_ramps]
    sheared = shear_tile(
        volume_plane,
        lefts,
        rights,
        chunks,
        chunks,
        halo,
        base_rows[:, 0],
        over_lanes(spare_rows[:, 0]),
        first_ramps,
        row_tables,
    )

    front = -(-(SHIFT_Y + MARGIN) // GROUP) * GROUP
    back = front + 3 * BLOCK
    mine = lambda x: lax.dynamic_slice_in_dim(x, row_index * BLOCK, BLOCK, 1)
    base_columns, spare_columns = group_starts(front - MARGIN - mine(shift_columns), BLOCK, GROUP)
    column_fractions = mine(fraction_columns)

    def second(view, rows_out):
        spread = lax.all_to_all(sheared[view], "row", split_axis=0, concat_axis=0, tiled=True)
        cosine, sine = shear_phase(column_fractions[view])
        return shear_columns(
            spread.reshape(row_devices, 2, line_count, BLOCK),
            front,
            back,
            base_columns[view] * GROUP,
            jnp.broadcast_to(spare_columns[view][None], (8, BLOCK)).astype(jnp.int32),
            (cosine.T, sine.T),
            column_tables,
            rows_out,
        )

    matrices = travel_matrices(travel_distance, forward, inverse)
    real, imaginary = matrices[:, 0], matrices[:, 1]
    along_rows = jnp.concatenate(
        [
            jnp.concatenate([real, -imaginary], 1),
            jnp.concatenate([imaginary, real], 1),
        ],
        2,
    )
    along_rows = jnp.swapaxes(along_rows, 1, 2).astype(jnp.bfloat16)
    spaced = jnp.pad(matrices, ((0, 0), (0, 0), (BLOCK - MARGIN, BLOCK - MARGIN), (0, 0)))
    real, imaginary = spaced[:, 0], spaced[:, 1]
    along_columns = jnp.concatenate(
        [
            jnp.concatenate([real, -imaginary], 1),
            jnp.concatenate([imaginary, real], 1),
        ],
        2,
    ).astype(jnp.bfloat16)

    moved_b = second(1, BLOCK)
    whole = lax.all_to_all(moved_b, ("row", "col"), split_axis=0, concat_axis=0, tiled=True)
    whole = whole.reshape(row_devices, column_devices, 2, BLOCK, BLOCK)
    own_lines = lambda x: lax.dynamic_slice_in_dim(x, column_index * BLOCK, BLOCK, 0)
    groups = BLOCK // GROUP
    turned = shear_whole(
        whole,
        halo,
        lax.dynamic_slice_in_dim(base_rows[1, 1], column_index * groups, groups, 0),
        over_lanes(own_lines(spare_rows[1, 1])),
        shear_phase(own_lines(fraction_rows[1, 1])),
        turned_tables,
    )
    turned = lax.all_to_all(turned, "col", split_axis=0, concat_axis=0, tiled=True)

    moved_a = second(0, line_count)
    tile = lax.all_to_all(moved_a, "row", split_axis=0, concat_axis=0, tiled=True)
    lefts, rights = exchange_chunks(lambda a, b: tile[a:b], plan, tiles)
    (rotated,) = shear_tile(
        tile,
        lefts,
        rights,
        chunks,
        chunks,
        halo,
        base_rows[:1, 1],
        over_lanes(spare_rows[:1, 1]),
        [x[None] for x in shear_phase(fraction_rows[0, 1])],
        row_tables,
    )

    half_b = travel_first(turned, (), wave_b, wave_b_halos, along_rows[1])
    left, right = from_both_sides(half_b[:1], half_b[-1:], "row")
    exit_b = travel_second(left, half_b, right, along_columns[1])

    halos = from_both_sides(rotated[:, :, :MARGIN], rotated[:, :, -MARGIN:], "row")
    half_a = travel_first(rotated, halos, wave_a, wave_a_halos, along_rows[0])
    left, right = from_both_sides(half_a[:1], half_a[-1:], "col")
    exit_a = travel_second(left, half_a, right, along_columns[0])
    return exit_a, exit_b


def swapped(value, axis, bit):
    mask = 2**bit
    pairs = [(source, source ^ mask) for source in range(lax.axis_size(axis))]
    return lax.ppermute(value, axis, pairs)


def padded_2(x, sides, width):
    for axis, dim in sides:
        devices, length = (lax.axis_size(axis), x.shape[dim])
        up = [(i, (i + 1) % devices) for i in range(devices - 1)]
        down = [(j, i) for i, j in up]
        last = lax.slice_in_dim(x, length - width, length, axis=dim)
        first = lax.slice_in_dim(x, 0, width, axis=dim)
        before = lax.ppermute(last, axis, up)
        after = lax.ppermute(first, axis, down)
        x = jnp.concatenate([before, x, after], axis=dim)
    return x


def fourier_tables(block_len, margin):
    window_len = block_len + 2 * margin
    frequency = jnp.arange(window_len, dtype=jnp.int32) - window_len // 2
    position = jnp.arange(window_len, dtype=jnp.int32)
    angles = (
        2.0
        * jnp.pi
        * jnp.mod(position[:, None] * frequency[None, :], window_len).astype(jnp.float32)
        / window_len
    )
    cosine = jnp.cos(angles)
    sines = jnp.sin(angles)
    forward = jnp.concatenate(
        [jnp.concatenate([cosine, -sines], 1), jnp.concatenate([sines, cosine], 1)], 0
    ).astype(jnp.bfloat16)
    target = jnp.arange(block_len, dtype=jnp.int32) + margin
    inverse_angle = (
        2.0
        * jnp.pi
        * jnp.mod(frequency[:, None] * target[None, :], window_len).astype(jnp.float32)
        / window_len
    )
    inverse_cosine = jnp.cos(inverse_angle) / window_len
    inverse_sine = jnp.sin(inverse_angle) / window_len
    inverse = jnp.concatenate(
        [
            jnp.concatenate([inverse_cosine, inverse_sine], 1),
            jnp.concatenate([-inverse_sine, inverse_cosine], 1),
        ],
        0,
    ).astype(jnp.bfloat16)
    return (forward, inverse, frequency.astype(jnp.float32))


def shear_ramp(fractions, frequency):
    window_len = frequency.shape[0]
    phases = -2.0 * jnp.pi / window_len * fractions[:, None] * frequency[None, :]
    nyquist = (jnp.arange(window_len) == 0)[None, :]
    ramp_real = jnp.where(nyquist, jnp.cos(jnp.pi * fractions)[:, None], jnp.cos(phases))
    ramp_imaginary = jnp.where(nyquist, 0.0, jnp.sin(phases))
    return (ramp_real, ramp_imaginary)


def travel_ramp(distance, frequency):
    window_len = frequency.shape[0]
    phases = -2.0 * jnp.pi / (window_len * window_len) * distance * frequency * frequency
    return (jnp.cos(phases)[None, :], jnp.sin(phases)[None, :])


def select_window(padded, starts, out_len):
    total_len = padded.shape[2]
    offset_range = total_len - out_len
    bit_count = max(offset_range, 1).bit_length()
    current = jnp.pad(padded, ((0, 0), (0, 0), (0, out_len + 2**bit_count - 1 - total_len)))
    for bit_number in reversed(range(bit_count)):
        stride = 2**bit_number
        kept_len = current.shape[2] - stride
        chosen = (starts // stride % 2 == 1)[None, :, None]
        current = jnp.where(
            chosen, current[:, :, stride : stride + kept_len], current[:, :, :kept_len]
        )
    return current


def line_pass(padded, extent, shifts, ramp_real, ramp_imaginary, tables):
    forward, inverse = (tables[0], tables[1])
    window_len = BLOCK + 2 * MARGIN
    line_count = padded.shape[1]
    blocks = (padded.shape[2] - 2 * extent) // BLOCK
    reach_len = blocks * BLOCK + 2 * MARGIN
    if shifts is None:
        shifted = padded
    else:
        starts = extent - MARGIN - shifts
        shifted = select_window(padded, starts, reach_len)
    middle = shifted[:, :, MARGIN : MARGIN + blocks * BLOCK].reshape(2, line_count, blocks, BLOCK)
    left_rim = shifted[:, :, : blocks * BLOCK].reshape(2, line_count, blocks, BLOCK)[..., :MARGIN]
    right_rim = shifted[:, :, 2 * MARGIN : 2 * MARGIN + blocks * BLOCK].reshape(
        2, line_count, blocks, BLOCK
    )[..., BLOCK - MARGIN :]
    windows = jnp.concatenate([left_rim, middle, right_rim], 3)
    spectrum = jnp.einsum(
        "cpms,cst->pmt",
        windows,
        forward.reshape(2, window_len, 2 * window_len),
        preferred_element_type=jnp.float32,
    )
    spec_real = spectrum[..., :window_len]
    spec_imaginary = spectrum[..., window_len:]
    factor_real = ramp_real[:, None, :]
    factor_imaginary = ramp_imaginary[:, None, :]
    ramped = jnp.concatenate(
        [
            spec_real * factor_real - spec_imaginary * factor_imaginary,
            spec_real * factor_imaginary + spec_imaginary * factor_real,
        ],
        -1,
    ).astype(jnp.bfloat16)
    result = jnp.einsum(
        "pms,scb->cpmb",
        ramped,
        inverse.reshape(2 * window_len, 2, BLOCK),
        preferred_element_type=jnp.float32,
    )
    return result.reshape(2, line_count, blocks * BLOCK).astype(jnp.bfloat16)


def single_pass(padded, extent, shifts, fractions, tables):
    ramp_real, ramp_imaginary = shear_ramp(fractions, tables[2])
    return line_pass(padded, extent, shifts, ramp_real, ramp_imaginary, tables)


def general_shear_columns(stacked, shifts, fractions, tables):
    halo_depth = SHIFT_X + MARGIN
    inputs = stacked.shape[0]
    column_devices = lax.axis_size("col")
    share = stacked.shape[2] // column_devices
    offset = lax.axis_index("col") * share
    spread = lax.all_to_all(stacked, "col", split_axis=2, concat_axis=3, tiled=True)
    padded = jnp.pad(spread, ((0, 0), (0, 0), (0, 0), (halo_depth, halo_depth)))
    row_shifts = lax.dynamic_slice_in_dim(shifts, offset, share, 1)
    row_fractions = lax.dynamic_slice_in_dim(fractions, offset, share, 1)
    sheared = jnp.stack(
        [
            single_pass(
                padded[min(0, inputs - 1)], halo_depth, row_shifts[0], row_fractions[0], tables
            )
        ]
    )
    return lax.all_to_all(sheared, "col", split_axis=3, concat_axis=2, tiled=True)


def shear_along_first(padded_lines, halo_depth, shifts, fractions, tables):
    flipped = jnp.swapaxes(padded_lines[0], 1, 2)
    moved = single_pass(flipped, halo_depth, shifts[0], fractions[0], tables)
    sheared = [jnp.swapaxes(moved, 1, 2)]
    return jnp.stack(sheared)


def shear_rows_pass(stacked, shifts, fractions, tables):
    halo_depth = SHIFT_Y + MARGIN
    row_devices = lax.axis_size("row")
    share = stacked.shape[3] // row_devices
    offset = lax.axis_index("row") * share
    spread = lax.all_to_all(stacked, "row", split_axis=3, concat_axis=2, tiled=True)
    padded = jnp.pad(spread, ((0, 0), (0, 0), (halo_depth, halo_depth), (0, 0)))
    column_shifts = lax.dynamic_slice_in_dim(shifts, offset, share, 1)
    column_fractions = lax.dynamic_slice_in_dim(fractions, offset, share, 1)
    sheared = shear_along_first(padded, halo_depth, column_shifts, column_fractions, tables)
    return lax.all_to_all(sheared, "row", split_axis=2, concat_axis=3, tiled=True)


def travel_local(extended, distance, tables):
    ramp_real, ramp_imaginary = travel_ramp(distance, tables[2])
    halfway = line_pass(extended, MARGIN, None, ramp_real, ramp_imaginary, tables)
    flipped = jnp.swapaxes(halfway, 1, 2)
    finished = line_pass(flipped, MARGIN, None, ramp_real, ramp_imaginary, tables)
    return jnp.swapaxes(finished, 1, 2)


def transmit(rotated, wave):
    phase_part = rotated[0].astype(jnp.float32)
    absorb_part = rotated[1].astype(jnp.float32)
    amplitude = jnp.exp(-ABSORB * absorb_part)
    through_real = amplitude * jnp.cos(phase_part)
    through_imaginary = amplitude * jnp.sin(phase_part)
    wave_real = wave[0].astype(jnp.float32)
    wave_imaginary = wave[1].astype(jnp.float32)
    return jnp.stack(
        [
            wave_real * through_real - wave_imaginary * through_imaginary,
            wave_real * through_imaginary + wave_imaginary * through_real,
        ]
    ).astype(jnp.bfloat16)


def general_on_device(
    volume_plane,
    wave_a,
    wave_b,
    shift_rows,
    fraction_rows,
    shift_columns,
    fraction_columns,
    travel_distance,
):
    tables = fourier_tables(BLOCK, MARGIN)
    source = volume_plane[None]
    results = []
    for member in range(2):
        stacked = general_shear_columns(
            source,
            shift_rows[member : member + 1, 0],
            fraction_rows[member : member + 1, 0],
            tables,
        )
        stacked = shear_rows_pass(
            stacked,
            shift_columns[member : member + 1],
            fraction_columns[member : member + 1],
            tables,
        )
        stacked = general_shear_columns(
            stacked,
            shift_rows[member : member + 1, 1],
            fraction_rows[member : member + 1, 1],
            tables,
        )
        results.append(stacked[0])
    view_one = results[0]
    view_two = results[1]
    turned = jnp.swapaxes(jnp.flip(view_two, 2), 1, 2)
    for bit_number in range(lax.axis_size("col").bit_length() - 1):
        turned = swapped(turned, "col", bit_number)
    product_a = transmit(view_one, wave_a)
    extended_a = padded_2(product_a, (("row", 1), ("col", 2)), MARGIN)
    exit_a = travel_local(extended_a, travel_distance[0], tables)
    product_b = transmit(turned, wave_b)
    extended_b = padded_2(product_b, (("row", 2), ("col", 1)), MARGIN)
    exit_b = travel_local(extended_b, travel_distance[1], tables)
    return (exit_a, exit_b)


def solution(mesh):
    def either(volume_plane, *rest):
        rows, width = volume_plane.shape[1:]
        fits = (
            rows == BLOCK * lax.axis_size("col")
            and width == BLOCK * lax.axis_size("row")
            and width >= SHIFT_X + MARGIN
        )
        chosen = on_device if fits else general_on_device
        return chosen(volume_plane, *rest)

    return jax.shard_map(
        either,
        mesh=mesh,
        in_specs=(
            P(None, "row", "col"),
            P(None, "row", "col"),
            P(None, "col", "row"),
            P(None, None, "row"),
            P(None, None, "row"),
            P(None, "col"),
            P(None, "col"),
            P(),
        ),
        out_specs=(P(None, "row", "col"), P(None, "col", "row")),
        check_vma=False,
    )
```

```python
import functools

import jax
import jax.numpy as jnp
import numpy as np
from jax import lax
from jax.experimental import pallas as pl
from jax.experimental.pallas import tpu as pltpu
from jax.sharding import PartitionSpec as P

BLOCK = 128
MARGIN = 32
SHIFT_X = 864
SHIFT_Y = 1728


ABSORB = 0.25

WINDOW = BLOCK + 2 * MARGIN
BINS = WINDOW // 2
GROUP = 16
GATHERED = 4
VMEM_LIMIT = 56 * 1024 * 1024


def angle_table(rows, columns):
    return 2.0 * np.pi * (np.outer(rows, columns) % WINDOW) / WINDOW


def real_tables():
    position = np.arange(WINDOW)
    bins = np.arange(BINS + 1)
    target = np.arange(BLOCK) + MARGIN
    forward = np.zeros((2 * BLOCK, 2 * BLOCK), np.float32)
    forward[:WINDOW, : BINS + 1] = np.cos(angle_table(position, bins))
    forward[:WINDOW, BLOCK + 1 : BLOCK + BINS] = -np.sin(angle_table(position, bins[1:BINS]))
    weight = np.where((bins == 0) | (bins == BINS), 1.0, 2.0) / WINDOW
    inverse = np.zeros((2 * BLOCK, BLOCK), np.float32)
    inverse[: BINS + 1] = np.cos(angle_table(bins, target)) * weight[:, None]
    inverse[BLOCK + 1 : BLOCK + BINS] = (
        -np.sin(angle_table(bins[1:BINS], target)) * weight[1:BINS, None]
    )
    return forward, inverse


def travel_matrices(distance, forward, inverse):
    frequency = jnp.arange(BLOCK, dtype=jnp.float32)
    phases = -2.0 * jnp.pi / (WINDOW * WINDOW) * distance[:, None] * frequency * frequency
    ramps = jnp.stack([jnp.cos(phases), jnp.sin(phases)], 1)
    ramps = jnp.concatenate([ramps, ramps], 2)
    scaled = ramps[..., None] * jnp.asarray(inverse)
    matrices = jnp.einsum(
        "pq,vrqu->vrpu",
        jnp.asarray(forward[:WINDOW]),
        scaled,
        precision=lax.Precision.HIGHEST,
    )
    return matrices


def lane_iota(rows):
    return lax.broadcasted_iota(jnp.int32, (rows, BLOCK), 1)


def shift_lines(strip, shifted, base, base_offset, spare, windows, chunk_offset, rows):
    def one_group(group, carry):
        first = pl.multiple_of(group * GROUP, GROUP)
        lines = pl.ds(first, GROUP)
        start = base[base_offset + group] + chunk_offset
        offset = spare[lines, :]
        later = offset >= BLOCK
        lane = lane_iota(GROUP) + (offset & (BLOCK - 1))
        wraps = lane >= BLOCK
        index = lane & (BLOCK - 1)
        for part in range(2):
            here = strip[start, part, lines, :].astype(jnp.float32)
            before = None
            for i in range(windows + 2):
                following = strip[start + i + 1, part, lines, :].astype(jnp.float32)
                turned = jnp.take_along_axis(jnp.where(later, following, here), index, axis=1)
                if before is not None:
                    shifted[i - 1, part, lines, :] = jnp.where(wraps, turned, before).astype(
                        jnp.bfloat16
                    )
                before = turned
                here = following
        return carry

    lax.fori_loop(0, rows // GROUP, one_group, 0)


def ramped_lines(shifted, first, count, rows, cosine, sine, forward):
    lower = shifted[first : first + count].reshape(count * 2 * rows, BLOCK)
    upper = shifted[first + 1 : first + 1 + count].reshape(count * 2 * rows, BLOCK)
    spectrum = jnp.dot(
        jnp.concatenate([lower, upper], 1), forward[...], preferred_element_type=jnp.float32
    )
    real = spectrum[:, :BLOCK].reshape(count * 2, rows, BLOCK)
    imaginary = spectrum[:, BLOCK:].reshape(count * 2, rows, BLOCK)
    ramp_real = cosine[...][None]
    ramp_imaginary = sine[...][None]
    ramped = jnp.concatenate(
        [
            (real * ramp_real - imaginary * ramp_imaginary).astype(jnp.bfloat16),
            (real * ramp_imaginary + imaginary * ramp_real).astype(jnp.bfloat16),
        ],
        2,
    )
    return ramped.reshape(count * 2 * rows, 2 * BLOCK)


def down_lines(vector):
    return jnp.broadcast_to(vector, (BLOCK, BLOCK)).T


def line_ramps(fractions, cosine, sine):
    bins = lane_iota(BLOCK).astype(jnp.float32)
    sine[...], cosine[...] = sine_cosine(down_lines(fractions) * bins * (-2.0 * np.pi / WINDOW))


def shear_tile_kernel(
    halo, tiles, rows, batch, wide, left_chunks, right_chunks, base, *refs
):
    lefts, refs = refs[: len(left_chunks)], refs[len(left_chunks) :]
    rights, refs = refs[: len(right_chunks)], refs[len(right_chunks) :]
    own, offsets, fractions, forward, inverse, out = refs[:6]
    strip, shifted, spare, cosine, sine = refs[6:]
    step = pl.program_id(0)
    groups = rows // GROUP
    end = halo + tiles + halo

    @pl.when(step == 0)
    def _():
        strip[end : end + 2] = jnp.zeros((2, 2, rows, BLOCK), jnp.bfloat16)

    def fill(piece, first, count):
        for i in range(count):
            if wide:
                strip[first + i] = piece[:, :, i * BLOCK : (i + 1) * BLOCK]
            else:
                strip[first + i] = piece[i]

    for piece, (near, far) in zip(lefts, left_chunks):
        fill(piece, halo - far, far - near + 1)
    for piece, (near, far) in zip(rights, right_chunks):
        fill(piece, halo + tiles + near - 1, far - near + 1)
    fill(own, halo, tiles)
    spare[...] = down_lines(offsets[0]).astype(jnp.int32)
    line_ramps(fractions[0], cosine, sine)
    shift_lines(strip, shifted, base, step * groups, spare, tiles, 0, rows)
    for first in range(0, tiles, batch):
        ramped = ramped_lines(shifted, first, batch, rows, cosine, sine, forward)
        result = jnp.dot(ramped, inverse[...], preferred_element_type=jnp.float32)
        out[first : first + batch] = result.astype(jnp.bfloat16).reshape(batch, 2, rows, BLOCK)


def shear_tile(own, lefts, rights, chunks, halo, base, spare, fractions, tables):
    wide = own.ndim == 3
    line_count = own.shape[-2]
    tiles = own.shape[2] // BLOCK if wide else own.shape[0]
    rows = BLOCK
    forward, inverse = tables

    def piece_spec(piece):
        if wide:
            return pl.BlockSpec((2, rows, piece.shape[2]), lambda i, *_: (0, i, 0))
        return pl.BlockSpec((piece.shape[0], 2, rows, BLOCK), lambda i, *_: (0, 0, i, 0))

    line_spec = pl.BlockSpec((1, 1, rows), lambda i, *_: (i, 0, 0))
    along = lambda x: x.astype(jnp.float32).reshape(-1, 1, rows)
    out_shape = jax.ShapeDtypeStruct((tiles, 2, line_count, BLOCK), jnp.bfloat16)
    out_spec = pl.BlockSpec((tiles, 2, rows, BLOCK), lambda i, *_: (0, 0, i, 0))
    kernel = functools.partial(
        shear_tile_kernel,
        halo,
        tiles,
        rows,
        tiles // 2 if tiles % 2 == 0 else tiles,
        wide,
        chunks,
        chunks,
    )
    return pl.pallas_call(
        kernel,
        grid_spec=pltpu.PrefetchScalarGridSpec(
            num_scalar_prefetch=1,
            grid=(line_count // rows,),
            in_specs=[piece_spec(p) for p in (*lefts, *rights, own)]
            + [line_spec] * 2
            + [
                pl.BlockSpec(forward.shape, lambda i, *_: (0, 0)),
                pl.BlockSpec(inverse.shape, lambda i, *_: (0, 0)),
            ],
            out_specs=out_spec,
            scratch_shapes=[
                pltpu.VMEM((halo + tiles + halo + 2, 2, rows, BLOCK), jnp.bfloat16),
                pltpu.VMEM((tiles + 1, 2, rows, BLOCK), jnp.bfloat16),
                pltpu.VMEM((rows, BLOCK), jnp.int32),
                pltpu.VMEM((rows, BLOCK), jnp.float32),
                pltpu.VMEM((rows, BLOCK), jnp.float32),
            ],
        ),
        out_shape=out_shape,
        compiler_params=pltpu.CompilerParams(vmem_limit_bytes=VMEM_LIMIT),
        name="shear_tile",
    )(base, *lefts, *rights, own, along(spare), along(fractions), forward, inverse)


def shear_whole_kernel(
    halo,
    devices,
    tiles,
    rows,
    base,
    own,
    offsets,
    fractions,
    forward,
    flipped,
    out,
    strip,
    shifted,
    spare,
    cosine,
    sine,
):
    step = pl.program_id(0)
    chunks = devices * tiles
    length = tiles * BLOCK

    @pl.when(step == 0)
    def _():
        strip[0:halo] = jnp.zeros((halo, 2, rows, BLOCK), jnp.bfloat16)
        strip[halo + chunks :] = jnp.zeros((halo + 2, 2, rows, BLOCK), jnp.bfloat16)
        for chunk in range(chunks):
            strip[halo + chunk] = own[chunk % tiles, chunk // tiles]
        out[0, :, 0:MARGIN, :] = jnp.zeros((2, MARGIN, rows), jnp.bfloat16)
        out[devices - 1, :, MARGIN + length :, :] = jnp.zeros((2, MARGIN, rows), jnp.bfloat16)
        spare[...] = down_lines(offsets[...]).astype(jnp.int32)
        line_ramps(fractions[...], cosine, sine)

    shift_lines(strip, shifted, base, 0, spare, tiles, step * tiles, rows)
    ramped = ramped_lines(shifted, 0, tiles, rows, cosine, sine, forward)
    target = devices - 1 - step
    for window in range(tiles):
        lines = ramped[window * 2 * rows : (window + 1) * 2 * rows]
        result = lax.dot_general(
            flipped[...], lines, (((1,), (1,)), ((), ())), preferred_element_type=jnp.float32
        ).astype(jnp.bfloat16)
        block = tiles - 1 - window
        low = MARGIN + block * BLOCK
        for part in range(2):
            piece = result[:, part * rows : (part + 1) * rows]
            out[target, part, low : low + BLOCK, :] = piece
            if block == 0:

                @pl.when(target > 0)
                def _():
                    out[target - 1, part, MARGIN + length :, :] = piece[:MARGIN]

            if block == tiles - 1:

                @pl.when(target < devices - 1)
                def _():
                    out[target + 1, part, 0:MARGIN, :] = piece[BLOCK - MARGIN :]


def shear_whole(own, halo, base, spare, fractions, tables):
    tiles, devices, _, rows, _ = own.shape
    forward, flipped = tables
    operands = (
        own,
        spare.astype(jnp.float32).reshape(1, rows),
        fractions.reshape(1, rows),
        forward,
        flipped,
    )
    full = lambda shape: pl.BlockSpec(shape, lambda i, *_: (0,) * len(shape))
    out = (devices, 2, tiles * BLOCK + 2 * MARGIN, rows)
    return pl.pallas_call(
        functools.partial(shear_whole_kernel, halo, devices, tiles, rows),
        grid_spec=pltpu.PrefetchScalarGridSpec(
            num_scalar_prefetch=1,
            grid=(devices,),
            in_specs=[full(x.shape) for x in operands],
            out_specs=full(out),
            scratch_shapes=[
                pltpu.VMEM((2 * halo + devices * tiles + 2, 2, rows, BLOCK), jnp.bfloat16),
                pltpu.VMEM((tiles + 1, 2, rows, BLOCK), jnp.bfloat16),
                pltpu.VMEM((rows, BLOCK), jnp.int32),
                pltpu.VMEM((rows, BLOCK), jnp.float32),
                pltpu.VMEM((rows, BLOCK), jnp.float32),
            ],
        ),
        out_shape=jax.ShapeDtypeStruct(out, jnp.bfloat16),
        compiler_params=pltpu.CompilerParams(vmem_limit_bytes=VMEM_LIMIT),
        name="shear_whole",
    )(base, *operands)


def shear_columns_kernel(
    front,
    blocks,
    length,
    rows_out,
    base,
    own,
    offsets,
    fractions,
    forward,
    inverse,
    out,
    strip,
    shifted,
    cosine,
    sine,
):
    step = pl.program_id(0)
    per_step = length // BLOCK
    total = strip.shape[1]

    @pl.when(step == 0)
    def _():
        strip[:, 0:front, :] = jnp.zeros((2, front, BLOCK), jnp.bfloat16)
        back = front + blocks * length
        strip[:, back:, :] = jnp.zeros((2, total - back, BLOCK), jnp.bfloat16)
        for block in range(blocks):
            for part in range(2):
                first = front + block * length
                strip[part, first : first + length, :] = own[block, part]
        bins = lax.broadcasted_iota(jnp.int32, (BLOCK, BLOCK), 0).astype(jnp.float32)
        sine[...], cosine[...] = sine_cosine(bins * fractions[...] * (-2.0 * np.pi / WINDOW))

    offset = jnp.broadcast_to(offsets[...], (8, BLOCK))
    row = lax.broadcasted_iota(jnp.int32, (8, BLOCK), 0) + (offset & 7)
    wraps = row >= 8
    index = row & 7

    def one_chunk(chunk):
        begin = pl.multiple_of(base[0] + chunk * BLOCK, GROUP)
        for part in range(2):
            value = strip[part, pl.ds(begin, 2 * BLOCK), :].astype(jnp.float32)
            value = value.reshape(2 * BLOCK // 8, 8, BLOCK)
            for bit in (64, 32, 16, 8):
                taken = ((offset & bit) != 0)[None]
                value = jnp.where(taken, value[bit // 8 :], value[: -(bit // 8)])
            pieces = [
                jnp.take_along_axis(value[i], index, axis=0) for i in range(BLOCK // 8 + 1)
            ]
            moved = [
                jnp.where(wraps, pieces[i + 1], pieces[i]) for i in range(BLOCK // 8)
            ]
            lanes = slice(part * BLOCK, (part + 1) * BLOCK)
            place = pl.ds(pl.multiple_of(chunk * BLOCK, BLOCK), BLOCK)
            shifted[place, lanes] = jnp.concatenate(moved, 0).astype(jnp.bfloat16)

    @pl.when(step == 0)
    def _():
        one_chunk(0)

    for window in range(per_step):
        one_chunk(step * per_step + window + 1)
    ramp_real = jnp.concatenate([cosine[...]] * 2, 1)
    ramp_imaginary = jnp.concatenate([sine[...]] * 2, 1)
    for window in range(per_step):
        first = pl.multiple_of((step * per_step + window) * BLOCK, BLOCK)
        spectrum = jnp.dot(
            forward[...], shifted[pl.ds(first, 2 * BLOCK), :], preferred_element_type=jnp.float32
        )
        real, imaginary = spectrum[:BLOCK], spectrum[BLOCK:]
        ramped = jnp.concatenate(
            [
                (real * ramp_real - imaginary * ramp_imaginary).astype(jnp.bfloat16),
                (real * ramp_imaginary + imaginary * ramp_real).astype(jnp.bfloat16),
            ],
            0,
        )
        result = jnp.dot(inverse[...], ramped, preferred_element_type=jnp.float32).astype(
            jnp.bfloat16
        )
        low = window * BLOCK
        block, within = low // rows_out, low % rows_out
        for part in range(2):
            out[block, part, within : within + BLOCK, :] = result[
                :, part * BLOCK : (part + 1) * BLOCK
            ]


def shear_columns(own, front, back, base, spare, fractions, tables, rows_out):
    blocks, _, length, _ = own.shape
    forward, inverse = tables
    operands = (
        own,
        spare.astype(jnp.int32).reshape(1, BLOCK),
        fractions.reshape(1, BLOCK),
        forward,
        inverse,
    )
    full = lambda shape: pl.BlockSpec(shape, lambda i, *_: (0,) * len(shape))
    pieces = blocks * length // rows_out
    per_step = pieces // blocks
    return pl.pallas_call(
        functools.partial(shear_columns_kernel, front, blocks, length, rows_out),
        grid_spec=pltpu.PrefetchScalarGridSpec(
            num_scalar_prefetch=1,
            grid=(blocks,),
            in_specs=[full(x.shape) for x in operands],
            out_specs=pl.BlockSpec((per_step, 2, rows_out, BLOCK), lambda i, *_: (i, 0, 0, 0)),
            scratch_shapes=[
                pltpu.VMEM((2, front + blocks * length + back, BLOCK), jnp.bfloat16),
                pltpu.VMEM((blocks * length + BLOCK, 2 * BLOCK), jnp.bfloat16),
                pltpu.VMEM((BLOCK, BLOCK), jnp.float32),
                pltpu.VMEM((BLOCK, BLOCK), jnp.float32),
            ],
        ),
        out_shape=jax.ShapeDtypeStruct((pieces, 2, rows_out, BLOCK), jnp.bfloat16),
        compiler_params=pltpu.CompilerParams(vmem_limit_bytes=VMEM_LIMIT),
        name="shear_columns",
    )(base, *operands)


def sine_cosine(angle):
    turns = jnp.round(angle * (2.0 / np.pi))
    rest = angle - turns * 1.5703125
    rest = rest - turns * 4.837512969970703125e-4
    rest = rest - turns * 7.549789954891882e-8
    square = rest * rest
    sine = rest + rest * square * (
        -1.6666654611e-1 + square * (8.3321608736e-3 - square * 1.9515295891e-4)
    )
    cosine = (
        1.0
        - 0.5 * square
        + square
        * square
        * (4.166664568298827e-2 + square * (-1.388731625493765e-3 + square * 2.443315711809948e-5))
    )
    quadrant = turns.astype(jnp.int32)
    odd = (quadrant & 1) != 0
    sine_out = jnp.where(odd, cosine, sine)
    cosine_out = jnp.where(odd, sine, cosine)
    sine_out = jnp.where((quadrant & 2) != 0, -sine_out, sine_out)
    cosine_out = jnp.where(((quadrant + 1) & 2) != 0, -cosine_out, cosine_out)
    return sine_out, cosine_out


def transmitted(rotated, wave):
    sine, cosine = sine_cosine(rotated[0].astype(jnp.float32))
    amplitude = jnp.exp(-ABSORB * rotated[1].astype(jnp.float32))
    through_real = amplitude * cosine
    through_imaginary = amplitude * sine
    wave_real = wave[0].astype(jnp.float32)
    wave_imaginary = wave[1].astype(jnp.float32)
    return (
        (wave_real * through_real - wave_imaginary * through_imaginary).astype(jnp.bfloat16),
        (wave_real * through_imaginary + wave_imaginary * through_real).astype(jnp.bfloat16),
    )


def travel_first_kernel(length, extended, *refs):
    if extended:
        body, wave, wave_top, wave_bottom, matrix, out, field = refs
        top = body.at[0, :, 0:MARGIN]
        middle = body.at[0, :, MARGIN : MARGIN + length]
        bottom = body.at[0, :, MARGIN + length :]
    else:
        body, top, bottom, wave, wave_top, wave_bottom, matrix, out, field = refs
        top, middle, bottom = top.at[0], body.at[0], bottom.at[0]
    pieces = [(0, MARGIN, top, wave_top, 0)]
    for first in range(0, length, BLOCK):
        pieces.append((MARGIN + first, BLOCK, middle, wave, first))
    pieces.append((MARGIN + length, MARGIN, bottom, wave_bottom, 0))
    for place, count, value, waves, first in pieces:
        lines = slice(first, first + count)
        parts = transmitted(
            [value[p, lines, :] for p in range(2)], [waves[p, lines, :] for p in range(2)]
        )
        for part in range(2):
            field[part, place : place + count, :] = parts[part]
    windows = [
        jnp.concatenate([field[0, m : m + WINDOW, :], field[1, m : m + WINDOW, :]], 0)
        for m in range(0, length, BLOCK)
    ]
    result = jnp.dot(
        matrix[...], jnp.concatenate(windows, 1), preferred_element_type=jnp.float32
    ).astype(jnp.bfloat16)
    for m in range(length // BLOCK):
        lanes = slice(m * BLOCK, (m + 1) * BLOCK)
        for part in range(2):
            out[0, part, lanes, :] = result[part * BLOCK : (part + 1) * BLOCK, lanes]


def travel_first(body, halos, wave, wave_halos, matrix):
    chunks = body.shape[0]
    length = wave.shape[1]
    chunk_spec = lambda x: pl.BlockSpec((1, 2, x.shape[2], BLOCK), lambda i: (i, 0, 0, 0))
    wide_spec = lambda x: pl.BlockSpec((2, x.shape[1], BLOCK), lambda i: (0, 0, i))
    return pl.pallas_call(
        functools.partial(travel_first_kernel, length, len(halos) == 0),
        grid=(chunks,),
        in_specs=[chunk_spec(body)]
        + [chunk_spec(x) for x in halos]
        + [wide_spec(x) for x in (wave, *wave_halos)]
        + [pl.BlockSpec(matrix.shape, lambda i: (0, 0))],
        out_specs=pl.BlockSpec((1, 2, length, BLOCK), lambda i: (i, 0, 0, 0)),
        out_shape=jax.ShapeDtypeStruct((chunks, 2, length, BLOCK), jnp.bfloat16),
        scratch_shapes=[pltpu.VMEM((2, length + 2 * MARGIN, BLOCK), jnp.bfloat16)],
        compiler_params=pltpu.CompilerParams(vmem_limit_bytes=VMEM_LIMIT),
        name="travel_first",
    )(body, *halos, wave, *wave_halos, matrix)


def travel_second_kernel(chunks, rows, left, body, right, matrix, out):
    parts = [[left[0, p]] + [body[m, p] for m in range(chunks)] + [right[0, p]] for p in range(2)]
    windows = [
        jnp.concatenate(parts[0][m : m + 3] + parts[1][m : m + 3], 1) for m in range(chunks)
    ]
    result = jnp.dot(
        jnp.concatenate(windows, 0), matrix[...], preferred_element_type=jnp.float32
    ).astype(jnp.bfloat16)
    for m in range(chunks):
        for part in range(2):
            out[part, :, m * BLOCK : (m + 1) * BLOCK] = result[
                m * rows : (m + 1) * rows, part * BLOCK : (part + 1) * BLOCK
            ]


def travel_second(left, body, right, matrix):
    chunks, _, length, _ = body.shape
    rows = BLOCK
    edge = pl.BlockSpec((1, 2, rows, BLOCK), lambda i: (0, 0, i, 0))
    return pl.pallas_call(
        functools.partial(travel_second_kernel, chunks, rows),
        grid=(length // rows,),
        in_specs=[
            edge,
            pl.BlockSpec((chunks, 2, rows, BLOCK), lambda i: (0, 0, i, 0)),
            edge,
            pl.BlockSpec(matrix.shape, lambda i: (0, 0)),
        ],
        out_specs=pl.BlockSpec((2, rows, chunks * BLOCK), lambda i: (0, i, 0)),
        out_shape=jax.ShapeDtypeStruct((2, length, chunks * BLOCK), jnp.bfloat16),
        compiler_params=pltpu.CompilerParams(vmem_limit_bytes=VMEM_LIMIT),
        name="travel_second",
    )(left, body, right, matrix)


def from_both_sides(first, last, axis):
    devices = lax.axis_size(axis)
    up = [(i, i + 1) for i in range(devices - 1)]
    down = [(j, i) for i, j in up]
    return lax.ppermute(last, axis, up), lax.ppermute(first, axis, down)


def halo_plan(line_count, row_devices, halo):
    share = line_count // row_devices
    reach = []
    for device in range(row_devices):
        ends = [device * share, (device + 1) * share - 1]
        most = max(
            -(-abs(2 * r + 1 - line_count) * SHIFT_X // (line_count - 1)) for r in ends
        )
        reach.append(-(-(min(most, SHIFT_X) + MARGIN) // BLOCK))
    plan = []
    for chunk in range(1, halo + 1):
        users = [d for d in range(row_devices) if reach[d] >= chunk]
        if plan and (plan[-1][2] == users or chunk % GATHERED != 1):
            plan[-1] = (plan[-1][0], chunk, plan[-1][2])
        else:
            plan.append((chunk, chunk, users))
    return plan


def exchange_chunks(piece, plan, tiles):
    columns = lax.axis_size("col")
    lefts, rights = [], []
    for near, far, users in plan:
        up = [
            (d * columns + c, d * columns + c + 1) for d in users for c in range(columns - 1)
        ]
        down = [(b, a) for a, b in up]
        lefts.append(lax.ppermute(piece(tiles - far, tiles - near + 1), ("row", "col"), up))
        rights.append(lax.ppermute(piece(near - 1, far), ("row", "col"), down))
    return lefts, rights


def group_starts(starts, group, unit):
    lines = starts.shape[-1]
    grouped = starts.reshape(*starts.shape[:-1], lines // group, group)
    base = jnp.min(grouped, -1) // unit
    spare = grouped - base[..., None] * unit
    return base.astype(jnp.int32), spare.reshape(starts.shape)


def on_device(
    volume_plane,
    wave_a,
    wave_b,
    shift_rows,
    fraction_rows,
    shift_columns,
    fraction_columns,
    travel_distance,
):
    _, line_count, width = volume_plane.shape
    row_devices, column_devices = lax.axis_size("row"), lax.axis_size("col")
    row_index, column_index = lax.axis_index("row"), lax.axis_index("col")
    tiles = width // BLOCK
    halo = -(-(SHIFT_X + MARGIN) // BLOCK)
    plan = halo_plan(line_count * row_devices, row_devices, halo)
    chunks = [(near, far) for near, far, _ in plan]

    forward, inverse = real_tables()
    half = lambda x: jnp.asarray(x, jnp.bfloat16)
    row_tables = (half(forward), half(inverse))
    column_tables = (half(forward.T), half(inverse.T))
    turned_tables = (half(forward), half(inverse[:, ::-1].T))

    lefts, rights = exchange_chunks(
        lambda a, b: volume_plane[:, :, a * BLOCK : b * BLOCK], plan, tiles
    )
    wave_a_halos = from_both_sides(wave_a[:, :MARGIN], wave_a[:, -MARGIN:], "row")
    wave_b_halos = from_both_sides(wave_b[:, :MARGIN], wave_b[:, -MARGIN:], "col")

    base_rows, spare_rows = group_starts(halo * BLOCK - MARGIN - shift_rows, GROUP, BLOCK)

    def first(view):
        return shear_tile(
            volume_plane,
            lefts,
            rights,
            chunks,
            halo,
            base_rows[view, 0],
            spare_rows[view, 0],
            fraction_rows[view, 0],
            row_tables,
        )

    front = -(-(SHIFT_Y + MARGIN) // GROUP) * GROUP
    back = front + 3 * BLOCK
    mine = lambda x: lax.dynamic_slice_in_dim(x, row_index * BLOCK, BLOCK, 1)
    base_columns, spare_columns = group_starts(front - MARGIN - mine(shift_columns), BLOCK, GROUP)
    column_fractions = mine(fraction_columns)

    def second(view, rows_out):
        spread = lax.all_to_all(first(view), "row", split_axis=0, concat_axis=0, tiled=True)
        return shear_columns(
            spread.reshape(row_devices, 2, line_count, BLOCK),
            front,
            back,
            base_columns[view] * GROUP,
            spare_columns[view],
            column_fractions[view],
            column_tables,
            rows_out,
        )

    matrices = travel_matrices(travel_distance, forward, inverse)
    real, imaginary = matrices[:, 0], matrices[:, 1]
    along_rows = jnp.concatenate(
        [
            jnp.concatenate([real, -imaginary], 1),
            jnp.concatenate([imaginary, real], 1),
        ],
        2,
    )
    along_rows = jnp.swapaxes(along_rows, 1, 2).astype(jnp.bfloat16)
    spaced = jnp.pad(matrices, ((0, 0), (0, 0), (BLOCK - MARGIN, BLOCK - MARGIN), (0, 0)))
    real, imaginary = spaced[:, 0], spaced[:, 1]
    along_columns = jnp.concatenate(
        [
            jnp.concatenate([real, -imaginary], 1),
            jnp.concatenate([imaginary, real], 1),
        ],
        2,
    ).astype(jnp.bfloat16)

    moved_b = second(1, BLOCK)
    whole = lax.all_to_all(moved_b, ("row", "col"), split_axis=0, concat_axis=0, tiled=True)
    whole = whole.reshape(row_devices, column_devices, 2, BLOCK, BLOCK)
    own_lines = lambda x: lax.dynamic_slice_in_dim(x, column_index * BLOCK, BLOCK, 0)
    groups = BLOCK // GROUP
    turned = shear_whole(
        whole,
        halo,
        lax.dynamic_slice_in_dim(base_rows[1, 1], column_index * groups, groups, 0),
        own_lines(spare_rows[1, 1]),
        own_lines(fraction_rows[1, 1]),
        turned_tables,
    )
    turned = lax.all_to_all(turned, "col", split_axis=0, concat_axis=0, tiled=True)

    moved_a = second(0, line_count)
    tile = lax.all_to_all(moved_a, "row", split_axis=0, concat_axis=0, tiled=True)
    lefts, rights = exchange_chunks(lambda a, b: tile[a:b], plan, tiles)
    rotated = shear_tile(
        tile,
        lefts,
        rights,
        chunks,
        halo,
        base_rows[0, 1],
        spare_rows[0, 1],
        fraction_rows[0, 1],
        row_tables,
    )

    half_b = travel_first(turned, (), wave_b, wave_b_halos, along_rows[1])
    left, right = from_both_sides(half_b[:1], half_b[-1:], "row")
    exit_b = travel_second(left, half_b, right, along_columns[1])

    halos = from_both_sides(rotated[:, :, :MARGIN], rotated[:, :, -MARGIN:], "row")
    half_a = travel_first(rotated, halos, wave_a, wave_a_halos, along_rows[0])
    left, right = from_both_sides(half_a[:1], half_a[-1:], "col")
    exit_a = travel_second(left, half_a, right, along_columns[0])
    return exit_a, exit_b


def swapped(value, axis, bit):
    mask = 2**bit
    pairs = [(source, source ^ mask) for source in range(lax.axis_size(axis))]
    return lax.ppermute(value, axis, pairs)


def padded_2(x, sides, width):
    for axis, dim in sides:
        devices, length = (lax.axis_size(axis), x.shape[dim])
        up = [(i, (i + 1) % devices) for i in range(devices - 1)]
        down = [(j, i) for i, j in up]
        last = lax.slice_in_dim(x, length - width, length, axis=dim)
        first = lax.slice_in_dim(x, 0, width, axis=dim)
        before = lax.ppermute(last, axis, up)
        after = lax.ppermute(first, axis, down)
        x = jnp.concatenate([before, x, after], axis=dim)
    return x


def fourier_tables(block_len, margin):
    window_len = block_len + 2 * margin
    frequency = jnp.arange(window_len, dtype=jnp.int32) - window_len // 2
    position = jnp.arange(window_len, dtype=jnp.int32)
    angles = (
        2.0
        * jnp.pi
        * jnp.mod(position[:, None] * frequency[None, :], window_len).astype(jnp.float32)
        / window_len
    )
    cosine = jnp.cos(angles)
    sines = jnp.sin(angles)
    forward = jnp.concatenate(
        [jnp.concatenate([cosine, -sines], 1), jnp.concatenate([sines, cosine], 1)], 0
    ).astype(jnp.bfloat16)
    target = jnp.arange(block_len, dtype=jnp.int32) + margin
    inverse_angle = (
        2.0
        * jnp.pi
        * jnp.mod(frequency[:, None] * target[None, :], window_len).astype(jnp.float32)
        / window_len
    )
    inverse_cosine = jnp.cos(inverse_angle) / window_len
    inverse_sine = jnp.sin(inverse_angle) / window_len
    inverse = jnp.concatenate(
        [
            jnp.concatenate([inverse_cosine, inverse_sine], 1),
            jnp.concatenate([-inverse_sine, inverse_cosine], 1),
        ],
        0,
    ).astype(jnp.bfloat16)
    return (forward, inverse, frequency.astype(jnp.float32))


def shear_ramp(fractions, frequency):
    window_len = frequency.shape[0]
    phases = -2.0 * jnp.pi / window_len * fractions[:, None] * frequency[None, :]
    nyquist = (jnp.arange(window_len) == 0)[None, :]
    ramp_real = jnp.where(nyquist, jnp.cos(jnp.pi * fractions)[:, None], jnp.cos(phases))
    ramp_imaginary = jnp.where(nyquist, 0.0, jnp.sin(phases))
    return (ramp_real, ramp_imaginary)


def travel_ramp(distance, frequency):
    window_len = frequency.shape[0]
    phases = -2.0 * jnp.pi / (window_len * window_len) * distance * frequency * frequency
    return (jnp.cos(phases)[None, :], jnp.sin(phases)[None, :])


def select_window(padded, starts, out_len):
    total_len = padded.shape[2]
    offset_range = total_len - out_len
    bit_count = max(offset_range, 1).bit_length()
    current = jnp.pad(padded, ((0, 0), (0, 0), (0, out_len + 2**bit_count - 1 - total_len)))
    for bit_number in reversed(range(bit_count)):
        stride = 2**bit_number
        kept_len = current.shape[2] - stride
        chosen = (starts // stride % 2 == 1)[None, :, None]
        current = jnp.where(
            chosen, current[:, :, stride : stride + kept_len], current[:, :, :kept_len]
        )
    return current


def line_pass(padded, extent, shifts, ramp_real, ramp_imaginary, tables):
    forward, inverse = (tables[0], tables[1])
    window_len = BLOCK + 2 * MARGIN
    line_count = padded.shape[1]
    blocks = (padded.shape[2] - 2 * extent) // BLOCK
    reach_len = blocks * BLOCK + 2 * MARGIN
    if shifts is None:
        shifted = padded
    else:
        starts = extent - MARGIN - shifts
        shifted = select_window(padded, starts, reach_len)
    middle = shifted[:, :, MARGIN : MARGIN + blocks * BLOCK].reshape(2, line_count, blocks, BLOCK)
    left_rim = shifted[:, :, : blocks * BLOCK].reshape(2, line_count, blocks, BLOCK)[..., :MARGIN]
    right_rim = shifted[:, :, 2 * MARGIN : 2 * MARGIN + blocks * BLOCK].reshape(
        2, line_count, blocks, BLOCK
    )[..., BLOCK - MARGIN :]
    windows = jnp.concatenate([left_rim, middle, right_rim], 3)
    spectrum = jnp.einsum(
        "cpms,cst->pmt",
        windows,
        forward.reshape(2, window_len, 2 * window_len),
        preferred_element_type=jnp.float32,
    )
    spec_real = spectrum[..., :window_len]
    spec_imaginary = spectrum[..., window_len:]
    factor_real = ramp_real[:, None, :]
    factor_imaginary = ramp_imaginary[:, None, :]
    ramped = jnp.concatenate(
        [
            spec_real * factor_real - spec_imaginary * factor_imaginary,
            spec_real * factor_imaginary + spec_imaginary * factor_real,
        ],
        -1,
    ).astype(jnp.bfloat16)
    result = jnp.einsum(
        "pms,scb->cpmb",
        ramped,
        inverse.reshape(2 * window_len, 2, BLOCK),
        preferred_element_type=jnp.float32,
    )
    return result.reshape(2, line_count, blocks * BLOCK).astype(jnp.bfloat16)


def single_pass(padded, extent, shifts, fractions, tables):
    ramp_real, ramp_imaginary = shear_ramp(fractions, tables[2])
    return line_pass(padded, extent, shifts, ramp_real, ramp_imaginary, tables)


def general_shear_columns(stacked, shifts, fractions, tables):
    halo_depth = SHIFT_X + MARGIN
    inputs = stacked.shape[0]
    column_devices = lax.axis_size("col")
    share = stacked.shape[2] // column_devices
    offset = lax.axis_index("col") * share
    spread = lax.all_to_all(stacked, "col", split_axis=2, concat_axis=3, tiled=True)
    padded = jnp.pad(spread, ((0, 0), (0, 0), (0, 0), (halo_depth, halo_depth)))
    row_shifts = lax.dynamic_slice_in_dim(shifts, offset, share, 1)
    row_fractions = lax.dynamic_slice_in_dim(fractions, offset, share, 1)
    sheared = jnp.stack(
        [
            single_pass(
                padded[min(0, inputs - 1)], halo_depth, row_shifts[0], row_fractions[0], tables
            )
        ]
    )
    return lax.all_to_all(sheared, "col", split_axis=3, concat_axis=2, tiled=True)


def shear_along_first(padded_lines, halo_depth, shifts, fractions, tables):
    flipped = jnp.swapaxes(padded_lines[0], 1, 2)
    moved = single_pass(flipped, halo_depth, shifts[0], fractions[0], tables)
    sheared = [jnp.swapaxes(moved, 1, 2)]
    return jnp.stack(sheared)


def shear_rows_pass(stacked, shifts, fractions, tables):
    halo_depth = SHIFT_Y + MARGIN
    row_devices = lax.axis_size("row")
    share = stacked.shape[3] // row_devices
    offset = lax.axis_index("row") * share
    spread = lax.all_to_all(stacked, "row", split_axis=3, concat_axis=2, tiled=True)
    padded = jnp.pad(spread, ((0, 0), (0, 0), (halo_depth, halo_depth), (0, 0)))
    column_shifts = lax.dynamic_slice_in_dim(shifts, offset, share, 1)
    column_fractions = lax.dynamic_slice_in_dim(fractions, offset, share, 1)
    sheared = shear_along_first(padded, halo_depth, column_shifts, column_fractions, tables)
    return lax.all_to_all(sheared, "row", split_axis=2, concat_axis=3, tiled=True)


def travel_local(extended, distance, tables):
    ramp_real, ramp_imaginary = travel_ramp(distance, tables[2])
    halfway = line_pass(extended, MARGIN, None, ramp_real, ramp_imaginary, tables)
    flipped = jnp.swapaxes(halfway, 1, 2)
    finished = line_pass(flipped, MARGIN, None, ramp_real, ramp_imaginary, tables)
    return jnp.swapaxes(finished, 1, 2)


def transmit(rotated, wave):
    phase_part = rotated[0].astype(jnp.float32)
    absorb_part = rotated[1].astype(jnp.float32)
    amplitude = jnp.exp(-ABSORB * absorb_part)
    through_real = amplitude * jnp.cos(phase_part)
    through_imaginary = amplitude * jnp.sin(phase_part)
    wave_real = wave[0].astype(jnp.float32)
    wave_imaginary = wave[1].astype(jnp.float32)
    return jnp.stack(
        [
            wave_real * through_real - wave_imaginary * through_imaginary,
            wave_real * through_imaginary + wave_imaginary * through_real,
        ]
    ).astype(jnp.bfloat16)


def general_on_device(
    volume_plane,
    wave_a,
    wave_b,
    shift_rows,
    fraction_rows,
    shift_columns,
    fraction_columns,
    travel_distance,
):
    tables = fourier_tables(BLOCK, MARGIN)
    source = volume_plane[None]
    results = []
    for member in range(2):
        stacked = general_shear_columns(
            source,
            shift_rows[member : member + 1, 0],
            fraction_rows[member : member + 1, 0],
            tables,
        )
        stacked = shear_rows_pass(
            stacked,
            shift_columns[member : member + 1],
            fraction_columns[member : member + 1],
            tables,
        )
        stacked = general_shear_columns(
            stacked,
            shift_rows[member : member + 1, 1],
            fraction_rows[member : member + 1, 1],
            tables,
        )
        results.append(stacked[0])
    view_one = results[0]
    view_two = results[1]
    turned = jnp.swapaxes(jnp.flip(view_two, 2), 1, 2)
    for bit_number in range(lax.axis_size("col").bit_length() - 1):
        turned = swapped(turned, "col", bit_number)
    product_a = transmit(view_one, wave_a)
    extended_a = padded_2(product_a, (("row", 1), ("col", 2)), MARGIN)
    exit_a = travel_local(extended_a, travel_distance[0], tables)
    product_b = transmit(turned, wave_b)
    extended_b = padded_2(product_b, (("row", 2), ("col", 1)), MARGIN)
    exit_b = travel_local(extended_b, travel_distance[1], tables)
    return (exit_a, exit_b)


def solution(mesh):
    def either(volume_plane, *rest):
        rows, width = volume_plane.shape[1:]
        fits = (
            rows == BLOCK * lax.axis_size("col")
            and width == BLOCK * lax.axis_size("row")
            and width >= SHIFT_X + MARGIN
        )
        chosen = on_device if fits else general_on_device
        return chosen(volume_plane, *rest)

    return jax.shard_map(
        either,
        mesh=mesh,
        in_specs=(
            P(None, "row", "col"),
            P(None, "row", "col"),
            P(None, "col", "row"),
            P(None, None, "row"),
            P(None, None, "row"),
            P(None, "col"),
            P(None, "col"),
            P(),
        ),
        out_specs=(P(None, "row", "col"), P(None, "col", "row")),
        check_vma=False,
    )
```

```python
import functools

import jax
import jax.numpy as jnp
import numpy as np
from jax import lax
from jax.experimental import pallas as pl
from jax.experimental.pallas import tpu as pltpu
from jax.sharding import PartitionSpec as P

BLOCK = 128
MARGIN = 32
SHIFT_X = 864
SHIFT_Y = 1728


ABSORB = 0.25

WINDOW = BLOCK + 2 * MARGIN
BINS = WINDOW // 2
GROUP = 16
PARTS = 2
VMEM_LIMIT = 56 * 1024 * 1024


def angle_table(rows, columns):
    return 2.0 * np.pi * (np.outer(rows, columns) % WINDOW) / WINDOW


def real_tables():
    position = np.arange(WINDOW)
    bins = np.arange(BINS + 1)
    target = np.arange(BLOCK) + MARGIN
    forward = np.zeros((2 * BLOCK, 2 * BLOCK), np.float32)
    forward[:WINDOW, : BINS + 1] = np.cos(angle_table(position, bins))
    forward[:WINDOW, BLOCK + 1 : BLOCK + BINS] = -np.sin(angle_table(position, bins[1:BINS]))
    weight = np.where((bins == 0) | (bins == BINS), 1.0, 2.0) / WINDOW
    inverse = np.zeros((2 * BLOCK, BLOCK), np.float32)
    inverse[: BINS + 1] = np.cos(angle_table(bins, target)) * weight[:, None]
    inverse[BLOCK + 1 : BLOCK + BINS] = (
        -np.sin(angle_table(bins[1:BINS], target)) * weight[1:BINS, None]
    )
    return forward, inverse


def travel_matrices(distance, forward, inverse):
    frequency = jnp.arange(BLOCK, dtype=jnp.float32)
    phases = -2.0 * jnp.pi / (WINDOW * WINDOW) * distance[:, None] * frequency * frequency
    ramps = jnp.stack([jnp.cos(phases), jnp.sin(phases)], 1)
    ramps = jnp.concatenate([ramps, ramps], 2)
    scaled = ramps[..., None] * jnp.asarray(inverse)
    matrices = jnp.einsum(
        "pq,vrqu->vrpu",
        jnp.asarray(forward[:WINDOW]),
        scaled,
        precision=lax.Precision.HIGHEST,
    )
    return matrices


def lane_iota(rows):
    return lax.broadcasted_iota(jnp.int32, (rows, BLOCK), 1)


def shift_lines(strip, shifted, base, base_offset, spare, windows, chunk_offset, rows):
    def one_group(group, carry):
        first = pl.multiple_of(group * GROUP, GROUP)
        lines = pl.ds(first, GROUP)
        start = base[base_offset + group] + chunk_offset
        offset = spare[lines, :]
        later = offset >= BLOCK
        lane = lane_iota(GROUP) + (offset & (BLOCK - 1))
        wraps = lane >= BLOCK
        index = lane & (BLOCK - 1)
        for part in range(2):
            here = strip[start, part, lines, :].astype(jnp.float32)
            before = None
            for i in range(windows + 2):
                following = strip[start + i + 1, part, lines, :].astype(jnp.float32)
                turned = jnp.take_along_axis(jnp.where(later, following, here), index, axis=1)
                if before is not None:
                    shifted[i - 1, part, lines, :] = jnp.where(wraps, turned, before).astype(
                        jnp.bfloat16
                    )
                before = turned
                here = following
        return carry

    lax.fori_loop(0, rows // GROUP, one_group, 0)


def ramped_lines(shifted, windows, rows, cosine, sine, forward):
    count = len(windows)
    lower = jnp.concatenate([shifted[m].reshape(2 * rows, BLOCK) for m in windows], 0)
    upper = jnp.concatenate([shifted[m + 1].reshape(2 * rows, BLOCK) for m in windows], 0)
    spectrum = jnp.dot(
        jnp.concatenate([lower, upper], 1), forward[...], preferred_element_type=jnp.float32
    )
    real = spectrum[:, :BLOCK].reshape(count * 2, rows, BLOCK)
    imaginary = spectrum[:, BLOCK:].reshape(count * 2, rows, BLOCK)
    ramp_real = cosine[...][None]
    ramp_imaginary = sine[...][None]
    ramped = jnp.concatenate(
        [
            (real * ramp_real - imaginary * ramp_imaginary).astype(jnp.bfloat16),
            (real * ramp_imaginary + imaginary * ramp_real).astype(jnp.bfloat16),
        ],
        2,
    )
    return ramped.reshape(count * 2 * rows, 2 * BLOCK)


def down_lines(vector):
    return jnp.broadcast_to(vector, (BLOCK, BLOCK)).T


def line_ramps(fractions, cosine, sine):
    bins = lane_iota(BLOCK).astype(jnp.float32)
    sine[...], cosine[...] = sine_cosine(down_lines(fractions) * bins * (-2.0 * np.pi / WINDOW))


def shear_tile_kernel(halo, tiles, rows, batch, wide, parts, base, rank, *refs):
    lefts, rights, refs = refs[:parts], refs[parts : 2 * parts], refs[2 * parts :]
    own, offsets, fractions, forward, inverse, out = refs[:6]
    strip, shifted, spare, cosine, sine = refs[6:]
    step = pl.program_id(0)
    groups = rows // GROUP
    end = halo + tiles + halo

    @pl.when(step == 0)
    def _():
        strip[end : end + 2] = jnp.zeros((2, 2, rows, BLOCK), jnp.bfloat16)

    def fill(piece, first, count):
        for i in range(count):
            if wide:
                strip[first + i] = piece[:, :, i * BLOCK : (i + 1) * BLOCK]
            else:
                strip[first + i] = piece[i]

    share = pl.num_programs(0) // parts
    for part in range(parts):

        @pl.when(step // share == part)
        def _():
            fill(lefts[part], 0, halo)
            fill(rights[part], halo + tiles, halo)

    fill(own, halo, tiles)
    spare[...] = down_lines(offsets[0]).astype(jnp.int32)
    line_ramps(fractions[0], cosine, sine)
    shift_lines(strip, shifted, base, step * groups, spare, tiles, 0, rows)
    for first in range(0, tiles, batch):
        windows = [slot ^ rank[0] for slot in range(first, first + batch)]
        ramped = ramped_lines(shifted, windows, rows, cosine, sine, forward)
        result = jnp.dot(ramped, inverse[...], preferred_element_type=jnp.float32)
        out[first : first + batch] = result.astype(jnp.bfloat16).reshape(batch, 2, rows, BLOCK)


def shear_tile(own, lefts, rights, first, halo, base, rank, spare, fractions, tables):
    wide = own.ndim == 3
    parts = len(lefts)
    part_lines = lefts[0].shape[-2]
    line_count = parts * part_lines
    tiles = own.shape[2] // BLOCK if wide else own.shape[0]
    rows = BLOCK
    share = part_lines // rows
    offset = first // rows
    forward, inverse = tables

    def piece_spec(piece, place):
        if wide:
            return pl.BlockSpec((2, rows, piece.shape[2]), lambda i, *_: (0, place(i), 0))
        return pl.BlockSpec((piece.shape[0], 2, rows, BLOCK), lambda i, *_: (0, 0, place(i), 0))

    halo_specs = [
        piece_spec(x, lambda i, part=part: jnp.clip(i - part * share, 0, share - 1))
        for x in (lefts[0], rights[0])
        for part in range(parts)
    ]
    line_spec = pl.BlockSpec((1, 1, rows), lambda i, *_: (i + offset, 0, 0))
    along = lambda x: x.astype(jnp.float32).reshape(-1, 1, rows)
    out_shape = jax.ShapeDtypeStruct((tiles, 2, line_count, BLOCK), jnp.bfloat16)
    out_spec = pl.BlockSpec((tiles, 2, rows, BLOCK), lambda i, *_: (0, 0, i, 0))
    groups = rows // GROUP
    kernel = functools.partial(
        shear_tile_kernel, halo, tiles, rows, tiles // 2 if tiles % 2 == 0 else tiles, wide, parts
    )
    return pl.pallas_call(
        kernel,
        grid_spec=pltpu.PrefetchScalarGridSpec(
            num_scalar_prefetch=2,
            grid=(line_count // rows,),
            in_specs=halo_specs
            + [piece_spec(own, lambda i: i + offset)]
            + [line_spec] * 2
            + [
                pl.BlockSpec(forward.shape, lambda i, *_: (0, 0)),
                pl.BlockSpec(inverse.shape, lambda i, *_: (0, 0)),
            ],
            out_specs=out_spec,
            scratch_shapes=[
                pltpu.VMEM((halo + tiles + halo + 2, 2, rows, BLOCK), jnp.bfloat16),
                pltpu.VMEM((tiles + 1, 2, rows, BLOCK), jnp.bfloat16),
                pltpu.VMEM((rows, BLOCK), jnp.int32),
                pltpu.VMEM((rows, BLOCK), jnp.float32),
                pltpu.VMEM((rows, BLOCK), jnp.float32),
            ],
        ),
        out_shape=out_shape,
        compiler_params=pltpu.CompilerParams(vmem_limit_bytes=VMEM_LIMIT),
        name="shear_tile",
    )(
        lax.slice_in_dim(base, offset * groups, offset * groups + line_count // GROUP),
        rank,
        *lefts,
        *rights,
        own,
        along(spare),
        along(fractions),
        forward,
        inverse,
    )


def shear_whole_kernel(
    halo,
    devices,
    tiles,
    rows,
    base,
    own,
    offsets,
    fractions,
    forward,
    flipped,
    out,
    strip,
    shifted,
    spare,
    cosine,
    sine,
):
    step = pl.program_id(0)
    chunks = devices * tiles
    length = tiles * BLOCK

    @pl.when(step == 0)
    def _():
        strip[0:halo] = jnp.zeros((halo, 2, rows, BLOCK), jnp.bfloat16)
        strip[halo + chunks :] = jnp.zeros((halo + 2, 2, rows, BLOCK), jnp.bfloat16)
        for chunk in range(chunks):
            strip[halo + chunk] = own[chunk % tiles, chunk // tiles]
        out[0, :, 0:MARGIN, :] = jnp.zeros((2, MARGIN, rows), jnp.bfloat16)
        out[devices - 1, :, MARGIN + length :, :] = jnp.zeros((2, MARGIN, rows), jnp.bfloat16)
        spare[...] = down_lines(offsets[...]).astype(jnp.int32)
        line_ramps(fractions[...], cosine, sine)

    shift_lines(strip, shifted, base, 0, spare, tiles, step * tiles, rows)
    ramped = ramped_lines(shifted, range(tiles), rows, cosine, sine, forward)
    target = devices - 1 - step
    for window in range(tiles):
        lines = ramped[window * 2 * rows : (window + 1) * 2 * rows]
        result = lax.dot_general(
            flipped[...], lines, (((1,), (1,)), ((), ())), preferred_element_type=jnp.float32
        ).astype(jnp.bfloat16)
        block = tiles - 1 - window
        low = MARGIN + block * BLOCK
        for part in range(2):
            piece = result[:, part * rows : (part + 1) * rows]
            out[target, part, low : low + BLOCK, :] = piece
            if block == 0:

                @pl.when(target > 0)
                def _():
                    out[target - 1, part, MARGIN + length :, :] = piece[:MARGIN]

            if block == tiles - 1:

                @pl.when(target < devices - 1)
                def _():
                    out[target + 1, part, 0:MARGIN, :] = piece[BLOCK - MARGIN :]


def shear_whole(own, halo, base, spare, fractions, tables):
    tiles, devices, _, rows, _ = own.shape
    forward, flipped = tables
    operands = (
        own,
        spare.astype(jnp.float32).reshape(1, rows),
        fractions.reshape(1, rows),
        forward,
        flipped,
    )
    full = lambda shape: pl.BlockSpec(shape, lambda i, *_: (0,) * len(shape))
    out = (devices, 2, tiles * BLOCK + 2 * MARGIN, rows)
    return pl.pallas_call(
        functools.partial(shear_whole_kernel, halo, devices, tiles, rows),
        grid_spec=pltpu.PrefetchScalarGridSpec(
            num_scalar_prefetch=1,
            grid=(devices,),
            in_specs=[full(x.shape) for x in operands],
            out_specs=full(out),
            scratch_shapes=[
                pltpu.VMEM((2 * halo + devices * tiles + 2, 2, rows, BLOCK), jnp.bfloat16),
                pltpu.VMEM((tiles + 1, 2, rows, BLOCK), jnp.bfloat16),
                pltpu.VMEM((rows, BLOCK), jnp.int32),
                pltpu.VMEM((rows, BLOCK), jnp.float32),
                pltpu.VMEM((rows, BLOCK), jnp.float32),
            ],
        ),
        out_shape=jax.ShapeDtypeStruct(out, jnp.bfloat16),
        compiler_params=pltpu.CompilerParams(vmem_limit_bytes=VMEM_LIMIT),
        name="shear_whole",
    )(base, *operands)


def shear_columns_kernel(front, blocks, length, rows_out, place, base, rank, *refs):
    owns, refs = refs[: len(place)], refs[len(place) :]
    offsets, fractions, forward, inverse, out, strip, shifted, cosine, sine = refs
    step = pl.program_id(0)
    per_step = length // BLOCK
    total = strip.shape[1]

    @pl.when(step == 0)
    def _():
        strip[:, 0:front, :] = jnp.zeros((2, front, BLOCK), jnp.bfloat16)
        back = front + blocks * length
        strip[:, back:, :] = jnp.zeros((2, total - back, BLOCK), jnp.bfloat16)
        for own, slots in zip(owns, place):
            count = own.shape[2]
            for i, (slot, within) in enumerate(slots):
                first = pl.multiple_of(front + (slot ^ rank[0]) * length + within, GROUP)
                for part in range(2):
                    strip[part, pl.ds(first, count), :] = own[i, part]
        bins = lax.broadcasted_iota(jnp.int32, (BLOCK, BLOCK), 0).astype(jnp.float32)
        sine[...], cosine[...] = sine_cosine(bins * fractions[...] * (-2.0 * np.pi / WINDOW))

    offset = jnp.broadcast_to(offsets[...], (8, BLOCK))
    row = lax.broadcasted_iota(jnp.int32, (8, BLOCK), 0) + (offset & 7)
    wraps = row >= 8
    index = row & 7
    block_rows = (step ^ rank[0]) * length

    def one_chunk(chunk):
        begin = pl.multiple_of(base[0] + block_rows + chunk * BLOCK, GROUP)
        for part in range(2):
            value = strip[part, pl.ds(begin, 2 * BLOCK), :].astype(jnp.float32)
            value = value.reshape(2 * BLOCK // 8, 8, BLOCK)
            for bit in (64, 32, 16, 8):
                taken = ((offset & bit) != 0)[None]
                value = jnp.where(taken, value[bit // 8 :], value[: -(bit // 8)])
            pieces = [
                jnp.take_along_axis(value[i], index, axis=0) for i in range(BLOCK // 8 + 1)
            ]
            moved = [
                jnp.where(wraps, pieces[i + 1], pieces[i]) for i in range(BLOCK // 8)
            ]
            shifted[chunk * BLOCK : (chunk + 1) * BLOCK, part * BLOCK : (part + 1) * BLOCK] = (
                jnp.concatenate(moved, 0).astype(jnp.bfloat16)
            )

    for chunk in range(per_step + 1):
        one_chunk(chunk)
    ramp_real = jnp.concatenate([cosine[...]] * 2, 1)
    ramp_imaginary = jnp.concatenate([sine[...]] * 2, 1)
    for window in range(per_step):
        low = window * BLOCK
        spectrum = jnp.dot(
            forward[...], shifted[low : low + 2 * BLOCK, :], preferred_element_type=jnp.float32
        )
        real, imaginary = spectrum[:BLOCK], spectrum[BLOCK:]
        ramped = jnp.concatenate(
            [
                (real * ramp_real - imaginary * ramp_imaginary).astype(jnp.bfloat16),
                (real * ramp_imaginary + imaginary * ramp_real).astype(jnp.bfloat16),
            ],
            0,
        )
        result = jnp.dot(inverse[...], ramped, preferred_element_type=jnp.float32).astype(
            jnp.bfloat16
        )
        block, within = low // rows_out, low % rows_out
        for part in range(2):
            out[block, part, within : within + BLOCK, :] = result[
                :, part * BLOCK : (part + 1) * BLOCK
            ]


def shear_columns(owns, place, blocks, front, back, base, rank, spare, fractions, tables, rows_out):
    length = sum(own.shape[0] * own.shape[2] for own in owns) // blocks
    forward, inverse = tables
    operands = (
        *owns,
        spare.astype(jnp.int32).reshape(1, BLOCK),
        fractions.reshape(1, BLOCK),
        forward,
        inverse,
    )
    full = lambda shape: pl.BlockSpec(shape, lambda i, *_: (0,) * len(shape))
    pieces = blocks * length // rows_out
    per_step = pieces // blocks
    return pl.pallas_call(
        functools.partial(shear_columns_kernel, front, blocks, length, rows_out, place),
        grid_spec=pltpu.PrefetchScalarGridSpec(
            num_scalar_prefetch=2,
            grid=(blocks,),
            in_specs=[full(x.shape) for x in operands],
            out_specs=pl.BlockSpec((per_step, 2, rows_out, BLOCK), lambda i, *_: (i, 0, 0, 0)),
            scratch_shapes=[
                pltpu.VMEM((2, front + blocks * length + back, BLOCK), jnp.bfloat16),
                pltpu.VMEM((length + BLOCK, 2 * BLOCK), jnp.bfloat16),
                pltpu.VMEM((BLOCK, BLOCK), jnp.float32),
                pltpu.VMEM((BLOCK, BLOCK), jnp.float32),
            ],
        ),
        out_shape=jax.ShapeDtypeStruct((pieces, 2, rows_out, BLOCK), jnp.bfloat16),
        compiler_params=pltpu.CompilerParams(vmem_limit_bytes=VMEM_LIMIT),
        name="shear_columns",
    )(base, rank, *operands)


def sine_cosine(angle):
    turns = jnp.round(angle * (2.0 / np.pi))
    rest = angle - turns * 1.5703125
    rest = rest - turns * 4.837512969970703125e-4
    rest = rest - turns * 7.549789954891882e-8
    square = rest * rest
    sine = rest + rest * square * (
        -1.6666654611e-1 + square * (8.3321608736e-3 - square * 1.9515295891e-4)
    )
    cosine = (
        1.0
        - 0.5 * square
        + square
        * square
        * (4.166664568298827e-2 + square * (-1.388731625493765e-3 + square * 2.443315711809948e-5))
    )
    quadrant = turns.astype(jnp.int32)
    odd = (quadrant & 1) != 0
    sine_out = jnp.where(odd, cosine, sine)
    cosine_out = jnp.where(odd, sine, cosine)
    sine_out = jnp.where((quadrant & 2) != 0, -sine_out, sine_out)
    cosine_out = jnp.where(((quadrant + 1) & 2) != 0, -cosine_out, cosine_out)
    return sine_out, cosine_out


def transmitted(rotated, wave):
    sine, cosine = sine_cosine(rotated[0].astype(jnp.float32))
    amplitude = jnp.exp(-ABSORB * rotated[1].astype(jnp.float32))
    through_real = amplitude * cosine
    through_imaginary = amplitude * sine
    wave_real = wave[0].astype(jnp.float32)
    wave_imaginary = wave[1].astype(jnp.float32)
    return (
        (wave_real * through_real - wave_imaginary * through_imaginary).astype(jnp.bfloat16),
        (wave_real * through_imaginary + wave_imaginary * through_real).astype(jnp.bfloat16),
    )


def travel_first_kernel(length, extended, *refs):
    if extended:
        body, wave, wave_top, wave_bottom, matrix, out, field = refs
        top = body.at[0, :, 0:MARGIN]
        middle = body.at[0, :, MARGIN : MARGIN + length]
        bottom = body.at[0, :, MARGIN + length :]
    else:
        body, top, bottom, wave, wave_top, wave_bottom, matrix, out, field = refs
        top, middle, bottom = top.at[0], body.at[0], bottom.at[0]
    pieces = [(0, MARGIN, top, wave_top, 0)]
    for first in range(0, length, BLOCK):
        pieces.append((MARGIN + first, BLOCK, middle, wave, first))
    pieces.append((MARGIN + length, MARGIN, bottom, wave_bottom, 0))
    for place, count, value, waves, first in pieces:
        lines = slice(first, first + count)
        parts = transmitted(
            [value[p, lines, :] for p in range(2)], [waves[p, lines, :] for p in range(2)]
        )
        for part in range(2):
            field[part, place : place + count, :] = parts[part]
    windows = [
        jnp.concatenate([field[0, m : m + WINDOW, :], field[1, m : m + WINDOW, :]], 0)
        for m in range(0, length, BLOCK)
    ]
    result = jnp.dot(
        matrix[...], jnp.concatenate(windows, 1), preferred_element_type=jnp.float32
    ).astype(jnp.bfloat16)
    for m in range(length // BLOCK):
        lanes = slice(m * BLOCK, (m + 1) * BLOCK)
        for part in range(2):
            out[0, part, lanes, :] = result[part * BLOCK : (part + 1) * BLOCK, lanes]


def travel_first(body, halos, wave, wave_halos, matrix):
    chunks = body.shape[0]
    length = wave.shape[1]
    chunk_spec = lambda x: pl.BlockSpec((1, 2, x.shape[2], BLOCK), lambda i: (i, 0, 0, 0))
    wide_spec = lambda x: pl.BlockSpec((2, x.shape[1], BLOCK), lambda i: (0, 0, i))
    return pl.pallas_call(
        functools.partial(travel_first_kernel, length, len(halos) == 0),
        grid=(chunks,),
        in_specs=[chunk_spec(body)]
        + [chunk_spec(x) for x in halos]
        + [wide_spec(x) for x in (wave, *wave_halos)]
        + [pl.BlockSpec(matrix.shape, lambda i: (0, 0))],
        out_specs=pl.BlockSpec((1, 2, length, BLOCK), lambda i: (i, 0, 0, 0)),
        out_shape=jax.ShapeDtypeStruct((chunks, 2, length, BLOCK), jnp.bfloat16),
        scratch_shapes=[pltpu.VMEM((2, length + 2 * MARGIN, BLOCK), jnp.bfloat16)],
        compiler_params=pltpu.CompilerParams(vmem_limit_bytes=VMEM_LIMIT),
        name="travel_first",
    )(body, *halos, wave, *wave_halos, matrix)


def travel_second_kernel(chunks, rows, left, body, right, matrix, out):
    parts = [[left[0, p]] + [body[m, p] for m in range(chunks)] + [right[0, p]] for p in range(2)]
    windows = [
        jnp.concatenate(parts[0][m : m + 3] + parts[1][m : m + 3], 1) for m in range(chunks)
    ]
    result = jnp.dot(
        jnp.concatenate(windows, 0), matrix[...], preferred_element_type=jnp.float32
    ).astype(jnp.bfloat16)
    for m in range(chunks):
        for part in range(2):
            out[part, :, m * BLOCK : (m + 1) * BLOCK] = result[
                m * rows : (m + 1) * rows, part * BLOCK : (part + 1) * BLOCK
            ]


def travel_second(left, body, right, matrix):
    chunks, _, length, _ = body.shape
    rows = BLOCK
    edge = pl.BlockSpec((1, 2, rows, BLOCK), lambda i: (0, 0, i, 0))
    return pl.pallas_call(
        functools.partial(travel_second_kernel, chunks, rows),
        grid=(length // rows,),
        in_specs=[
            edge,
            pl.BlockSpec((chunks, 2, rows, BLOCK), lambda i: (0, 0, i, 0)),
            edge,
            pl.BlockSpec(matrix.shape, lambda i: (0, 0)),
        ],
        out_specs=pl.BlockSpec((2, rows, chunks * BLOCK), lambda i: (0, i, 0)),
        out_shape=jax.ShapeDtypeStruct((2, length, chunks * BLOCK), jnp.bfloat16),
        compiler_params=pltpu.CompilerParams(vmem_limit_bytes=VMEM_LIMIT),
        name="travel_second",
    )(left, body, right, matrix)


def from_both_sides(first, last, axis):
    devices = lax.axis_size(axis)
    up = [(i, i + 1) for i in range(devices - 1)]
    down = [(j, i) for i, j in up]
    return lax.ppermute(last, axis, up), lax.ppermute(first, axis, down)


def swapped_shares(slots):
    devices = lax.axis_size("row")
    return [slots[0]] + [
        lax.ppermute(slots[s], "row", [(i, i ^ s) for i in range(devices)])
        for s in range(1, devices)
    ]


def group_starts(starts, group, unit):
    lines = starts.shape[-1]
    grouped = starts.reshape(*starts.shape[:-1], lines // group, group)
    base = jnp.min(grouped, -1) // unit
    spare = grouped - base[..., None] * unit
    return base.astype(jnp.int32), spare.reshape(starts.shape)


def on_device(
    volume_plane,
    wave_a,
    wave_b,
    shift_rows,
    fraction_rows,
    shift_columns,
    fraction_columns,
    travel_distance,
):
    _, line_count, width = volume_plane.shape
    row_devices, column_devices = lax.axis_size("row"), lax.axis_size("col")
    row_index, column_index = lax.axis_index("row"), lax.axis_index("col")
    tiles = width // BLOCK
    halo = -(-(SHIFT_X + MARGIN) // BLOCK)
    reach = halo * BLOCK

    forward, inverse = real_tables()
    half = lambda x: jnp.asarray(x, jnp.bfloat16)
    row_tables = (half(forward), half(inverse))
    column_tables = (half(forward.T), half(inverse.T))
    turned_tables = (half(forward), half(inverse[:, ::-1].T))
    in_order = jnp.zeros((1,), jnp.int32)
    by_rank = row_index.astype(jnp.int32).reshape(1)

    part_lines = line_count // PARTS
    lefts, rights = [], []
    for part in range(PARTS):
        lines = volume_plane[:, part * part_lines : (part + 1) * part_lines]
        left, right = from_both_sides(lines[:, :, :reach], lines[:, :, width - reach :], "col")
        lefts.append(left)
        rights.append(right)
    wave_a_halos = from_both_sides(wave_a[:, :MARGIN], wave_a[:, -MARGIN:], "row")
    wave_b_halos = from_both_sides(wave_b[:, :MARGIN], wave_b[:, -MARGIN:], "col")
    lefts[-1], rights[-1], wave_a_halos, wave_b_halos = lax.optimization_barrier(
        (lefts[-1], rights[-1], wave_a_halos, wave_b_halos)
    )

    base_rows, spare_rows = group_starts(reach - MARGIN - shift_rows, GROUP, BLOCK)

    front = -(-(SHIFT_Y + MARGIN) // GROUP) * GROUP
    back = front + 3 * BLOCK
    mine = lambda x: lax.dynamic_slice_in_dim(x, row_index * BLOCK, BLOCK, 1)
    base_columns, spare_columns = group_starts(front - MARGIN - mine(shift_columns), BLOCK, GROUP)
    column_fractions = mine(fraction_columns)

    def first(view, begin, lefts, rights, rank):
        return shear_tile(
            volume_plane,
            lefts,
            rights,
            begin,
            halo,
            base_rows[view, 0],
            rank,
            spare_rows[view, 0],
            fraction_rows[view, 0],
            row_tables,
        )

    def second(view, pieces, place, rank, rows_out):
        return shear_columns(
            pieces,
            place,
            row_devices,
            front,
            back,
            base_columns[view] * GROUP,
            rank,
            spare_columns[view],
            column_fractions[view],
            column_tables,
            rows_out,
        )

    matrices = travel_matrices(travel_distance, forward, inverse)
    real, imaginary = matrices[:, 0], matrices[:, 1]
    along_rows = jnp.concatenate(
        [
            jnp.concatenate([real, -imaginary], 1),
            jnp.concatenate([imaginary, real], 1),
        ],
        2,
    )
    along_rows = jnp.swapaxes(along_rows, 1, 2).astype(jnp.bfloat16)
    spaced = jnp.pad(matrices, ((0, 0), (0, 0), (BLOCK - MARGIN, BLOCK - MARGIN), (0, 0)))
    real, imaginary = spaced[:, 0], spaced[:, 1]
    along_columns = jnp.concatenate(
        [
            jnp.concatenate([real, -imaginary], 1),
            jnp.concatenate([imaginary, real], 1),
        ],
        2,
    ).astype(jnp.bfloat16)

    spread = []
    for part in range(PARTS):
        sheared = first(1, part * part_lines, lefts[part : part + 1], rights[part : part + 1], in_order)
        spread.append(lax.all_to_all(sheared, "row", split_axis=0, concat_axis=0, tiled=True))
    place = [[(b, part * part_lines) for b in range(row_devices)] for part in range(PARTS)]
    moved_b = second(1, spread, place, in_order, BLOCK)
    whole = lax.all_to_all(moved_b, ("row", "col"), split_axis=0, concat_axis=0, tiled=True)
    whole = whole.reshape(row_devices, column_devices, 2, BLOCK, BLOCK)
    own_lines = lambda x: lax.dynamic_slice_in_dim(x, column_index * BLOCK, BLOCK, 0)
    groups = BLOCK // GROUP
    turned = shear_whole(
        whole,
        halo,
        lax.dynamic_slice_in_dim(base_rows[1, 1], column_index * groups, groups, 0),
        own_lines(spare_rows[1, 1]),
        own_lines(fraction_rows[1, 1]),
        turned_tables,
    )

    slots = first(0, 0, lefts, rights, by_rank)
    pieces = swapped_shares([slots[s : s + 1] for s in range(row_devices)])
    moved_a = second(0, pieces, [[(s, 0)] for s in range(row_devices)], by_rank, line_count)
    pieces = jnp.concatenate(swapped_shares([moved_a[s : s + 1] for s in range(row_devices)]), 0)
    tile = jnp.concatenate(
        [lax.dynamic_slice_in_dim(pieces, row_index ^ d, 1, 0) for d in range(row_devices)], 0
    )
    left, right = from_both_sides(tile[:halo], tile[tiles - halo :], "col")
    rotated = shear_tile(
        tile,
        [left],
        [right],
        0,
        halo,
        base_rows[0, 1],
        in_order,
        spare_rows[0, 1],
        fraction_rows[0, 1],
        row_tables,
    )

    turned, left, right = lax.optimization_barrier((turned, left, right))
    turned = lax.all_to_all(turned, "col", split_axis=0, concat_axis=0, tiled=True)
    half_b = travel_first(turned, (), wave_b, wave_b_halos, along_rows[1])
    left, right = from_both_sides(half_b[:1], half_b[-1:], "row")
    exit_b = travel_second(left, half_b, right, along_columns[1])

    halos = from_both_sides(rotated[:, :, :MARGIN], rotated[:, :, -MARGIN:], "row")
    half_a = travel_first(rotated, halos, wave_a, wave_a_halos, along_rows[0])
    left, right = from_both_sides(half_a[:1], half_a[-1:], "col")
    exit_a = travel_second(left, half_a, right, along_columns[0])
    return exit_a, exit_b


def swapped(value, axis, bit):
    mask = 2**bit
    pairs = [(source, source ^ mask) for source in range(lax.axis_size(axis))]
    return lax.ppermute(value, axis, pairs)


def padded_2(x, sides, width):
    for axis, dim in sides:
        devices, length = (lax.axis_size(axis), x.shape[dim])
        up = [(i, (i + 1) % devices) for i in range(devices - 1)]
        down = [(j, i) for i, j in up]
        last = lax.slice_in_dim(x, length - width, length, axis=dim)
        first = lax.slice_in_dim(x, 0, width, axis=dim)
        before = lax.ppermute(last, axis, up)
        after = lax.ppermute(first, axis, down)
        x = jnp.concatenate([before, x, after], axis=dim)
    return x


def fourier_tables(block_len, margin):
    window_len = block_len + 2 * margin
    frequency = jnp.arange(window_len, dtype=jnp.int32) - window_len // 2
    position = jnp.arange(window_len, dtype=jnp.int32)
    angles = (
        2.0
        * jnp.pi
        * jnp.mod(position[:, None] * frequency[None, :], window_len).astype(jnp.float32)
        / window_len
    )
    cosine = jnp.cos(angles)
    sines = jnp.sin(angles)
    forward = jnp.concatenate(
        [jnp.concatenate([cosine, -sines], 1), jnp.concatenate([sines, cosine], 1)], 0
    ).astype(jnp.bfloat16)
    target = jnp.arange(block_len, dtype=jnp.int32) + margin
    inverse_angle = (
        2.0
        * jnp.pi
        * jnp.mod(frequency[:, None] * target[None, :], window_len).astype(jnp.float32)
        / window_len
    )
    inverse_cosine = jnp.cos(inverse_angle) / window_len
    inverse_sine = jnp.sin(inverse_angle) / window_len
    inverse = jnp.concatenate(
        [
            jnp.concatenate([inverse_cosine, inverse_sine], 1),
            jnp.concatenate([-inverse_sine, inverse_cosine], 1),
        ],
        0,
    ).astype(jnp.bfloat16)
    return (forward, inverse, frequency.astype(jnp.float32))


def shear_ramp(fractions, frequency):
    window_len = frequency.shape[0]
    phases = -2.0 * jnp.pi / window_len * fractions[:, None] * frequency[None, :]
    nyquist = (jnp.arange(window_len) == 0)[None, :]
    ramp_real = jnp.where(nyquist, jnp.cos(jnp.pi * fractions)[:, None], jnp.cos(phases))
    ramp_imaginary = jnp.where(nyquist, 0.0, jnp.sin(phases))
    return (ramp_real, ramp_imaginary)


def travel_ramp(distance, frequency):
    window_len = frequency.shape[0]
    phases = -2.0 * jnp.pi / (window_len * window_len) * distance * frequency * frequency
    return (jnp.cos(phases)[None, :], jnp.sin(phases)[None, :])


def select_window(padded, starts, out_len):
    total_len = padded.shape[2]
    offset_range = total_len - out_len
    bit_count = max(offset_range, 1).bit_length()
    current = jnp.pad(padded, ((0, 0), (0, 0), (0, out_len + 2**bit_count - 1 - total_len)))
    for bit_number in reversed(range(bit_count)):
        stride = 2**bit_number
        kept_len = current.shape[2] - stride
        chosen = (starts // stride % 2 == 1)[None, :, None]
        current = jnp.where(
            chosen, current[:, :, stride : stride + kept_len], current[:, :, :kept_len]
        )
    return current


def line_pass(padded, extent, shifts, ramp_real, ramp_imaginary, tables):
    forward, inverse = (tables[0], tables[1])
    window_len = BLOCK + 2 * MARGIN
    line_count = padded.shape[1]
    blocks = (padded.shape[2] - 2 * extent) // BLOCK
    reach_len = blocks * BLOCK + 2 * MARGIN
    if shifts is None:
        shifted = padded
    else:
        starts = extent - MARGIN - shifts
        shifted = select_window(padded, starts, reach_len)
    middle = shifted[:, :, MARGIN : MARGIN + blocks * BLOCK].reshape(2, line_count, blocks, BLOCK)
    left_rim = shifted[:, :, : blocks * BLOCK].reshape(2, line_count, blocks, BLOCK)[..., :MARGIN]
    right_rim = shifted[:, :, 2 * MARGIN : 2 * MARGIN + blocks * BLOCK].reshape(
        2, line_count, blocks, BLOCK
    )[..., BLOCK - MARGIN :]
    windows = jnp.concatenate([left_rim, middle, right_rim], 3)
    spectrum = jnp.einsum(
        "cpms,cst->pmt",
        windows,
        forward.reshape(2, window_len, 2 * window_len),
        preferred_element_type=jnp.float32,
    )
    spec_real = spectrum[..., :window_len]
    spec_imaginary = spectrum[..., window_len:]
    factor_real = ramp_real[:, None, :]
    factor_imaginary = ramp_imaginary[:, None, :]
    ramped = jnp.concatenate(
        [
            spec_real * factor_real - spec_imaginary * factor_imaginary,
            spec_real * factor_imaginary + spec_imaginary * factor_real,
        ],
        -1,
    ).astype(jnp.bfloat16)
    result = jnp.einsum(
        "pms,scb->cpmb",
        ramped,
        inverse.reshape(2 * window_len, 2, BLOCK),
        preferred_element_type=jnp.float32,
    )
    return result.reshape(2, line_count, blocks * BLOCK).astype(jnp.bfloat16)


def single_pass(padded, extent, shifts, fractions, tables):
    ramp_real, ramp_imaginary = shear_ramp(fractions, tables[2])
    return line_pass(padded, extent, shifts, ramp_real, ramp_imaginary, tables)


def general_shear_columns(stacked, shifts, fractions, tables):
    halo_depth = SHIFT_X + MARGIN
    inputs = stacked.shape[0]
    column_devices = lax.axis_size("col")
    share = stacked.shape[2] // column_devices
    offset = lax.axis_index("col") * share
    spread = lax.all_to_all(stacked, "col", split_axis=2, concat_axis=3, tiled=True)
    padded = jnp.pad(spread, ((0, 0), (0, 0), (0, 0), (halo_depth, halo_depth)))
    row_shifts = lax.dynamic_slice_in_dim(shifts, offset, share, 1)
    row_fractions = lax.dynamic_slice_in_dim(fractions, offset, share, 1)
    sheared = jnp.stack(
        [
            single_pass(
                padded[min(0, inputs - 1)], halo_depth, row_shifts[0], row_fractions[0], tables
            )
        ]
    )
    return lax.all_to_all(sheared, "col", split_axis=3, concat_axis=2, tiled=True)


def shear_along_first(padded_lines, halo_depth, shifts, fractions, tables):
    flipped = jnp.swapaxes(padded_lines[0], 1, 2)
    moved = single_pass(flipped, halo_depth, shifts[0], fractions[0], tables)
    sheared = [jnp.swapaxes(moved, 1, 2)]
    return jnp.stack(sheared)


def shear_rows_pass(stacked, shifts, fractions, tables):
    halo_depth = SHIFT_Y + MARGIN
    row_devices = lax.axis_size("row")
    share = stacked.shape[3] // row_devices
    offset = lax.axis_index("row") * share
    spread = lax.all_to_all(stacked, "row", split_axis=3, concat_axis=2, tiled=True)
    padded = jnp.pad(spread, ((0, 0), (0, 0), (halo_depth, halo_depth), (0, 0)))
    column_shifts = lax.dynamic_slice_in_dim(shifts, offset, share, 1)
    column_fractions = lax.dynamic_slice_in_dim(fractions, offset, share, 1)
    sheared = shear_along_first(padded, halo_depth, column_shifts, column_fractions, tables)
    return lax.all_to_all(sheared, "row", split_axis=2, concat_axis=3, tiled=True)


def travel_local(extended, distance, tables):
    ramp_real, ramp_imaginary = travel_ramp(distance, tables[2])
    halfway = line_pass(extended, MARGIN, None, ramp_real, ramp_imaginary, tables)
    flipped = jnp.swapaxes(halfway, 1, 2)
    finished = line_pass(flipped, MARGIN, None, ramp_real, ramp_imaginary, tables)
    return jnp.swapaxes(finished, 1, 2)


def transmit(rotated, wave):
    phase_part = rotated[0].astype(jnp.float32)
    absorb_part = rotated[1].astype(jnp.float32)
    amplitude = jnp.exp(-ABSORB * absorb_part)
    through_real = amplitude * jnp.cos(phase_part)
    through_imaginary = amplitude * jnp.sin(phase_part)
    wave_real = wave[0].astype(jnp.float32)
    wave_imaginary = wave[1].astype(jnp.float32)
    return jnp.stack(
        [
            wave_real * through_real - wave_imaginary * through_imaginary,
            wave_real * through_imaginary + wave_imaginary * through_real,
        ]
    ).astype(jnp.bfloat16)


def general_on_device(
    volume_plane,
    wave_a,
    wave_b,
    shift_rows,
    fraction_rows,
    shift_columns,
    fraction_columns,
    travel_distance,
):
    tables = fourier_tables(BLOCK, MARGIN)
    source = volume_plane[None]
    results = []
    for member in range(2):
        stacked = general_shear_columns(
            source,
            shift_rows[member : member + 1, 0],
            fraction_rows[member : member + 1, 0],
            tables,
        )
        stacked = shear_rows_pass(
            stacked,
            shift_columns[member : member + 1],
            fraction_columns[member : member + 1],
            tables,
        )
        stacked = general_shear_columns(
            stacked,
            shift_rows[member : member + 1, 1],
            fraction_rows[member : member + 1, 1],
            tables,
        )
        results.append(stacked[0])
    view_one = results[0]
    view_two = results[1]
    turned = jnp.swapaxes(jnp.flip(view_two, 2), 1, 2)
    for bit_number in range(lax.axis_size("col").bit_length() - 1):
        turned = swapped(turned, "col", bit_number)
    product_a = transmit(view_one, wave_a)
    extended_a = padded_2(product_a, (("row", 1), ("col", 2)), MARGIN)
    exit_a = travel_local(extended_a, travel_distance[0], tables)
    product_b = transmit(turned, wave_b)
    extended_b = padded_2(product_b, (("row", 2), ("col", 1)), MARGIN)
    exit_b = travel_local(extended_b, travel_distance[1], tables)
    return (exit_a, exit_b)


def solution(mesh):
    def either(volume_plane, *rest):
        rows, width = volume_plane.shape[1:]
        fits = (
            rows == BLOCK * lax.axis_size("col")
            and width == BLOCK * lax.axis_size("row")
            and width >= SHIFT_X + MARGIN
        )
        chosen = on_device if fits else general_on_device
        return chosen(volume_plane, *rest)

    return jax.shard_map(
        either,
        mesh=mesh,
        in_specs=(
            P(None, "row", "col"),
            P(None, "row", "col"),
            P(None, "col", "row"),
            P(None, None, "row"),
            P(None, None, "row"),
            P(None, "col"),
            P(None, "col"),
            P(),
        ),
        out_specs=(P(None, "row", "col"), P(None, "col", "row")),
        check_vma=False,
    )
```

```python
import functools

import jax
import jax.numpy as jnp
import numpy as np
from jax import lax
from jax.experimental import pallas as pl
from jax.experimental.pallas import tpu as pltpu
from jax.sharding import PartitionSpec as P

BLOCK = 128
MARGIN = 32
SHIFT_X = 864
SHIFT_Y = 1728


ABSORB = 0.25

WINDOW = BLOCK + 2 * MARGIN
BINS = WINDOW // 2
GROUP = 16
PARTS = 2
VMEM_LIMIT = 56 * 1024 * 1024


def angle_table(rows, columns):
    return 2.0 * np.pi * (np.outer(rows, columns) % WINDOW) / WINDOW


def real_tables():
    position = np.arange(WINDOW)
    bins = np.arange(BINS + 1)
    target = np.arange(BLOCK) + MARGIN
    forward = np.zeros((2 * BLOCK, 2 * BLOCK), np.float32)
    forward[:WINDOW, : BINS + 1] = np.cos(angle_table(position, bins))
    forward[:WINDOW, BLOCK + 1 : BLOCK + BINS] = -np.sin(angle_table(position, bins[1:BINS]))
    weight = np.where((bins == 0) | (bins == BINS), 1.0, 2.0) / WINDOW
    inverse = np.zeros((2 * BLOCK, BLOCK), np.float32)
    inverse[: BINS + 1] = np.cos(angle_table(bins, target)) * weight[:, None]
    inverse[BLOCK + 1 : BLOCK + BINS] = (
        -np.sin(angle_table(bins[1:BINS], target)) * weight[1:BINS, None]
    )
    return forward, inverse


def travel_matrices(distance, forward, inverse):
    frequency = jnp.arange(BLOCK, dtype=jnp.float32)
    phases = -2.0 * jnp.pi / (WINDOW * WINDOW) * distance[:, None] * frequency * frequency
    ramps = jnp.stack([jnp.cos(phases), jnp.sin(phases)], 1)
    ramps = jnp.concatenate([ramps, ramps], 2)
    scaled = ramps[..., None] * jnp.asarray(inverse)
    matrices = jnp.einsum(
        "pq,vrqu->vrpu",
        jnp.asarray(forward[:WINDOW]),
        scaled,
        precision=lax.Precision.HIGHEST,
    )
    return matrices


def lane_iota(rows):
    return lax.broadcasted_iota(jnp.int32, (rows, BLOCK), 1)


def shift_lines(strip, shifted, base, base_offset, spare, windows, chunk_offset, rows):
    def one_group(group, carry):
        first = pl.multiple_of(group * GROUP, GROUP)
        lines = pl.ds(first, GROUP)
        start = base[base_offset + group] + chunk_offset
        offset = spare[lines, :]
        later = offset >= BLOCK
        lane = lane_iota(GROUP) + (offset & (BLOCK - 1))
        wraps = lane >= BLOCK
        index = lane & (BLOCK - 1)
        for part in range(2):
            here = strip[start, part, lines, :].astype(jnp.float32)
            before = None
            for i in range(windows + 2):
                following = strip[start + i + 1, part, lines, :].astype(jnp.float32)
                turned = jnp.take_along_axis(jnp.where(later, following, here), index, axis=1)
                if before is not None:
                    shifted[i - 1, part, lines, :] = jnp.where(wraps, turned, before).astype(
                        jnp.bfloat16
                    )
                before = turned
                here = following
        return carry

    lax.fori_loop(0, rows // GROUP, one_group, 0)


def ramped_lines(shifted, windows, rows, cosine, sine, forward):
    count = len(windows)
    lower = jnp.concatenate([shifted[m].reshape(2 * rows, BLOCK) for m in windows], 0)
    upper = jnp.concatenate([shifted[m + 1].reshape(2 * rows, BLOCK) for m in windows], 0)
    spectrum = jnp.dot(
        jnp.concatenate([lower, upper], 1), forward[...], preferred_element_type=jnp.float32
    )
    real = spectrum[:, :BLOCK].reshape(count * 2, rows, BLOCK)
    imaginary = spectrum[:, BLOCK:].reshape(count * 2, rows, BLOCK)
    ramp_real = cosine[...][None]
    ramp_imaginary = sine[...][None]
    ramped = jnp.concatenate(
        [
            (real * ramp_real - imaginary * ramp_imaginary).astype(jnp.bfloat16),
            (real * ramp_imaginary + imaginary * ramp_real).astype(jnp.bfloat16),
        ],
        2,
    )
    return ramped.reshape(count * 2 * rows, 2 * BLOCK)


def down_lines(vector):
    return jnp.broadcast_to(vector, (BLOCK, BLOCK)).T


def line_ramps(fractions, cosine, sine):
    bins = lane_iota(BLOCK).astype(jnp.float32)
    sine[...], cosine[...] = sine_cosine(down_lines(fractions) * bins * (-2.0 * np.pi / WINDOW))


def shear_tile_kernel(halo, tiles, rows, batch, wide, parts, base, rank, *refs):
    lefts, rights, refs = refs[:parts], refs[parts : 2 * parts], refs[2 * parts :]
    own, offsets, fractions, forward, inverse, out = refs[:6]
    strip, shifted, spare, cosine, sine = refs[6:]
    step = pl.program_id(0)
    groups = rows // GROUP
    end = halo + tiles + halo

    @pl.when(step == 0)
    def _():
        strip[end : end + 2] = jnp.zeros((2, 2, rows, BLOCK), jnp.bfloat16)

    def fill(piece, first, count):
        for i in range(count):
            if wide:
                strip[first + i] = piece[:, :, i * BLOCK : (i + 1) * BLOCK]
            else:
                strip[first + i] = piece[i]

    share = pl.num_programs(0) // parts
    for part in range(parts):

        @pl.when(step // share == part)
        def _():
            fill(lefts[part], 0, halo)
            fill(rights[part], halo + tiles, halo)

    fill(own, halo, tiles)
    spare[...] = down_lines(offsets[0]).astype(jnp.int32)
    line_ramps(fractions[0], cosine, sine)
    shift_lines(strip, shifted, base, step * groups, spare, tiles, 0, rows)
    for first in range(0, tiles, batch):
        windows = [slot ^ rank[0] for slot in range(first, first + batch)]
        ramped = ramped_lines(shifted, windows, rows, cosine, sine, forward)
        result = jnp.dot(ramped, inverse[...], preferred_element_type=jnp.float32)
        out[first : first + batch] = result.astype(jnp.bfloat16).reshape(batch, 2, rows, BLOCK)


def shear_tile(own, lefts, rights, first, halo, base, rank, spare, fractions, tables):
    wide = own.ndim == 3
    parts = len(lefts)
    part_lines = lefts[0].shape[-2]
    line_count = parts * part_lines
    tiles = own.shape[2] // BLOCK if wide else own.shape[0]
    rows = BLOCK
    share = part_lines // rows
    offset = first // rows
    forward, inverse = tables

    def piece_spec(piece, place):
        if wide:
            return pl.BlockSpec((2, rows, piece.shape[2]), lambda i, *_: (0, place(i), 0))
        return pl.BlockSpec((piece.shape[0], 2, rows, BLOCK), lambda i, *_: (0, 0, place(i), 0))

    halo_specs = [
        piece_spec(x, lambda i, part=part: jnp.clip(i - part * share, 0, share - 1))
        for x in (lefts[0], rights[0])
        for part in range(parts)
    ]
    line_spec = pl.BlockSpec((1, 1, rows), lambda i, *_: (i + offset, 0, 0))
    along = lambda x: x.astype(jnp.float32).reshape(-1, 1, rows)
    out_shape = jax.ShapeDtypeStruct((tiles, 2, line_count, BLOCK), jnp.bfloat16)
    out_spec = pl.BlockSpec((tiles, 2, rows, BLOCK), lambda i, *_: (0, 0, i, 0))
    groups = rows // GROUP
    kernel = functools.partial(
        shear_tile_kernel, halo, tiles, rows, tiles // 2 if tiles % 2 == 0 else tiles, wide, parts
    )
    return pl.pallas_call(
        kernel,
        grid_spec=pltpu.PrefetchScalarGridSpec(
            num_scalar_prefetch=2,
            grid=(line_count // rows,),
            in_specs=halo_specs
            + [piece_spec(own, lambda i: i + offset)]
            + [line_spec] * 2
            + [
                pl.BlockSpec(forward.shape, lambda i, *_: (0, 0)),
                pl.BlockSpec(inverse.shape, lambda i, *_: (0, 0)),
            ],
            out_specs=out_spec,
            scratch_shapes=[
                pltpu.VMEM((halo + tiles + halo + 2, 2, rows, BLOCK), jnp.bfloat16),
                pltpu.VMEM((tiles + 1, 2, rows, BLOCK), jnp.bfloat16),
                pltpu.VMEM((rows, BLOCK), jnp.int32),
                pltpu.VMEM((rows, BLOCK), jnp.float32),
                pltpu.VMEM((rows, BLOCK), jnp.float32),
            ],
        ),
        out_shape=out_shape,
        compiler_params=pltpu.CompilerParams(vmem_limit_bytes=VMEM_LIMIT),
        name="shear_tile",
    )(
        lax.slice_in_dim(base, offset * groups, offset * groups + line_count // GROUP),
        rank,
        *lefts,
        *rights,
        own,
        along(spare),
        along(fractions),
        forward,
        inverse,
    )


def shear_whole_kernel(
    halo,
    devices,
    tiles,
    rows,
    base,
    own,
    offsets,
    fractions,
    forward,
    flipped,
    out,
    strip,
    shifted,
    spare,
    cosine,
    sine,
):
    step = pl.program_id(0)
    chunks = devices * tiles
    length = tiles * BLOCK

    @pl.when(step == 0)
    def _():
        strip[0:halo] = jnp.zeros((halo, 2, rows, BLOCK), jnp.bfloat16)
        strip[halo + chunks :] = jnp.zeros((halo + 2, 2, rows, BLOCK), jnp.bfloat16)
        for chunk in range(chunks):
            strip[halo + chunk] = own[chunk % tiles, chunk // tiles]
        out[0, :, 0:MARGIN, :] = jnp.zeros((2, MARGIN, rows), jnp.bfloat16)
        out[devices - 1, :, MARGIN + length :, :] = jnp.zeros((2, MARGIN, rows), jnp.bfloat16)
        spare[...] = down_lines(offsets[...]).astype(jnp.int32)
        line_ramps(fractions[...], cosine, sine)

    shift_lines(strip, shifted, base, 0, spare, tiles, step * tiles, rows)
    ramped = ramped_lines(shifted, range(tiles), rows, cosine, sine, forward)
    target = devices - 1 - step
    for window in range(tiles):
        lines = ramped[window * 2 * rows : (window + 1) * 2 * rows]
        result = lax.dot_general(
            flipped[...], lines, (((1,), (1,)), ((), ())), preferred_element_type=jnp.float32
        ).astype(jnp.bfloat16)
        block = tiles - 1 - window
        low = MARGIN + block * BLOCK
        for part in range(2):
            piece = result[:, part * rows : (part + 1) * rows]
            out[target, part, low : low + BLOCK, :] = piece
            if block == 0:

                @pl.when(target > 0)
                def _():
                    out[target - 1, part, MARGIN + length :, :] = piece[:MARGIN]

            if block == tiles - 1:

                @pl.when(target < devices - 1)
                def _():
                    out[target + 1, part, 0:MARGIN, :] = piece[BLOCK - MARGIN :]


def shear_whole(own, halo, base, spare, fractions, tables):
    tiles, devices, _, rows, _ = own.shape
    forward, flipped = tables
    operands = (
        own,
        spare.astype(jnp.float32).reshape(1, rows),
        fractions.reshape(1, rows),
        forward,
        flipped,
    )
    full = lambda shape: pl.BlockSpec(shape, lambda i, *_: (0,) * len(shape))
    out = (devices, 2, tiles * BLOCK + 2 * MARGIN, rows)
    return pl.pallas_call(
        functools.partial(shear_whole_kernel, halo, devices, tiles, rows),
        grid_spec=pltpu.PrefetchScalarGridSpec(
            num_scalar_prefetch=1,
            grid=(devices,),
            in_specs=[full(x.shape) for x in operands],
            out_specs=full(out),
            scratch_shapes=[
                pltpu.VMEM((2 * halo + devices * tiles + 2, 2, rows, BLOCK), jnp.bfloat16),
                pltpu.VMEM((tiles + 1, 2, rows, BLOCK), jnp.bfloat16),
                pltpu.VMEM((rows, BLOCK), jnp.int32),
                pltpu.VMEM((rows, BLOCK), jnp.float32),
                pltpu.VMEM((rows, BLOCK), jnp.float32),
            ],
        ),
        out_shape=jax.ShapeDtypeStruct(out, jnp.bfloat16),
        compiler_params=pltpu.CompilerParams(vmem_limit_bytes=VMEM_LIMIT),
        name="shear_whole",
    )(base, *operands)


def shear_columns_kernel(front, blocks, length, rows_out, place, base, rank, *refs):
    owns, refs = refs[: len(place)], refs[len(place) :]
    offsets, fractions, forward, inverse, out, strip, shifted, cosine, sine = refs
    step = pl.program_id(0)
    per_step = length // BLOCK
    total = strip.shape[1]

    @pl.when(step == 0)
    def _():
        strip[:, 0:front, :] = jnp.zeros((2, front, BLOCK), jnp.bfloat16)
        back = front + blocks * length
        strip[:, back:, :] = jnp.zeros((2, total - back, BLOCK), jnp.bfloat16)
        for own, slots in zip(owns, place):
            count = own.shape[2]
            for i, (slot, within) in enumerate(slots):
                first = pl.multiple_of(front + (slot ^ rank[0]) * length + within, GROUP)
                for part in range(2):
                    strip[part, pl.ds(first, count), :] = own[i, part]
        bins = lax.broadcasted_iota(jnp.int32, (BLOCK, BLOCK), 0).astype(jnp.float32)
        sine[...], cosine[...] = sine_cosine(bins * fractions[...] * (-2.0 * np.pi / WINDOW))

    offset = jnp.broadcast_to(offsets[...], (8, BLOCK))
    row = lax.broadcasted_iota(jnp.int32, (8, BLOCK), 0) + (offset & 7)
    wraps = row >= 8
    index = row & 7
    block_rows = (step ^ rank[0]) * length

    def one_chunk(chunk):
        begin = pl.multiple_of(base[0] + block_rows + chunk * BLOCK, GROUP)
        for part in range(2):
            value = strip[part, pl.ds(begin, 2 * BLOCK), :].astype(jnp.float32)
            value = value.reshape(2 * BLOCK // 8, 8, BLOCK)
            for bit in (64, 32, 16, 8):
                taken = ((offset & bit) != 0)[None]
                value = jnp.where(taken, value[bit // 8 :], value[: -(bit // 8)])
            pieces = [
                jnp.take_along_axis(value[i], index, axis=0) for i in range(BLOCK // 8 + 1)
            ]
            moved = [
                jnp.where(wraps, pieces[i + 1], pieces[i]) for i in range(BLOCK // 8)
            ]
            shifted[chunk * BLOCK : (chunk + 1) * BLOCK, part * BLOCK : (part + 1) * BLOCK] = (
                jnp.concatenate(moved, 0).astype(jnp.bfloat16)
            )

    for chunk in range(per_step + 1):
        one_chunk(chunk)
    ramp_real = jnp.concatenate([cosine[...]] * 2, 1)
    ramp_imaginary = jnp.concatenate([sine[...]] * 2, 1)
    for window in range(per_step):
        low = window * BLOCK
        spectrum = jnp.dot(
            forward[...], shifted[low : low + 2 * BLOCK, :], preferred_element_type=jnp.float32
        )
        real, imaginary = spectrum[:BLOCK], spectrum[BLOCK:]
        ramped = jnp.concatenate(
            [
                (real * ramp_real - imaginary * ramp_imaginary).astype(jnp.bfloat16),
                (real * ramp_imaginary + imaginary * ramp_real).astype(jnp.bfloat16),
            ],
            0,
        )
        result = jnp.dot(inverse[...], ramped, preferred_element_type=jnp.float32).astype(
            jnp.bfloat16
        )
        block, within = low // rows_out, low % rows_out
        for part in range(2):
            out[block, part, within : within + BLOCK, :] = result[
                :, part * BLOCK : (part + 1) * BLOCK
            ]


def shear_columns(owns, place, blocks, front, back, base, rank, spare, fractions, tables, rows_out):
    length = sum(own.shape[0] * own.shape[2] for own in owns) // blocks
    forward, inverse = tables
    operands = (
        *owns,
        spare.astype(jnp.int32).reshape(1, BLOCK),
        fractions.reshape(1, BLOCK),
        forward,
        inverse,
    )
    full = lambda shape: pl.BlockSpec(shape, lambda i, *_: (0,) * len(shape))
    pieces = blocks * length // rows_out
    per_step = pieces // blocks
    return pl.pallas_call(
        functools.partial(shear_columns_kernel, front, blocks, length, rows_out, place),
        grid_spec=pltpu.PrefetchScalarGridSpec(
            num_scalar_prefetch=2,
            grid=(blocks,),
            in_specs=[full(x.shape) for x in operands],
            out_specs=pl.BlockSpec((per_step, 2, rows_out, BLOCK), lambda i, *_: (i, 0, 0, 0)),
            scratch_shapes=[
                pltpu.VMEM((2, front + blocks * length + back, BLOCK), jnp.bfloat16),
                pltpu.VMEM((length + BLOCK, 2 * BLOCK), jnp.bfloat16),
                pltpu.VMEM((BLOCK, BLOCK), jnp.float32),
                pltpu.VMEM((BLOCK, BLOCK), jnp.float32),
            ],
        ),
        out_shape=jax.ShapeDtypeStruct((pieces, 2, rows_out, BLOCK), jnp.bfloat16),
        compiler_params=pltpu.CompilerParams(vmem_limit_bytes=VMEM_LIMIT),
        name="shear_columns",
    )(base, rank, *operands)


def sine_cosine(angle):
    turns = jnp.round(angle * (2.0 / np.pi))
    rest = angle - turns * 1.5703125
    rest = rest - turns * 4.837512969970703125e-4
    rest = rest - turns * 7.549789954891882e-8
    square = rest * rest
    sine = rest + rest * square * (
        -1.6666654611e-1 + square * (8.3321608736e-3 - square * 1.9515295891e-4)
    )
    cosine = (
        1.0
        - 0.5 * square
        + square
        * square
        * (4.166664568298827e-2 + square * (-1.388731625493765e-3 + square * 2.443315711809948e-5))
    )
    quadrant = turns.astype(jnp.int32)
    odd = (quadrant & 1) != 0
    sine_out = jnp.where(odd, cosine, sine)
    cosine_out = jnp.where(odd, sine, cosine)
    sine_out = jnp.where((quadrant & 2) != 0, -sine_out, sine_out)
    cosine_out = jnp.where(((quadrant + 1) & 2) != 0, -cosine_out, cosine_out)
    return sine_out, cosine_out


def transmitted(rotated, wave):
    sine, cosine = sine_cosine(rotated[0].astype(jnp.float32))
    amplitude = jnp.exp(-ABSORB * rotated[1].astype(jnp.float32))
    through_real = amplitude * cosine
    through_imaginary = amplitude * sine
    wave_real = wave[0].astype(jnp.float32)
    wave_imaginary = wave[1].astype(jnp.float32)
    return (
        (wave_real * through_real - wave_imaginary * through_imaginary).astype(jnp.bfloat16),
        (wave_real * through_imaginary + wave_imaginary * through_real).astype(jnp.bfloat16),
    )


def travel_first_kernel(length, extended, *refs):
    if extended:
        body, wave, wave_top, wave_bottom, matrix, out, field = refs
        top = body.at[0, :, 0:MARGIN]
        middle = body.at[0, :, MARGIN : MARGIN + length]
        bottom = body.at[0, :, MARGIN + length :]
    else:
        body, top, bottom, wave, wave_top, wave_bottom, matrix, out, field = refs
        top, middle, bottom = top.at[0], body.at[0], bottom.at[0]
    pieces = [(0, MARGIN, top, wave_top, 0)]
    for first in range(0, length, BLOCK):
        pieces.append((MARGIN + first, BLOCK, middle, wave, first))
    pieces.append((MARGIN + length, MARGIN, bottom, wave_bottom, 0))
    for place, count, value, waves, first in pieces:
        lines = slice(first, first + count)
        parts = transmitted(
            [value[p, lines, :] for p in range(2)], [waves[p, lines, :] for p in range(2)]
        )
        for part in range(2):
            field[part, place : place + count, :] = parts[part]
    windows = [
        jnp.concatenate([field[0, m : m + WINDOW, :], field[1, m : m + WINDOW, :]], 0)
        for m in range(0, length, BLOCK)
    ]
    result = jnp.dot(
        matrix[...], jnp.concatenate(windows, 1), preferred_element_type=jnp.float32
    ).astype(jnp.bfloat16)
    for m in range(length // BLOCK):
        lanes = slice(m * BLOCK, (m + 1) * BLOCK)
        for part in range(2):
            out[0, part, lanes, :] = result[part * BLOCK : (part + 1) * BLOCK, lanes]


def travel_first(body, halos, wave, wave_halos, matrix):
    chunks = body.shape[0]
    length = wave.shape[1]
    chunk_spec = lambda x: pl.BlockSpec((1, 2, x.shape[2], BLOCK), lambda i: (i, 0, 0, 0))
    wide_spec = lambda x: pl.BlockSpec((2, x.shape[1], BLOCK), lambda i: (0, 0, i))
    return pl.pallas_call(
        functools.partial(travel_first_kernel, length, len(halos) == 0),
        grid=(chunks,),
        in_specs=[chunk_spec(body)]
        + [chunk_spec(x) for x in halos]
        + [wide_spec(x) for x in (wave, *wave_halos)]
        + [pl.BlockSpec(matrix.shape, lambda i: (0, 0))],
        out_specs=pl.BlockSpec((1, 2, length, BLOCK), lambda i: (i, 0, 0, 0)),
        out_shape=jax.ShapeDtypeStruct((chunks, 2, length, BLOCK), jnp.bfloat16),
        scratch_shapes=[pltpu.VMEM((2, length + 2 * MARGIN, BLOCK), jnp.bfloat16)],
        compiler_params=pltpu.CompilerParams(vmem_limit_bytes=VMEM_LIMIT),
        name="travel_first",
    )(body, *halos, wave, *wave_halos, matrix)


def travel_second_kernel(chunks, rows, left, body, right, matrix, out):
    parts = [[left[0, p]] + [body[m, p] for m in range(chunks)] + [right[0, p]] for p in range(2)]
    windows = [
        jnp.concatenate(parts[0][m : m + 3] + parts[1][m : m + 3], 1) for m in range(chunks)
    ]
    result = jnp.dot(
        jnp.concatenate(windows, 0), matrix[...], preferred_element_type=jnp.float32
    ).astype(jnp.bfloat16)
    for m in range(chunks):
        for part in range(2):
            out[part, :, m * BLOCK : (m + 1) * BLOCK] = result[
                m * rows : (m + 1) * rows, part * BLOCK : (part + 1) * BLOCK
            ]


def travel_second(left, body, right, matrix):
    chunks, _, length, _ = body.shape
    rows = BLOCK
    edge = pl.BlockSpec((1, 2, rows, BLOCK), lambda i: (0, 0, i, 0))
    return pl.pallas_call(
        functools.partial(travel_second_kernel, chunks, rows),
        grid=(length // rows,),
        in_specs=[
            edge,
            pl.BlockSpec((chunks, 2, rows, BLOCK), lambda i: (0, 0, i, 0)),
            edge,
            pl.BlockSpec(matrix.shape, lambda i: (0, 0)),
        ],
        out_specs=pl.BlockSpec((2, rows, chunks * BLOCK), lambda i: (0, i, 0)),
        out_shape=jax.ShapeDtypeStruct((2, length, chunks * BLOCK), jnp.bfloat16),
        compiler_params=pltpu.CompilerParams(vmem_limit_bytes=VMEM_LIMIT),
        name="travel_second",
    )(left, body, right, matrix)


def from_both_sides(first, last, axis):
    devices = lax.axis_size(axis)
    up = [(i, i + 1) for i in range(devices - 1)]
    down = [(j, i) for i, j in up]
    return lax.ppermute(last, axis, up), lax.ppermute(first, axis, down)


def after(value, *others):
    return lax.optimization_barrier((value, others))[0]


def ordered_kernel(rank, *refs):
    count = len(refs) - 2
    out, arrived = refs[count], refs[count + 1]
    copies = [
        pltpu.make_async_copy(refs[s], out.at[pl.ds(s ^ rank[0], 1)], arrived.at[s])
        for s in range(count)
    ]
    for copy in copies:
        copy.start()
    for copy in copies:
        copy.wait()


def ordered(pieces, rank):
    count = len(pieces)
    shape = (count, *pieces[0].shape[1:])
    anywhere = pl.BlockSpec(memory_space=pl.ANY)
    return pl.pallas_call(
        ordered_kernel,
        grid_spec=pltpu.PrefetchScalarGridSpec(
            num_scalar_prefetch=1,
            grid=(1,),
            in_specs=[anywhere] * count,
            out_specs=anywhere,
            scratch_shapes=[pltpu.SemaphoreType.DMA((count,))],
        ),
        out_shape=jax.ShapeDtypeStruct(shape, pieces[0].dtype),
        name="ordered",
    )(rank, *pieces)


def swapped_shares(slots):
    devices = lax.axis_size("row")
    return [slots[0]] + [
        lax.ppermute(slots[s], "row", [(i, i ^ s) for i in range(devices)])
        for s in range(1, devices)
    ]


def group_starts(starts, group, unit):
    lines = starts.shape[-1]
    grouped = starts.reshape(*starts.shape[:-1], lines // group, group)
    base = jnp.min(grouped, -1) // unit
    spare = grouped - base[..., None] * unit
    return base.astype(jnp.int32), spare.reshape(starts.shape)


def on_device(
    volume_plane,
    wave_a,
    wave_b,
    shift_rows,
    fraction_rows,
    shift_columns,
    fraction_columns,
    travel_distance,
):
    _, line_count, width = volume_plane.shape
    row_devices, column_devices = lax.axis_size("row"), lax.axis_size("col")
    row_index, column_index = lax.axis_index("row"), lax.axis_index("col")
    tiles = width // BLOCK
    halo = -(-(SHIFT_X + MARGIN) // BLOCK)
    reach = halo * BLOCK

    forward, inverse = real_tables()
    half = lambda x: jnp.asarray(x, jnp.bfloat16)
    row_tables = (half(forward), half(inverse))
    column_tables = (half(forward.T), half(inverse.T))
    turned_tables = (half(forward), half(inverse[:, ::-1].T))
    in_order = jnp.zeros((1,), jnp.int32)
    by_rank = row_index.astype(jnp.int32).reshape(1)

    part_lines = line_count // PARTS
    lefts, rights = [], []
    for part in range(PARTS):
        lines = volume_plane[:, part * part_lines : (part + 1) * part_lines]
        left, right = from_both_sides(lines[:, :, :reach], lines[:, :, width - reach :], "col")
        lefts.append(left)
        rights.append(right)
    wave_a_halos = from_both_sides(wave_a[:, :MARGIN], wave_a[:, -MARGIN:], "row")
    wave_b_halos = from_both_sides(wave_b[:, :MARGIN], wave_b[:, -MARGIN:], "col")

    base_rows, spare_rows = group_starts(reach - MARGIN - shift_rows, GROUP, BLOCK)

    front = -(-(SHIFT_Y + MARGIN) // GROUP) * GROUP
    back = front + 3 * BLOCK
    mine = lambda x: lax.dynamic_slice_in_dim(x, row_index * BLOCK, BLOCK, 1)
    base_columns, spare_columns = group_starts(front - MARGIN - mine(shift_columns), BLOCK, GROUP)
    column_fractions = mine(fraction_columns)

    def first(view, begin, lefts, rights, rank):
        return shear_tile(
            volume_plane,
            lefts,
            rights,
            begin,
            halo,
            base_rows[view, 0],
            rank,
            spare_rows[view, 0],
            fraction_rows[view, 0],
            row_tables,
        )

    def second(view, pieces, place, rank, rows_out):
        return shear_columns(
            pieces,
            place,
            row_devices,
            front,
            back,
            base_columns[view] * GROUP,
            rank,
            spare_columns[view],
            column_fractions[view],
            column_tables,
            rows_out,
        )

    matrices = travel_matrices(travel_distance, forward, inverse)
    real, imaginary = matrices[:, 0], matrices[:, 1]
    along_rows = jnp.concatenate(
        [
            jnp.concatenate([real, -imaginary], 1),
            jnp.concatenate([imaginary, real], 1),
        ],
        2,
    )
    along_rows = jnp.swapaxes(along_rows, 1, 2).astype(jnp.bfloat16)
    spaced = jnp.pad(matrices, ((0, 0), (0, 0), (BLOCK - MARGIN, BLOCK - MARGIN), (0, 0)))
    real, imaginary = spaced[:, 0], spaced[:, 1]
    along_columns = jnp.concatenate(
        [
            jnp.concatenate([real, -imaginary], 1),
            jnp.concatenate([imaginary, real], 1),
        ],
        2,
    ).astype(jnp.bfloat16)

    spread, sheared = [], ()
    for part in range(PARTS):
        left, right = after((lefts[part], rights[part]), sheared)
        sheared = first(1, part * part_lines, [left], [right], in_order)
        spread.append(lax.all_to_all(sheared, "row", split_axis=0, concat_axis=0, tiled=True))
    spread, wave_a_halos, wave_b_halos = lax.optimization_barrier(
        (spread, wave_a_halos, wave_b_halos)
    )
    place = [[(b, part * part_lines) for b in range(row_devices)] for part in range(PARTS)]
    moved_b = second(1, spread, place, in_order, BLOCK)
    whole = lax.all_to_all(moved_b, ("row", "col"), split_axis=0, concat_axis=0, tiled=True)
    whole = whole.reshape(row_devices, column_devices, 2, BLOCK, BLOCK)
    own_lines = lambda x: lax.dynamic_slice_in_dim(x, column_index * BLOCK, BLOCK, 0)
    groups = BLOCK // GROUP
    turned = shear_whole(
        whole,
        halo,
        lax.dynamic_slice_in_dim(base_rows[1, 1], column_index * groups, groups, 0),
        own_lines(spare_rows[1, 1]),
        own_lines(fraction_rows[1, 1]),
        turned_tables,
    )

    lefts, rights = after((lefts, rights), sheared)
    slots = first(0, 0, lefts, rights, by_rank)
    pieces = swapped_shares([slots[s : s + 1] for s in range(row_devices)])
    pieces = after(pieces, moved_b)
    moved_a = second(0, pieces, [[(s, 0)] for s in range(row_devices)], by_rank, line_count)
    pieces = swapped_shares([moved_a[s : s + 1] for s in range(row_devices)])
    tile = ordered(pieces, by_rank)
    left, right = from_both_sides(tile[:halo], tile[tiles - halo :], "col")
    rotated = shear_tile(
        tile,
        [left],
        [right],
        0,
        halo,
        base_rows[0, 1],
        in_order,
        spare_rows[0, 1],
        fraction_rows[0, 1],
        row_tables,
    )

    turned, left, right = lax.optimization_barrier((turned, left, right))
    turned = lax.all_to_all(turned, "col", split_axis=0, concat_axis=0, tiled=True)
    half_b = travel_first(turned, (), wave_b, wave_b_halos, along_rows[1])
    left, right = from_both_sides(half_b[:1], half_b[-1:], "row")
    exit_b = travel_second(left, half_b, right, along_columns[1])

    halos = from_both_sides(rotated[:, :, :MARGIN], rotated[:, :, -MARGIN:], "row")
    half_a = travel_first(rotated, halos, wave_a, wave_a_halos, along_rows[0])
    left, right = from_both_sides(half_a[:1], half_a[-1:], "col")
    exit_a = travel_second(left, half_a, right, along_columns[0])
    return exit_a, exit_b


def swapped(value, axis, bit):
    mask = 2**bit
    pairs = [(source, source ^ mask) for source in range(lax.axis_size(axis))]
    return lax.ppermute(value, axis, pairs)


def padded_2(x, sides, width):
    for axis, dim in sides:
        devices, length = (lax.axis_size(axis), x.shape[dim])
        up = [(i, (i + 1) % devices) for i in range(devices - 1)]
        down = [(j, i) for i, j in up]
        last = lax.slice_in_dim(x, length - width, length, axis=dim)
        first = lax.slice_in_dim(x, 0, width, axis=dim)
        before = lax.ppermute(last, axis, up)
        after = lax.ppermute(first, axis, down)
        x = jnp.concatenate([before, x, after], axis=dim)
    return x


def fourier_tables(block_len, margin):
    window_len = block_len + 2 * margin
    frequency = jnp.arange(window_len, dtype=jnp.int32) - window_len // 2
    position = jnp.arange(window_len, dtype=jnp.int32)
    angles = (
        2.0
        * jnp.pi
        * jnp.mod(position[:, None] * frequency[None, :], window_len).astype(jnp.float32)
        / window_len
    )
    cosine = jnp.cos(angles)
    sines = jnp.sin(angles)
    forward = jnp.concatenate(
        [jnp.concatenate([cosine, -sines], 1), jnp.concatenate([sines, cosine], 1)], 0
    ).astype(jnp.bfloat16)
    target = jnp.arange(block_len, dtype=jnp.int32) + margin
    inverse_angle = (
        2.0
        * jnp.pi
        * jnp.mod(frequency[:, None] * target[None, :], window_len).astype(jnp.float32)
        / window_len
    )
    inverse_cosine = jnp.cos(inverse_angle) / window_len
    inverse_sine = jnp.sin(inverse_angle) / window_len
    inverse = jnp.concatenate(
        [
            jnp.concatenate([inverse_cosine, inverse_sine], 1),
            jnp.concatenate([-inverse_sine, inverse_cosine], 1),
        ],
        0,
    ).astype(jnp.bfloat16)
    return (forward, inverse, frequency.astype(jnp.float32))


def shear_ramp(fractions, frequency):
    window_len = frequency.shape[0]
    phases = -2.0 * jnp.pi / window_len * fractions[:, None] * frequency[None, :]
    nyquist = (jnp.arange(window_len) == 0)[None, :]
    ramp_real = jnp.where(nyquist, jnp.cos(jnp.pi * fractions)[:, None], jnp.cos(phases))
    ramp_imaginary = jnp.where(nyquist, 0.0, jnp.sin(phases))
    return (ramp_real, ramp_imaginary)


def travel_ramp(distance, frequency):
    window_len = frequency.shape[0]
    phases = -2.0 * jnp.pi / (window_len * window_len) * distance * frequency * frequency
    return (jnp.cos(phases)[None, :], jnp.sin(phases)[None, :])


def select_window(padded, starts, out_len):
    total_len = padded.shape[2]
    offset_range = total_len - out_len
    bit_count = max(offset_range, 1).bit_length()
    current = jnp.pad(padded, ((0, 0), (0, 0), (0, out_len + 2**bit_count - 1 - total_len)))
    for bit_number in reversed(range(bit_count)):
        stride = 2**bit_number
        kept_len = current.shape[2] - stride
        chosen = (starts // stride % 2 == 1)[None, :, None]
        current = jnp.where(
            chosen, current[:, :, stride : stride + kept_len], current[:, :, :kept_len]
        )
    return current


def line_pass(padded, extent, shifts, ramp_real, ramp_imaginary, tables):
    forward, inverse = (tables[0], tables[1])
    window_len = BLOCK + 2 * MARGIN
    line_count = padded.shape[1]
    blocks = (padded.shape[2] - 2 * extent) // BLOCK
    reach_len = blocks * BLOCK + 2 * MARGIN
    if shifts is None:
        shifted = padded
    else:
        starts = extent - MARGIN - shifts
        shifted = select_window(padded, starts, reach_len)
    middle = shifted[:, :, MARGIN : MARGIN + blocks * BLOCK].reshape(2, line_count, blocks, BLOCK)
    left_rim = shifted[:, :, : blocks * BLOCK].reshape(2, line_count, blocks, BLOCK)[..., :MARGIN]
    right_rim = shifted[:, :, 2 * MARGIN : 2 * MARGIN + blocks * BLOCK].reshape(
        2, line_count, blocks, BLOCK
    )[..., BLOCK - MARGIN :]
    windows = jnp.concatenate([left_rim, middle, right_rim], 3)
    spectrum = jnp.einsum(
        "cpms,cst->pmt",
        windows,
        forward.reshape(2, window_len, 2 * window_len),
        preferred_element_type=jnp.float32,
    )
    spec_real = spectrum[..., :window_len]
    spec_imaginary = spectrum[..., window_len:]
    factor_real = ramp_real[:, None, :]
    factor_imaginary = ramp_imaginary[:, None, :]
    ramped = jnp.concatenate(
        [
            spec_real * factor_real - spec_imaginary * factor_imaginary,
            spec_real * factor_imaginary + spec_imaginary * factor_real,
        ],
        -1,
    ).astype(jnp.bfloat16)
    result = jnp.einsum(
        "pms,scb->cpmb",
        ramped,
        inverse.reshape(2 * window_len, 2, BLOCK),
        preferred_element_type=jnp.float32,
    )
    return result.reshape(2, line_count, blocks * BLOCK).astype(jnp.bfloat16)


def single_pass(padded, extent, shifts, fractions, tables):
    ramp_real, ramp_imaginary = shear_ramp(fractions, tables[2])
    return line_pass(padded, extent, shifts, ramp_real, ramp_imaginary, tables)


def general_shear_columns(stacked, shifts, fractions, tables):
    halo_depth = SHIFT_X + MARGIN
    inputs = stacked.shape[0]
    column_devices = lax.axis_size("col")
    share = stacked.shape[2] // column_devices
    offset = lax.axis_index("col") * share
    spread = lax.all_to_all(stacked, "col", split_axis=2, concat_axis=3, tiled=True)
    padded = jnp.pad(spread, ((0, 0), (0, 0), (0, 0), (halo_depth, halo_depth)))
    row_shifts = lax.dynamic_slice_in_dim(shifts, offset, share, 1)
    row_fractions = lax.dynamic_slice_in_dim(fractions, offset, share, 1)
    sheared = jnp.stack(
        [
            single_pass(
                padded[min(0, inputs - 1)], halo_depth, row_shifts[0], row_fractions[0], tables
            )
        ]
    )
    return lax.all_to_all(sheared, "col", split_axis=3, concat_axis=2, tiled=True)


def shear_along_first(padded_lines, halo_depth, shifts, fractions, tables):
    flipped = jnp.swapaxes(padded_lines[0], 1, 2)
    moved = single_pass(flipped, halo_depth, shifts[0], fractions[0], tables)
    sheared = [jnp.swapaxes(moved, 1, 2)]
    return jnp.stack(sheared)


def shear_rows_pass(stacked, shifts, fractions, tables):
    halo_depth = SHIFT_Y + MARGIN
    row_devices = lax.axis_size("row")
    share = stacked.shape[3] // row_devices
    offset = lax.axis_index("row") * share
    spread = lax.all_to_all(stacked, "row", split_axis=3, concat_axis=2, tiled=True)
    padded = jnp.pad(spread, ((0, 0), (0, 0), (halo_depth, halo_depth), (0, 0)))
    column_shifts = lax.dynamic_slice_in_dim(shifts, offset, share, 1)
    column_fractions = lax.dynamic_slice_in_dim(fractions, offset, share, 1)
    sheared = shear_along_first(padded, halo_depth, column_shifts, column_fractions, tables)
    return lax.all_to_all(sheared, "row", split_axis=2, concat_axis=3, tiled=True)


def travel_local(extended, distance, tables):
    ramp_real, ramp_imaginary = travel_ramp(distance, tables[2])
    halfway = line_pass(extended, MARGIN, None, ramp_real, ramp_imaginary, tables)
    flipped = jnp.swapaxes(halfway, 1, 2)
    finished = line_pass(flipped, MARGIN, None, ramp_real, ramp_imaginary, tables)
    return jnp.swapaxes(finished, 1, 2)


def transmit(rotated, wave):
    phase_part = rotated[0].astype(jnp.float32)
    absorb_part = rotated[1].astype(jnp.float32)
    amplitude = jnp.exp(-ABSORB * absorb_part)
    through_real = amplitude * jnp.cos(phase_part)
    through_imaginary = amplitude * jnp.sin(phase_part)
    wave_real = wave[0].astype(jnp.float32)
    wave_imaginary = wave[1].astype(jnp.float32)
    return jnp.stack(
        [
            wave_real * through_real - wave_imaginary * through_imaginary,
            wave_real * through_imaginary + wave_imaginary * through_real,
        ]
    ).astype(jnp.bfloat16)


def general_on_device(
    volume_plane,
    wave_a,
    wave_b,
    shift_rows,
    fraction_rows,
    shift_columns,
    fraction_columns,
    travel_distance,
):
    tables = fourier_tables(BLOCK, MARGIN)
    source = volume_plane[None]
    results = []
    for member in range(2):
        stacked = general_shear_columns(
            source,
            shift_rows[member : member + 1, 0],
            fraction_rows[member : member + 1, 0],
            tables,
        )
        stacked = shear_rows_pass(
            stacked,
            shift_columns[member : member + 1],
            fraction_columns[member : member + 1],
            tables,
        )
        stacked = general_shear_columns(
            stacked,
            shift_rows[member : member + 1, 1],
            fraction_rows[member : member + 1, 1],
            tables,
        )
        results.append(stacked[0])
    view_one = results[0]
    view_two = results[1]
    turned = jnp.swapaxes(jnp.flip(view_two, 2), 1, 2)
    for bit_number in range(lax.axis_size("col").bit_length() - 1):
        turned = swapped(turned, "col", bit_number)
    product_a = transmit(view_one, wave_a)
    extended_a = padded_2(product_a, (("row", 1), ("col", 2)), MARGIN)
    exit_a = travel_local(extended_a, travel_distance[0], tables)
    product_b = transmit(turned, wave_b)
    extended_b = padded_2(product_b, (("row", 2), ("col", 1)), MARGIN)
    exit_b = travel_local(extended_b, travel_distance[1], tables)
    return (exit_a, exit_b)


def solution(mesh):
    def either(volume_plane, *rest):
        rows, width = volume_plane.shape[1:]
        fits = (
            rows == BLOCK * lax.axis_size("col")
            and width == BLOCK * lax.axis_size("row")
            and width >= SHIFT_X + MARGIN
        )
        chosen = on_device if fits else general_on_device
        return chosen(volume_plane, *rest)

    return jax.shard_map(
        either,
        mesh=mesh,
        in_specs=(
            P(None, "row", "col"),
            P(None, "row", "col"),
            P(None, "col", "row"),
            P(None, None, "row"),
            P(None, None, "row"),
            P(None, "col"),
            P(None, "col"),
            P(),
        ),
        out_specs=(P(None, "row", "col"), P(None, "col", "row")),
        check_vma=False,
    )
```

```python
import functools

import jax
import jax.numpy as jnp
import numpy as np
from jax import lax
from jax.experimental import pallas as pl
from jax.experimental.pallas import tpu as pltpu
from jax.sharding import PartitionSpec as P

BLOCK = 128
MARGIN = 32
SHIFT_X = 864
SHIFT_Y = 1728


ABSORB = 0.25

WINDOW = BLOCK + 2 * MARGIN
BINS = WINDOW // 2
GROUP = 16
PARTS = 2
VMEM_LIMIT = 56 * 1024 * 1024


def angle_table(rows, columns):
    return 2.0 * np.pi * (np.outer(rows, columns) % WINDOW) / WINDOW


def real_tables():
    position = np.arange(WINDOW)
    bins = np.arange(BINS + 1)
    target = np.arange(BLOCK) + MARGIN
    forward = np.zeros((2 * BLOCK, 2 * BLOCK), np.float32)
    forward[:WINDOW, : BINS + 1] = np.cos(angle_table(position, bins))
    forward[:WINDOW, BLOCK + 1 : BLOCK + BINS] = -np.sin(angle_table(position, bins[1:BINS]))
    weight = np.where((bins == 0) | (bins == BINS), 1.0, 2.0) / WINDOW
    inverse = np.zeros((2 * BLOCK, BLOCK), np.float32)
    inverse[: BINS + 1] = np.cos(angle_table(bins, target)) * weight[:, None]
    inverse[BLOCK + 1 : BLOCK + BINS] = (
        -np.sin(angle_table(bins[1:BINS], target)) * weight[1:BINS, None]
    )
    return forward, inverse


def travel_matrices(distance, forward, inverse):
    frequency = jnp.arange(BLOCK, dtype=jnp.float32)
    phases = -2.0 * jnp.pi / (WINDOW * WINDOW) * distance[:, None] * frequency * frequency
    ramps = jnp.stack([jnp.cos(phases), jnp.sin(phases)], 1)
    ramps = jnp.concatenate([ramps, ramps], 2)
    scaled = ramps[..., None] * jnp.asarray(inverse)
    matrices = jnp.einsum(
        "pq,vrqu->vrpu",
        jnp.asarray(forward[:WINDOW]),
        scaled,
        precision=lax.Precision.HIGHEST,
    )
    return matrices


def lane_iota(rows):
    return lax.broadcasted_iota(jnp.int32, (rows, BLOCK), 1)


def shift_lines(strip, shifted, base, base_offset, spare, windows, chunk_offset, rows):
    def one_group(group, carry):
        first = pl.multiple_of(group * GROUP, GROUP)
        lines = pl.ds(first, GROUP)
        start = base[base_offset + group] + chunk_offset
        offset = spare[lines, :]
        later = offset >= BLOCK
        lane = lane_iota(GROUP) + (offset & (BLOCK - 1))
        wraps = lane >= BLOCK
        index = lane & (BLOCK - 1)
        for part in range(2):
            here = strip[start, part, lines, :].astype(jnp.float32)
            before = None
            for i in range(windows + 2):
                following = strip[start + i + 1, part, lines, :].astype(jnp.float32)
                turned = jnp.take_along_axis(jnp.where(later, following, here), index, axis=1)
                if before is not None:
                    shifted[i - 1, part, lines, :] = jnp.where(wraps, turned, before).astype(
                        jnp.bfloat16
                    )
                before = turned
                here = following
        return carry

    lax.fori_loop(0, rows // GROUP, one_group, 0)


def ramped_lines(shifted, windows, rows, cosine, sine, forward):
    count = len(windows)
    lower = jnp.concatenate([shifted[m].reshape(2 * rows, BLOCK) for m in windows], 0)
    upper = jnp.concatenate([shifted[m + 1].reshape(2 * rows, BLOCK) for m in windows], 0)
    spectrum = jnp.dot(
        jnp.concatenate([lower, upper], 1), forward[...], preferred_element_type=jnp.float32
    )
    real = spectrum[:, :BLOCK].reshape(count * 2, rows, BLOCK)
    imaginary = spectrum[:, BLOCK:].reshape(count * 2, rows, BLOCK)
    ramp_real = cosine[...][None]
    ramp_imaginary = sine[...][None]
    ramped = jnp.concatenate(
        [
            (real * ramp_real - imaginary * ramp_imaginary).astype(jnp.bfloat16),
            (real * ramp_imaginary + imaginary * ramp_real).astype(jnp.bfloat16),
        ],
        2,
    )
    return ramped.reshape(count * 2 * rows, 2 * BLOCK)


def down_lines(vector):
    return jnp.broadcast_to(vector, (BLOCK, BLOCK)).T


def line_ramps(fractions, cosine, sine):
    bins = lane_iota(BLOCK).astype(jnp.float32)
    sine[...], cosine[...] = sine_cosine(down_lines(fractions) * bins * (-2.0 * np.pi / WINDOW))


def shear_tile_kernel(halo, tiles, rows, batch, wide, parts, base, rank, *refs):
    lefts, rights, refs = refs[:parts], refs[parts : 2 * parts], refs[2 * parts :]
    own, offsets, fractions, forward, inverse, out = refs[:6]
    strip, shifted, spare, cosine, sine = refs[6:]
    step = pl.program_id(0)
    groups = rows // GROUP
    end = halo + tiles + halo

    @pl.when(step == 0)
    def _():
        strip[end : end + 2] = jnp.zeros((2, 2, rows, BLOCK), jnp.bfloat16)

    def fill(piece, first, count):
        for i in range(count):
            if wide:
                strip[first + i] = piece[:, :, i * BLOCK : (i + 1) * BLOCK]
            else:
                strip[first + i] = piece[i]

    share = pl.num_programs(0) // parts
    for part in range(parts):

        @pl.when(step // share == part)
        def _():
            fill(lefts[part], 0, halo)
            fill(rights[part], halo + tiles, halo)

    fill(own, halo, tiles)
    spare[...] = down_lines(offsets[0]).astype(jnp.int32)
    line_ramps(fractions[0], cosine, sine)
    shift_lines(strip, shifted, base, step * groups, spare, tiles, 0, rows)
    for first in range(0, tiles, batch):
        windows = [slot ^ rank[0] for slot in range(first, first + batch)]
        ramped = ramped_lines(shifted, windows, rows, cosine, sine, forward)
        result = jnp.dot(ramped, inverse[...], preferred_element_type=jnp.float32)
        out[first : first + batch] = result.astype(jnp.bfloat16).reshape(batch, 2, rows, BLOCK)


def shear_tile(own, lefts, rights, first, halo, base, rank, spare, fractions, tables):
    wide = own.ndim == 3
    parts = len(lefts)
    part_lines = lefts[0].shape[-2]
    line_count = parts * part_lines
    tiles = own.shape[2] // BLOCK if wide else own.shape[0]
    rows = BLOCK
    share = part_lines // rows
    offset = first // rows
    forward, inverse = tables

    def piece_spec(piece, place):
        if wide:
            return pl.BlockSpec((2, rows, piece.shape[2]), lambda i, *_: (0, place(i), 0))
        return pl.BlockSpec((piece.shape[0], 2, rows, BLOCK), lambda i, *_: (0, 0, place(i), 0))

    halo_specs = [
        piece_spec(x, lambda i, part=part: jnp.clip(i - part * share, 0, share - 1))
        for x in (lefts[0], rights[0])
        for part in range(parts)
    ]
    line_spec = pl.BlockSpec((1, 1, rows), lambda i, *_: (i + offset, 0, 0))
    along = lambda x: x.astype(jnp.float32).reshape(-1, 1, rows)
    out_shape = jax.ShapeDtypeStruct((tiles, 2, line_count, BLOCK), jnp.bfloat16)
    out_spec = pl.BlockSpec((tiles, 2, rows, BLOCK), lambda i, *_: (0, 0, i, 0))
    groups = rows // GROUP
    kernel = functools.partial(
        shear_tile_kernel, halo, tiles, rows, tiles // 2 if tiles % 2 == 0 else tiles, wide, parts
    )
    return pl.pallas_call(
        kernel,
        grid_spec=pltpu.PrefetchScalarGridSpec(
            num_scalar_prefetch=2,
            grid=(line_count // rows,),
            in_specs=halo_specs
            + [piece_spec(own, lambda i: i + offset)]
            + [line_spec] * 2
            + [
                pl.BlockSpec(forward.shape, lambda i, *_: (0, 0)),
                pl.BlockSpec(inverse.shape, lambda i, *_: (0, 0)),
            ],
            out_specs=out_spec,
            scratch_shapes=[
                pltpu.VMEM((halo + tiles + halo + 2, 2, rows, BLOCK), jnp.bfloat16),
                pltpu.VMEM((tiles + 1, 2, rows, BLOCK), jnp.bfloat16),
                pltpu.VMEM((rows, BLOCK), jnp.int32),
                pltpu.VMEM((rows, BLOCK), jnp.float32),
                pltpu.VMEM((rows, BLOCK), jnp.float32),
            ],
        ),
        out_shape=out_shape,
        compiler_params=pltpu.CompilerParams(vmem_limit_bytes=VMEM_LIMIT),
        name="shear_tile",
    )(
        lax.slice_in_dim(base, offset * groups, offset * groups + line_count // GROUP),
        rank,
        *lefts,
        *rights,
        own,
        along(spare),
        along(fractions),
        forward,
        inverse,
    )


def shear_whole_kernel(
    halo,
    devices,
    tiles,
    rows,
    base,
    own,
    offsets,
    fractions,
    forward,
    flipped,
    out,
    strip,
    shifted,
    spare,
    cosine,
    sine,
):
    step = pl.program_id(0)
    chunks = devices * tiles
    length = tiles * BLOCK

    @pl.when(step == 0)
    def _():
        strip[0:halo] = jnp.zeros((halo, 2, rows, BLOCK), jnp.bfloat16)
        strip[halo + chunks :] = jnp.zeros((halo + 2, 2, rows, BLOCK), jnp.bfloat16)
        for chunk in range(chunks):
            strip[halo + chunk] = own[chunk % tiles, chunk // tiles]
        out[0, :, 0:MARGIN, :] = jnp.zeros((2, MARGIN, rows), jnp.bfloat16)
        out[devices - 1, :, MARGIN + length :, :] = jnp.zeros((2, MARGIN, rows), jnp.bfloat16)
        spare[...] = down_lines(offsets[...]).astype(jnp.int32)
        line_ramps(fractions[...], cosine, sine)

    shift_lines(strip, shifted, base, 0, spare, tiles, step * tiles, rows)
    ramped = ramped_lines(shifted, range(tiles), rows, cosine, sine, forward)
    target = devices - 1 - step
    for window in range(tiles):
        lines = ramped[window * 2 * rows : (window + 1) * 2 * rows]
        result = lax.dot_general(
            flipped[...], lines, (((1,), (1,)), ((), ())), preferred_element_type=jnp.float32
        ).astype(jnp.bfloat16)
        block = tiles - 1 - window
        low = MARGIN + block * BLOCK
        for part in range(2):
            piece = result[:, part * rows : (part + 1) * rows]
            out[target, part, low : low + BLOCK, :] = piece
            if block == 0:

                @pl.when(target > 0)
                def _():
                    out[target - 1, part, MARGIN + length :, :] = piece[:MARGIN]

            if block == tiles - 1:

                @pl.when(target < devices - 1)
                def _():
                    out[target + 1, part, 0:MARGIN, :] = piece[BLOCK - MARGIN :]


def shear_whole(own, halo, base, spare, fractions, tables):
    tiles, devices, _, rows, _ = own.shape
    forward, flipped = tables
    operands = (
        own,
        spare.astype(jnp.float32).reshape(1, rows),
        fractions.reshape(1, rows),
        forward,
        flipped,
    )
    full = lambda shape: pl.BlockSpec(shape, lambda i, *_: (0,) * len(shape))
    out = (devices, 2, tiles * BLOCK + 2 * MARGIN, rows)
    return pl.pallas_call(
        functools.partial(shear_whole_kernel, halo, devices, tiles, rows),
        grid_spec=pltpu.PrefetchScalarGridSpec(
            num_scalar_prefetch=1,
            grid=(devices,),
            in_specs=[full(x.shape) for x in operands],
            out_specs=full(out),
            scratch_shapes=[
                pltpu.VMEM((2 * halo + devices * tiles + 2, 2, rows, BLOCK), jnp.bfloat16),
                pltpu.VMEM((tiles + 1, 2, rows, BLOCK), jnp.bfloat16),
                pltpu.VMEM((rows, BLOCK), jnp.int32),
                pltpu.VMEM((rows, BLOCK), jnp.float32),
                pltpu.VMEM((rows, BLOCK), jnp.float32),
            ],
        ),
        out_shape=jax.ShapeDtypeStruct(out, jnp.bfloat16),
        compiler_params=pltpu.CompilerParams(vmem_limit_bytes=VMEM_LIMIT),
        name="shear_whole",
    )(base, *operands)


def shear_columns_kernel(front, blocks, length, rows_out, place, base, rank, *refs):
    owns, refs = refs[: len(place)], refs[len(place) :]
    offsets, fractions, forward, inverse, out, strip, shifted, cosine, sine = refs
    step = pl.program_id(0)
    per_step = length // BLOCK
    total = strip.shape[1]

    @pl.when(step == 0)
    def _():
        strip[:, 0:front, :] = jnp.zeros((2, front, BLOCK), jnp.bfloat16)
        back = front + blocks * length
        strip[:, back:, :] = jnp.zeros((2, total - back, BLOCK), jnp.bfloat16)
        for own, slots in zip(owns, place):
            count = own.shape[2]
            for i, (slot, within) in enumerate(slots):
                first = pl.multiple_of(front + (slot ^ rank[0]) * length + within, GROUP)
                for part in range(2):
                    strip[part, pl.ds(first, count), :] = own[i, part]
        bins = lax.broadcasted_iota(jnp.int32, (BLOCK, BLOCK), 0).astype(jnp.float32)
        sine[...], cosine[...] = sine_cosine(bins * fractions[...] * (-2.0 * np.pi / WINDOW))

    offset = jnp.broadcast_to(offsets[...], (8, BLOCK))
    row = lax.broadcasted_iota(jnp.int32, (8, BLOCK), 0) + (offset & 7)
    wraps = row >= 8
    index = row & 7
    block_rows = (step ^ rank[0]) * length

    def one_chunk(chunk):
        begin = pl.multiple_of(base[0] + block_rows + chunk * BLOCK, GROUP)
        for part in range(2):
            value = strip[part, pl.ds(begin, 2 * BLOCK), :].astype(jnp.float32)
            value = value.reshape(2 * BLOCK // 8, 8, BLOCK)
            for bit in (64, 32, 16, 8):
                taken = ((offset & bit) != 0)[None]
                value = jnp.where(taken, value[bit // 8 :], value[: -(bit // 8)])
            pieces = [
                jnp.take_along_axis(value[i], index, axis=0) for i in range(BLOCK // 8 + 1)
            ]
            moved = [
                jnp.where(wraps, pieces[i + 1], pieces[i]) for i in range(BLOCK // 8)
            ]
            shifted[chunk * BLOCK : (chunk + 1) * BLOCK, part * BLOCK : (part + 1) * BLOCK] = (
                jnp.concatenate(moved, 0).astype(jnp.bfloat16)
            )

    for chunk in range(per_step + 1):
        one_chunk(chunk)
    ramp_real = jnp.concatenate([cosine[...]] * 2, 1)
    ramp_imaginary = jnp.concatenate([sine[...]] * 2, 1)
    for window in range(per_step):
        low = window * BLOCK
        spectrum = jnp.dot(
            forward[...], shifted[low : low + 2 * BLOCK, :], preferred_element_type=jnp.float32
        )
        real, imaginary = spectrum[:BLOCK], spectrum[BLOCK:]
        ramped = jnp.concatenate(
            [
                (real * ramp_real - imaginary * ramp_imaginary).astype(jnp.bfloat16),
                (real * ramp_imaginary + imaginary * ramp_real).astype(jnp.bfloat16),
            ],
            0,
        )
        result = jnp.dot(inverse[...], ramped, preferred_element_type=jnp.float32).astype(
            jnp.bfloat16
        )
        block, within = low // rows_out, low % rows_out
        for part in range(2):
            out[block, part, within : within + BLOCK, :] = result[
                :, part * BLOCK : (part + 1) * BLOCK
            ]


def shear_columns(owns, place, blocks, front, back, base, rank, spare, fractions, tables, rows_out):
    length = sum(own.shape[0] * own.shape[2] for own in owns) // blocks
    forward, inverse = tables
    operands = (
        *owns,
        spare.astype(jnp.int32).reshape(1, BLOCK),
        fractions.reshape(1, BLOCK),
        forward,
        inverse,
    )
    full = lambda shape: pl.BlockSpec(shape, lambda i, *_: (0,) * len(shape))
    pieces = blocks * length // rows_out
    per_step = pieces // blocks
    return pl.pallas_call(
        functools.partial(shear_columns_kernel, front, blocks, length, rows_out, place),
        grid_spec=pltpu.PrefetchScalarGridSpec(
            num_scalar_prefetch=2,
            grid=(blocks,),
            in_specs=[full(x.shape) for x in operands],
            out_specs=pl.BlockSpec((per_step, 2, rows_out, BLOCK), lambda i, *_: (i, 0, 0, 0)),
            scratch_shapes=[
                pltpu.VMEM((2, front + blocks * length + back, BLOCK), jnp.bfloat16),
                pltpu.VMEM((length + BLOCK, 2 * BLOCK), jnp.bfloat16),
                pltpu.VMEM((BLOCK, BLOCK), jnp.float32),
                pltpu.VMEM((BLOCK, BLOCK), jnp.float32),
            ],
        ),
        out_shape=jax.ShapeDtypeStruct((pieces, 2, rows_out, BLOCK), jnp.bfloat16),
        compiler_params=pltpu.CompilerParams(vmem_limit_bytes=VMEM_LIMIT),
        name="shear_columns",
    )(base, rank, *operands)


def sine_cosine(angle):
    turns = jnp.round(angle * (2.0 / np.pi))
    rest = angle - turns * 1.5703125
    rest = rest - turns * 4.837512969970703125e-4
    rest = rest - turns * 7.549789954891882e-8
    square = rest * rest
    sine = rest + rest * square * (
        -1.6666654611e-1 + square * (8.3321608736e-3 - square * 1.9515295891e-4)
    )
    cosine = (
        1.0
        - 0.5 * square
        + square
        * square
        * (4.166664568298827e-2 + square * (-1.388731625493765e-3 + square * 2.443315711809948e-5))
    )
    quadrant = turns.astype(jnp.int32)
    odd = (quadrant & 1) != 0
    sine_out = jnp.where(odd, cosine, sine)
    cosine_out = jnp.where(odd, sine, cosine)
    sine_out = jnp.where((quadrant & 2) != 0, -sine_out, sine_out)
    cosine_out = jnp.where(((quadrant + 1) & 2) != 0, -cosine_out, cosine_out)
    return sine_out, cosine_out


def transmitted(rotated, wave):
    sine, cosine = sine_cosine(rotated[0].astype(jnp.float32))
    amplitude = jnp.exp(-ABSORB * rotated[1].astype(jnp.float32))
    through_real = amplitude * cosine
    through_imaginary = amplitude * sine
    wave_real = wave[0].astype(jnp.float32)
    wave_imaginary = wave[1].astype(jnp.float32)
    return (
        (wave_real * through_real - wave_imaginary * through_imaginary).astype(jnp.bfloat16),
        (wave_real * through_imaginary + wave_imaginary * through_real).astype(jnp.bfloat16),
    )


def travel_first_kernel(length, extended, *refs):
    if extended:
        body, wave, wave_top, wave_bottom, matrix, out, field = refs
        top = body.at[0, :, 0:MARGIN]
        middle = body.at[0, :, MARGIN : MARGIN + length]
        bottom = body.at[0, :, MARGIN + length :]
    else:
        body, top, bottom, wave, wave_top, wave_bottom, matrix, out, field = refs
        top, middle, bottom = top.at[0], body.at[0], bottom.at[0]
    pieces = [(0, MARGIN, top, wave_top, 0)]
    for first in range(0, length, BLOCK):
        pieces.append((MARGIN + first, BLOCK, middle, wave, first))
    pieces.append((MARGIN + length, MARGIN, bottom, wave_bottom, 0))
    for place, count, value, waves, first in pieces:
        lines = slice(first, first + count)
        parts = transmitted(
            [value[p, lines, :] for p in range(2)], [waves[p, lines, :] for p in range(2)]
        )
        for part in range(2):
            field[part, place : place + count, :] = parts[part]
    windows = [
        jnp.concatenate([field[0, m : m + WINDOW, :], field[1, m : m + WINDOW, :]], 0)
        for m in range(0, length, BLOCK)
    ]
    result = jnp.dot(
        matrix[...], jnp.concatenate(windows, 1), preferred_element_type=jnp.float32
    ).astype(jnp.bfloat16)
    for m in range(length // BLOCK):
        lanes = slice(m * BLOCK, (m + 1) * BLOCK)
        for part in range(2):
            out[0, part, lanes, :] = result[part * BLOCK : (part + 1) * BLOCK, lanes]


def travel_first(body, halos, wave, wave_halos, matrix):
    chunks = body.shape[0]
    length = wave.shape[1]
    chunk_spec = lambda x: pl.BlockSpec((1, 2, x.shape[2], BLOCK), lambda i: (i, 0, 0, 0))
    wide_spec = lambda x: pl.BlockSpec((2, x.shape[1], BLOCK), lambda i: (0, 0, i))
    return pl.pallas_call(
        functools.partial(travel_first_kernel, length, len(halos) == 0),
        grid=(chunks,),
        in_specs=[chunk_spec(body)]
        + [chunk_spec(x) for x in halos]
        + [wide_spec(x) for x in (wave, *wave_halos)]
        + [pl.BlockSpec(matrix.shape, lambda i: (0, 0))],
        out_specs=pl.BlockSpec((1, 2, length, BLOCK), lambda i: (i, 0, 0, 0)),
        out_shape=jax.ShapeDtypeStruct((chunks, 2, length, BLOCK), jnp.bfloat16),
        scratch_shapes=[pltpu.VMEM((2, length + 2 * MARGIN, BLOCK), jnp.bfloat16)],
        compiler_params=pltpu.CompilerParams(vmem_limit_bytes=VMEM_LIMIT),
        name="travel_first",
    )(body, *halos, wave, *wave_halos, matrix)


def travel_second_kernel(chunks, rows, left, body, right, matrix, out):
    parts = [[left[0, p]] + [body[m, p] for m in range(chunks)] + [right[0, p]] for p in range(2)]
    windows = [
        jnp.concatenate(parts[0][m : m + 3] + parts[1][m : m + 3], 1) for m in range(chunks)
    ]
    result = jnp.dot(
        jnp.concatenate(windows, 0), matrix[...], preferred_element_type=jnp.float32
    ).astype(jnp.bfloat16)
    for m in range(chunks):
        for part in range(2):
            out[part, :, m * BLOCK : (m + 1) * BLOCK] = result[
                m * rows : (m + 1) * rows, part * BLOCK : (part + 1) * BLOCK
            ]


def travel_second(left, body, right, matrix):
    chunks, _, length, _ = body.shape
    rows = BLOCK
    edge = pl.BlockSpec((1, 2, rows, BLOCK), lambda i: (0, 0, i, 0))
    return pl.pallas_call(
        functools.partial(travel_second_kernel, chunks, rows),
        grid=(length // rows,),
        in_specs=[
            edge,
            pl.BlockSpec((chunks, 2, rows, BLOCK), lambda i: (0, 0, i, 0)),
            edge,
            pl.BlockSpec(matrix.shape, lambda i: (0, 0)),
        ],
        out_specs=pl.BlockSpec((2, rows, chunks * BLOCK), lambda i: (0, i, 0)),
        out_shape=jax.ShapeDtypeStruct((2, length, chunks * BLOCK), jnp.bfloat16),
        compiler_params=pltpu.CompilerParams(vmem_limit_bytes=VMEM_LIMIT),
        name="travel_second",
    )(left, body, right, matrix)


def from_both_sides(first, last, axis):
    devices = lax.axis_size(axis)
    up = [(i, i + 1) for i in range(devices - 1)]
    down = [(j, i) for i, j in up]
    return lax.ppermute(last, axis, up), lax.ppermute(first, axis, down)


def after(value, *others):
    return lax.optimization_barrier((value, others))[0]


def ordered_kernel(rank, *refs):
    pieces, out = refs[:-1], refs[-1]
    for s, piece in enumerate(pieces):

        @pl.when(pl.program_id(0) == s)
        def _():
            out[...] = piece[...]


def ordered(pieces, rank):
    count = len(pieces)
    block = pieces[0].shape
    shape = (count, *block[1:])
    rest = (0,) * (len(block) - 1)
    return pl.pallas_call(
        ordered_kernel,
        grid_spec=pltpu.PrefetchScalarGridSpec(
            num_scalar_prefetch=1,
            grid=(count,),
            in_specs=[pl.BlockSpec(block, lambda i, rank: (0, *rest))] * count,
            out_specs=pl.BlockSpec(block, lambda i, rank: (i ^ rank[0], *rest)),
        ),
        out_shape=jax.ShapeDtypeStruct(shape, pieces[0].dtype),
        compiler_params=pltpu.CompilerParams(vmem_limit_bytes=VMEM_LIMIT),
        name="ordered",
    )(rank, *pieces)


def swapped_shares(slots):
    devices = lax.axis_size("row")
    return [slots[0]] + [
        lax.ppermute(slots[s], "row", [(i, i ^ s) for i in range(devices)])
        for s in range(1, devices)
    ]


def group_starts(starts, group, unit):
    lines = starts.shape[-1]
    grouped = starts.reshape(*starts.shape[:-1], lines // group, group)
    base = jnp.min(grouped, -1) // unit
    spare = grouped - base[..., None] * unit
    return base.astype(jnp.int32), spare.reshape(starts.shape)


def on_device(
    volume_plane,
    wave_a,
    wave_b,
    shift_rows,
    fraction_rows,
    shift_columns,
    fraction_columns,
    travel_distance,
):
    _, line_count, width = volume_plane.shape
    row_devices, column_devices = lax.axis_size("row"), lax.axis_size("col")
    row_index, column_index = lax.axis_index("row"), lax.axis_index("col")
    tiles = width // BLOCK
    halo = -(-(SHIFT_X + MARGIN) // BLOCK)
    reach = halo * BLOCK

    forward, inverse = real_tables()
    half = lambda x: jnp.asarray(x, jnp.bfloat16)
    row_tables = (half(forward), half(inverse))
    column_tables = (half(forward.T), half(inverse.T))
    turned_tables = (half(forward), half(inverse[:, ::-1].T))
    in_order = jnp.zeros((1,), jnp.int32)
    by_rank = row_index.astype(jnp.int32).reshape(1)

    part_lines = line_count // PARTS
    lefts, rights = [], []
    for part in range(PARTS):
        lines = volume_plane[:, part * part_lines : (part + 1) * part_lines]
        left, right = from_both_sides(lines[:, :, :reach], lines[:, :, width - reach :], "col")
        lefts.append(left)
        rights.append(right)
    wave_a_halos = from_both_sides(wave_a[:, :MARGIN], wave_a[:, -MARGIN:], "row")
    wave_b_halos = from_both_sides(wave_b[:, :MARGIN], wave_b[:, -MARGIN:], "col")

    base_rows, spare_rows = group_starts(reach - MARGIN - shift_rows, GROUP, BLOCK)

    front = -(-(SHIFT_Y + MARGIN) // GROUP) * GROUP
    back = front + 3 * BLOCK
    mine = lambda x: lax.dynamic_slice_in_dim(x, row_index * BLOCK, BLOCK, 1)
    base_columns, spare_columns = group_starts(front - MARGIN - mine(shift_columns), BLOCK, GROUP)
    column_fractions = mine(fraction_columns)

    def first(view, begin, lefts, rights, rank):
        return shear_tile(
            volume_plane,
            lefts,
            rights,
            begin,
            halo,
            base_rows[view, 0],
            rank,
            spare_rows[view, 0],
            fraction_rows[view, 0],
            row_tables,
        )

    def second(view, pieces, place, rank, rows_out):
        return shear_columns(
            pieces,
            place,
            row_devices,
            front,
            back,
            base_columns[view] * GROUP,
            rank,
            spare_columns[view],
            column_fractions[view],
            column_tables,
            rows_out,
        )

    matrices = travel_matrices(travel_distance, forward, inverse)
    real, imaginary = matrices[:, 0], matrices[:, 1]
    along_rows = jnp.concatenate(
        [
            jnp.concatenate([real, -imaginary], 1),
            jnp.concatenate([imaginary, real], 1),
        ],
        2,
    )
    along_rows = jnp.swapaxes(along_rows, 1, 2).astype(jnp.bfloat16)
    spaced = jnp.pad(matrices, ((0, 0), (0, 0), (BLOCK - MARGIN, BLOCK - MARGIN), (0, 0)))
    real, imaginary = spaced[:, 0], spaced[:, 1]
    along_columns = jnp.concatenate(
        [
            jnp.concatenate([real, -imaginary], 1),
            jnp.concatenate([imaginary, real], 1),
        ],
        2,
    ).astype(jnp.bfloat16)

    spread, sheared = [], ()
    for part in range(PARTS):
        left, right = after((lefts[part], rights[part]), sheared)
        sheared = first(1, part * part_lines, [left], [right], in_order)
        spread.append(lax.all_to_all(sheared, "row", split_axis=0, concat_axis=0, tiled=True))
    lefts, rights = after((lefts, rights), sheared)
    slots = first(0, 0, lefts, rights, by_rank)
    spread, wave_a_halos, wave_b_halos, slots = lax.optimization_barrier(
        (spread, wave_a_halos, wave_b_halos, slots)
    )
    pieces = swapped_shares([slots[s : s + 1] for s in range(row_devices)])

    place = [[(b, part * part_lines) for b in range(row_devices)] for part in range(PARTS)]
    moved_b = second(1, spread, place, in_order, BLOCK)
    whole = lax.all_to_all(moved_b, ("row", "col"), split_axis=0, concat_axis=0, tiled=True)
    whole = whole.reshape(row_devices, column_devices, 2, BLOCK, BLOCK)
    own_lines = lambda x: lax.dynamic_slice_in_dim(x, column_index * BLOCK, BLOCK, 0)
    groups = BLOCK // GROUP
    turned = shear_whole(
        whole,
        halo,
        lax.dynamic_slice_in_dim(base_rows[1, 1], column_index * groups, groups, 0),
        own_lines(spare_rows[1, 1]),
        own_lines(fraction_rows[1, 1]),
        turned_tables,
    )

    pieces = after(pieces, moved_b)
    moved_a = second(0, pieces, [[(s, 0)] for s in range(row_devices)], by_rank, line_count)
    pieces = swapped_shares([moved_a[s : s + 1] for s in range(row_devices)])
    tile = ordered(pieces, by_rank)
    left, right = from_both_sides(tile[:halo], tile[tiles - halo :], "col")
    rotated = shear_tile(
        tile,
        [left],
        [right],
        0,
        halo,
        base_rows[0, 1],
        in_order,
        spare_rows[0, 1],
        fraction_rows[0, 1],
        row_tables,
    )

    turned, left, right = lax.optimization_barrier((turned, left, right))
    turned = lax.all_to_all(turned, "col", split_axis=0, concat_axis=0, tiled=True)
    half_b = travel_first(turned, (), wave_b, wave_b_halos, along_rows[1])
    left, right = from_both_sides(half_b[:1], half_b[-1:], "row")
    exit_b = travel_second(left, half_b, right, along_columns[1])

    halos = from_both_sides(rotated[:, :, :MARGIN], rotated[:, :, -MARGIN:], "row")
    half_a = travel_first(rotated, halos, wave_a, wave_a_halos, along_rows[0])
    left, right = from_both_sides(half_a[:1], half_a[-1:], "col")
    exit_a = travel_second(left, half_a, right, along_columns[0])
    return exit_a, exit_b


def swapped(value, axis, bit):
    mask = 2**bit
    pairs = [(source, source ^ mask) for source in range(lax.axis_size(axis))]
    return lax.ppermute(value, axis, pairs)


def padded_2(x, sides, width):
    for axis, dim in sides:
        devices, length = (lax.axis_size(axis), x.shape[dim])
        up = [(i, (i + 1) % devices) for i in range(devices - 1)]
        down = [(j, i) for i, j in up]
        last = lax.slice_in_dim(x, length - width, length, axis=dim)
        first = lax.slice_in_dim(x, 0, width, axis=dim)
        before = lax.ppermute(last, axis, up)
        after = lax.ppermute(first, axis, down)
        x = jnp.concatenate([before, x, after], axis=dim)
    return x


def fourier_tables(block_len, margin):
    window_len = block_len + 2 * margin
    frequency = jnp.arange(window_len, dtype=jnp.int32) - window_len // 2
    position = jnp.arange(window_len, dtype=jnp.int32)
    angles = (
        2.0
        * jnp.pi
        * jnp.mod(position[:, None] * frequency[None, :], window_len).astype(jnp.float32)
        / window_len
    )
    cosine = jnp.cos(angles)
    sines = jnp.sin(angles)
    forward = jnp.concatenate(
        [jnp.concatenate([cosine, -sines], 1), jnp.concatenate([sines, cosine], 1)], 0
    ).astype(jnp.bfloat16)
    target = jnp.arange(block_len, dtype=jnp.int32) + margin
    inverse_angle = (
        2.0
        * jnp.pi
        * jnp.mod(frequency[:, None] * target[None, :], window_len).astype(jnp.float32)
        / window_len
    )
    inverse_cosine = jnp.cos(inverse_angle) / window_len
    inverse_sine = jnp.sin(inverse_angle) / window_len
    inverse = jnp.concatenate(
        [
            jnp.concatenate([inverse_cosine, inverse_sine], 1),
            jnp.concatenate([-inverse_sine, inverse_cosine], 1),
        ],
        0,
    ).astype(jnp.bfloat16)
    return (forward, inverse, frequency.astype(jnp.float32))


def shear_ramp(fractions, frequency):
    window_len = frequency.shape[0]
    phases = -2.0 * jnp.pi / window_len * fractions[:, None] * frequency[None, :]
    nyquist = (jnp.arange(window_len) == 0)[None, :]
    ramp_real = jnp.where(nyquist, jnp.cos(jnp.pi * fractions)[:, None], jnp.cos(phases))
    ramp_imaginary = jnp.where(nyquist, 0.0, jnp.sin(phases))
    return (ramp_real, ramp_imaginary)


def travel_ramp(distance, frequency):
    window_len = frequency.shape[0]
    phases = -2.0 * jnp.pi / (window_len * window_len) * distance * frequency * frequency
    return (jnp.cos(phases)[None, :], jnp.sin(phases)[None, :])


def select_window(padded, starts, out_len):
    total_len = padded.shape[2]
    offset_range = total_len - out_len
    bit_count = max(offset_range, 1).bit_length()
    current = jnp.pad(padded, ((0, 0), (0, 0), (0, out_len + 2**bit_count - 1 - total_len)))
    for bit_number in reversed(range(bit_count)):
        stride = 2**bit_number
        kept_len = current.shape[2] - stride
        chosen = (starts // stride % 2 == 1)[None, :, None]
        current = jnp.where(
            chosen, current[:, :, stride : stride + kept_len], current[:, :, :kept_len]
        )
    return current


def line_pass(padded, extent, shifts, ramp_real, ramp_imaginary, tables):
    forward, inverse = (tables[0], tables[1])
    window_len = BLOCK + 2 * MARGIN
    line_count = padded.shape[1]
    blocks = (padded.shape[2] - 2 * extent) // BLOCK
    reach_len = blocks * BLOCK + 2 * MARGIN
    if shifts is None:
        shifted = padded
    else:
        starts = extent - MARGIN - shifts
        shifted = select_window(padded, starts, reach_len)
    middle = shifted[:, :, MARGIN : MARGIN + blocks * BLOCK].reshape(2, line_count, blocks, BLOCK)
    left_rim = shifted[:, :, : blocks * BLOCK].reshape(2, line_count, blocks, BLOCK)[..., :MARGIN]
    right_rim = shifted[:, :, 2 * MARGIN : 2 * MARGIN + blocks * BLOCK].reshape(
        2, line_count, blocks, BLOCK
    )[..., BLOCK - MARGIN :]
    windows = jnp.concatenate([left_rim, middle, right_rim], 3)
    spectrum = jnp.einsum(
        "cpms,cst->pmt",
        windows,
        forward.reshape(2, window_len, 2 * window_len),
        preferred_element_type=jnp.float32,
    )
    spec_real = spectrum[..., :window_len]
    spec_imaginary = spectrum[..., window_len:]
    factor_real = ramp_real[:, None, :]
    factor_imaginary = ramp_imaginary[:, None, :]
    ramped = jnp.concatenate(
        [
            spec_real * factor_real - spec_imaginary * factor_imaginary,
            spec_real * factor_imaginary + spec_imaginary * factor_real,
        ],
        -1,
    ).astype(jnp.bfloat16)
    result = jnp.einsum(
        "pms,scb->cpmb",
        ramped,
        inverse.reshape(2 * window_len, 2, BLOCK),
        preferred_element_type=jnp.float32,
    )
    return result.reshape(2, line_count, blocks * BLOCK).astype(jnp.bfloat16)


def single_pass(padded, extent, shifts, fractions, tables):
    ramp_real, ramp_imaginary = shear_ramp(fractions, tables[2])
    return line_pass(padded, extent, shifts, ramp_real, ramp_imaginary, tables)


def general_shear_columns(stacked, shifts, fractions, tables):
    halo_depth = SHIFT_X + MARGIN
    inputs = stacked.shape[0]
    column_devices = lax.axis_size("col")
    share = stacked.shape[2] // column_devices
    offset = lax.axis_index("col") * share
    spread = lax.all_to_all(stacked, "col", split_axis=2, concat_axis=3, tiled=True)
    padded = jnp.pad(spread, ((0, 0), (0, 0), (0, 0), (halo_depth, halo_depth)))
    row_shifts = lax.dynamic_slice_in_dim(shifts, offset, share, 1)
    row_fractions = lax.dynamic_slice_in_dim(fractions, offset, share, 1)
    sheared = jnp.stack(
        [
            single_pass(
                padded[min(0, inputs - 1)], halo_depth, row_shifts[0], row_fractions[0], tables
            )
        ]
    )
    return lax.all_to_all(sheared, "col", split_axis=3, concat_axis=2, tiled=True)


def shear_along_first(padded_lines, halo_depth, shifts, fractions, tables):
    flipped = jnp.swapaxes(padded_lines[0], 1, 2)
    moved = single_pass(flipped, halo_depth, shifts[0], fractions[0], tables)
    sheared = [jnp.swapaxes(moved, 1, 2)]
    return jnp.stack(sheared)


def shear_rows_pass(stacked, shifts, fractions, tables):
    halo_depth = SHIFT_Y + MARGIN
    row_devices = lax.axis_size("row")
    share = stacked.shape[3] // row_devices
    offset = lax.axis_index("row") * share
    spread = lax.all_to_all(stacked, "row", split_axis=3, concat_axis=2, tiled=True)
    padded = jnp.pad(spread, ((0, 0), (0, 0), (halo_depth, halo_depth), (0, 0)))
    column_shifts = lax.dynamic_slice_in_dim(shifts, offset, share, 1)
    column_fractions = lax.dynamic_slice_in_dim(fractions, offset, share, 1)
    sheared = shear_along_first(padded, halo_depth, column_shifts, column_fractions, tables)
    return lax.all_to_all(sheared, "row", split_axis=2, concat_axis=3, tiled=True)


def travel_local(extended, distance, tables):
    ramp_real, ramp_imaginary = travel_ramp(distance, tables[2])
    halfway = line_pass(extended, MARGIN, None, ramp_real, ramp_imaginary, tables)
    flipped = jnp.swapaxes(halfway, 1, 2)
    finished = line_pass(flipped, MARGIN, None, ramp_real, ramp_imaginary, tables)
    return jnp.swapaxes(finished, 1, 2)


def transmit(rotated, wave):
    phase_part = rotated[0].astype(jnp.float32)
    absorb_part = rotated[1].astype(jnp.float32)
    amplitude = jnp.exp(-ABSORB * absorb_part)
    through_real = amplitude * jnp.cos(phase_part)
    through_imaginary = amplitude * jnp.sin(phase_part)
    wave_real = wave[0].astype(jnp.float32)
    wave_imaginary = wave[1].astype(jnp.float32)
    return jnp.stack(
        [
            wave_real * through_real - wave_imaginary * through_imaginary,
            wave_real * through_imaginary + wave_imaginary * through_real,
        ]
    ).astype(jnp.bfloat16)


def general_on_device(
    volume_plane,
    wave_a,
    wave_b,
    shift_rows,
    fraction_rows,
    shift_columns,
    fraction_columns,
    travel_distance,
):
    tables = fourier_tables(BLOCK, MARGIN)
    source = volume_plane[None]
    results = []
    for member in range(2):
        stacked = general_shear_columns(
            source,
            shift_rows[member : member + 1, 0],
            fraction_rows[member : member + 1, 0],
            tables,
        )
        stacked = shear_rows_pass(
            stacked,
            shift_columns[member : member + 1],
            fraction_columns[member : member + 1],
            tables,
        )
        stacked = general_shear_columns(
            stacked,
            shift_rows[member : member + 1, 1],
            fraction_rows[member : member + 1, 1],
            tables,
        )
        results.append(stacked[0])
    view_one = results[0]
    view_two = results[1]
    turned = jnp.swapaxes(jnp.flip(view_two, 2), 1, 2)
    for bit_number in range(lax.axis_size("col").bit_length() - 1):
        turned = swapped(turned, "col", bit_number)
    product_a = transmit(view_one, wave_a)
    extended_a = padded_2(product_a, (("row", 1), ("col", 2)), MARGIN)
    exit_a = travel_local(extended_a, travel_distance[0], tables)
    product_b = transmit(turned, wave_b)
    extended_b = padded_2(product_b, (("row", 2), ("col", 1)), MARGIN)
    exit_b = travel_local(extended_b, travel_distance[1], tables)
    return (exit_a, exit_b)


def solution(mesh):
    def either(volume_plane, *rest):
        rows, width = volume_plane.shape[1:]
        fits = (
            rows == BLOCK * lax.axis_size("col")
            and width == BLOCK * lax.axis_size("row")
            and width >= SHIFT_X + MARGIN
        )
        chosen = on_device if fits else general_on_device
        return chosen(volume_plane, *rest)

    return jax.shard_map(
        either,
        mesh=mesh,
        in_specs=(
            P(None, "row", "col"),
            P(None, "row", "col"),
            P(None, "col", "row"),
            P(None, None, "row"),
            P(None, None, "row"),
            P(None, "col"),
            P(None, "col"),
            P(),
        ),
        out_specs=(P(None, "row", "col"), P(None, "col", "row")),
        check_vma=False,
    )
```

```python
import functools

import jax
import jax.numpy as jnp
import numpy as np
from jax import lax
from jax.experimental import pallas as pl
from jax.experimental.pallas import tpu as pltpu
from jax.sharding import PartitionSpec as P

BLOCK = 128
MARGIN = 32
SHIFT_X = 864
SHIFT_Y = 1728


ABSORB = 0.25

WINDOW = BLOCK + 2 * MARGIN
BINS = WINDOW // 2
GROUP = 16
PARTS = 2
ROWS = 256
STEPS = 2
VMEM_LIMIT = 56 * 1024 * 1024


def angle_table(rows, columns):
    return 2.0 * np.pi * (np.outer(rows, columns) % WINDOW) / WINDOW


def real_tables():
    position = np.arange(WINDOW)
    bins = np.arange(BINS + 1)
    target = np.arange(BLOCK) + MARGIN
    forward = np.zeros((2 * BLOCK, 2 * BLOCK), np.float32)
    forward[:WINDOW, : BINS + 1] = np.cos(angle_table(position, bins))
    forward[:WINDOW, BLOCK + 1 : BLOCK + BINS] = -np.sin(angle_table(position, bins[1:BINS]))
    weight = np.where((bins == 0) | (bins == BINS), 1.0, 2.0) / WINDOW
    inverse = np.zeros((2 * BLOCK, BLOCK), np.float32)
    inverse[: BINS + 1] = np.cos(angle_table(bins, target)) * weight[:, None]
    inverse[BLOCK + 1 : BLOCK + BINS] = (
        -np.sin(angle_table(bins[1:BINS], target)) * weight[1:BINS, None]
    )
    return forward, inverse


def travel_matrices(distance, forward, inverse):
    frequency = jnp.arange(BLOCK, dtype=jnp.float32)
    phases = -2.0 * jnp.pi / (WINDOW * WINDOW) * distance[:, None] * frequency * frequency
    ramps = jnp.stack([jnp.cos(phases), jnp.sin(phases)], 1)
    ramps = jnp.concatenate([ramps, ramps], 2)
    scaled = ramps[..., None] * jnp.asarray(inverse)
    matrices = jnp.einsum(
        "pq,vrqu->vrpu",
        jnp.asarray(forward[:WINDOW]),
        scaled,
        precision=lax.Precision.HIGHEST,
    )
    return matrices


def lane_iota(rows):
    return lax.broadcasted_iota(jnp.int32, (rows, BLOCK), 1)


def shift_lines(strip, shifted, base, base_offset, spare, windows, chunk_offset, rows):
    def one_group(group, carry):
        first = pl.multiple_of(group * GROUP, GROUP)
        lines = pl.ds(first, GROUP)
        start = base[base_offset + group] + chunk_offset
        offset = spare[lines, :]
        later = offset >= BLOCK
        lane = lane_iota(GROUP) + (offset & (BLOCK - 1))
        wraps = lane >= BLOCK
        index = lane & (BLOCK - 1)
        for part in range(2):
            here = strip[start, part, lines, :].astype(jnp.float32)
            before = None
            for i in range(windows + 2):
                following = strip[start + i + 1, part, lines, :].astype(jnp.float32)
                turned = jnp.take_along_axis(jnp.where(later, following, here), index, axis=1)
                if before is not None:
                    shifted[i - 1, part, lines, :] = jnp.where(wraps, turned, before).astype(
                        jnp.bfloat16
                    )
                before = turned
                here = following
        return carry

    lax.fori_loop(0, rows // GROUP, one_group, 0, unroll=4)


def ramped_lines(shifted, windows, rows, cosine, sine, forward):
    count = len(windows)
    lower = jnp.concatenate([shifted[m].reshape(2 * rows, BLOCK) for m in windows], 0)
    upper = jnp.concatenate([shifted[m + 1].reshape(2 * rows, BLOCK) for m in windows], 0)
    spectrum = jnp.dot(
        jnp.concatenate([lower, upper], 1), forward[...], preferred_element_type=jnp.float32
    )
    real = spectrum[:, :BLOCK].reshape(count * 2, rows, BLOCK)
    imaginary = spectrum[:, BLOCK:].reshape(count * 2, rows, BLOCK)
    ramp_real = cosine[...][None]
    ramp_imaginary = sine[...][None]
    ramped = jnp.concatenate(
        [
            (real * ramp_real - imaginary * ramp_imaginary).astype(jnp.bfloat16),
            (real * ramp_imaginary + imaginary * ramp_real).astype(jnp.bfloat16),
        ],
        2,
    )
    return ramped.reshape(count * 2 * rows, 2 * BLOCK)


def down_lines(vector):
    return jnp.broadcast_to(vector, (BLOCK, vector.shape[1])).T


def line_ramps(fractions, cosine, sine):
    bins = lane_iota(fractions.shape[1]).astype(jnp.float32)
    sine[...], cosine[...] = sine_cosine(down_lines(fractions) * bins * (-2.0 * np.pi / WINDOW))


def shear_tile_kernel(halo, tiles, rows, batch, wide, parts, base, rank, *refs):
    lefts, rights, refs = refs[:parts], refs[parts : 2 * parts], refs[2 * parts :]
    own, offsets, fractions, forward, inverse, out = refs[:6]
    strip, shifted, spare, cosine, sine = refs[6:]
    step = pl.program_id(0)
    groups = rows // GROUP
    end = halo + tiles + halo

    @pl.when(step == 0)
    def _():
        strip[end : end + 2] = jnp.zeros((2, 2, rows, BLOCK), jnp.bfloat16)

    def fill(piece, first, count):
        for i in range(count):
            if wide:
                strip[first + i] = piece[:, :, i * BLOCK : (i + 1) * BLOCK]
            else:
                strip[first + i] = piece[i]

    share = pl.num_programs(0) // parts
    for part in range(parts):

        @pl.when(step // share == part)
        def _():
            fill(lefts[part], 0, halo)
            fill(rights[part], halo + tiles, halo)

    fill(own, halo, tiles)
    spare[...] = down_lines(offsets[0]).astype(jnp.int32)
    line_ramps(fractions[0], cosine, sine)
    shift_lines(strip, shifted, base, step * groups, spare, tiles, 0, rows)
    for first in range(0, tiles, batch):
        windows = [slot ^ rank[0] for slot in range(first, first + batch)]
        ramped = ramped_lines(shifted, windows, rows, cosine, sine, forward)
        result = jnp.dot(ramped, inverse[...], preferred_element_type=jnp.float32)
        out[first : first + batch] = result.astype(jnp.bfloat16).reshape(batch, 2, rows, BLOCK)


def shear_tile(own, lefts, rights, first, halo, base, rank, spare, fractions, tables):
    wide = own.ndim == 3
    parts = len(lefts)
    part_lines = lefts[0].shape[-2]
    line_count = parts * part_lines
    tiles = own.shape[2] // BLOCK if wide else own.shape[0]
    rows = min(part_lines, ROWS)
    share = part_lines // rows
    offset = first // rows
    forward, inverse = tables

    def piece_spec(piece, place):
        if wide:
            return pl.BlockSpec((2, rows, piece.shape[2]), lambda i, *_: (0, place(i), 0))
        return pl.BlockSpec((piece.shape[0], 2, rows, BLOCK), lambda i, *_: (0, 0, place(i), 0))

    halo_specs = [
        piece_spec(x, lambda i, part=part: jnp.clip(i - part * share, 0, share - 1))
        for x in (lefts[0], rights[0])
        for part in range(parts)
    ]
    line_spec = pl.BlockSpec((1, 1, rows), lambda i, *_: (i + offset, 0, 0))
    along = lambda x: x.astype(jnp.float32).reshape(-1, 1, rows)
    out_shape = jax.ShapeDtypeStruct((tiles, 2, line_count, BLOCK), jnp.bfloat16)
    out_spec = pl.BlockSpec((tiles, 2, rows, BLOCK), lambda i, *_: (0, 0, i, 0))
    groups = rows // GROUP
    kernel = functools.partial(
        shear_tile_kernel, halo, tiles, rows, tiles // 4 if tiles % 4 == 0 else tiles, wide, parts
    )
    return pl.pallas_call(
        kernel,
        grid_spec=pltpu.PrefetchScalarGridSpec(
            num_scalar_prefetch=2,
            grid=(line_count // rows,),
            in_specs=halo_specs
            + [piece_spec(own, lambda i: i + offset)]
            + [line_spec] * 2
            + [
                pl.BlockSpec(forward.shape, lambda i, *_: (0, 0)),
                pl.BlockSpec(inverse.shape, lambda i, *_: (0, 0)),
            ],
            out_specs=out_spec,
            scratch_shapes=[
                pltpu.VMEM((halo + tiles + halo + 2, 2, rows, BLOCK), jnp.bfloat16),
                pltpu.VMEM((tiles + 1, 2, rows, BLOCK), jnp.bfloat16),
                pltpu.VMEM((rows, BLOCK), jnp.int32),
                pltpu.VMEM((rows, BLOCK), jnp.float32),
                pltpu.VMEM((rows, BLOCK), jnp.float32),
            ],
        ),
        out_shape=out_shape,
        compiler_params=pltpu.CompilerParams(vmem_limit_bytes=VMEM_LIMIT),
        name="shear_tile",
    )(
        lax.slice_in_dim(base, offset * groups, offset * groups + line_count // GROUP),
        rank,
        *lefts,
        *rights,
        own,
        along(spare),
        along(fractions),
        forward,
        inverse,
    )


def shear_whole_kernel(
    halo,
    devices,
    tiles,
    rows,
    base,
    own,
    offsets,
    fractions,
    forward,
    flipped,
    out,
    strip,
    shifted,
    spare,
    cosine,
    sine,
):
    step = pl.program_id(0)
    chunks = devices * tiles
    length = tiles * BLOCK

    @pl.when(step == 0)
    def _():
        strip[0:halo] = jnp.zeros((halo, 2, rows, BLOCK), jnp.bfloat16)
        strip[halo + chunks :] = jnp.zeros((halo + 2, 2, rows, BLOCK), jnp.bfloat16)
        for chunk in range(chunks):
            strip[halo + chunk] = own[chunk % tiles, chunk // tiles]
        out[0, :, 0:MARGIN, :] = jnp.zeros((2, MARGIN, rows), jnp.bfloat16)
        out[devices - 1, :, MARGIN + length :, :] = jnp.zeros((2, MARGIN, rows), jnp.bfloat16)
        spare[...] = down_lines(offsets[...]).astype(jnp.int32)
        line_ramps(fractions[...], cosine, sine)

    shift_lines(strip, shifted, base, 0, spare, tiles, step * tiles, rows)
    ramped = ramped_lines(shifted, range(tiles), rows, cosine, sine, forward)
    target = devices - 1 - step
    result = lax.dot_general(
        flipped[...], ramped, (((1,), (1,)), ((), ())), preferred_element_type=jnp.float32
    ).astype(jnp.bfloat16)
    for window in range(tiles):
        block = tiles - 1 - window
        low = MARGIN + block * BLOCK
        for part in range(2):
            lanes = (2 * window + part) * rows
            piece = result[:, lanes : lanes + rows]
            out[target, part, low : low + BLOCK, :] = piece
            if block == 0:

                @pl.when(target > 0)
                def _():
                    out[target - 1, part, MARGIN + length :, :] = piece[:MARGIN]

            if block == tiles - 1:

                @pl.when(target < devices - 1)
                def _():
                    out[target + 1, part, 0:MARGIN, :] = piece[BLOCK - MARGIN :]


def shear_whole(own, halo, base, spare, fractions, tables):
    tiles, devices, _, rows, _ = own.shape
    forward, flipped = tables
    operands = (
        own,
        spare.astype(jnp.float32).reshape(1, rows),
        fractions.reshape(1, rows),
        forward,
        flipped,
    )
    full = lambda shape: pl.BlockSpec(shape, lambda i, *_: (0,) * len(shape))
    out = (devices, 2, tiles * BLOCK + 2 * MARGIN, rows)
    return pl.pallas_call(
        functools.partial(shear_whole_kernel, halo, devices, tiles, rows),
        grid_spec=pltpu.PrefetchScalarGridSpec(
            num_scalar_prefetch=1,
            grid=(devices,),
            in_specs=[full(x.shape) for x in operands],
            out_specs=full(out),
            scratch_shapes=[
                pltpu.VMEM((2 * halo + devices * tiles + 2, 2, rows, BLOCK), jnp.bfloat16),
                pltpu.VMEM((tiles + 1, 2, rows, BLOCK), jnp.bfloat16),
                pltpu.VMEM((rows, BLOCK), jnp.int32),
                pltpu.VMEM((rows, BLOCK), jnp.float32),
                pltpu.VMEM((rows, BLOCK), jnp.float32),
            ],
        ),
        out_shape=jax.ShapeDtypeStruct(out, jnp.bfloat16),
        compiler_params=pltpu.CompilerParams(vmem_limit_bytes=VMEM_LIMIT),
        name="shear_whole",
    )(base, *operands)


def shear_columns_kernel(front, blocks, length, rows_out, place, base, rank, *refs):
    owns, refs = refs[: len(place)], refs[len(place) :]
    offsets, fractions, forward, inverse, out, strip, shifted, cosine, sine = refs
    step = pl.program_id(0)
    per_step = length // BLOCK
    per_grid = blocks // pl.num_programs(0)
    total = strip.shape[1]

    @pl.when(step == 0)
    def _():
        strip[:, 0:front, :] = jnp.zeros((2, front, BLOCK), jnp.bfloat16)
        back = front + blocks * length
        strip[:, back:, :] = jnp.zeros((2, total - back, BLOCK), jnp.bfloat16)
        for own, slots in zip(owns, place):
            count = own.shape[2]
            for i, (slot, within) in enumerate(slots):
                first = pl.multiple_of(front + (slot ^ rank[0]) * length + within, GROUP)
                for part in range(2):
                    strip[part, pl.ds(first, count), :] = own[i, part]
        bins = lax.broadcasted_iota(jnp.int32, (BLOCK, BLOCK), 0).astype(jnp.float32)
        sine[...], cosine[...] = sine_cosine(bins * fractions[...] * (-2.0 * np.pi / WINDOW))

    offset = jnp.broadcast_to(offsets[...], (8, BLOCK))
    row = lax.broadcasted_iota(jnp.int32, (8, BLOCK), 0) + (offset & 7)
    wraps = row >= 8
    index = row & 7

    def one_chunk(block_rows, chunk):
        begin = pl.multiple_of(base[0] + block_rows + chunk * BLOCK, GROUP)
        for part in range(2):
            value = strip[part, pl.ds(begin, 2 * BLOCK), :].astype(jnp.float32)
            value = value.reshape(2 * BLOCK // 8, 8, BLOCK)
            for bit in (64, 32, 16, 8):
                taken = ((offset & bit) != 0)[None]
                value = jnp.where(taken, value[bit // 8 :], value[: -(bit // 8)])
            pieces = [
                jnp.take_along_axis(value[i], index, axis=0) for i in range(BLOCK // 8 + 1)
            ]
            moved = [
                jnp.where(wraps, pieces[i + 1], pieces[i]) for i in range(BLOCK // 8)
            ]
            shifted[chunk * BLOCK : (chunk + 1) * BLOCK, part * BLOCK : (part + 1) * BLOCK] = (
                jnp.concatenate(moved, 0).astype(jnp.bfloat16)
            )

    def one_block(local, carry):
        block_rows = ((step * per_grid + local) ^ rank[0]) * length
        for chunk in range(per_step + 1):
            one_chunk(block_rows, chunk)
        windows = [shifted[m * BLOCK : (m + 2) * BLOCK, :] for m in range(per_step)]
        spectrum = jnp.dot(
            forward[...], jnp.concatenate(windows, 1), preferred_element_type=jnp.float32
        )
        ramp_real = jnp.concatenate([cosine[...]] * (2 * per_step), 1)
        ramp_imaginary = jnp.concatenate([sine[...]] * (2 * per_step), 1)
        real, imaginary = spectrum[:BLOCK], spectrum[BLOCK:]
        ramped = jnp.concatenate(
            [
                (real * ramp_real - imaginary * ramp_imaginary).astype(jnp.bfloat16),
                (real * ramp_imaginary + imaginary * ramp_real).astype(jnp.bfloat16),
            ],
            0,
        )
        result = jnp.dot(inverse[...], ramped, preferred_element_type=jnp.float32)
        result = result.astype(jnp.bfloat16)
        for window in range(per_step):
            piece, within = window * BLOCK // rows_out, window * BLOCK % rows_out
            for part in range(2):
                lanes = (2 * window + part) * BLOCK
                out[local * (length // rows_out) + piece, part, within : within + BLOCK, :] = (
                    result[:, lanes : lanes + BLOCK]
                )
        return carry

    lax.fori_loop(0, per_grid, one_block, 0)


def shear_columns(owns, place, blocks, front, back, base, rank, spare, fractions, tables, rows_out):
    length = sum(own.shape[0] * own.shape[2] for own in owns) // blocks
    forward, inverse = tables
    operands = (
        *owns,
        spare.astype(jnp.int32).reshape(1, BLOCK),
        fractions.reshape(1, BLOCK),
        forward,
        inverse,
    )
    full = lambda shape: pl.BlockSpec(shape, lambda i, *_: (0,) * len(shape))
    pieces = blocks * length // rows_out
    steps = STEPS if blocks % STEPS == 0 else 1
    return pl.pallas_call(
        functools.partial(shear_columns_kernel, front, blocks, length, rows_out, place),
        grid_spec=pltpu.PrefetchScalarGridSpec(
            num_scalar_prefetch=2,
            grid=(steps,),
            in_specs=[full(x.shape) for x in operands],
            out_specs=pl.BlockSpec(
                (pieces // steps, 2, rows_out, BLOCK), lambda i, *_: (i, 0, 0, 0)
            ),
            scratch_shapes=[
                pltpu.VMEM((2, front + blocks * length + back, BLOCK), jnp.bfloat16),
                pltpu.VMEM((length + BLOCK, 2 * BLOCK), jnp.bfloat16),
                pltpu.VMEM((BLOCK, BLOCK), jnp.float32),
                pltpu.VMEM((BLOCK, BLOCK), jnp.float32),
            ],
        ),
        out_shape=jax.ShapeDtypeStruct((pieces, 2, rows_out, BLOCK), jnp.bfloat16),
        compiler_params=pltpu.CompilerParams(vmem_limit_bytes=VMEM_LIMIT),
        name="shear_columns",
    )(base, rank, *operands)


def sine_cosine(angle):
    turns = jnp.round(angle * (2.0 / np.pi))
    rest = angle - turns * 1.5703125
    rest = rest - turns * 4.837512969970703125e-4
    rest = rest - turns * 7.549789954891882e-8
    square = rest * rest
    sine = rest + rest * square * (
        -1.6666654611e-1 + square * (8.3321608736e-3 - square * 1.9515295891e-4)
    )
    cosine = (
        1.0
        - 0.5 * square
        + square
        * square
        * (4.166664568298827e-2 + square * (-1.388731625493765e-3 + square * 2.443315711809948e-5))
    )
    quadrant = turns.astype(jnp.int32)
    odd = (quadrant & 1) != 0
    sine_out = jnp.where(odd, cosine, sine)
    cosine_out = jnp.where(odd, sine, cosine)
    sine_out = jnp.where((quadrant & 2) != 0, -sine_out, sine_out)
    cosine_out = jnp.where(((quadrant + 1) & 2) != 0, -cosine_out, cosine_out)
    return sine_out, cosine_out


def transmitted(rotated, wave):
    sine, cosine = sine_cosine(rotated[0].astype(jnp.float32))
    amplitude = jnp.exp(-ABSORB * rotated[1].astype(jnp.float32))
    through_real = amplitude * cosine
    through_imaginary = amplitude * sine
    wave_real = wave[0].astype(jnp.float32)
    wave_imaginary = wave[1].astype(jnp.float32)
    return (
        (wave_real * through_real - wave_imaginary * through_imaginary).astype(jnp.bfloat16),
        (wave_real * through_imaginary + wave_imaginary * through_real).astype(jnp.bfloat16),
    )


def travel_first_kernel(length, count, extended, *refs):
    if extended:
        body, wave, wave_top, wave_bottom, matrix, out, field = refs
    else:
        body, top, bottom, wave, wave_top, wave_bottom, matrix, out, field = refs
    for chunk in range(count):
        if extended:
            tops = body.at[chunk, :, 0:MARGIN]
            middle = body.at[chunk, :, MARGIN : MARGIN + length]
            bottoms = body.at[chunk, :, MARGIN + length :]
        else:
            tops, middle, bottoms = top.at[chunk], body.at[chunk], bottom.at[chunk]
        pieces = [(0, MARGIN, tops, wave_top, 0)]
        for first in range(0, length, BLOCK):
            pieces.append((MARGIN + first, BLOCK, middle, wave, first))
        pieces.append((MARGIN + length, MARGIN, bottoms, wave_bottom, 0))
        across = slice(chunk * BLOCK, (chunk + 1) * BLOCK)
        for place, height, value, waves, first in pieces:
            lines = slice(first, first + height)
            parts = transmitted(
                [value[p, lines, :] for p in range(2)],
                [waves[p, lines, across] for p in range(2)],
            )
            for part in range(2):
                field[part, place : place + height, across] = parts[part]
    for m in range(0, length, BLOCK):
        window = jnp.concatenate([field[0, m : m + WINDOW, :], field[1, m : m + WINDOW, :]], 0)
        result = jnp.dot(matrix[...], window, preferred_element_type=jnp.float32)
        result = result.astype(jnp.bfloat16)
        for chunk in range(count):
            across = slice(chunk * BLOCK, (chunk + 1) * BLOCK)
            for part in range(2):
                out[chunk, part, m : m + BLOCK, :] = result[
                    part * BLOCK : (part + 1) * BLOCK, across
                ]


def travel_first(body, halos, wave, wave_halos, matrix):
    chunks = body.shape[0]
    count = chunks // STEPS if chunks % STEPS == 0 else chunks
    length = wave.shape[1]
    chunk_spec = lambda x: pl.BlockSpec((count, 2, x.shape[2], BLOCK), lambda i: (i, 0, 0, 0))
    wide_spec = lambda x: pl.BlockSpec((2, x.shape[1], count * BLOCK), lambda i: (0, 0, i))
    return pl.pallas_call(
        functools.partial(travel_first_kernel, length, count, len(halos) == 0),
        grid=(chunks // count,),
        in_specs=[chunk_spec(body)]
        + [chunk_spec(x) for x in halos]
        + [wide_spec(x) for x in (wave, *wave_halos)]
        + [pl.BlockSpec(matrix.shape, lambda i: (0, 0))],
        out_specs=pl.BlockSpec((count, 2, length, BLOCK), lambda i: (i, 0, 0, 0)),
        out_shape=jax.ShapeDtypeStruct((chunks, 2, length, BLOCK), jnp.bfloat16),
        scratch_shapes=[pltpu.VMEM((2, length + 2 * MARGIN, count * BLOCK), jnp.bfloat16)],
        compiler_params=pltpu.CompilerParams(vmem_limit_bytes=VMEM_LIMIT),
        name="travel_first",
    )(body, *halos, wave, *wave_halos, matrix)


def travel_second_kernel(chunks, rows, left, body, right, matrix, out):
    parts = [[left[0, p]] + [body[m, p] for m in range(chunks)] + [right[0, p]] for p in range(2)]
    windows = [
        jnp.concatenate(parts[0][m : m + 3] + parts[1][m : m + 3], 1) for m in range(chunks)
    ]
    result = jnp.dot(
        jnp.concatenate(windows, 0), matrix[...], preferred_element_type=jnp.float32
    ).astype(jnp.bfloat16)
    for m in range(chunks):
        for part in range(2):
            out[part, :, m * BLOCK : (m + 1) * BLOCK] = result[
                m * rows : (m + 1) * rows, part * BLOCK : (part + 1) * BLOCK
            ]


def travel_second(left, body, right, matrix):
    chunks, _, length, _ = body.shape
    rows = length // STEPS if length % (STEPS * BLOCK) == 0 else length
    edge = pl.BlockSpec((1, 2, rows, BLOCK), lambda i: (0, 0, i, 0))
    return pl.pallas_call(
        functools.partial(travel_second_kernel, chunks, rows),
        grid=(length // rows,),
        in_specs=[
            edge,
            pl.BlockSpec((chunks, 2, rows, BLOCK), lambda i: (0, 0, i, 0)),
            edge,
            pl.BlockSpec(matrix.shape, lambda i: (0, 0)),
        ],
        out_specs=pl.BlockSpec((2, rows, chunks * BLOCK), lambda i: (0, i, 0)),
        out_shape=jax.ShapeDtypeStruct((2, length, chunks * BLOCK), jnp.bfloat16),
        compiler_params=pltpu.CompilerParams(vmem_limit_bytes=VMEM_LIMIT),
        name="travel_second",
    )(left, body, right, matrix)


def from_both_sides(first, last, axis):
    devices = lax.axis_size(axis)
    up = [(i, i + 1) for i in range(devices - 1)]
    down = [(j, i) for i, j in up]
    return lax.ppermute(last, axis, up), lax.ppermute(first, axis, down)


def after(value, *others):
    return lax.optimization_barrier((value, others))[0]


def ordered_kernel(halo, rank, *refs):
    pieces, (out, first, last) = refs[:-3], refs[-3:]
    count = len(pieces)
    for s, piece in enumerate(pieces):
        place = s ^ rank[0]
        out[place] = piece[0]

        @pl.when(place < halo)
        def _():
            first[place] = piece[0]

        @pl.when(place >= count - halo)
        def _():
            last[place - (count - halo)] = piece[0]


def ordered(pieces, halo, rank):
    count = len(pieces)
    block = pieces[0].shape
    shapes = [(n, *block[1:]) for n in (count, halo, halo)]
    full = lambda shape: pl.BlockSpec(shape, lambda i, *_: (0,) * len(shape))
    return pl.pallas_call(
        functools.partial(ordered_kernel, halo),
        grid_spec=pltpu.PrefetchScalarGridSpec(
            num_scalar_prefetch=1,
            grid=(1,),
            in_specs=[full(block)] * count,
            out_specs=[full(shape) for shape in shapes],
        ),
        out_shape=[jax.ShapeDtypeStruct(shape, pieces[0].dtype) for shape in shapes],
        compiler_params=pltpu.CompilerParams(vmem_limit_bytes=VMEM_LIMIT),
        name="ordered",
    )(rank, *pieces)


def swapped_shares(slots):
    devices = lax.axis_size("row")
    return [slots[0]] + [
        lax.ppermute(slots[s], "row", [(i, i ^ s) for i in range(devices)])
        for s in range(1, devices)
    ]


def group_starts(starts, group, unit):
    lines = starts.shape[-1]
    grouped = starts.reshape(*starts.shape[:-1], lines // group, group)
    base = jnp.min(grouped, -1) // unit
    spare = grouped - base[..., None] * unit
    return base.astype(jnp.int32), spare.reshape(starts.shape)


def on_device(
    volume_plane,
    wave_a,
    wave_b,
    shift_rows,
    fraction_rows,
    shift_columns,
    fraction_columns,
    travel_distance,
):
    _, line_count, width = volume_plane.shape
    row_devices, column_devices = lax.axis_size("row"), lax.axis_size("col")
    row_index, column_index = lax.axis_index("row"), lax.axis_index("col")
    tiles = width // BLOCK
    halo = -(-(SHIFT_X + MARGIN) // BLOCK)
    reach = halo * BLOCK

    forward, inverse = real_tables()
    half = lambda x: jnp.asarray(x, jnp.bfloat16)
    row_tables = (half(forward), half(inverse))
    column_tables = (half(forward.T), half(inverse.T))
    turned_tables = (half(forward), half(inverse[:, ::-1].T))
    in_order = jnp.zeros((1,), jnp.int32)
    by_rank = row_index.astype(jnp.int32).reshape(1)

    part_lines = line_count // PARTS
    lefts, rights, edges = [], [], ()
    for part in range(PARTS):
        lines = after(volume_plane, edges)[:, part * part_lines : (part + 1) * part_lines]
        edges = (lines[:, :, :reach], lines[:, :, width - reach :])
        left, right = from_both_sides(*edges, "col")
        lefts.append(left)
        rights.append(right)

    base_rows, spare_rows = group_starts(reach - MARGIN - shift_rows, GROUP, BLOCK)

    front = -(-(SHIFT_Y + MARGIN) // GROUP) * GROUP
    back = front + 3 * BLOCK
    mine = lambda x: lax.dynamic_slice_in_dim(x, row_index * BLOCK, BLOCK, 1)
    base_columns, spare_columns = group_starts(front - MARGIN - mine(shift_columns), BLOCK, GROUP)
    column_fractions = mine(fraction_columns)

    def first(view, begin, lefts, rights, rank):
        return shear_tile(
            volume_plane,
            lefts,
            rights,
            begin,
            halo,
            base_rows[view, 0],
            rank,
            spare_rows[view, 0],
            fraction_rows[view, 0],
            row_tables,
        )

    def second(view, pieces, place, rank, rows_out):
        return shear_columns(
            pieces,
            place,
            row_devices,
            front,
            back,
            base_columns[view] * GROUP,
            rank,
            spare_columns[view],
            column_fractions[view],
            column_tables,
            rows_out,
        )

    matrices = travel_matrices(travel_distance, forward, inverse)
    real, imaginary = matrices[:, 0], matrices[:, 1]
    along_rows = jnp.concatenate(
        [
            jnp.concatenate([real, -imaginary], 1),
            jnp.concatenate([imaginary, real], 1),
        ],
        2,
    )
    along_rows = jnp.swapaxes(along_rows, 1, 2).astype(jnp.bfloat16)
    spaced = jnp.pad(matrices, ((0, 0), (0, 0), (BLOCK - MARGIN, BLOCK - MARGIN), (0, 0)))
    real, imaginary = spaced[:, 0], spaced[:, 1]
    along_columns = jnp.concatenate(
        [
            jnp.concatenate([real, -imaginary], 1),
            jnp.concatenate([imaginary, real], 1),
        ],
        2,
    ).astype(jnp.bfloat16)

    spread, sheared = [], ()
    for part in range(PARTS):
        left, right = after((lefts[part], rights[part]), sheared)
        sheared = first(1, part * part_lines, [left], [right], in_order)
        spread.append(lax.all_to_all(sheared, "row", split_axis=0, concat_axis=0, tiled=True))
    lefts, rights = after((lefts, rights), sheared)
    slots = first(0, 0, lefts, rights, by_rank)
    spread = after(spread, slots)
    pieces = swapped_shares([slots[s : s + 1] for s in range(row_devices)])

    place = [[(b, part * part_lines) for b in range(row_devices)] for part in range(PARTS)]
    moved_b = second(1, spread, place, in_order, BLOCK)
    whole = lax.all_to_all(moved_b, ("row", "col"), split_axis=0, concat_axis=0, tiled=True)
    margin_a = after((wave_a[:, :MARGIN], wave_a[:, -MARGIN:]), moved_b)
    margin_b = after((wave_b[:, :MARGIN], wave_b[:, -MARGIN:]), moved_b)
    wave_a_halos = from_both_sides(*margin_a, "row")
    wave_b_halos = from_both_sides(*margin_b, "col")
    whole, wave_a_halos, wave_b_halos = lax.optimization_barrier(
        (whole, wave_a_halos, wave_b_halos)
    )
    whole = whole.reshape(row_devices, column_devices, 2, BLOCK, BLOCK)
    own_lines = lambda x: lax.dynamic_slice_in_dim(x, column_index * BLOCK, BLOCK, 0)
    groups = BLOCK // GROUP
    turned = shear_whole(
        whole,
        halo,
        lax.dynamic_slice_in_dim(base_rows[1, 1], column_index * groups, groups, 0),
        own_lines(spare_rows[1, 1]),
        own_lines(fraction_rows[1, 1]),
        turned_tables,
    )

    pieces = after(pieces, moved_b)
    moved_a = second(0, pieces, [[(s, 0)] for s in range(row_devices)], by_rank, line_count)
    pieces = swapped_shares([moved_a[s : s + 1] for s in range(row_devices)])
    tile, low, high = ordered(pieces, halo, by_rank)
    left, right = from_both_sides(low, high, "col")
    rotated = shear_tile(
        tile,
        [left],
        [right],
        0,
        halo,
        base_rows[0, 1],
        in_order,
        spare_rows[0, 1],
        fraction_rows[0, 1],
        row_tables,
    )

    turned = lax.all_to_all(turned, "col", split_axis=0, concat_axis=0, tiled=True)
    half_b = travel_first(turned, (), wave_b, wave_b_halos, along_rows[1])
    left, right = from_both_sides(half_b[:1], half_b[-1:], "row")
    exit_b = travel_second(left, half_b, right, along_columns[1])

    halos = from_both_sides(rotated[:, :, :MARGIN], rotated[:, :, -MARGIN:], "row")
    half_a = travel_first(rotated, halos, wave_a, wave_a_halos, along_rows[0])
    left, right = from_both_sides(half_a[:1], half_a[-1:], "col")
    exit_a = travel_second(left, half_a, right, along_columns[0])
    return exit_a, exit_b


def swapped(value, axis, bit):
    mask = 2**bit
    pairs = [(source, source ^ mask) for source in range(lax.axis_size(axis))]
    return lax.ppermute(value, axis, pairs)


def padded_2(x, sides, width):
    for axis, dim in sides:
        devices, length = (lax.axis_size(axis), x.shape[dim])
        up = [(i, (i + 1) % devices) for i in range(devices - 1)]
        down = [(j, i) for i, j in up]
        last = lax.slice_in_dim(x, length - width, length, axis=dim)
        first = lax.slice_in_dim(x, 0, width, axis=dim)
        before = lax.ppermute(last, axis, up)
        after = lax.ppermute(first, axis, down)
        x = jnp.concatenate([before, x, after], axis=dim)
    return x


def fourier_tables(block_len, margin):
    window_len = block_len + 2 * margin
    frequency = jnp.arange(window_len, dtype=jnp.int32) - window_len // 2
    position = jnp.arange(window_len, dtype=jnp.int32)
    angles = (
        2.0
        * jnp.pi
        * jnp.mod(position[:, None] * frequency[None, :], window_len).astype(jnp.float32)
        / window_len
    )
    cosine = jnp.cos(angles)
    sines = jnp.sin(angles)
    forward = jnp.concatenate(
        [jnp.concatenate([cosine, -sines], 1), jnp.concatenate([sines, cosine], 1)], 0
    ).astype(jnp.bfloat16)
    target = jnp.arange(block_len, dtype=jnp.int32) + margin
    inverse_angle = (
        2.0
        * jnp.pi
        * jnp.mod(frequency[:, None] * target[None, :], window_len).astype(jnp.float32)
        / window_len
    )
    inverse_cosine = jnp.cos(inverse_angle) / window_len
    inverse_sine = jnp.sin(inverse_angle) / window_len
    inverse = jnp.concatenate(
        [
            jnp.concatenate([inverse_cosine, inverse_sine], 1),
            jnp.concatenate([-inverse_sine, inverse_cosine], 1),
        ],
        0,
    ).astype(jnp.bfloat16)
    return (forward, inverse, frequency.astype(jnp.float32))


def shear_ramp(fractions, frequency):
    window_len = frequency.shape[0]
    phases = -2.0 * jnp.pi / window_len * fractions[:, None] * frequency[None, :]
    nyquist = (jnp.arange(window_len) == 0)[None, :]
    ramp_real = jnp.where(nyquist, jnp.cos(jnp.pi * fractions)[:, None], jnp.cos(phases))
    ramp_imaginary = jnp.where(nyquist, 0.0, jnp.sin(phases))
    return (ramp_real, ramp_imaginary)


def travel_ramp(distance, frequency):
    window_len = frequency.shape[0]
    phases = -2.0 * jnp.pi / (window_len * window_len) * distance * frequency * frequency
    return (jnp.cos(phases)[None, :], jnp.sin(phases)[None, :])


def select_window(padded, starts, out_len):
    total_len = padded.shape[2]
    offset_range = total_len - out_len
    bit_count = max(offset_range, 1).bit_length()
    current = jnp.pad(padded, ((0, 0), (0, 0), (0, out_len + 2**bit_count - 1 - total_len)))
    for bit_number in reversed(range(bit_count)):
        stride = 2**bit_number
        kept_len = current.shape[2] - stride
        chosen = (starts // stride % 2 == 1)[None, :, None]
        current = jnp.where(
            chosen, current[:, :, stride : stride + kept_len], current[:, :, :kept_len]
        )
    return current


def line_pass(padded, extent, shifts, ramp_real, ramp_imaginary, tables):
    forward, inverse = (tables[0], tables[1])
    window_len = BLOCK + 2 * MARGIN
    line_count = padded.shape[1]
    blocks = (padded.shape[2] - 2 * extent) // BLOCK
    reach_len = blocks * BLOCK + 2 * MARGIN
    if shifts is None:
        shifted = padded
    else:
        starts = extent - MARGIN - shifts
        shifted = select_window(padded, starts, reach_len)
    middle = shifted[:, :, MARGIN : MARGIN + blocks * BLOCK].reshape(2, line_count, blocks, BLOCK)
    left_rim = shifted[:, :, : blocks * BLOCK].reshape(2, line_count, blocks, BLOCK)[..., :MARGIN]
    right_rim = shifted[:, :, 2 * MARGIN : 2 * MARGIN + blocks * BLOCK].reshape(
        2, line_count, blocks, BLOCK
    )[..., BLOCK - MARGIN :]
    windows = jnp.concatenate([left_rim, middle, right_rim], 3)
    spectrum = jnp.einsum(
        "cpms,cst->pmt",
        windows,
        forward.reshape(2, window_len, 2 * window_len),
        preferred_element_type=jnp.float32,
    )
    spec_real = spectrum[..., :window_len]
    spec_imaginary = spectrum[..., window_len:]
    factor_real = ramp_real[:, None, :]
    factor_imaginary = ramp_imaginary[:, None, :]
    ramped = jnp.concatenate(
        [
            spec_real * factor_real - spec_imaginary * factor_imaginary,
            spec_real * factor_imaginary + spec_imaginary * factor_real,
        ],
        -1,
    ).astype(jnp.bfloat16)
    result = jnp.einsum(
        "pms,scb->cpmb",
        ramped,
        inverse.reshape(2 * window_len, 2, BLOCK),
        preferred_element_type=jnp.float32,
    )
    return result.reshape(2, line_count, blocks * BLOCK).astype(jnp.bfloat16)


def single_pass(padded, extent, shifts, fractions, tables):
    ramp_real, ramp_imaginary = shear_ramp(fractions, tables[2])
    return line_pass(padded, extent, shifts, ramp_real, ramp_imaginary, tables)


def general_shear_columns(stacked, shifts, fractions, tables):
    halo_depth = SHIFT_X + MARGIN
    inputs = stacked.shape[0]
    column_devices = lax.axis_size("col")
    share = stacked.shape[2] // column_devices
    offset = lax.axis_index("col") * share
    spread = lax.all_to_all(stacked, "col", split_axis=2, concat_axis=3, tiled=True)
    padded = jnp.pad(spread, ((0, 0), (0, 0), (0, 0), (halo_depth, halo_depth)))
    row_shifts = lax.dynamic_slice_in_dim(shifts, offset, share, 1)
    row_fractions = lax.dynamic_slice_in_dim(fractions, offset, share, 1)
    sheared = jnp.stack(
        [
            single_pass(
                padded[min(0, inputs - 1)], halo_depth, row_shifts[0], row_fractions[0], tables
            )
        ]
    )
    return lax.all_to_all(sheared, "col", split_axis=3, concat_axis=2, tiled=True)


def shear_along_first(padded_lines, halo_depth, shifts, fractions, tables):
    flipped = jnp.swapaxes(padded_lines[0], 1, 2)
    moved = single_pass(flipped, halo_depth, shifts[0], fractions[0], tables)
    sheared = [jnp.swapaxes(moved, 1, 2)]
    return jnp.stack(sheared)


def shear_rows_pass(stacked, shifts, fractions, tables):
    halo_depth = SHIFT_Y + MARGIN
    row_devices = lax.axis_size("row")
    share = stacked.shape[3] // row_devices
    offset = lax.axis_index("row") * share
    spread = lax.all_to_all(stacked, "row", split_axis=3, concat_axis=2, tiled=True)
    padded = jnp.pad(spread, ((0, 0), (0, 0), (halo_depth, halo_depth), (0, 0)))
    column_shifts = lax.dynamic_slice_in_dim(shifts, offset, share, 1)
    column_fractions = lax.dynamic_slice_in_dim(fractions, offset, share, 1)
    sheared = shear_along_first(padded, halo_depth, column_shifts, column_fractions, tables)
    return lax.all_to_all(sheared, "row", split_axis=2, concat_axis=3, tiled=True)


def travel_local(extended, distance, tables):
    ramp_real, ramp_imaginary = travel_ramp(distance, tables[2])
    halfway = line_pass(extended, MARGIN, None, ramp_real, ramp_imaginary, tables)
    flipped = jnp.swapaxes(halfway, 1, 2)
    finished = line_pass(flipped, MARGIN, None, ramp_real, ramp_imaginary, tables)
    return jnp.swapaxes(finished, 1, 2)


def transmit(rotated, wave):
    phase_part = rotated[0].astype(jnp.float32)
    absorb_part = rotated[1].astype(jnp.float32)
    amplitude = jnp.exp(-ABSORB * absorb_part)
    through_real = amplitude * jnp.cos(phase_part)
    through_imaginary = amplitude * jnp.sin(phase_part)
    wave_real = wave[0].astype(jnp.float32)
    wave_imaginary = wave[1].astype(jnp.float32)
    return jnp.stack(
        [
            wave_real * through_real - wave_imaginary * through_imaginary,
            wave_real * through_imaginary + wave_imaginary * through_real,
        ]
    ).astype(jnp.bfloat16)


def general_on_device(
    volume_plane,
    wave_a,
    wave_b,
    shift_rows,
    fraction_rows,
    shift_columns,
    fraction_columns,
    travel_distance,
):
    tables = fourier_tables(BLOCK, MARGIN)
    source = volume_plane[None]
    results = []
    for member in range(2):
        stacked = general_shear_columns(
            source,
            shift_rows[member : member + 1, 0],
            fraction_rows[member : member + 1, 0],
            tables,
        )
        stacked = shear_rows_pass(
            stacked,
            shift_columns[member : member + 1],
            fraction_columns[member : member + 1],
            tables,
        )
        stacked = general_shear_columns(
            stacked,
            shift_rows[member : member + 1, 1],
            fraction_rows[member : member + 1, 1],
            tables,
        )
        results.append(stacked[0])
    view_one = results[0]
    view_two = results[1]
    turned = jnp.swapaxes(jnp.flip(view_two, 2), 1, 2)
    for bit_number in range(lax.axis_size("col").bit_length() - 1):
        turned = swapped(turned, "col", bit_number)
    product_a = transmit(view_one, wave_a)
    extended_a = padded_2(product_a, (("row", 1), ("col", 2)), MARGIN)
    exit_a = travel_local(extended_a, travel_distance[0], tables)
    product_b = transmit(turned, wave_b)
    extended_b = padded_2(product_b, (("row", 2), ("col", 1)), MARGIN)
    exit_b = travel_local(extended_b, travel_distance[1], tables)
    return (exit_a, exit_b)


def solution(mesh):
    def either(volume_plane, *rest):
        rows, width = volume_plane.shape[1:]
        fits = (
            rows == BLOCK * lax.axis_size("col")
            and width == BLOCK * lax.axis_size("row")
            and width >= SHIFT_X + MARGIN
        )
        chosen = on_device if fits else general_on_device
        return chosen(volume_plane, *rest)

    return jax.shard_map(
        either,
        mesh=mesh,
        in_specs=(
            P(None, "row", "col"),
            P(None, "row", "col"),
            P(None, "col", "row"),
            P(None, None, "row"),
            P(None, None, "row"),
            P(None, "col"),
            P(None, "col"),
            P(),
        ),
        out_specs=(P(None, "row", "col"), P(None, "col", "row")),
        check_vma=False,
    )
```

```python
import functools

import jax
import jax.numpy as jnp
import numpy as np
from jax import lax
from jax.experimental import pallas as pl
from jax.experimental.pallas import tpu as pltpu
from jax.sharding import PartitionSpec as P

BLOCK = 128
MARGIN = 32
SHIFT_X = 864
SHIFT_Y = 1728


ABSORB = 0.25

WINDOW = BLOCK + 2 * MARGIN
BINS = WINDOW // 2
GROUP = 16
PARTS = 2
ROWS = 256
STEPS = 2
VMEM_LIMIT = 56 * 1024 * 1024


def angle_table(rows, columns):
    return 2.0 * np.pi * (np.outer(rows, columns) % WINDOW) / WINDOW


def real_tables():
    position = np.arange(WINDOW)
    bins = np.arange(BINS + 1)
    target = np.arange(BLOCK) + MARGIN
    forward = np.zeros((2 * BLOCK, 2 * BLOCK), np.float32)
    forward[:WINDOW, : BINS + 1] = np.cos(angle_table(position, bins))
    forward[:WINDOW, BLOCK + 1 : BLOCK + BINS] = -np.sin(angle_table(position, bins[1:BINS]))
    weight = np.where((bins == 0) | (bins == BINS), 1.0, 2.0) / WINDOW
    inverse = np.zeros((2 * BLOCK, BLOCK), np.float32)
    inverse[: BINS + 1] = np.cos(angle_table(bins, target)) * weight[:, None]
    inverse[BLOCK + 1 : BLOCK + BINS] = (
        -np.sin(angle_table(bins[1:BINS], target)) * weight[1:BINS, None]
    )
    return forward, inverse


def travel_matrices(distance, forward, inverse):
    frequency = jnp.arange(BLOCK, dtype=jnp.float32)
    phases = -2.0 * jnp.pi / (WINDOW * WINDOW) * distance[:, None] * frequency * frequency
    ramps = jnp.stack([jnp.cos(phases), jnp.sin(phases)], 1)
    ramps = jnp.concatenate([ramps, ramps], 2)
    scaled = ramps[..., None] * jnp.asarray(inverse)
    matrices = jnp.einsum(
        "pq,vrqu->vrpu",
        jnp.asarray(forward[:WINDOW]),
        scaled,
        precision=lax.Precision.HIGHEST,
    )
    return matrices


def lane_iota(rows):
    return lax.broadcasted_iota(jnp.int32, (rows, BLOCK), 1)


def shift_lines(strip, shifted, base, base_offset, spare, windows, chunk_offset, rows):
    def one_group(group, carry):
        first = pl.multiple_of(group * GROUP, GROUP)
        lines = pl.ds(first, GROUP)
        start = base[base_offset + group] + chunk_offset
        offset = spare[lines, :]
        later = offset >= BLOCK
        lane = lane_iota(GROUP) + (offset & (BLOCK - 1))
        wraps = lane >= BLOCK
        index = lane & (BLOCK - 1)
        for part in range(2):
            here = strip[start, part, lines, :].astype(jnp.float32)
            before = None
            for i in range(windows + 2):
                following = strip[start + i + 1, part, lines, :].astype(jnp.float32)
                turned = jnp.take_along_axis(jnp.where(later, following, here), index, axis=1)
                if before is not None:
                    shifted[i - 1, part, lines, :] = jnp.where(wraps, turned, before).astype(
                        jnp.bfloat16
                    )
                before = turned
                here = following
        return carry

    lax.fori_loop(0, rows // GROUP, one_group, 0, unroll=4)


def ramped_lines(shifted, windows, rows, cosine, sine, forward):
    count = len(windows)
    lower = jnp.concatenate([shifted[m].reshape(2 * rows, BLOCK) for m in windows], 0)
    upper = jnp.concatenate([shifted[m + 1].reshape(2 * rows, BLOCK) for m in windows], 0)
    spectrum = jnp.dot(
        jnp.concatenate([lower, upper], 1), forward[...], preferred_element_type=jnp.float32
    )
    real = spectrum[:, :BLOCK].reshape(count * 2, rows, BLOCK)
    imaginary = spectrum[:, BLOCK:].reshape(count * 2, rows, BLOCK)
    ramp_real = cosine[...][None]
    ramp_imaginary = sine[...][None]
    ramped = jnp.concatenate(
        [
            (real * ramp_real - imaginary * ramp_imaginary).astype(jnp.bfloat16),
            (real * ramp_imaginary + imaginary * ramp_real).astype(jnp.bfloat16),
        ],
        2,
    )
    return ramped.reshape(count * 2 * rows, 2 * BLOCK)


def down_lines(vector):
    return jnp.broadcast_to(vector, (BLOCK, vector.shape[1])).T


def line_ramps(fractions, cosine, sine):
    bins = lane_iota(fractions.shape[1]).astype(jnp.float32)
    sine[...], cosine[...] = sine_cosine(down_lines(fractions) * bins * (-2.0 * np.pi / WINDOW))


def shear_tile_kernel(halo, tiles, rows, batch, wide, parts, sent, base, rank, *refs):
    lefts, rights, refs = refs[:parts], refs[parts : 2 * parts], refs[2 * parts :]
    waves, refs = refs[: int(sent)], refs[int(sent) :]
    own, offsets, fractions, forward, inverse, out = refs[:6]
    strip, shifted, spare, cosine, sine = refs[6:]
    step = pl.program_id(0)
    groups = rows // GROUP
    end = halo + tiles + halo

    @pl.when(step == 0)
    def _():
        strip[end : end + 2] = jnp.zeros((2, 2, rows, BLOCK), jnp.bfloat16)

    def fill(piece, first, count):
        for i in range(count):
            if wide:
                strip[first + i] = piece[:, :, i * BLOCK : (i + 1) * BLOCK]
            else:
                strip[first + i] = piece[i]

    share = pl.num_programs(0) // parts
    for part in range(parts):

        @pl.when(step // share == part)
        def _():
            fill(lefts[part], 0, halo)
            fill(rights[part], halo + tiles, halo)

    fill(own, halo, tiles)
    spare[...] = down_lines(offsets[0]).astype(jnp.int32)
    line_ramps(fractions[0], cosine, sine)
    shift_lines(strip, shifted, base, step * groups, spare, tiles, 0, rows)
    for first in range(0, tiles, batch):
        windows = [slot if sent else slot ^ rank[0] for slot in range(first, first + batch)]
        ramped = ramped_lines(shifted, windows, rows, cosine, sine, forward)
        result = jnp.dot(ramped, inverse[...], preferred_element_type=jnp.float32)
        result = result.astype(jnp.bfloat16).reshape(batch, 2, rows, BLOCK)
        if sent:
            for i, window in enumerate(windows):
                wave = waves[0][:, :, window * BLOCK : (window + 1) * BLOCK]
                for part, value in enumerate(transmitted(result[i], wave)):
                    out[window, part] = value
        else:
            out[first : first + batch] = result


def shear_tile(own, lefts, rights, first, halo, base, rank, spare, fractions, tables, *waves):
    wide = own.ndim == 3
    parts = len(lefts)
    part_lines = lefts[0].shape[-2]
    line_count = parts * part_lines
    tiles = own.shape[2] // BLOCK if wide else own.shape[0]
    rows = min(part_lines, ROWS)
    share = part_lines // rows
    offset = first // rows
    forward, inverse = tables

    def piece_spec(piece, place):
        if wide:
            return pl.BlockSpec((2, rows, piece.shape[2]), lambda i, *_: (0, place(i), 0))
        return pl.BlockSpec((piece.shape[0], 2, rows, BLOCK), lambda i, *_: (0, 0, place(i), 0))

    halo_specs = [
        piece_spec(x, lambda i, part=part: jnp.clip(i - part * share, 0, share - 1))
        for x in (lefts[0], rights[0])
        for part in range(parts)
    ]
    line_spec = pl.BlockSpec((1, 1, rows), lambda i, *_: (i + offset, 0, 0))
    along = lambda x: x.astype(jnp.float32).reshape(-1, 1, rows)
    out_shape = jax.ShapeDtypeStruct((tiles, 2, line_count, BLOCK), jnp.bfloat16)
    out_spec = pl.BlockSpec((tiles, 2, rows, BLOCK), lambda i, *_: (0, 0, i, 0))
    groups = rows // GROUP
    kernel = functools.partial(
        shear_tile_kernel,
        halo,
        tiles,
        rows,
        tiles // 4 if tiles % 4 == 0 else tiles,
        wide,
        parts,
        len(waves) > 0,
    )
    return pl.pallas_call(
        kernel,
        grid_spec=pltpu.PrefetchScalarGridSpec(
            num_scalar_prefetch=2,
            grid=(line_count // rows,),
            in_specs=halo_specs
            + [pl.BlockSpec((2, rows, x.shape[2]), lambda i, *_: (0, i + offset, 0)) for x in waves]
            + [piece_spec(own, lambda i: i + offset)]
            + [line_spec] * 2
            + [
                pl.BlockSpec(forward.shape, lambda i, *_: (0, 0)),
                pl.BlockSpec(inverse.shape, lambda i, *_: (0, 0)),
            ],
            out_specs=out_spec,
            scratch_shapes=[
                pltpu.VMEM((halo + tiles + halo + 2, 2, rows, BLOCK), jnp.bfloat16),
                pltpu.VMEM((tiles + 1, 2, rows, BLOCK), jnp.bfloat16),
                pltpu.VMEM((rows, BLOCK), jnp.int32),
                pltpu.VMEM((rows, BLOCK), jnp.float32),
                pltpu.VMEM((rows, BLOCK), jnp.float32),
            ],
        ),
        out_shape=out_shape,
        compiler_params=pltpu.CompilerParams(vmem_limit_bytes=VMEM_LIMIT),
        name="shear_tile",
    )(
        lax.slice_in_dim(base, offset * groups, offset * groups + line_count // GROUP),
        rank,
        *lefts,
        *rights,
        *waves,
        own,
        along(spare),
        along(fractions),
        forward,
        inverse,
    )


def shear_whole_kernel(
    halo,
    devices,
    tiles,
    rows,
    base,
    own,
    offsets,
    fractions,
    forward,
    flipped,
    out,
    strip,
    shifted,
    spare,
    cosine,
    sine,
):
    step = pl.program_id(0)
    chunks = devices * tiles
    length = tiles * BLOCK

    @pl.when(step == 0)
    def _():
        strip[0:halo] = jnp.zeros((halo, 2, rows, BLOCK), jnp.bfloat16)
        strip[halo + chunks :] = jnp.zeros((halo + 2, 2, rows, BLOCK), jnp.bfloat16)
        for chunk in range(chunks):
            strip[halo + chunk] = own[chunk % tiles, chunk // tiles]
        out[0, :, 0:MARGIN, :] = jnp.zeros((2, MARGIN, rows), jnp.bfloat16)
        out[devices - 1, :, MARGIN + length :, :] = jnp.zeros((2, MARGIN, rows), jnp.bfloat16)
        spare[...] = down_lines(offsets[...]).astype(jnp.int32)
        line_ramps(fractions[...], cosine, sine)

    shift_lines(strip, shifted, base, 0, spare, tiles, step * tiles, rows)
    ramped = ramped_lines(shifted, range(tiles), rows, cosine, sine, forward)
    target = devices - 1 - step
    result = lax.dot_general(
        flipped[...], ramped, (((1,), (1,)), ((), ())), preferred_element_type=jnp.float32
    ).astype(jnp.bfloat16)
    for window in range(tiles):
        block = tiles - 1 - window
        low = MARGIN + block * BLOCK
        for part in range(2):
            lanes = (2 * window + part) * rows
            piece = result[:, lanes : lanes + rows]
            out[target, part, low : low + BLOCK, :] = piece
            if block == 0:

                @pl.when(target > 0)
                def _():
                    out[target - 1, part, MARGIN + length :, :] = piece[:MARGIN]

            if block == tiles - 1:

                @pl.when(target < devices - 1)
                def _():
                    out[target + 1, part, 0:MARGIN, :] = piece[BLOCK - MARGIN :]


def shear_whole(own, halo, base, spare, fractions, tables):
    tiles, devices, _, rows, _ = own.shape
    forward, flipped = tables
    operands = (
        own,
        spare.astype(jnp.float32).reshape(1, rows),
        fractions.reshape(1, rows),
        forward,
        flipped,
    )
    full = lambda shape: pl.BlockSpec(shape, lambda i, *_: (0,) * len(shape))
    out = (devices, 2, tiles * BLOCK + 2 * MARGIN, rows)
    return pl.pallas_call(
        functools.partial(shear_whole_kernel, halo, devices, tiles, rows),
        grid_spec=pltpu.PrefetchScalarGridSpec(
            num_scalar_prefetch=1,
            grid=(devices,),
            in_specs=[full(x.shape) for x in operands],
            out_specs=full(out),
            scratch_shapes=[
                pltpu.VMEM((2 * halo + devices * tiles + 2, 2, rows, BLOCK), jnp.bfloat16),
                pltpu.VMEM((tiles + 1, 2, rows, BLOCK), jnp.bfloat16),
                pltpu.VMEM((rows, BLOCK), jnp.int32),
                pltpu.VMEM((rows, BLOCK), jnp.float32),
                pltpu.VMEM((rows, BLOCK), jnp.float32),
            ],
        ),
        out_shape=jax.ShapeDtypeStruct(out, jnp.bfloat16),
        compiler_params=pltpu.CompilerParams(vmem_limit_bytes=VMEM_LIMIT),
        name="shear_whole",
    )(base, *operands)


def shear_columns_kernel(front, blocks, length, rows_out, place, base, rank, *refs):
    owns, refs = refs[: len(place)], refs[len(place) :]
    offsets, fractions, forward, inverse, out, strip, shifted, cosine, sine = refs
    step = pl.program_id(0)
    per_step = length // BLOCK
    per_grid = blocks // pl.num_programs(0)
    total = strip.shape[1]

    @pl.when(step == 0)
    def _():
        strip[:, 0:front, :] = jnp.zeros((2, front, BLOCK), jnp.bfloat16)
        back = front + blocks * length
        strip[:, back:, :] = jnp.zeros((2, total - back, BLOCK), jnp.bfloat16)
        for own, slots in zip(owns, place):
            count = own.shape[2]
            for i, (slot, within) in enumerate(slots):
                first = front + slot * length + within
                for part in range(2):
                    strip[part, first : first + count, :] = own[i, part]
        bins = lax.broadcasted_iota(jnp.int32, (BLOCK, BLOCK), 0).astype(jnp.float32)
        sine[...], cosine[...] = sine_cosine(bins * fractions[...] * (-2.0 * np.pi / WINDOW))

    offset = jnp.broadcast_to(offsets[...], (8, BLOCK))
    row = lax.broadcasted_iota(jnp.int32, (8, BLOCK), 0) + (offset & 7)
    wraps = row >= 8
    index = row & 7

    def one_chunk(block_rows, chunk):
        begin = pl.multiple_of(base[0] + block_rows + chunk * BLOCK, GROUP)
        for part in range(2):
            value = strip[part, pl.ds(begin, 2 * BLOCK), :].astype(jnp.float32)
            value = value.reshape(2 * BLOCK // 8, 8, BLOCK)
            for bit in (64, 32, 16, 8):
                taken = ((offset & bit) != 0)[None]
                value = jnp.where(taken, value[bit // 8 :], value[: -(bit // 8)])
            pieces = [
                jnp.take_along_axis(value[i], index, axis=0) for i in range(BLOCK // 8 + 1)
            ]
            moved = [
                jnp.where(wraps, pieces[i + 1], pieces[i]) for i in range(BLOCK // 8)
            ]
            shifted[chunk * BLOCK : (chunk + 1) * BLOCK, part * BLOCK : (part + 1) * BLOCK] = (
                jnp.concatenate(moved, 0).astype(jnp.bfloat16)
            )

    def one_block(local, carry):
        block_rows = ((step * per_grid + local) ^ rank[0]) * length
        for chunk in range(per_step + 1):
            one_chunk(block_rows, chunk)
        windows = [shifted[m * BLOCK : (m + 2) * BLOCK, :] for m in range(per_step)]
        spectrum = jnp.dot(
            forward[...], jnp.concatenate(windows, 1), preferred_element_type=jnp.float32
        )
        ramp_real = jnp.concatenate([cosine[...]] * (2 * per_step), 1)
        ramp_imaginary = jnp.concatenate([sine[...]] * (2 * per_step), 1)
        real, imaginary = spectrum[:BLOCK], spectrum[BLOCK:]
        ramped = jnp.concatenate(
            [
                (real * ramp_real - imaginary * ramp_imaginary).astype(jnp.bfloat16),
                (real * ramp_imaginary + imaginary * ramp_real).astype(jnp.bfloat16),
            ],
            0,
        )
        result = jnp.dot(inverse[...], ramped, preferred_element_type=jnp.float32)
        result = result.astype(jnp.bfloat16)
        for window in range(per_step):
            piece, within = window * BLOCK // rows_out, window * BLOCK % rows_out
            for part in range(2):
                lanes = (2 * window + part) * BLOCK
                out[local * (length // rows_out) + piece, part, within : within + BLOCK, :] = (
                    result[:, lanes : lanes + BLOCK]
                )
        return carry

    lax.fori_loop(0, per_grid, one_block, 0)


def shear_columns(owns, place, blocks, front, back, base, rank, spare, fractions, tables, rows_out):
    length = sum(own.shape[0] * own.shape[2] for own in owns) // blocks
    forward, inverse = tables
    operands = (
        *owns,
        spare.astype(jnp.int32).reshape(1, BLOCK),
        fractions.reshape(1, BLOCK),
        forward,
        inverse,
    )
    full = lambda shape: pl.BlockSpec(shape, lambda i, *_: (0,) * len(shape))
    pieces = blocks * length // rows_out
    steps = STEPS if blocks % STEPS == 0 else 1
    return pl.pallas_call(
        functools.partial(shear_columns_kernel, front, blocks, length, rows_out, place),
        grid_spec=pltpu.PrefetchScalarGridSpec(
            num_scalar_prefetch=2,
            grid=(steps,),
            in_specs=[full(x.shape) for x in operands],
            out_specs=pl.BlockSpec(
                (pieces // steps, 2, rows_out, BLOCK), lambda i, *_: (i, 0, 0, 0)
            ),
            scratch_shapes=[
                pltpu.VMEM((2, front + blocks * length + back, BLOCK), jnp.bfloat16),
                pltpu.VMEM((length + BLOCK, 2 * BLOCK), jnp.bfloat16),
                pltpu.VMEM((BLOCK, BLOCK), jnp.float32),
                pltpu.VMEM((BLOCK, BLOCK), jnp.float32),
            ],
        ),
        out_shape=jax.ShapeDtypeStruct((pieces, 2, rows_out, BLOCK), jnp.bfloat16),
        compiler_params=pltpu.CompilerParams(vmem_limit_bytes=VMEM_LIMIT),
        name="shear_columns",
    )(base, rank, *operands)


def sine_cosine(angle):
    turns = jnp.round(angle * (2.0 / np.pi))
    rest = angle - turns * 1.5703125
    rest = rest - turns * 4.837512969970703125e-4
    rest = rest - turns * 7.549789954891882e-8
    square = rest * rest
    sine = rest + rest * square * (
        -1.6666654611e-1 + square * (8.3321608736e-3 - square * 1.9515295891e-4)
    )
    cosine = (
        1.0
        - 0.5 * square
        + square
        * square
        * (4.166664568298827e-2 + square * (-1.388731625493765e-3 + square * 2.443315711809948e-5))
    )
    quadrant = turns.astype(jnp.int32)
    odd = (quadrant & 1) != 0
    sine_out = jnp.where(odd, cosine, sine)
    cosine_out = jnp.where(odd, sine, cosine)
    sine_out = jnp.where((quadrant & 2) != 0, -sine_out, sine_out)
    cosine_out = jnp.where(((quadrant + 1) & 2) != 0, -cosine_out, cosine_out)
    return sine_out, cosine_out


def transmitted(rotated, wave):
    sine, cosine = sine_cosine(rotated[0].astype(jnp.float32))
    amplitude = jnp.exp(-ABSORB * rotated[1].astype(jnp.float32))
    through_real = amplitude * cosine
    through_imaginary = amplitude * sine
    wave_real = wave[0].astype(jnp.float32)
    wave_imaginary = wave[1].astype(jnp.float32)
    return (
        (wave_real * through_real - wave_imaginary * through_imaginary).astype(jnp.bfloat16),
        (wave_real * through_imaginary + wave_imaginary * through_real).astype(jnp.bfloat16),
    )


def travel_first_kernel(length, count, sent, *refs):
    if sent:
        body, top, bottom, matrix, out, field = refs
        for chunk in range(count):
            across = slice(chunk * BLOCK, (chunk + 1) * BLOCK)
            for part in range(2):
                field[part, 0:MARGIN, across] = top[chunk, part]
                field[part, MARGIN : MARGIN + length, across] = body[chunk, part]
                field[part, MARGIN + length :, across] = bottom[chunk, part]
    else:
        body, wave, wave_top, wave_bottom, matrix, out, field = refs
        pieces = [(0, MARGIN, wave_top, 0)]
        pieces += [(MARGIN + first, BLOCK, wave, first) for first in range(0, length, BLOCK)]
        pieces += [(MARGIN + length, MARGIN, wave_bottom, 0)]
        for chunk in range(count):
            across = slice(chunk * BLOCK, (chunk + 1) * BLOCK)
            for place, height, waves, first in pieces:
                parts = transmitted(
                    [body[chunk, p, place : place + height, :] for p in range(2)],
                    [waves[p, first : first + height, across] for p in range(2)],
                )
                for part in range(2):
                    field[part, place : place + height, across] = parts[part]
    for m in range(0, length, BLOCK):
        window = jnp.concatenate([field[0, m : m + WINDOW, :], field[1, m : m + WINDOW, :]], 0)
        result = jnp.dot(matrix[...], window, preferred_element_type=jnp.float32)
        result = result.astype(jnp.bfloat16)
        for chunk in range(count):
            across = slice(chunk * BLOCK, (chunk + 1) * BLOCK)
            for part in range(2):
                out[chunk, part, m : m + BLOCK, :] = result[
                    part * BLOCK : (part + 1) * BLOCK, across
                ]


def travel_first(body, halos, waves, matrix):
    chunks = body.shape[0]
    count = chunks // STEPS if chunks % STEPS == 0 else chunks
    length = body.shape[2] if len(halos) > 0 else body.shape[2] - 2 * MARGIN
    chunk_spec = lambda x: pl.BlockSpec((count, 2, x.shape[2], BLOCK), lambda i: (i, 0, 0, 0))
    wide_spec = lambda x: pl.BlockSpec((2, x.shape[1], count * BLOCK), lambda i: (0, 0, i))
    return pl.pallas_call(
        functools.partial(travel_first_kernel, length, count, len(halos) > 0),
        grid=(chunks // count,),
        in_specs=[chunk_spec(x) for x in (body, *halos)]
        + [wide_spec(x) for x in waves]
        + [pl.BlockSpec(matrix.shape, lambda i: (0, 0))],
        out_specs=pl.BlockSpec((count, 2, length, BLOCK), lambda i: (i, 0, 0, 0)),
        out_shape=jax.ShapeDtypeStruct((chunks, 2, length, BLOCK), jnp.bfloat16),
        scratch_shapes=[pltpu.VMEM((2, length + 2 * MARGIN, count * BLOCK), jnp.bfloat16)],
        compiler_params=pltpu.CompilerParams(vmem_limit_bytes=VMEM_LIMIT),
        name="travel_first",
    )(body, *halos, *waves, matrix)


def travel_second_kernel(chunks, rows, left, body, right, matrix, out):
    parts = [[left[0, p]] + [body[m, p] for m in range(chunks)] + [right[0, p]] for p in range(2)]
    windows = [
        jnp.concatenate(parts[0][m : m + 3] + parts[1][m : m + 3], 1) for m in range(chunks)
    ]
    result = jnp.dot(
        jnp.concatenate(windows, 0), matrix[...], preferred_element_type=jnp.float32
    ).astype(jnp.bfloat16)
    for m in range(chunks):
        for part in range(2):
            out[part, :, m * BLOCK : (m + 1) * BLOCK] = result[
                m * rows : (m + 1) * rows, part * BLOCK : (part + 1) * BLOCK
            ]


def travel_second(left, body, right, matrix):
    chunks, _, length, _ = body.shape
    rows = length // STEPS if length % (STEPS * BLOCK) == 0 else length
    edge = pl.BlockSpec((1, 2, rows, BLOCK), lambda i: (0, 0, i, 0))
    return pl.pallas_call(
        functools.partial(travel_second_kernel, chunks, rows),
        grid=(length // rows,),
        in_specs=[
            edge,
            pl.BlockSpec((chunks, 2, rows, BLOCK), lambda i: (0, 0, i, 0)),
            edge,
            pl.BlockSpec(matrix.shape, lambda i: (0, 0)),
        ],
        out_specs=pl.BlockSpec((2, rows, chunks * BLOCK), lambda i: (0, i, 0)),
        out_shape=jax.ShapeDtypeStruct((2, length, chunks * BLOCK), jnp.bfloat16),
        compiler_params=pltpu.CompilerParams(vmem_limit_bytes=VMEM_LIMIT),
        name="travel_second",
    )(left, body, right, matrix)


def from_both_sides(first, last, axis):
    devices = lax.axis_size(axis)
    up = [(i, i + 1) for i in range(devices - 1)]
    down = [(j, i) for i, j in up]
    return lax.ppermute(last, axis, up), lax.ppermute(first, axis, down)


def after(value, *others):
    return lax.optimization_barrier((value, others))[0]


def ordered_kernel(halo, rank, *refs):
    pieces, (out, first, last) = refs[:-3], refs[-3:]
    count = len(pieces)
    for s, piece in enumerate(pieces):
        place = s ^ rank[0]
        out[place] = piece[0]

        @pl.when(place < halo)
        def _():
            first[place] = piece[0]

        @pl.when(place >= count - halo)
        def _():
            last[place - (count - halo)] = piece[0]


def ordered(pieces, halo, rank):
    count = len(pieces)
    block = pieces[0].shape
    shapes = [(n, *block[1:]) for n in (count, halo, halo)]
    full = lambda shape: pl.BlockSpec(shape, lambda i, *_: (0,) * len(shape))
    return pl.pallas_call(
        functools.partial(ordered_kernel, halo),
        grid_spec=pltpu.PrefetchScalarGridSpec(
            num_scalar_prefetch=1,
            grid=(1,),
            in_specs=[full(block)] * count,
            out_specs=[full(shape) for shape in shapes],
        ),
        out_shape=[jax.ShapeDtypeStruct(shape, pieces[0].dtype) for shape in shapes],
        compiler_params=pltpu.CompilerParams(vmem_limit_bytes=VMEM_LIMIT),
        name="ordered",
    )(rank, *pieces)


def swapped_shares(slots):
    devices = lax.axis_size("row")
    return [slots[0]] + [
        lax.ppermute(slots[s], "row", [(i, i ^ s) for i in range(devices)])
        for s in range(1, devices)
    ]


def group_starts(starts, group, unit):
    lines = starts.shape[-1]
    grouped = starts.reshape(*starts.shape[:-1], lines // group, group)
    base = jnp.min(grouped, -1) // unit
    spare = grouped - base[..., None] * unit
    return base.astype(jnp.int32), spare.reshape(starts.shape)


def on_device(
    volume_plane,
    wave_a,
    wave_b,
    shift_rows,
    fraction_rows,
    shift_columns,
    fraction_columns,
    travel_distance,
):
    _, line_count, width = volume_plane.shape
    row_devices, column_devices = lax.axis_size("row"), lax.axis_size("col")
    row_index, column_index = lax.axis_index("row"), lax.axis_index("col")
    tiles = width // BLOCK
    halo = -(-(SHIFT_X + MARGIN) // BLOCK)
    reach = halo * BLOCK

    forward, inverse = real_tables()
    half = lambda x: jnp.asarray(x, jnp.bfloat16)
    row_tables = (half(forward), half(inverse))
    column_tables = (half(forward.T), half(inverse.T))
    turned_tables = (half(forward), half(inverse[:, ::-1].T))
    in_order = jnp.zeros((1,), jnp.int32)
    by_rank = row_index.astype(jnp.int32).reshape(1)

    part_lines = line_count // PARTS
    lefts, rights, edges = [], [], ()
    for part in range(PARTS):
        lines = after(volume_plane, edges)[:, part * part_lines : (part + 1) * part_lines]
        edges = (lines[:, :, :reach], lines[:, :, width - reach :])
        left, right = from_both_sides(*edges, "col")
        lefts.append(left)
        rights.append(right)

    base_rows, spare_rows = group_starts(reach - MARGIN - shift_rows, GROUP, BLOCK)

    front = -(-(SHIFT_Y + MARGIN) // GROUP) * GROUP
    back = front + 3 * BLOCK
    mine = lambda x: lax.dynamic_slice_in_dim(x, row_index * BLOCK, BLOCK, 1)
    base_columns, spare_columns = group_starts(front - MARGIN - mine(shift_columns), BLOCK, GROUP)
    column_fractions = mine(fraction_columns)

    def first(view, begin, lefts, rights, rank):
        return shear_tile(
            volume_plane,
            lefts,
            rights,
            begin,
            halo,
            base_rows[view, 0],
            rank,
            spare_rows[view, 0],
            fraction_rows[view, 0],
            row_tables,
        )

    def second(view, pieces, place, rank, rows_out):
        return shear_columns(
            pieces,
            place,
            row_devices,
            front,
            back,
            base_columns[view] * GROUP,
            rank,
            spare_columns[view],
            column_fractions[view],
            column_tables,
            rows_out,
        )

    matrices = travel_matrices(travel_distance, forward, inverse)
    real, imaginary = matrices[:, 0], matrices[:, 1]
    along_rows = jnp.concatenate(
        [
            jnp.concatenate([real, -imaginary], 1),
            jnp.concatenate([imaginary, real], 1),
        ],
        2,
    )
    along_rows = jnp.swapaxes(along_rows, 1, 2).astype(jnp.bfloat16)
    spaced = jnp.pad(matrices, ((0, 0), (0, 0), (BLOCK - MARGIN, BLOCK - MARGIN), (0, 0)))
    real, imaginary = spaced[:, 0], spaced[:, 1]
    along_columns = jnp.concatenate(
        [
            jnp.concatenate([real, -imaginary], 1),
            jnp.concatenate([imaginary, real], 1),
        ],
        2,
    ).astype(jnp.bfloat16)

    spread, sheared = [], ()
    for part in range(PARTS):
        left, right = after((lefts[part], rights[part]), sheared)
        sheared = first(1, part * part_lines, [left], [right], in_order)
        spread.append(lax.all_to_all(sheared, "row", split_axis=0, concat_axis=0, tiled=True))
    lefts, rights = after((lefts, rights), sheared)
    sheared_a = first(0, 0, lefts, rights, in_order)
    sheared_a = after(sheared_a, spread)
    spread_a = lax.all_to_all(sheared_a, "row", split_axis=0, concat_axis=0, tiled=True)
    margin = after((wave_b[:, :MARGIN], wave_b[:, -MARGIN:]), sheared)
    wave_b_halos = from_both_sides(*margin, "col")
    spread, wave_b_halos = lax.optimization_barrier((spread, wave_b_halos))

    place = [[(b, part * part_lines) for b in range(row_devices)] for part in range(PARTS)]
    moved_b = second(1, spread, place, in_order, BLOCK)
    moved_b, spread_a = lax.optimization_barrier((moved_b, spread_a))
    whole = lax.all_to_all(moved_b, ("row", "col"), split_axis=0, concat_axis=0, tiled=True)
    whole = whole.reshape(row_devices, column_devices, 2, BLOCK, BLOCK)
    own_lines = lambda x: lax.dynamic_slice_in_dim(x, column_index * BLOCK, BLOCK, 0)
    groups = BLOCK // GROUP
    turned = shear_whole(
        whole,
        halo,
        lax.dynamic_slice_in_dim(base_rows[1, 1], column_index * groups, groups, 0),
        own_lines(spare_rows[1, 1]),
        own_lines(fraction_rows[1, 1]),
        turned_tables,
    )

    moved_a = second(
        0, [spread_a], [[(b, 0) for b in range(row_devices)]], by_rank, line_count
    )
    pieces = swapped_shares([moved_a[s : s + 1] for s in range(row_devices)])
    tile, low, high = ordered(pieces, halo, by_rank)
    left, right = from_both_sides(low, high, "col")
    field_a = shear_tile(
        tile,
        [left],
        [right],
        0,
        halo,
        base_rows[0, 1],
        in_order,
        spare_rows[0, 1],
        fraction_rows[0, 1],
        row_tables,
        wave_a,
    )

    turned = after(turned, (left, right))
    turned = lax.all_to_all(turned, "col", split_axis=0, concat_axis=0, tiled=True)

    halos = from_both_sides(field_a[:, :, :MARGIN], field_a[:, :, -MARGIN:], "row")
    half_a = travel_first(field_a, halos, (), along_rows[0])
    left, right = from_both_sides(half_a[:1], half_a[-1:], "col")
    exit_a = travel_second(left, half_a, right, along_columns[0])

    half_b = travel_first(turned, (), (wave_b, *wave_b_halos), along_rows[1])
    left, right = from_both_sides(half_b[:1], half_b[-1:], "row")
    exit_b = travel_second(left, half_b, right, along_columns[1])
    return exit_a, exit_b


def swapped(value, axis, bit):
    mask = 2**bit
    pairs = [(source, source ^ mask) for source in range(lax.axis_size(axis))]
    return lax.ppermute(value, axis, pairs)


def padded_2(x, sides, width):
    for axis, dim in sides:
        devices, length = (lax.axis_size(axis), x.shape[dim])
        up = [(i, (i + 1) % devices) for i in range(devices - 1)]
        down = [(j, i) for i, j in up]
        last = lax.slice_in_dim(x, length - width, length, axis=dim)
        first = lax.slice_in_dim(x, 0, width, axis=dim)
        before = lax.ppermute(last, axis, up)
        after = lax.ppermute(first, axis, down)
        x = jnp.concatenate([before, x, after], axis=dim)
    return x


def fourier_tables(block_len, margin):
    window_len = block_len + 2 * margin
    frequency = jnp.arange(window_len, dtype=jnp.int32) - window_len // 2
    position = jnp.arange(window_len, dtype=jnp.int32)
    angles = (
        2.0
        * jnp.pi
        * jnp.mod(position[:, None] * frequency[None, :], window_len).astype(jnp.float32)
        / window_len
    )
    cosine = jnp.cos(angles)
    sines = jnp.sin(angles)
    forward = jnp.concatenate(
        [jnp.concatenate([cosine, -sines], 1), jnp.concatenate([sines, cosine], 1)], 0
    ).astype(jnp.bfloat16)
    target = jnp.arange(block_len, dtype=jnp.int32) + margin
    inverse_angle = (
        2.0
        * jnp.pi
        * jnp.mod(frequency[:, None] * target[None, :], window_len).astype(jnp.float32)
        / window_len
    )
    inverse_cosine = jnp.cos(inverse_angle) / window_len
    inverse_sine = jnp.sin(inverse_angle) / window_len
    inverse = jnp.concatenate(
        [
            jnp.concatenate([inverse_cosine, inverse_sine], 1),
            jnp.concatenate([-inverse_sine, inverse_cosine], 1),
        ],
        0,
    ).astype(jnp.bfloat16)
    return (forward, inverse, frequency.astype(jnp.float32))


def shear_ramp(fractions, frequency):
    window_len = frequency.shape[0]
    phases = -2.0 * jnp.pi / window_len * fractions[:, None] * frequency[None, :]
    nyquist = (jnp.arange(window_len) == 0)[None, :]
    ramp_real = jnp.where(nyquist, jnp.cos(jnp.pi * fractions)[:, None], jnp.cos(phases))
    ramp_imaginary = jnp.where(nyquist, 0.0, jnp.sin(phases))
    return (ramp_real, ramp_imaginary)


def travel_ramp(distance, frequency):
    window_len = frequency.shape[0]
    phases = -2.0 * jnp.pi / (window_len * window_len) * distance * frequency * frequency
    return (jnp.cos(phases)[None, :], jnp.sin(phases)[None, :])


def select_window(padded, starts, out_len):
    total_len = padded.shape[2]
    offset_range = total_len - out_len
    bit_count = max(offset_range, 1).bit_length()
    current = jnp.pad(padded, ((0, 0), (0, 0), (0, out_len + 2**bit_count - 1 - total_len)))
    for bit_number in reversed(range(bit_count)):
        stride = 2**bit_number
        kept_len = current.shape[2] - stride
        chosen = (starts // stride % 2 == 1)[None, :, None]
        current = jnp.where(
            chosen, current[:, :, stride : stride + kept_len], current[:, :, :kept_len]
        )
    return current


def line_pass(padded, extent, shifts, ramp_real, ramp_imaginary, tables):
    forward, inverse = (tables[0], tables[1])
    window_len = BLOCK + 2 * MARGIN
    line_count = padded.shape[1]
    blocks = (padded.shape[2] - 2 * extent) // BLOCK
    reach_len = blocks * BLOCK + 2 * MARGIN
    if shifts is None:
        shifted = padded
    else:
        starts = extent - MARGIN - shifts
        shifted = select_window(padded, starts, reach_len)
    middle = shifted[:, :, MARGIN : MARGIN + blocks * BLOCK].reshape(2, line_count, blocks, BLOCK)
    left_rim = shifted[:, :, : blocks * BLOCK].reshape(2, line_count, blocks, BLOCK)[..., :MARGIN]
    right_rim = shifted[:, :, 2 * MARGIN : 2 * MARGIN + blocks * BLOCK].reshape(
        2, line_count, blocks, BLOCK
    )[..., BLOCK - MARGIN :]
    windows = jnp.concatenate([left_rim, middle, right_rim], 3)
    spectrum = jnp.einsum(
        "cpms,cst->pmt",
        windows,
        forward.reshape(2, window_len, 2 * window_len),
        preferred_element_type=jnp.float32,
    )
    spec_real = spectrum[..., :window_len]
    spec_imaginary = spectrum[..., window_len:]
    factor_real = ramp_real[:, None, :]
    factor_imaginary = ramp_imaginary[:, None, :]
    ramped = jnp.concatenate(
        [
            spec_real * factor_real - spec_imaginary * factor_imaginary,
            spec_real * factor_imaginary + spec_imaginary * factor_real,
        ],
        -1,
    ).astype(jnp.bfloat16)
    result = jnp.einsum(
        "pms,scb->cpmb",
        ramped,
        inverse.reshape(2 * window_len, 2, BLOCK),
        preferred_element_type=jnp.float32,
    )
    return result.reshape(2, line_count, blocks * BLOCK).astype(jnp.bfloat16)


def single_pass(padded, extent, shifts, fractions, tables):
    ramp_real, ramp_imaginary = shear_ramp(fractions, tables[2])
    return line_pass(padded, extent, shifts, ramp_real, ramp_imaginary, tables)


def general_shear_columns(stacked, shifts, fractions, tables):
    halo_depth = SHIFT_X + MARGIN
    inputs = stacked.shape[0]
    column_devices = lax.axis_size("col")
    share = stacked.shape[2] // column_devices
    offset = lax.axis_index("col") * share
    spread = lax.all_to_all(stacked, "col", split_axis=2, concat_axis=3, tiled=True)
    padded = jnp.pad(spread, ((0, 0), (0, 0), (0, 0), (halo_depth, halo_depth)))
    row_shifts = lax.dynamic_slice_in_dim(shifts, offset, share, 1)
    row_fractions = lax.dynamic_slice_in_dim(fractions, offset, share, 1)
    sheared = jnp.stack(
        [
            single_pass(
                padded[min(0, inputs - 1)], halo_depth, row_shifts[0], row_fractions[0], tables
            )
        ]
    )
    return lax.all_to_all(sheared, "col", split_axis=3, concat_axis=2, tiled=True)


def shear_along_first(padded_lines, halo_depth, shifts, fractions, tables):
    flipped = jnp.swapaxes(padded_lines[0], 1, 2)
    moved = single_pass(flipped, halo_depth, shifts[0], fractions[0], tables)
    sheared = [jnp.swapaxes(moved, 1, 2)]
    return jnp.stack(sheared)


def shear_rows_pass(stacked, shifts, fractions, tables):
    halo_depth = SHIFT_Y + MARGIN
    row_devices = lax.axis_size("row")
    share = stacked.shape[3] // row_devices
    offset = lax.axis_index("row") * share
    spread = lax.all_to_all(stacked, "row", split_axis=3, concat_axis=2, tiled=True)
    padded = jnp.pad(spread, ((0, 0), (0, 0), (halo_depth, halo_depth), (0, 0)))
    column_shifts = lax.dynamic_slice_in_dim(shifts, offset, share, 1)
    column_fractions = lax.dynamic_slice_in_dim(fractions, offset, share, 1)
    sheared = shear_along_first(padded, halo_depth, column_shifts, column_fractions, tables)
    return lax.all_to_all(sheared, "row", split_axis=2, concat_axis=3, tiled=True)


def travel_local(extended, distance, tables):
    ramp_real, ramp_imaginary = travel_ramp(distance, tables[2])
    halfway = line_pass(extended, MARGIN, None, ramp_real, ramp_imaginary, tables)
    flipped = jnp.swapaxes(halfway, 1, 2)
    finished = line_pass(flipped, MARGIN, None, ramp_real, ramp_imaginary, tables)
    return jnp.swapaxes(finished, 1, 2)


def transmit(rotated, wave):
    phase_part = rotated[0].astype(jnp.float32)
    absorb_part = rotated[1].astype(jnp.float32)
    amplitude = jnp.exp(-ABSORB * absorb_part)
    through_real = amplitude * jnp.cos(phase_part)
    through_imaginary = amplitude * jnp.sin(phase_part)
    wave_real = wave[0].astype(jnp.float32)
    wave_imaginary = wave[1].astype(jnp.float32)
    return jnp.stack(
        [
            wave_real * through_real - wave_imaginary * through_imaginary,
            wave_real * through_imaginary + wave_imaginary * through_real,
        ]
    ).astype(jnp.bfloat16)


def general_on_device(
    volume_plane,
    wave_a,
    wave_b,
    shift_rows,
    fraction_rows,
    shift_columns,
    fraction_columns,
    travel_distance,
):
    tables = fourier_tables(BLOCK, MARGIN)
    source = volume_plane[None]
    results = []
    for member in range(2):
        stacked = general_shear_columns(
            source,
            shift_rows[member : member + 1, 0],
            fraction_rows[member : member + 1, 0],
            tables,
        )
        stacked = shear_rows_pass(
            stacked,
            shift_columns[member : member + 1],
            fraction_columns[member : member + 1],
            tables,
        )
        stacked = general_shear_columns(
            stacked,
            shift_rows[member : member + 1, 1],
            fraction_rows[member : member + 1, 1],
            tables,
        )
        results.append(stacked[0])
    view_one = results[0]
    view_two = results[1]
    turned = jnp.swapaxes(jnp.flip(view_two, 2), 1, 2)
    for bit_number in range(lax.axis_size("col").bit_length() - 1):
        turned = swapped(turned, "col", bit_number)
    product_a = transmit(view_one, wave_a)
    extended_a = padded_2(product_a, (("row", 1), ("col", 2)), MARGIN)
    exit_a = travel_local(extended_a, travel_distance[0], tables)
    product_b = transmit(turned, wave_b)
    extended_b = padded_2(product_b, (("row", 2), ("col", 1)), MARGIN)
    exit_b = travel_local(extended_b, travel_distance[1], tables)
    return (exit_a, exit_b)


def solution(mesh):
    def either(volume_plane, *rest):
        rows, width = volume_plane.shape[1:]
        fits = (
            rows == BLOCK * lax.axis_size("col")
            and width == BLOCK * lax.axis_size("row")
            and width >= SHIFT_X + MARGIN
        )
        chosen = on_device if fits else general_on_device
        return chosen(volume_plane, *rest)

    return jax.shard_map(
        either,
        mesh=mesh,
        in_specs=(
            P(None, "row", "col"),
            P(None, "row", "col"),
            P(None, "col", "row"),
            P(None, None, "row"),
            P(None, None, "row"),
            P(None, "col"),
            P(None, "col"),
            P(),
        ),
        out_specs=(P(None, "row", "col"), P(None, "col", "row")),
        check_vma=False,
    )
```

```python
import functools

import jax
import jax.numpy as jnp
import numpy as np
from jax import lax
from jax.experimental import pallas as pl
from jax.experimental.pallas import tpu as pltpu
from jax.sharding import PartitionSpec as P

BLOCK = 128
MARGIN = 32
SHIFT_X = 864
SHIFT_Y = 1728


ABSORB = 0.25

WINDOW = BLOCK + 2 * MARGIN
BINS = WINDOW // 2
GROUP = 16
PARTS = 2
ROWS = 256
STEPS = 2
VMEM_LIMIT = 56 * 1024 * 1024


def angle_table(rows, columns):
    return 2.0 * np.pi * (np.outer(rows, columns) % WINDOW) / WINDOW


def real_tables():
    position = np.arange(WINDOW)
    bins = np.arange(BINS + 1)
    target = np.arange(BLOCK) + MARGIN
    forward = np.zeros((2 * BLOCK, 2 * BLOCK), np.float32)
    forward[:WINDOW, : BINS + 1] = np.cos(angle_table(position, bins))
    forward[:WINDOW, BLOCK + 1 : BLOCK + BINS] = -np.sin(angle_table(position, bins[1:BINS]))
    weight = np.where((bins == 0) | (bins == BINS), 1.0, 2.0) / WINDOW
    inverse = np.zeros((2 * BLOCK, BLOCK), np.float32)
    inverse[: BINS + 1] = np.cos(angle_table(bins, target)) * weight[:, None]
    inverse[BLOCK + 1 : BLOCK + BINS] = (
        -np.sin(angle_table(bins[1:BINS], target)) * weight[1:BINS, None]
    )
    return forward, inverse


def travel_matrices(distance, forward, inverse):
    frequency = jnp.arange(BLOCK, dtype=jnp.float32)
    phases = -2.0 * jnp.pi / (WINDOW * WINDOW) * distance[:, None] * frequency * frequency
    ramps = jnp.stack([jnp.cos(phases), jnp.sin(phases)], 1)
    ramps = jnp.concatenate([ramps, ramps], 2)
    scaled = ramps[..., None] * jnp.asarray(inverse)
    matrices = jnp.einsum(
        "pq,vrqu->vrpu",
        jnp.asarray(forward[:WINDOW]),
        scaled,
        precision=lax.Precision.HIGHEST,
    )
    return matrices


def lane_iota(rows):
    return lax.broadcasted_iota(jnp.int32, (rows, BLOCK), 1)


def shift_lines(strip, shifted, base, base_offset, spare, windows, chunk_offset, rows):
    def one_group(group, carry):
        first = pl.multiple_of(group * GROUP, GROUP)
        lines = pl.ds(first, GROUP)
        start = base[base_offset + group] + chunk_offset
        offset = spare[lines, :]
        later = offset >= BLOCK
        lane = lane_iota(GROUP) + (offset & (BLOCK - 1))
        wraps = lane >= BLOCK
        index = lane & (BLOCK - 1)
        for part in range(2):
            here = strip[start, part, lines, :].astype(jnp.float32)
            before = None
            for i in range(windows + 2):
                following = strip[start + i + 1, part, lines, :].astype(jnp.float32)
                turned = jnp.take_along_axis(jnp.where(later, following, here), index, axis=1)
                if before is not None:
                    shifted[i - 1, part, lines, :] = jnp.where(wraps, turned, before).astype(
                        jnp.bfloat16
                    )
                before = turned
                here = following
        return carry

    lax.fori_loop(0, rows // GROUP, one_group, 0, unroll=4)


def ramped_lines(shifted, windows, rows, cosine, sine, forward):
    count = len(windows)
    lower = jnp.concatenate([shifted[m].reshape(2 * rows, BLOCK) for m in windows], 0)
    upper = jnp.concatenate([shifted[m + 1].reshape(2 * rows, BLOCK) for m in windows], 0)
    spectrum = jnp.dot(
        jnp.concatenate([lower, upper], 1), forward[...], preferred_element_type=jnp.float32
    )
    real = spectrum[:, :BLOCK].reshape(count * 2, rows, BLOCK)
    imaginary = spectrum[:, BLOCK:].reshape(count * 2, rows, BLOCK)
    ramp_real = cosine[...][None]
    ramp_imaginary = sine[...][None]
    ramped = jnp.concatenate(
        [
            (real * ramp_real - imaginary * ramp_imaginary).astype(jnp.bfloat16),
            (real * ramp_imaginary + imaginary * ramp_real).astype(jnp.bfloat16),
        ],
        2,
    )
    return ramped.reshape(count * 2 * rows, 2 * BLOCK)


def down_lines(vector):
    return jnp.broadcast_to(vector, (BLOCK, vector.shape[1])).T


def line_ramps(fractions, cosine, sine):
    bins = lane_iota(fractions.shape[1]).astype(jnp.float32)
    sine[...], cosine[...] = sine_cosine(down_lines(fractions) * bins * (-2.0 * np.pi / WINDOW))


def shear_tile_kernel(halo, tiles, rows, batch, wide, parts, sent, base, rank, *refs):
    lefts, rights, refs = refs[:parts], refs[parts : 2 * parts], refs[2 * parts :]
    waves, refs = refs[: int(sent)], refs[int(sent) :]
    own, offsets, fractions, forward, inverse, out = refs[:6]
    strip, shifted, spare, cosine, sine = refs[6:]
    step = pl.program_id(0)
    groups = rows // GROUP
    end = halo + tiles + halo

    @pl.when(step == 0)
    def _():
        strip[end : end + 2] = jnp.zeros((2, 2, rows, BLOCK), jnp.bfloat16)

    def fill(piece, first, count):
        for i in range(count):
            if wide:
                strip[first + i] = piece[:, :, i * BLOCK : (i + 1) * BLOCK]
            else:
                strip[first + i] = piece[i]

    share = pl.num_programs(0) // parts
    for part in range(parts):

        @pl.when(step // share == part)
        def _():
            fill(lefts[part], 0, halo)
            fill(rights[part], halo + tiles, halo)

    fill(own, halo, tiles)
    spare[...] = down_lines(offsets[0]).astype(jnp.int32)
    line_ramps(fractions[0], cosine, sine)
    shift_lines(strip, shifted, base, step * groups, spare, tiles, 0, rows)
    for first in range(0, tiles, batch):
        windows = [slot if sent else slot ^ rank[0] for slot in range(first, first + batch)]
        ramped = ramped_lines(shifted, windows, rows, cosine, sine, forward)
        result = jnp.dot(ramped, inverse[...], preferred_element_type=jnp.float32)
        result = result.astype(jnp.bfloat16).reshape(batch, 2, rows, BLOCK)
        if sent:
            for i, window in enumerate(windows):
                wave = waves[0][:, :, window * BLOCK : (window + 1) * BLOCK]
                for part, value in enumerate(transmitted(result[i], wave)):
                    out[window, part] = value
        else:
            out[first : first + batch] = result


def shear_tile(own, lefts, rights, first, halo, base, rank, spare, fractions, tables, *waves):
    wide = own.ndim == 3
    parts = len(lefts)
    part_lines = lefts[0].shape[-2]
    line_count = parts * part_lines
    tiles = own.shape[2] // BLOCK if wide else own.shape[0]
    rows = min(part_lines, ROWS)
    share = part_lines // rows
    offset = first // rows
    forward, inverse = tables

    def piece_spec(piece, place):
        if wide:
            return pl.BlockSpec((2, rows, piece.shape[2]), lambda i, *_: (0, place(i), 0))
        return pl.BlockSpec((piece.shape[0], 2, rows, BLOCK), lambda i, *_: (0, 0, place(i), 0))

    halo_specs = [
        piece_spec(x, lambda i, part=part: jnp.clip(i - part * share, 0, share - 1))
        for x in (lefts[0], rights[0])
        for part in range(parts)
    ]
    line_spec = pl.BlockSpec((1, 1, rows), lambda i, *_: (i + offset, 0, 0))
    along = lambda x: x.astype(jnp.float32).reshape(-1, 1, rows)
    out_shape = jax.ShapeDtypeStruct((tiles, 2, line_count, BLOCK), jnp.bfloat16)
    out_spec = pl.BlockSpec((tiles, 2, rows, BLOCK), lambda i, *_: (0, 0, i, 0))
    groups = rows // GROUP
    kernel = functools.partial(
        shear_tile_kernel,
        halo,
        tiles,
        rows,
        tiles // 4 if tiles % 4 == 0 else tiles,
        wide,
        parts,
        len(waves) > 0,
    )
    return pl.pallas_call(
        kernel,
        grid_spec=pltpu.PrefetchScalarGridSpec(
            num_scalar_prefetch=2,
            grid=(line_count // rows,),
            in_specs=halo_specs
            + [pl.BlockSpec((2, rows, x.shape[2]), lambda i, *_: (0, i + offset, 0)) for x in waves]
            + [piece_spec(own, lambda i: i + offset)]
            + [line_spec] * 2
            + [
                pl.BlockSpec(forward.shape, lambda i, *_: (0, 0)),
                pl.BlockSpec(inverse.shape, lambda i, *_: (0, 0)),
            ],
            out_specs=out_spec,
            scratch_shapes=[
                pltpu.VMEM((halo + tiles + halo + 2, 2, rows, BLOCK), jnp.bfloat16),
                pltpu.VMEM((tiles + 1, 2, rows, BLOCK), jnp.bfloat16),
                pltpu.VMEM((rows, BLOCK), jnp.int32),
                pltpu.VMEM((rows, BLOCK), jnp.float32),
                pltpu.VMEM((rows, BLOCK), jnp.float32),
            ],
        ),
        out_shape=out_shape,
        compiler_params=pltpu.CompilerParams(vmem_limit_bytes=VMEM_LIMIT),
        name="shear_tile",
    )(
        lax.slice_in_dim(base, offset * groups, offset * groups + line_count // GROUP),
        rank,
        *lefts,
        *rights,
        *waves,
        own,
        along(spare),
        along(fractions),
        forward,
        inverse,
    )


def shear_whole_kernel(
    halo,
    devices,
    tiles,
    rows,
    base,
    own,
    offsets,
    fractions,
    forward,
    flipped,
    out,
    strip,
    shifted,
    spare,
    cosine,
    sine,
):
    step = pl.program_id(0)
    chunks = devices * tiles
    length = tiles * BLOCK

    @pl.when(step == 0)
    def _():
        strip[0:halo] = jnp.zeros((halo, 2, rows, BLOCK), jnp.bfloat16)
        strip[halo + chunks :] = jnp.zeros((halo + 2, 2, rows, BLOCK), jnp.bfloat16)
        for chunk in range(chunks):
            strip[halo + chunk] = own[chunk % tiles, chunk // tiles]
        out[0, :, 0:MARGIN, :] = jnp.zeros((2, MARGIN, rows), jnp.bfloat16)
        out[devices - 1, :, MARGIN + length :, :] = jnp.zeros((2, MARGIN, rows), jnp.bfloat16)
        spare[...] = down_lines(offsets[...]).astype(jnp.int32)
        line_ramps(fractions[...], cosine, sine)

    shift_lines(strip, shifted, base, 0, spare, tiles, step * tiles, rows)
    ramped = ramped_lines(shifted, range(tiles), rows, cosine, sine, forward)
    target = devices - 1 - step
    result = lax.dot_general(
        flipped[...], ramped, (((1,), (1,)), ((), ())), preferred_element_type=jnp.float32
    ).astype(jnp.bfloat16)
    for window in range(tiles):
        block = tiles - 1 - window
        low = MARGIN + block * BLOCK
        for part in range(2):
            lanes = (2 * window + part) * rows
            piece = result[:, lanes : lanes + rows]
            out[target, part, low : low + BLOCK, :] = piece
            if block == 0:

                @pl.when(target > 0)
                def _():
                    out[target - 1, part, MARGIN + length :, :] = piece[:MARGIN]

            if block == tiles - 1:

                @pl.when(target < devices - 1)
                def _():
                    out[target + 1, part, 0:MARGIN, :] = piece[BLOCK - MARGIN :]


def shear_whole(own, halo, base, spare, fractions, tables):
    tiles, devices, _, rows, _ = own.shape
    forward, flipped = tables
    operands = (
        own,
        spare.astype(jnp.float32).reshape(1, rows),
        fractions.reshape(1, rows),
        forward,
        flipped,
    )
    full = lambda shape: pl.BlockSpec(shape, lambda i, *_: (0,) * len(shape))
    out = (devices, 2, tiles * BLOCK + 2 * MARGIN, rows)
    return pl.pallas_call(
        functools.partial(shear_whole_kernel, halo, devices, tiles, rows),
        grid_spec=pltpu.PrefetchScalarGridSpec(
            num_scalar_prefetch=1,
            grid=(devices,),
            in_specs=[full(x.shape) for x in operands],
            out_specs=full(out),
            scratch_shapes=[
                pltpu.VMEM((2 * halo + devices * tiles + 2, 2, rows, BLOCK), jnp.bfloat16),
                pltpu.VMEM((tiles + 1, 2, rows, BLOCK), jnp.bfloat16),
                pltpu.VMEM((rows, BLOCK), jnp.int32),
                pltpu.VMEM((rows, BLOCK), jnp.float32),
                pltpu.VMEM((rows, BLOCK), jnp.float32),
            ],
        ),
        out_shape=jax.ShapeDtypeStruct(out, jnp.bfloat16),
        compiler_params=pltpu.CompilerParams(vmem_limit_bytes=VMEM_LIMIT),
        name="shear_whole",
    )(base, *operands)


def shear_columns_kernel(front, blocks, length, rows_out, place, base, rank, *refs):
    owns, refs = refs[: len(place)], refs[len(place) :]
    offsets, fractions, forward, inverse, out, strip, shifted, cosine, sine = refs
    step = pl.program_id(0)
    per_step = length // BLOCK
    per_grid = blocks // pl.num_programs(0)
    total = strip.shape[1]

    @pl.when(step == 0)
    def _():
        strip[:, 0:front, :] = jnp.zeros((2, front, BLOCK), jnp.bfloat16)
        back = front + blocks * length
        strip[:, back:, :] = jnp.zeros((2, total - back, BLOCK), jnp.bfloat16)
        for own, slots in zip(owns, place):
            count = own.shape[2]
            for i, (slot, within) in enumerate(slots):
                first = pl.multiple_of(front + (slot ^ rank[0]) * length + within, GROUP)
                for part in range(2):
                    strip[part, pl.ds(first, count), :] = own[i, part]
        bins = lax.broadcasted_iota(jnp.int32, (BLOCK, BLOCK), 0).astype(jnp.float32)
        sine[...], cosine[...] = sine_cosine(bins * fractions[...] * (-2.0 * np.pi / WINDOW))

    offset = jnp.broadcast_to(offsets[...], (8, BLOCK))
    row = lax.broadcasted_iota(jnp.int32, (8, BLOCK), 0) + (offset & 7)
    wraps = row >= 8
    index = row & 7

    def one_chunk(block_rows, chunk):
        begin = pl.multiple_of(base[0] + block_rows + chunk * BLOCK, GROUP)
        for part in range(2):
            value = strip[part, pl.ds(begin, 2 * BLOCK), :].astype(jnp.float32)
            value = value.reshape(2 * BLOCK // 8, 8, BLOCK)
            for bit in (64, 32, 16, 8):
                taken = ((offset & bit) != 0)[None]
                value = jnp.where(taken, value[bit // 8 :], value[: -(bit // 8)])
            pieces = [
                jnp.take_along_axis(value[i], index, axis=0) for i in range(BLOCK // 8 + 1)
            ]
            moved = [
                jnp.where(wraps, pieces[i + 1], pieces[i]) for i in range(BLOCK // 8)
            ]
            shifted[chunk * BLOCK : (chunk + 1) * BLOCK, part * BLOCK : (part + 1) * BLOCK] = (
                jnp.concatenate(moved, 0).astype(jnp.bfloat16)
            )

    def one_block(local, carry):
        block_rows = ((step * per_grid + local) ^ rank[0]) * length
        for chunk in range(per_step + 1):
            one_chunk(block_rows, chunk)
        windows = [shifted[m * BLOCK : (m + 2) * BLOCK, :] for m in range(per_step)]
        spectrum = jnp.dot(
            forward[...], jnp.concatenate(windows, 1), preferred_element_type=jnp.float32
        )
        ramp_real = jnp.concatenate([cosine[...]] * (2 * per_step), 1)
        ramp_imaginary = jnp.concatenate([sine[...]] * (2 * per_step), 1)
        real, imaginary = spectrum[:BLOCK], spectrum[BLOCK:]
        ramped = jnp.concatenate(
            [
                (real * ramp_real - imaginary * ramp_imaginary).astype(jnp.bfloat16),
                (real * ramp_imaginary + imaginary * ramp_real).astype(jnp.bfloat16),
            ],
            0,
        )
        result = jnp.dot(inverse[...], ramped, preferred_element_type=jnp.float32)
        result = result.astype(jnp.bfloat16)
        for window in range(per_step):
            piece, within = window * BLOCK // rows_out, window * BLOCK % rows_out
            for part in range(2):
                lanes = (2 * window + part) * BLOCK
                out[local * (length // rows_out) + piece, part, within : within + BLOCK, :] = (
                    result[:, lanes : lanes + BLOCK]
                )
        return carry

    lax.fori_loop(0, per_grid, one_block, 0)


def shear_columns(owns, place, blocks, front, back, base, rank, spare, fractions, tables, rows_out):
    length = sum(own.shape[0] * own.shape[2] for own in owns) // blocks
    forward, inverse = tables
    operands = (
        *owns,
        spare.astype(jnp.int32).reshape(1, BLOCK),
        fractions.reshape(1, BLOCK),
        forward,
        inverse,
    )
    full = lambda shape: pl.BlockSpec(shape, lambda i, *_: (0,) * len(shape))
    pieces = blocks * length // rows_out
    steps = STEPS if blocks % STEPS == 0 else 1
    return pl.pallas_call(
        functools.partial(shear_columns_kernel, front, blocks, length, rows_out, place),
        grid_spec=pltpu.PrefetchScalarGridSpec(
            num_scalar_prefetch=2,
            grid=(steps,),
            in_specs=[full(x.shape) for x in operands],
            out_specs=pl.BlockSpec(
                (pieces // steps, 2, rows_out, BLOCK), lambda i, *_: (i, 0, 0, 0)
            ),
            scratch_shapes=[
                pltpu.VMEM((2, front + blocks * length + back, BLOCK), jnp.bfloat16),
                pltpu.VMEM((length + BLOCK, 2 * BLOCK), jnp.bfloat16),
                pltpu.VMEM((BLOCK, BLOCK), jnp.float32),
                pltpu.VMEM((BLOCK, BLOCK), jnp.float32),
            ],
        ),
        out_shape=jax.ShapeDtypeStruct((pieces, 2, rows_out, BLOCK), jnp.bfloat16),
        compiler_params=pltpu.CompilerParams(vmem_limit_bytes=VMEM_LIMIT),
        name="shear_columns",
    )(base, rank, *operands)


def sine_cosine(angle):
    turns = jnp.round(angle * (2.0 / np.pi))
    rest = angle - turns * 1.5703125
    rest = rest - turns * 4.837512969970703125e-4
    rest = rest - turns * 7.549789954891882e-8
    square = rest * rest
    sine = rest + rest * square * (
        -1.6666654611e-1 + square * (8.3321608736e-3 - square * 1.9515295891e-4)
    )
    cosine = (
        1.0
        - 0.5 * square
        + square
        * square
        * (4.166664568298827e-2 + square * (-1.388731625493765e-3 + square * 2.443315711809948e-5))
    )
    quadrant = turns.astype(jnp.int32)
    odd = (quadrant & 1) != 0
    sine_out = jnp.where(odd, cosine, sine)
    cosine_out = jnp.where(odd, sine, cosine)
    sine_out = jnp.where((quadrant & 2) != 0, -sine_out, sine_out)
    cosine_out = jnp.where(((quadrant + 1) & 2) != 0, -cosine_out, cosine_out)
    return sine_out, cosine_out


def transmitted(rotated, wave):
    sine, cosine = sine_cosine(rotated[0].astype(jnp.float32))
    amplitude = jnp.exp(-ABSORB * rotated[1].astype(jnp.float32))
    through_real = amplitude * cosine
    through_imaginary = amplitude * sine
    wave_real = wave[0].astype(jnp.float32)
    wave_imaginary = wave[1].astype(jnp.float32)
    return (
        (wave_real * through_real - wave_imaginary * through_imaginary).astype(jnp.bfloat16),
        (wave_real * through_imaginary + wave_imaginary * through_real).astype(jnp.bfloat16),
    )


def travel_first_kernel(length, count, sent, *refs):
    if sent:
        body, top, bottom, matrix, out, field = refs
        for chunk in range(count):
            across = slice(chunk * BLOCK, (chunk + 1) * BLOCK)
            for part in range(2):
                field[part, 0:MARGIN, across] = top[chunk, part]
                field[part, MARGIN : MARGIN + length, across] = body[chunk, part]
                field[part, MARGIN + length :, across] = bottom[chunk, part]
    else:
        body, wave, wave_top, wave_bottom, matrix, out, field = refs
        pieces = [(0, MARGIN, wave_top, 0)]
        pieces += [(MARGIN + first, BLOCK, wave, first) for first in range(0, length, BLOCK)]
        pieces += [(MARGIN + length, MARGIN, wave_bottom, 0)]
        for chunk in range(count):
            across = slice(chunk * BLOCK, (chunk + 1) * BLOCK)
            for place, height, waves, first in pieces:
                parts = transmitted(
                    [body[chunk, p, place : place + height, :] for p in range(2)],
                    [waves[p, first : first + height, across] for p in range(2)],
                )
                for part in range(2):
                    field[part, place : place + height, across] = parts[part]
    for m in range(0, length, BLOCK):
        window = jnp.concatenate([field[0, m : m + WINDOW, :], field[1, m : m + WINDOW, :]], 0)
        result = jnp.dot(matrix[...], window, preferred_element_type=jnp.float32)
        result = result.astype(jnp.bfloat16)
        for chunk in range(count):
            across = slice(chunk * BLOCK, (chunk + 1) * BLOCK)
            for part in range(2):
                out[chunk, part, m : m + BLOCK, :] = result[
                    part * BLOCK : (part + 1) * BLOCK, across
                ]


def travel_first(body, halos, waves, matrix):
    chunks = body.shape[0]
    count = chunks // STEPS if chunks % STEPS == 0 else chunks
    length = body.shape[2] if len(halos) > 0 else body.shape[2] - 2 * MARGIN
    chunk_spec = lambda x: pl.BlockSpec((count, 2, x.shape[2], BLOCK), lambda i: (i, 0, 0, 0))
    wide_spec = lambda x: pl.BlockSpec((2, x.shape[1], count * BLOCK), lambda i: (0, 0, i))
    return pl.pallas_call(
        functools.partial(travel_first_kernel, length, count, len(halos) > 0),
        grid=(chunks // count,),
        in_specs=[chunk_spec(x) for x in (body, *halos)]
        + [wide_spec(x) for x in waves]
        + [pl.BlockSpec(matrix.shape, lambda i: (0, 0))],
        out_specs=pl.BlockSpec((count, 2, length, BLOCK), lambda i: (i, 0, 0, 0)),
        out_shape=jax.ShapeDtypeStruct((chunks, 2, length, BLOCK), jnp.bfloat16),
        scratch_shapes=[pltpu.VMEM((2, length + 2 * MARGIN, count * BLOCK), jnp.bfloat16)],
        compiler_params=pltpu.CompilerParams(vmem_limit_bytes=VMEM_LIMIT),
        name="travel_first",
    )(body, *halos, *waves, matrix)


def travel_second_kernel(chunks, rows, left, body, right, matrix, out):
    parts = [[left[0, p]] + [body[m, p] for m in range(chunks)] + [right[0, p]] for p in range(2)]
    windows = [
        jnp.concatenate(parts[0][m : m + 3] + parts[1][m : m + 3], 1) for m in range(chunks)
    ]
    result = jnp.dot(
        jnp.concatenate(windows, 0), matrix[...], preferred_element_type=jnp.float32
    ).astype(jnp.bfloat16)
    for m in range(chunks):
        for part in range(2):
            out[part, :, m * BLOCK : (m + 1) * BLOCK] = result[
                m * rows : (m + 1) * rows, part * BLOCK : (part + 1) * BLOCK
            ]


def travel_second(left, body, right, matrix):
    chunks, _, length, _ = body.shape
    rows = length // STEPS if length % (STEPS * BLOCK) == 0 else length
    edge = pl.BlockSpec((1, 2, rows, BLOCK), lambda i: (0, 0, i, 0))
    return pl.pallas_call(
        functools.partial(travel_second_kernel, chunks, rows),
        grid=(length // rows,),
        in_specs=[
            edge,
            pl.BlockSpec((chunks, 2, rows, BLOCK), lambda i: (0, 0, i, 0)),
            edge,
            pl.BlockSpec(matrix.shape, lambda i: (0, 0)),
        ],
        out_specs=pl.BlockSpec((2, rows, chunks * BLOCK), lambda i: (0, i, 0)),
        out_shape=jax.ShapeDtypeStruct((2, length, chunks * BLOCK), jnp.bfloat16),
        compiler_params=pltpu.CompilerParams(vmem_limit_bytes=VMEM_LIMIT),
        name="travel_second",
    )(left, body, right, matrix)


def from_both_sides(first, last, axis):
    devices = lax.axis_size(axis)
    up = [(i, i + 1) for i in range(devices - 1)]
    down = [(j, i) for i, j in up]
    return lax.ppermute(last, axis, up), lax.ppermute(first, axis, down)


def after(value, *others):
    return lax.optimization_barrier((value, others))[0]


def ordered_kernel(halo, rank, *refs):
    pieces, (out, first, last) = refs[:-3], refs[-3:]
    count = len(pieces)
    for s, piece in enumerate(pieces):
        place = s ^ rank[0]
        out[place] = piece[0]

        @pl.when(place < halo)
        def _():
            first[place] = piece[0]

        @pl.when(place >= count - halo)
        def _():
            last[place - (count - halo)] = piece[0]


def ordered(pieces, halo, rank):
    count = len(pieces)
    block = pieces[0].shape
    shapes = [(n, *block[1:]) for n in (count, halo, halo)]
    full = lambda shape: pl.BlockSpec(shape, lambda i, *_: (0,) * len(shape))
    return pl.pallas_call(
        functools.partial(ordered_kernel, halo),
        grid_spec=pltpu.PrefetchScalarGridSpec(
            num_scalar_prefetch=1,
            grid=(1,),
            in_specs=[full(block)] * count,
            out_specs=[full(shape) for shape in shapes],
        ),
        out_shape=[jax.ShapeDtypeStruct(shape, pieces[0].dtype) for shape in shapes],
        compiler_params=pltpu.CompilerParams(vmem_limit_bytes=VMEM_LIMIT),
        name="ordered",
    )(rank, *pieces)


def swapped_shares(slots):
    devices = lax.axis_size("row")
    return [slots[0]] + [
        lax.ppermute(slots[s], "row", [(i, i ^ s) for i in range(devices)])
        for s in range(1, devices)
    ]


def group_starts(starts, group, unit):
    lines = starts.shape[-1]
    grouped = starts.reshape(*starts.shape[:-1], lines // group, group)
    base = jnp.min(grouped, -1) // unit
    spare = grouped - base[..., None] * unit
    return base.astype(jnp.int32), spare.reshape(starts.shape)


def on_device(
    volume_plane,
    wave_a,
    wave_b,
    shift_rows,
    fraction_rows,
    shift_columns,
    fraction_columns,
    travel_distance,
):
    _, line_count, width = volume_plane.shape
    row_devices, column_devices = lax.axis_size("row"), lax.axis_size("col")
    row_index, column_index = lax.axis_index("row"), lax.axis_index("col")
    tiles = width // BLOCK
    halo = -(-(SHIFT_X + MARGIN) // BLOCK)
    reach = halo * BLOCK

    forward, inverse = real_tables()
    half = lambda x: jnp.asarray(x, jnp.bfloat16)
    row_tables = (half(forward), half(inverse))
    column_tables = (half(forward.T), half(inverse.T))
    turned_tables = (half(forward), half(inverse[:, ::-1].T))
    in_order = jnp.zeros((1,), jnp.int32)
    by_rank = row_index.astype(jnp.int32).reshape(1)

    part_lines = line_count // PARTS
    lefts, rights, edges = [], [], ()
    for part in range(PARTS):
        lines = after(volume_plane, edges)[:, part * part_lines : (part + 1) * part_lines]
        edges = (lines[:, :, :reach], lines[:, :, width - reach :])
        left, right = from_both_sides(*edges, "col")
        lefts.append(left)
        rights.append(right)

    base_rows, spare_rows = group_starts(reach - MARGIN - shift_rows, GROUP, BLOCK)

    front = -(-(SHIFT_Y + MARGIN) // GROUP) * GROUP
    back = front + 3 * BLOCK
    mine = lambda x: lax.dynamic_slice_in_dim(x, row_index * BLOCK, BLOCK, 1)
    base_columns, spare_columns = group_starts(front - MARGIN - mine(shift_columns), BLOCK, GROUP)
    column_fractions = mine(fraction_columns)

    def first(view, begin, lefts, rights, rank):
        return shear_tile(
            volume_plane,
            lefts,
            rights,
            begin,
            halo,
            base_rows[view, 0],
            rank,
            spare_rows[view, 0],
            fraction_rows[view, 0],
            row_tables,
        )

    def second(view, pieces, place, rank, rows_out):
        return shear_columns(
            pieces,
            place,
            row_devices,
            front,
            back,
            base_columns[view] * GROUP,
            rank,
            spare_columns[view],
            column_fractions[view],
            column_tables,
            rows_out,
        )

    matrices = travel_matrices(travel_distance, forward, inverse)
    real, imaginary = matrices[:, 0], matrices[:, 1]
    along_rows = jnp.concatenate(
        [
            jnp.concatenate([real, -imaginary], 1),
            jnp.concatenate([imaginary, real], 1),
        ],
        2,
    )
    along_rows = jnp.swapaxes(along_rows, 1, 2).astype(jnp.bfloat16)
    spaced = jnp.pad(matrices, ((0, 0), (0, 0), (BLOCK - MARGIN, BLOCK - MARGIN), (0, 0)))
    real, imaginary = spaced[:, 0], spaced[:, 1]
    along_columns = jnp.concatenate(
        [
            jnp.concatenate([real, -imaginary], 1),
            jnp.concatenate([imaginary, real], 1),
        ],
        2,
    ).astype(jnp.bfloat16)

    spread, sheared = [], ()
    for part in range(PARTS):
        left, right = after((lefts[part], rights[part]), sheared)
        sheared = first(1, part * part_lines, [left], [right], in_order)
        spread.append(lax.all_to_all(sheared, "row", split_axis=0, concat_axis=0, tiled=True))
    lefts, rights = after((lefts, rights), sheared)
    slots = first(0, 0, lefts, rights, by_rank)
    shares = [slots[s : s + 1] for s in range(row_devices)]
    spread, shares = lax.optimization_barrier((spread, shares))
    pieces = swapped_shares(shares)

    place = [[(b, part * part_lines) for b in range(row_devices)] for part in range(PARTS)]
    moved_b = second(1, spread, place, in_order, BLOCK)
    whole = lax.all_to_all(moved_b, ("row", "col"), split_axis=0, concat_axis=0, tiled=True)
    whole = whole.reshape(row_devices, column_devices, 2, BLOCK, BLOCK)
    own_lines = lambda x: lax.dynamic_slice_in_dim(x, column_index * BLOCK, BLOCK, 0)
    groups = BLOCK // GROUP
    turned = shear_whole(
        whole,
        halo,
        lax.dynamic_slice_in_dim(base_rows[1, 1], column_index * groups, groups, 0),
        own_lines(spare_rows[1, 1]),
        own_lines(fraction_rows[1, 1]),
        turned_tables,
    )

    pieces = after(pieces, moved_b)
    moved_a = second(0, pieces, [[(s, 0)] for s in range(row_devices)], by_rank, line_count)
    pieces = swapped_shares([moved_a[s : s + 1] for s in range(row_devices)])
    tile, low, high = ordered(pieces, halo, by_rank)
    left, right = from_both_sides(low, high, "col")

    margin = after((wave_b[:, :MARGIN], wave_b[:, -MARGIN:]), turned)
    wave_b_halos = from_both_sides(*margin, "col")
    turned = lax.all_to_all(turned, "col", split_axis=0, concat_axis=0, tiled=True)
    half_b = travel_first(turned, (), (wave_b, *wave_b_halos), along_rows[1])
    low, high = from_both_sides(half_b[:1], half_b[-1:], "row")
    exit_b = travel_second(low, half_b, high, along_columns[1])

    left, right = after((left, right), exit_b)
    field_a = shear_tile(
        tile,
        [left],
        [right],
        0,
        halo,
        base_rows[0, 1],
        in_order,
        spare_rows[0, 1],
        fraction_rows[0, 1],
        row_tables,
        wave_a,
    )
    halos = from_both_sides(field_a[:, :, :MARGIN], field_a[:, :, -MARGIN:], "row")
    half_a = travel_first(field_a, halos, (), along_rows[0])
    low, high = from_both_sides(half_a[:1], half_a[-1:], "col")
    exit_a = travel_second(low, half_a, high, along_columns[0])
    return exit_a, exit_b


def swapped(value, axis, bit):
    mask = 2**bit
    pairs = [(source, source ^ mask) for source in range(lax.axis_size(axis))]
    return lax.ppermute(value, axis, pairs)


def padded_2(x, sides, width):
    for axis, dim in sides:
        devices, length = (lax.axis_size(axis), x.shape[dim])
        up = [(i, (i + 1) % devices) for i in range(devices - 1)]
        down = [(j, i) for i, j in up]
        last = lax.slice_in_dim(x, length - width, length, axis=dim)
        first = lax.slice_in_dim(x, 0, width, axis=dim)
        before = lax.ppermute(last, axis, up)
        after = lax.ppermute(first, axis, down)
        x = jnp.concatenate([before, x, after], axis=dim)
    return x


def fourier_tables(block_len, margin):
    window_len = block_len + 2 * margin
    frequency = jnp.arange(window_len, dtype=jnp.int32) - window_len // 2
    position = jnp.arange(window_len, dtype=jnp.int32)
    angles = (
        2.0
        * jnp.pi
        * jnp.mod(position[:, None] * frequency[None, :], window_len).astype(jnp.float32)
        / window_len
    )
    cosine = jnp.cos(angles)
    sines = jnp.sin(angles)
    forward = jnp.concatenate(
        [jnp.concatenate([cosine, -sines], 1), jnp.concatenate([sines, cosine], 1)], 0
    ).astype(jnp.bfloat16)
    target = jnp.arange(block_len, dtype=jnp.int32) + margin
    inverse_angle = (
        2.0
        * jnp.pi
        * jnp.mod(frequency[:, None] * target[None, :], window_len).astype(jnp.float32)
        / window_len
    )
    inverse_cosine = jnp.cos(inverse_angle) / window_len
    inverse_sine = jnp.sin(inverse_angle) / window_len
    inverse = jnp.concatenate(
        [
            jnp.concatenate([inverse_cosine, inverse_sine], 1),
            jnp.concatenate([-inverse_sine, inverse_cosine], 1),
        ],
        0,
    ).astype(jnp.bfloat16)
    return (forward, inverse, frequency.astype(jnp.float32))


def shear_ramp(fractions, frequency):
    window_len = frequency.shape[0]
    phases = -2.0 * jnp.pi / window_len * fractions[:, None] * frequency[None, :]
    nyquist = (jnp.arange(window_len) == 0)[None, :]
    ramp_real = jnp.where(nyquist, jnp.cos(jnp.pi * fractions)[:, None], jnp.cos(phases))
    ramp_imaginary = jnp.where(nyquist, 0.0, jnp.sin(phases))
    return (ramp_real, ramp_imaginary)


def travel_ramp(distance, frequency):
    window_len = frequency.shape[0]
    phases = -2.0 * jnp.pi / (window_len * window_len) * distance * frequency * frequency
    return (jnp.cos(phases)[None, :], jnp.sin(phases)[None, :])


def select_window(padded, starts, out_len):
    total_len = padded.shape[2]
    offset_range = total_len - out_len
    bit_count = max(offset_range, 1).bit_length()
    current = jnp.pad(padded, ((0, 0), (0, 0), (0, out_len + 2**bit_count - 1 - total_len)))
    for bit_number in reversed(range(bit_count)):
        stride = 2**bit_number
        kept_len = current.shape[2] - stride
        chosen = (starts // stride % 2 == 1)[None, :, None]
        current = jnp.where(
            chosen, current[:, :, stride : stride + kept_len], current[:, :, :kept_len]
        )
    return current


def line_pass(padded, extent, shifts, ramp_real, ramp_imaginary, tables):
    forward, inverse = (tables[0], tables[1])
    window_len = BLOCK + 2 * MARGIN
    line_count = padded.shape[1]
    blocks = (padded.shape[2] - 2 * extent) // BLOCK
    reach_len = blocks * BLOCK + 2 * MARGIN
    if shifts is None:
        shifted = padded
    else:
        starts = extent - MARGIN - shifts
        shifted = select_window(padded, starts, reach_len)
    middle = shifted[:, :, MARGIN : MARGIN + blocks * BLOCK].reshape(2, line_count, blocks, BLOCK)
    left_rim = shifted[:, :, : blocks * BLOCK].reshape(2, line_count, blocks, BLOCK)[..., :MARGIN]
    right_rim = shifted[:, :, 2 * MARGIN : 2 * MARGIN + blocks * BLOCK].reshape(
        2, line_count, blocks, BLOCK
    )[..., BLOCK - MARGIN :]
    windows = jnp.concatenate([left_rim, middle, right_rim], 3)
    spectrum = jnp.einsum(
        "cpms,cst->pmt",
        windows,
        forward.reshape(2, window_len, 2 * window_len),
        preferred_element_type=jnp.float32,
    )
    spec_real = spectrum[..., :window_len]
    spec_imaginary = spectrum[..., window_len:]
    factor_real = ramp_real[:, None, :]
    factor_imaginary = ramp_imaginary[:, None, :]
    ramped = jnp.concatenate(
        [
            spec_real * factor_real - spec_imaginary * factor_imaginary,
            spec_real * factor_imaginary + spec_imaginary * factor_real,
        ],
        -1,
    ).astype(jnp.bfloat16)
    result = jnp.einsum(
        "pms,scb->cpmb",
        ramped,
        inverse.reshape(2 * window_len, 2, BLOCK),
        preferred_element_type=jnp.float32,
    )
    return result.reshape(2, line_count, blocks * BLOCK).astype(jnp.bfloat16)


def single_pass(padded, extent, shifts, fractions, tables):
    ramp_real, ramp_imaginary = shear_ramp(fractions, tables[2])
    return line_pass(padded, extent, shifts, ramp_real, ramp_imaginary, tables)


def general_shear_columns(stacked, shifts, fractions, tables):
    halo_depth = SHIFT_X + MARGIN
    inputs = stacked.shape[0]
    column_devices = lax.axis_size("col")
    share = stacked.shape[2] // column_devices
    offset = lax.axis_index("col") * share
    spread = lax.all_to_all(stacked, "col", split_axis=2, concat_axis=3, tiled=True)
    padded = jnp.pad(spread, ((0, 0), (0, 0), (0, 0), (halo_depth, halo_depth)))
    row_shifts = lax.dynamic_slice_in_dim(shifts, offset, share, 1)
    row_fractions = lax.dynamic_slice_in_dim(fractions, offset, share, 1)
    sheared = jnp.stack(
        [
            single_pass(
                padded[min(0, inputs - 1)], halo_depth, row_shifts[0], row_fractions[0], tables
            )
        ]
    )
    return lax.all_to_all(sheared, "col", split_axis=3, concat_axis=2, tiled=True)


def shear_along_first(padded_lines, halo_depth, shifts, fractions, tables):
    flipped = jnp.swapaxes(padded_lines[0], 1, 2)
    moved = single_pass(flipped, halo_depth, shifts[0], fractions[0], tables)
    sheared = [jnp.swapaxes(moved, 1, 2)]
    return jnp.stack(sheared)


def shear_rows_pass(stacked, shifts, fractions, tables):
    halo_depth = SHIFT_Y + MARGIN
    row_devices = lax.axis_size("row")
    share = stacked.shape[3] // row_devices
    offset = lax.axis_index("row") * share
    spread = lax.all_to_all(stacked, "row", split_axis=3, concat_axis=2, tiled=True)
    padded = jnp.pad(spread, ((0, 0), (0, 0), (halo_depth, halo_depth), (0, 0)))
    column_shifts = lax.dynamic_slice_in_dim(shifts, offset, share, 1)
    column_fractions = lax.dynamic_slice_in_dim(fractions, offset, share, 1)
    sheared = shear_along_first(padded, halo_depth, column_shifts, column_fractions, tables)
    return lax.all_to_all(sheared, "row", split_axis=2, concat_axis=3, tiled=True)


def travel_local(extended, distance, tables):
    ramp_real, ramp_imaginary = travel_ramp(distance, tables[2])
    halfway = line_pass(extended, MARGIN, None, ramp_real, ramp_imaginary, tables)
    flipped = jnp.swapaxes(halfway, 1, 2)
    finished = line_pass(flipped, MARGIN, None, ramp_real, ramp_imaginary, tables)
    return jnp.swapaxes(finished, 1, 2)


def transmit(rotated, wave):
    phase_part = rotated[0].astype(jnp.float32)
    absorb_part = rotated[1].astype(jnp.float32)
    amplitude = jnp.exp(-ABSORB * absorb_part)
    through_real = amplitude * jnp.cos(phase_part)
    through_imaginary = amplitude * jnp.sin(phase_part)
    wave_real = wave[0].astype(jnp.float32)
    wave_imaginary = wave[1].astype(jnp.float32)
    return jnp.stack(
        [
            wave_real * through_real - wave_imaginary * through_imaginary,
            wave_real * through_imaginary + wave_imaginary * through_real,
        ]
    ).astype(jnp.bfloat16)


def general_on_device(
    volume_plane,
    wave_a,
    wave_b,
    shift_rows,
    fraction_rows,
    shift_columns,
    fraction_columns,
    travel_distance,
):
    tables = fourier_tables(BLOCK, MARGIN)
    source = volume_plane[None]
    results = []
    for member in range(2):
        stacked = general_shear_columns(
            source,
            shift_rows[member : member + 1, 0],
            fraction_rows[member : member + 1, 0],
            tables,
        )
        stacked = shear_rows_pass(
            stacked,
            shift_columns[member : member + 1],
            fraction_columns[member : member + 1],
            tables,
        )
        stacked = general_shear_columns(
            stacked,
            shift_rows[member : member + 1, 1],
            fraction_rows[member : member + 1, 1],
            tables,
        )
        results.append(stacked[0])
    view_one = results[0]
    view_two = results[1]
    turned = jnp.swapaxes(jnp.flip(view_two, 2), 1, 2)
    for bit_number in range(lax.axis_size("col").bit_length() - 1):
        turned = swapped(turned, "col", bit_number)
    product_a = transmit(view_one, wave_a)
    extended_a = padded_2(product_a, (("row", 1), ("col", 2)), MARGIN)
    exit_a = travel_local(extended_a, travel_distance[0], tables)
    product_b = transmit(turned, wave_b)
    extended_b = padded_2(product_b, (("row", 2), ("col", 1)), MARGIN)
    exit_b = travel_local(extended_b, travel_distance[1], tables)
    return (exit_a, exit_b)


def solution(mesh):
    def either(volume_plane, *rest):
        rows, width = volume_plane.shape[1:]
        fits = (
            rows == BLOCK * lax.axis_size("col")
            and width == BLOCK * lax.axis_size("row")
            and width >= SHIFT_X + MARGIN
        )
        chosen = on_device if fits else general_on_device
        return chosen(volume_plane, *rest)

    return jax.shard_map(
        either,
        mesh=mesh,
        in_specs=(
            P(None, "row", "col"),
            P(None, "row", "col"),
            P(None, "col", "row"),
            P(None, None, "row"),
            P(None, None, "row"),
            P(None, "col"),
            P(None, "col"),
            P(),
        ),
        out_specs=(P(None, "row", "col"), P(None, "col", "row")),
        check_vma=False,
    )
```

```python
import functools

import jax
import jax.numpy as jnp
import numpy as np
from jax import lax
from jax.experimental import pallas as pl
from jax.experimental.pallas import tpu as pltpu
from jax.sharding import PartitionSpec as P

BLOCK = 128
MARGIN = 32
SHIFT_X = 864
SHIFT_Y = 1728


ABSORB = 0.25

WINDOW = BLOCK + 2 * MARGIN
BINS = WINDOW // 2
GROUP = 16
PARTS = 2
ROWS = 256
STEPS = 2
VMEM_LIMIT = 56 * 1024 * 1024


def angle_table(rows, columns):
    return 2.0 * np.pi * (np.outer(rows, columns) % WINDOW) / WINDOW


def real_tables():
    position = np.arange(WINDOW)
    bins = np.arange(BINS + 1)
    target = np.arange(BLOCK) + MARGIN
    forward = np.zeros((2 * BLOCK, 2 * BLOCK), np.float32)
    forward[:WINDOW, : BINS + 1] = np.cos(angle_table(position, bins))
    forward[:WINDOW, BLOCK + 1 : BLOCK + BINS] = -np.sin(angle_table(position, bins[1:BINS]))
    weight = np.where((bins == 0) | (bins == BINS), 1.0, 2.0) / WINDOW
    inverse = np.zeros((2 * BLOCK, BLOCK), np.float32)
    inverse[: BINS + 1] = np.cos(angle_table(bins, target)) * weight[:, None]
    inverse[BLOCK + 1 : BLOCK + BINS] = (
        -np.sin(angle_table(bins[1:BINS], target)) * weight[1:BINS, None]
    )
    return forward, inverse


def travel_matrices(distance, forward, inverse):
    frequency = jnp.arange(BLOCK, dtype=jnp.float32)
    phases = -2.0 * jnp.pi / (WINDOW * WINDOW) * distance[:, None] * frequency * frequency
    ramps = jnp.stack([jnp.cos(phases), jnp.sin(phases)], 1)
    ramps = jnp.concatenate([ramps, ramps], 2)
    scaled = ramps[..., None] * jnp.asarray(inverse)
    matrices = jnp.einsum(
        "pq,vrqu->vrpu",
        jnp.asarray(forward[:WINDOW]),
        scaled,
        precision=lax.Precision.HIGHEST,
    )
    return matrices


def lane_iota(rows):
    return lax.broadcasted_iota(jnp.int32, (rows, BLOCK), 1)


def shift_lines(strip, shifted, base, base_offset, spare, windows, chunk_offset, rows):
    def one_group(group, carry):
        first = pl.multiple_of(group * GROUP, GROUP)
        lines = pl.ds(first, GROUP)
        start = base[base_offset + group] + chunk_offset
        offset = spare[lines, :]
        later = offset >= BLOCK
        lane = lane_iota(GROUP) + (offset & (BLOCK - 1))
        wraps = lane >= BLOCK
        index = lane & (BLOCK - 1)
        for part in range(2):
            here = strip[start, part, lines, :].astype(jnp.float32)
            before = None
            for i in range(windows + 2):
                following = strip[start + i + 1, part, lines, :].astype(jnp.float32)
                turned = jnp.take_along_axis(jnp.where(later, following, here), index, axis=1)
                if before is not None:
                    shifted[i - 1, part, lines, :] = jnp.where(wraps, turned, before).astype(
                        jnp.bfloat16
                    )
                before = turned
                here = following
        return carry

    lax.fori_loop(0, rows // GROUP, one_group, 0, unroll=4)


def ramped_lines(shifted, windows, rows, cosine, sine, forward):
    count = len(windows)
    lower = jnp.concatenate([shifted[m].reshape(2 * rows, BLOCK) for m in windows], 0)
    upper = jnp.concatenate([shifted[m + 1].reshape(2 * rows, BLOCK) for m in windows], 0)
    spectrum = jnp.dot(
        jnp.concatenate([lower, upper], 1), forward[...], preferred_element_type=jnp.float32
    )
    real = spectrum[:, :BLOCK].reshape(count * 2, rows, BLOCK)
    imaginary = spectrum[:, BLOCK:].reshape(count * 2, rows, BLOCK)
    ramp_real = cosine[...][None]
    ramp_imaginary = sine[...][None]
    ramped = jnp.concatenate(
        [
            (real * ramp_real - imaginary * ramp_imaginary).astype(jnp.bfloat16),
            (real * ramp_imaginary + imaginary * ramp_real).astype(jnp.bfloat16),
        ],
        2,
    )
    return ramped.reshape(count * 2 * rows, 2 * BLOCK)


def down_lines(vector):
    return jnp.broadcast_to(vector, (BLOCK, vector.shape[1])).T


def line_ramps(fractions, cosine, sine):
    bins = lane_iota(fractions.shape[1]).astype(jnp.float32)
    sine[...], cosine[...] = sine_cosine(down_lines(fractions) * bins * (-2.0 * np.pi / WINDOW))


def shear_tile_kernel(halo, tiles, rows, batch, wide, parts, sent, base, rank, *refs):
    lefts, rights, refs = refs[:parts], refs[parts : 2 * parts], refs[2 * parts :]
    waves, refs = refs[: int(sent)], refs[int(sent) :]
    own, offsets, fractions, forward, inverse, out = refs[:6]
    strip, shifted, spare, cosine, sine = refs[6:]
    step = pl.program_id(0)
    groups = rows // GROUP
    end = halo + tiles + halo

    @pl.when(step == 0)
    def _():
        strip[end : end + 2] = jnp.zeros((2, 2, rows, BLOCK), jnp.bfloat16)

    def fill(piece, first, count):
        for i in range(count):
            if wide:
                strip[first + i] = piece[:, :, i * BLOCK : (i + 1) * BLOCK]
            else:
                strip[first + i] = piece[i]

    share = pl.num_programs(0) // parts
    for part in range(parts):

        @pl.when(step // share == part)
        def _():
            fill(lefts[part], 0, halo)
            fill(rights[part], halo + tiles, halo)

    fill(own, halo, tiles)
    spare[...] = down_lines(offsets[0]).astype(jnp.int32)
    line_ramps(fractions[0], cosine, sine)
    shift_lines(strip, shifted, base, step * groups, spare, tiles, 0, rows)
    for first in range(0, tiles, batch):
        windows = [slot if sent else slot ^ rank[0] for slot in range(first, first + batch)]
        ramped = ramped_lines(shifted, windows, rows, cosine, sine, forward)
        result = jnp.dot(ramped, inverse[...], preferred_element_type=jnp.float32)
        result = result.astype(jnp.bfloat16).reshape(batch, 2, rows, BLOCK)
        if sent:
            for i, window in enumerate(windows):
                wave = waves[0][:, :, window * BLOCK : (window + 1) * BLOCK]
                for part, value in enumerate(transmitted(result[i], wave)):
                    out[window, part] = value
        else:
            out[first : first + batch] = result


def shear_tile(own, lefts, rights, first, lines, halo, base, rank, spare, fractions, tables, *waves):
    wide = own.ndim == 3
    parts = len(lefts)
    line_count = lines
    part_lines = line_count // parts
    tiles = own.shape[2] // BLOCK if wide else own.shape[0]
    rows = min(part_lines, ROWS)
    share = part_lines // rows
    offset = first // rows
    forward, inverse = tables

    def piece_spec(piece, place):
        if wide:
            return pl.BlockSpec((2, rows, piece.shape[2]), lambda i, *_: (0, place(i), 0))
        return pl.BlockSpec((piece.shape[0], 2, rows, BLOCK), lambda i, *_: (0, 0, place(i), 0))

    halo_specs = [
        piece_spec(x, lambda i, part=part: jnp.clip(i - part * share, 0, share - 1))
        for x in (lefts[0], rights[0])
        for part in range(parts)
    ]
    line_spec = pl.BlockSpec((1, 1, rows), lambda i, *_: (i + offset, 0, 0))
    along = lambda x: x.astype(jnp.float32).reshape(-1, 1, rows)
    out_shape = jax.ShapeDtypeStruct((tiles, 2, line_count, BLOCK), jnp.bfloat16)
    out_spec = pl.BlockSpec((tiles, 2, rows, BLOCK), lambda i, *_: (0, 0, i, 0))
    groups = rows // GROUP
    kernel = functools.partial(
        shear_tile_kernel,
        halo,
        tiles,
        rows,
        tiles // 4 if tiles % 4 == 0 else tiles,
        wide,
        parts,
        len(waves) > 0,
    )
    return pl.pallas_call(
        kernel,
        grid_spec=pltpu.PrefetchScalarGridSpec(
            num_scalar_prefetch=2,
            grid=(line_count // rows,),
            in_specs=halo_specs
            + [pl.BlockSpec((2, rows, x.shape[2]), lambda i, *_: (0, i + offset, 0)) for x in waves]
            + [piece_spec(own, lambda i: i + offset)]
            + [line_spec] * 2
            + [
                pl.BlockSpec(forward.shape, lambda i, *_: (0, 0)),
                pl.BlockSpec(inverse.shape, lambda i, *_: (0, 0)),
            ],
            out_specs=out_spec,
            scratch_shapes=[
                pltpu.VMEM((halo + tiles + halo + 2, 2, rows, BLOCK), jnp.bfloat16),
                pltpu.VMEM((tiles + 1, 2, rows, BLOCK), jnp.bfloat16),
                pltpu.VMEM((rows, BLOCK), jnp.int32),
                pltpu.VMEM((rows, BLOCK), jnp.float32),
                pltpu.VMEM((rows, BLOCK), jnp.float32),
            ],
        ),
        out_shape=out_shape,
        compiler_params=pltpu.CompilerParams(vmem_limit_bytes=VMEM_LIMIT),
        name="shear_tile",
    )(
        lax.slice_in_dim(base, offset * groups, offset * groups + line_count // GROUP),
        rank,
        *lefts,
        *rights,
        *waves,
        own,
        along(spare),
        along(fractions),
        forward,
        inverse,
    )


def shear_whole_kernel(
    halo,
    devices,
    tiles,
    rows,
    base,
    own,
    offsets,
    fractions,
    forward,
    flipped,
    out,
    strip,
    shifted,
    spare,
    cosine,
    sine,
):
    step = pl.program_id(0)
    chunks = devices * tiles
    length = tiles * BLOCK

    @pl.when(step == 0)
    def _():
        strip[0:halo] = jnp.zeros((halo, 2, rows, BLOCK), jnp.bfloat16)
        strip[halo + chunks :] = jnp.zeros((halo + 2, 2, rows, BLOCK), jnp.bfloat16)
        for chunk in range(chunks):
            strip[halo + chunk] = own[chunk % tiles, chunk // tiles]
        out[0, :, 0:MARGIN, :] = jnp.zeros((2, MARGIN, rows), jnp.bfloat16)
        out[devices - 1, :, MARGIN + length :, :] = jnp.zeros((2, MARGIN, rows), jnp.bfloat16)
        spare[...] = down_lines(offsets[...]).astype(jnp.int32)
        line_ramps(fractions[...], cosine, sine)

    shift_lines(strip, shifted, base, 0, spare, tiles, step * tiles, rows)
    ramped = ramped_lines(shifted, range(tiles), rows, cosine, sine, forward)
    target = devices - 1 - step
    result = lax.dot_general(
        flipped[...], ramped, (((1,), (1,)), ((), ())), preferred_element_type=jnp.float32
    ).astype(jnp.bfloat16)
    for window in range(tiles):
        block = tiles - 1 - window
        low = MARGIN + block * BLOCK
        for part in range(2):
            lanes = (2 * window + part) * rows
            piece = result[:, lanes : lanes + rows]
            out[target, part, low : low + BLOCK, :] = piece
            if block == 0:

                @pl.when(target > 0)
                def _():
                    out[target - 1, part, MARGIN + length :, :] = piece[:MARGIN]

            if block == tiles - 1:

                @pl.when(target < devices - 1)
                def _():
                    out[target + 1, part, 0:MARGIN, :] = piece[BLOCK - MARGIN :]


def shear_whole(own, halo, base, spare, fractions, tables):
    tiles, devices, _, rows, _ = own.shape
    forward, flipped = tables
    operands = (
        own,
        spare.astype(jnp.float32).reshape(1, rows),
        fractions.reshape(1, rows),
        forward,
        flipped,
    )
    full = lambda shape: pl.BlockSpec(shape, lambda i, *_: (0,) * len(shape))
    out = (devices, 2, tiles * BLOCK + 2 * MARGIN, rows)
    return pl.pallas_call(
        functools.partial(shear_whole_kernel, halo, devices, tiles, rows),
        grid_spec=pltpu.PrefetchScalarGridSpec(
            num_scalar_prefetch=1,
            grid=(devices,),
            in_specs=[full(x.shape) for x in operands],
            out_specs=full(out),
            scratch_shapes=[
                pltpu.VMEM((2 * halo + devices * tiles + 2, 2, rows, BLOCK), jnp.bfloat16),
                pltpu.VMEM((tiles + 1, 2, rows, BLOCK), jnp.bfloat16),
                pltpu.VMEM((rows, BLOCK), jnp.int32),
                pltpu.VMEM((rows, BLOCK), jnp.float32),
                pltpu.VMEM((rows, BLOCK), jnp.float32),
            ],
        ),
        out_shape=jax.ShapeDtypeStruct(out, jnp.bfloat16),
        compiler_params=pltpu.CompilerParams(vmem_limit_bytes=VMEM_LIMIT),
        name="shear_whole",
    )(base, *operands)


def shear_columns_kernel(front, blocks, length, rows_out, place, base, rank, *refs):
    owns, refs = refs[: len(place)], refs[len(place) :]
    offsets, fractions, forward, inverse, out, strip, shifted, cosine, sine = refs
    step = pl.program_id(0)
    per_step = length // BLOCK
    per_grid = blocks // pl.num_programs(0)
    total = strip.shape[1]

    @pl.when(step == 0)
    def _():
        strip[:, 0:front, :] = jnp.zeros((2, front, BLOCK), jnp.bfloat16)
        back = front + blocks * length
        strip[:, back:, :] = jnp.zeros((2, total - back, BLOCK), jnp.bfloat16)
        for own, slots in zip(owns, place):
            count = own.shape[2]
            for i, (slot, within) in enumerate(slots):
                first = pl.multiple_of(front + (slot ^ rank[0]) * length + within, GROUP)
                for part in range(2):
                    strip[part, pl.ds(first, count), :] = own[i, part]
        bins = lax.broadcasted_iota(jnp.int32, (BLOCK, BLOCK), 0).astype(jnp.float32)
        sine[...], cosine[...] = sine_cosine(bins * fractions[...] * (-2.0 * np.pi / WINDOW))

    offset = jnp.broadcast_to(offsets[...], (8, BLOCK))
    row = lax.broadcasted_iota(jnp.int32, (8, BLOCK), 0) + (offset & 7)
    wraps = row >= 8
    index = row & 7

    def one_chunk(block_rows, chunk):
        begin = pl.multiple_of(base[0] + block_rows + chunk * BLOCK, GROUP)
        for part in range(2):
            value = strip[part, pl.ds(begin, 2 * BLOCK), :].astype(jnp.float32)
            value = value.reshape(2 * BLOCK // 8, 8, BLOCK)
            for bit in (64, 32, 16, 8):
                taken = ((offset & bit) != 0)[None]
                value = jnp.where(taken, value[bit // 8 :], value[: -(bit // 8)])
            pieces = [
                jnp.take_along_axis(value[i], index, axis=0) for i in range(BLOCK // 8 + 1)
            ]
            moved = [
                jnp.where(wraps, pieces[i + 1], pieces[i]) for i in range(BLOCK // 8)
            ]
            shifted[chunk * BLOCK : (chunk + 1) * BLOCK, part * BLOCK : (part + 1) * BLOCK] = (
                jnp.concatenate(moved, 0).astype(jnp.bfloat16)
            )

    def one_block(local, carry):
        block_rows = ((step * per_grid + local) ^ rank[0]) * length
        for chunk in range(per_step + 1):
            one_chunk(block_rows, chunk)
        windows = [shifted[m * BLOCK : (m + 2) * BLOCK, :] for m in range(per_step)]
        spectrum = jnp.dot(
            forward[...], jnp.concatenate(windows, 1), preferred_element_type=jnp.float32
        )
        ramp_real = jnp.concatenate([cosine[...]] * (2 * per_step), 1)
        ramp_imaginary = jnp.concatenate([sine[...]] * (2 * per_step), 1)
        real, imaginary = spectrum[:BLOCK], spectrum[BLOCK:]
        ramped = jnp.concatenate(
            [
                (real * ramp_real - imaginary * ramp_imaginary).astype(jnp.bfloat16),
                (real * ramp_imaginary + imaginary * ramp_real).astype(jnp.bfloat16),
            ],
            0,
        )
        result = jnp.dot(inverse[...], ramped, preferred_element_type=jnp.float32)
        result = result.astype(jnp.bfloat16)
        for window in range(per_step):
            piece, within = window * BLOCK // rows_out, window * BLOCK % rows_out
            for part in range(2):
                lanes = (2 * window + part) * BLOCK
                out[local * (length // rows_out) + piece, part, within : within + BLOCK, :] = (
                    result[:, lanes : lanes + BLOCK]
                )
        return carry

    lax.fori_loop(0, per_grid, one_block, 0)


def shear_columns(owns, place, blocks, front, back, base, rank, spare, fractions, tables, rows_out):
    length = sum(own.shape[0] * own.shape[2] for own in owns) // blocks
    forward, inverse = tables
    operands = (
        *owns,
        spare.astype(jnp.int32).reshape(1, BLOCK),
        fractions.reshape(1, BLOCK),
        forward,
        inverse,
    )
    full = lambda shape: pl.BlockSpec(shape, lambda i, *_: (0,) * len(shape))
    pieces = blocks * length // rows_out
    steps = STEPS if blocks % STEPS == 0 else 1
    return pl.pallas_call(
        functools.partial(shear_columns_kernel, front, blocks, length, rows_out, place),
        grid_spec=pltpu.PrefetchScalarGridSpec(
            num_scalar_prefetch=2,
            grid=(steps,),
            in_specs=[full(x.shape) for x in operands],
            out_specs=pl.BlockSpec(
                (pieces // steps, 2, rows_out, BLOCK), lambda i, *_: (i, 0, 0, 0)
            ),
            scratch_shapes=[
                pltpu.VMEM((2, front + blocks * length + back, BLOCK), jnp.bfloat16),
                pltpu.VMEM((length + BLOCK, 2 * BLOCK), jnp.bfloat16),
                pltpu.VMEM((BLOCK, BLOCK), jnp.float32),
                pltpu.VMEM((BLOCK, BLOCK), jnp.float32),
            ],
        ),
        out_shape=jax.ShapeDtypeStruct((pieces, 2, rows_out, BLOCK), jnp.bfloat16),
        compiler_params=pltpu.CompilerParams(vmem_limit_bytes=VMEM_LIMIT),
        name="shear_columns",
    )(base, rank, *operands)


def sine_cosine(angle):
    turns = jnp.round(angle * (2.0 / np.pi))
    rest = angle - turns * 1.5703125
    rest = rest - turns * 4.837512969970703125e-4
    rest = rest - turns * 7.549789954891882e-8
    square = rest * rest
    sine = rest + rest * square * (
        -1.6666654611e-1 + square * (8.3321608736e-3 - square * 1.9515295891e-4)
    )
    cosine = (
        1.0
        - 0.5 * square
        + square
        * square
        * (4.166664568298827e-2 + square * (-1.388731625493765e-3 + square * 2.443315711809948e-5))
    )
    quadrant = turns.astype(jnp.int32)
    odd = (quadrant & 1) != 0
    sine_out = jnp.where(odd, cosine, sine)
    cosine_out = jnp.where(odd, sine, cosine)
    sine_out = jnp.where((quadrant & 2) != 0, -sine_out, sine_out)
    cosine_out = jnp.where(((quadrant + 1) & 2) != 0, -cosine_out, cosine_out)
    return sine_out, cosine_out


def transmitted(rotated, wave):
    sine, cosine = sine_cosine(rotated[0].astype(jnp.float32))
    amplitude = jnp.exp(-ABSORB * rotated[1].astype(jnp.float32))
    through_real = amplitude * cosine
    through_imaginary = amplitude * sine
    wave_real = wave[0].astype(jnp.float32)
    wave_imaginary = wave[1].astype(jnp.float32)
    return (
        (wave_real * through_real - wave_imaginary * through_imaginary).astype(jnp.bfloat16),
        (wave_real * through_imaginary + wave_imaginary * through_real).astype(jnp.bfloat16),
    )


def travel_first_kernel(length, count, sent, *refs):
    if sent:
        body, top, bottom, matrix, out, field = refs
        for chunk in range(count):
            across = slice(chunk * BLOCK, (chunk + 1) * BLOCK)
            for part in range(2):
                field[part, 0:MARGIN, across] = top[chunk, part]
                field[part, MARGIN : MARGIN + length, across] = body[chunk, part]
                field[part, MARGIN + length :, across] = bottom[chunk, part]
    else:
        body, wave, wave_top, wave_bottom, matrix, out, field = refs
        pieces = [(0, MARGIN, wave_top, 0)]
        pieces += [(MARGIN + first, BLOCK, wave, first) for first in range(0, length, BLOCK)]
        pieces += [(MARGIN + length, MARGIN, wave_bottom, 0)]
        for chunk in range(count):
            across = slice(chunk * BLOCK, (chunk + 1) * BLOCK)
            for place, height, waves, first in pieces:
                parts = transmitted(
                    [body[chunk, p, place : place + height, :] for p in range(2)],
                    [waves[p, first : first + height, across] for p in range(2)],
                )
                for part in range(2):
                    field[part, place : place + height, across] = parts[part]
    for m in range(0, length, BLOCK):
        window = jnp.concatenate([field[0, m : m + WINDOW, :], field[1, m : m + WINDOW, :]], 0)
        result = jnp.dot(matrix[...], window, preferred_element_type=jnp.float32)
        result = result.astype(jnp.bfloat16)
        for chunk in range(count):
            across = slice(chunk * BLOCK, (chunk + 1) * BLOCK)
            for part in range(2):
                out[chunk, part, m : m + BLOCK, :] = result[
                    part * BLOCK : (part + 1) * BLOCK, across
                ]


def travel_first(body, halos, waves, matrix):
    chunks = body.shape[0]
    count = chunks // STEPS if chunks % STEPS == 0 else chunks
    length = body.shape[2] if len(halos) > 0 else body.shape[2] - 2 * MARGIN
    chunk_spec = lambda x: pl.BlockSpec((count, 2, x.shape[2], BLOCK), lambda i: (i, 0, 0, 0))
    wide_spec = lambda x: pl.BlockSpec((2, x.shape[1], count * BLOCK), lambda i: (0, 0, i))
    return pl.pallas_call(
        functools.partial(travel_first_kernel, length, count, len(halos) > 0),
        grid=(chunks // count,),
        in_specs=[chunk_spec(x) for x in (body, *halos)]
        + [wide_spec(x) for x in waves]
        + [pl.BlockSpec(matrix.shape, lambda i: (0, 0))],
        out_specs=pl.BlockSpec((count, 2, length, BLOCK), lambda i: (i, 0, 0, 0)),
        out_shape=jax.ShapeDtypeStruct((chunks, 2, length, BLOCK), jnp.bfloat16),
        scratch_shapes=[pltpu.VMEM((2, length + 2 * MARGIN, count * BLOCK), jnp.bfloat16)],
        compiler_params=pltpu.CompilerParams(vmem_limit_bytes=VMEM_LIMIT),
        name="travel_first",
    )(body, *halos, *waves, matrix)


def travel_second_kernel(chunks, rows, left, body, right, matrix, out):
    parts = [[left[0, p]] + [body[m, p] for m in range(chunks)] + [right[0, p]] for p in range(2)]
    windows = [
        jnp.concatenate(parts[0][m : m + 3] + parts[1][m : m + 3], 1) for m in range(chunks)
    ]
    result = jnp.dot(
        jnp.concatenate(windows, 0), matrix[...], preferred_element_type=jnp.float32
    ).astype(jnp.bfloat16)
    for m in range(chunks):
        for part in range(2):
            out[part, :, m * BLOCK : (m + 1) * BLOCK] = result[
                m * rows : (m + 1) * rows, part * BLOCK : (part + 1) * BLOCK
            ]


def travel_second(left, body, right, matrix):
    chunks, _, length, _ = body.shape
    rows = length // STEPS if length % (STEPS * BLOCK) == 0 else length
    edge = pl.BlockSpec((1, 2, rows, BLOCK), lambda i: (0, 0, i, 0))
    return pl.pallas_call(
        functools.partial(travel_second_kernel, chunks, rows),
        grid=(length // rows,),
        in_specs=[
            edge,
            pl.BlockSpec((chunks, 2, rows, BLOCK), lambda i: (0, 0, i, 0)),
            edge,
            pl.BlockSpec(matrix.shape, lambda i: (0, 0)),
        ],
        out_specs=pl.BlockSpec((2, rows, chunks * BLOCK), lambda i: (0, i, 0)),
        out_shape=jax.ShapeDtypeStruct((2, length, chunks * BLOCK), jnp.bfloat16),
        compiler_params=pltpu.CompilerParams(vmem_limit_bytes=VMEM_LIMIT),
        name="travel_second",
    )(left, body, right, matrix)


def from_both_sides(first, last, axis):
    devices = lax.axis_size(axis)
    up = [(i, i + 1) for i in range(devices - 1)]
    down = [(j, i) for i, j in up]
    return lax.ppermute(last, axis, up), lax.ppermute(first, axis, down)


def after(value, *others):
    return lax.optimization_barrier((value, others))[0]


def ordered_kernel(halo, rank, *refs):
    pieces, (out, first, last) = refs[:-3], refs[-3:]
    count = len(pieces)
    for s, piece in enumerate(pieces):
        place = s ^ rank[0]
        out[place] = piece[0]

        @pl.when(place < halo)
        def _():
            first[place] = piece[0]

        @pl.when(place >= count - halo)
        def _():
            last[place - (count - halo)] = piece[0]


def ordered(pieces, halo, rank):
    count = len(pieces)
    block = pieces[0].shape
    shapes = [(n, *block[1:]) for n in (count, halo, halo)]
    full = lambda shape: pl.BlockSpec(shape, lambda i, *_: (0,) * len(shape))
    return pl.pallas_call(
        functools.partial(ordered_kernel, halo),
        grid_spec=pltpu.PrefetchScalarGridSpec(
            num_scalar_prefetch=1,
            grid=(1,),
            in_specs=[full(block)] * count,
            out_specs=[full(shape) for shape in shapes],
        ),
        out_shape=[jax.ShapeDtypeStruct(shape, pieces[0].dtype) for shape in shapes],
        compiler_params=pltpu.CompilerParams(vmem_limit_bytes=VMEM_LIMIT),
        name="ordered",
    )(rank, *pieces)


def swapped_shares(slots):
    devices = lax.axis_size("row")
    return [slots[0]] + [
        lax.ppermute(slots[s], "row", [(i, i ^ s) for i in range(devices)])
        for s in range(1, devices)
    ]


def group_starts(starts, group, unit):
    lines = starts.shape[-1]
    grouped = starts.reshape(*starts.shape[:-1], lines // group, group)
    base = jnp.min(grouped, -1) // unit
    spare = grouped - base[..., None] * unit
    return base.astype(jnp.int32), spare.reshape(starts.shape)


def on_device(
    volume_plane,
    wave_a,
    wave_b,
    shift_rows,
    fraction_rows,
    shift_columns,
    fraction_columns,
    travel_distance,
):
    _, line_count, width = volume_plane.shape
    row_devices, column_devices = lax.axis_size("row"), lax.axis_size("col")
    row_index, column_index = lax.axis_index("row"), lax.axis_index("col")
    tiles = width // BLOCK
    halo = -(-(SHIFT_X + MARGIN) // BLOCK)
    reach = halo * BLOCK

    forward, inverse = real_tables()
    half = lambda x: jnp.asarray(x, jnp.bfloat16)
    row_tables = (half(forward), half(inverse))
    column_tables = (half(forward.T), half(inverse.T))
    turned_tables = (half(forward), half(inverse[:, ::-1].T))
    in_order = jnp.zeros((1,), jnp.int32)
    by_rank = row_index.astype(jnp.int32).reshape(1)

    part_lines = line_count // PARTS
    lefts, rights, edges = [], [], ()
    for part in range(PARTS):
        lines = after(volume_plane, edges)[:, part * part_lines : (part + 1) * part_lines]
        edges = (lines[:, :, :reach], lines[:, :, width - reach :])
        if part == PARTS - 1:
            fill = ((0, 0), (0, 0), (0, reach - line_count))
            margins = (wave_b[:, :MARGIN], wave_b[:, -MARGIN:])
            edges = [
                jnp.concatenate([edge, jnp.pad(margin, fill)], 1)
                for edge, margin in zip(edges, margins)
            ]
        left, right = from_both_sides(*edges, "col")
        lefts.append(left)
        rights.append(right)
    wave_b_halos = [x[-1][:, part_lines:, :line_count] for x in (lefts, rights)]

    base_rows, spare_rows = group_starts(reach - MARGIN - shift_rows, GROUP, BLOCK)

    front = -(-(SHIFT_Y + MARGIN) // GROUP) * GROUP
    back = front + 3 * BLOCK
    mine = lambda x: lax.dynamic_slice_in_dim(x, row_index * BLOCK, BLOCK, 1)
    base_columns, spare_columns = group_starts(front - MARGIN - mine(shift_columns), BLOCK, GROUP)
    column_fractions = mine(fraction_columns)

    def first(view, begin, lefts, rights, rank):
        return shear_tile(
            volume_plane,
            lefts,
            rights,
            begin,
            len(lefts) * part_lines,
            halo,
            base_rows[view, 0],
            rank,
            spare_rows[view, 0],
            fraction_rows[view, 0],
            row_tables,
        )

    def second(view, pieces, place, rank, rows_out):
        return shear_columns(
            pieces,
            place,
            row_devices,
            front,
            back,
            base_columns[view] * GROUP,
            rank,
            spare_columns[view],
            column_fractions[view],
            column_tables,
            rows_out,
        )

    matrices = travel_matrices(travel_distance, forward, inverse)
    real, imaginary = matrices[:, 0], matrices[:, 1]
    along_rows = jnp.concatenate(
        [
            jnp.concatenate([real, -imaginary], 1),
            jnp.concatenate([imaginary, real], 1),
        ],
        2,
    )
    along_rows = jnp.swapaxes(along_rows, 1, 2).astype(jnp.bfloat16)
    spaced = jnp.pad(matrices, ((0, 0), (0, 0), (BLOCK - MARGIN, BLOCK - MARGIN), (0, 0)))
    real, imaginary = spaced[:, 0], spaced[:, 1]
    along_columns = jnp.concatenate(
        [
            jnp.concatenate([real, -imaginary], 1),
            jnp.concatenate([imaginary, real], 1),
        ],
        2,
    ).astype(jnp.bfloat16)

    spread, sheared = [], ()
    for part in range(PARTS):
        left, right = after((lefts[part], rights[part]), sheared)
        sheared = first(1, part * part_lines, [left], [right], in_order)
        spread.append(lax.all_to_all(sheared, "row", split_axis=0, concat_axis=0, tiled=True))
    lefts, rights = after((lefts, rights), sheared)
    slots = first(0, 0, lefts, rights, by_rank)
    shares = [slots[s : s + 1] for s in range(row_devices)]
    spread, shares = lax.optimization_barrier((spread, shares))
    pieces = swapped_shares(shares)

    place = [[(b, part * part_lines) for b in range(row_devices)] for part in range(PARTS)]
    moved_b = second(1, spread, place, in_order, BLOCK)
    whole = lax.all_to_all(moved_b, ("row", "col"), split_axis=0, concat_axis=0, tiled=True)
    pieces = after(pieces, moved_b)
    moved_a = second(0, pieces, [[(s, 0)] for s in range(row_devices)], by_rank, line_count)
    moved_a, whole = lax.optimization_barrier((moved_a, whole))
    whole = whole.reshape(row_devices, column_devices, 2, BLOCK, BLOCK)
    own_lines = lambda x: lax.dynamic_slice_in_dim(x, column_index * BLOCK, BLOCK, 0)
    groups = BLOCK // GROUP
    turned = shear_whole(
        whole,
        halo,
        lax.dynamic_slice_in_dim(base_rows[1, 1], column_index * groups, groups, 0),
        own_lines(spare_rows[1, 1]),
        own_lines(fraction_rows[1, 1]),
        turned_tables,
    )

    pieces = swapped_shares([moved_a[s : s + 1] for s in range(row_devices)])
    tile, low, high = ordered(pieces, halo, by_rank)
    left, right = from_both_sides(low, high, "col")

    turned = lax.all_to_all(turned, "col", split_axis=0, concat_axis=0, tiled=True)
    half_b = travel_first(turned, (), (wave_b, *wave_b_halos), along_rows[1])
    low, high = from_both_sides(half_b[:1], half_b[-1:], "row")
    exit_b = travel_second(low, half_b, high, along_columns[1])

    left, right = after((left, right), exit_b)
    field_a = shear_tile(
        tile,
        [left],
        [right],
        0,
        line_count,
        halo,
        base_rows[0, 1],
        in_order,
        spare_rows[0, 1],
        fraction_rows[0, 1],
        row_tables,
        wave_a,
    )
    halos = from_both_sides(field_a[:, :, :MARGIN], field_a[:, :, -MARGIN:], "row")
    half_a = travel_first(field_a, halos, (), along_rows[0])
    low, high = from_both_sides(half_a[:1], half_a[-1:], "col")
    exit_a = travel_second(low, half_a, high, along_columns[0])
    return exit_a, exit_b


def swapped(value, axis, bit):
    mask = 2**bit
    pairs = [(source, source ^ mask) for source in range(lax.axis_size(axis))]
    return lax.ppermute(value, axis, pairs)


def padded_2(x, sides, width):
    for axis, dim in sides:
        devices, length = (lax.axis_size(axis), x.shape[dim])
        up = [(i, (i + 1) % devices) for i in range(devices - 1)]
        down = [(j, i) for i, j in up]
        last = lax.slice_in_dim(x, length - width, length, axis=dim)
        first = lax.slice_in_dim(x, 0, width, axis=dim)
        before = lax.ppermute(last, axis, up)
        after = lax.ppermute(first, axis, down)
        x = jnp.concatenate([before, x, after], axis=dim)
    return x


def fourier_tables(block_len, margin):
    window_len = block_len + 2 * margin
    frequency = jnp.arange(window_len, dtype=jnp.int32) - window_len // 2
    position = jnp.arange(window_len, dtype=jnp.int32)
    angles = (
        2.0
        * jnp.pi
        * jnp.mod(position[:, None] * frequency[None, :], window_len).astype(jnp.float32)
        / window_len
    )
    cosine = jnp.cos(angles)
    sines = jnp.sin(angles)
    forward = jnp.concatenate(
        [jnp.concatenate([cosine, -sines], 1), jnp.concatenate([sines, cosine], 1)], 0
    ).astype(jnp.bfloat16)
    target = jnp.arange(block_len, dtype=jnp.int32) + margin
    inverse_angle = (
        2.0
        * jnp.pi
        * jnp.mod(frequency[:, None] * target[None, :], window_len).astype(jnp.float32)
        / window_len
    )
    inverse_cosine = jnp.cos(inverse_angle) / window_len
    inverse_sine = jnp.sin(inverse_angle) / window_len
    inverse = jnp.concatenate(
        [
            jnp.concatenate([inverse_cosine, inverse_sine], 1),
            jnp.concatenate([-inverse_sine, inverse_cosine], 1),
        ],
        0,
    ).astype(jnp.bfloat16)
    return (forward, inverse, frequency.astype(jnp.float32))


def shear_ramp(fractions, frequency):
    window_len = frequency.shape[0]
    phases = -2.0 * jnp.pi / window_len * fractions[:, None] * frequency[None, :]
    nyquist = (jnp.arange(window_len) == 0)[None, :]
    ramp_real = jnp.where(nyquist, jnp.cos(jnp.pi * fractions)[:, None], jnp.cos(phases))
    ramp_imaginary = jnp.where(nyquist, 0.0, jnp.sin(phases))
    return (ramp_real, ramp_imaginary)


def travel_ramp(distance, frequency):
    window_len = frequency.shape[0]
    phases = -2.0 * jnp.pi / (window_len * window_len) * distance * frequency * frequency
    return (jnp.cos(phases)[None, :], jnp.sin(phases)[None, :])


def select_window(padded, starts, out_len):
    total_len = padded.shape[2]
    offset_range = total_len - out_len
    bit_count = max(offset_range, 1).bit_length()
    current = jnp.pad(padded, ((0, 0), (0, 0), (0, out_len + 2**bit_count - 1 - total_len)))
    for bit_number in reversed(range(bit_count)):
        stride = 2**bit_number
        kept_len = current.shape[2] - stride
        chosen = (starts // stride % 2 == 1)[None, :, None]
        current = jnp.where(
            chosen, current[:, :, stride : stride + kept_len], current[:, :, :kept_len]
        )
    return current


def line_pass(padded, extent, shifts, ramp_real, ramp_imaginary, tables):
    forward, inverse = (tables[0], tables[1])
    window_len = BLOCK + 2 * MARGIN
    line_count = padded.shape[1]
    blocks = (padded.shape[2] - 2 * extent) // BLOCK
    reach_len = blocks * BLOCK + 2 * MARGIN
    if shifts is None:
        shifted = padded
    else:
        starts = extent - MARGIN - shifts
        shifted = select_window(padded, starts, reach_len)
    middle = shifted[:, :, MARGIN : MARGIN + blocks * BLOCK].reshape(2, line_count, blocks, BLOCK)
    left_rim = shifted[:, :, : blocks * BLOCK].reshape(2, line_count, blocks, BLOCK)[..., :MARGIN]
    right_rim = shifted[:, :, 2 * MARGIN : 2 * MARGIN + blocks * BLOCK].reshape(
        2, line_count, blocks, BLOCK
    )[..., BLOCK - MARGIN :]
    windows = jnp.concatenate([left_rim, middle, right_rim], 3)
    spectrum = jnp.einsum(
        "cpms,cst->pmt",
        windows,
        forward.reshape(2, window_len, 2 * window_len),
        preferred_element_type=jnp.float32,
    )
    spec_real = spectrum[..., :window_len]
    spec_imaginary = spectrum[..., window_len:]
    factor_real = ramp_real[:, None, :]
    factor_imaginary = ramp_imaginary[:, None, :]
    ramped = jnp.concatenate(
        [
            spec_real * factor_real - spec_imaginary * factor_imaginary,
            spec_real * factor_imaginary + spec_imaginary * factor_real,
        ],
        -1,
    ).astype(jnp.bfloat16)
    result = jnp.einsum(
        "pms,scb->cpmb",
        ramped,
        inverse.reshape(2 * window_len, 2, BLOCK),
        preferred_element_type=jnp.float32,
    )
    return result.reshape(2, line_count, blocks * BLOCK).astype(jnp.bfloat16)


def single_pass(padded, extent, shifts, fractions, tables):
    ramp_real, ramp_imaginary = shear_ramp(fractions, tables[2])
    return line_pass(padded, extent, shifts, ramp_real, ramp_imaginary, tables)


def general_shear_columns(stacked, shifts, fractions, tables):
    halo_depth = SHIFT_X + MARGIN
    inputs = stacked.shape[0]
    column_devices = lax.axis_size("col")
    share = stacked.shape[2] // column_devices
    offset = lax.axis_index("col") * share
    spread = lax.all_to_all(stacked, "col", split_axis=2, concat_axis=3, tiled=True)
    padded = jnp.pad(spread, ((0, 0), (0, 0), (0, 0), (halo_depth, halo_depth)))
    row_shifts = lax.dynamic_slice_in_dim(shifts, offset, share, 1)
    row_fractions = lax.dynamic_slice_in_dim(fractions, offset, share, 1)
    sheared = jnp.stack(
        [
            single_pass(
                padded[min(0, inputs - 1)], halo_depth, row_shifts[0], row_fractions[0], tables
            )
        ]
    )
    return lax.all_to_all(sheared, "col", split_axis=3, concat_axis=2, tiled=True)


def shear_along_first(padded_lines, halo_depth, shifts, fractions, tables):
    flipped = jnp.swapaxes(padded_lines[0], 1, 2)
    moved = single_pass(flipped, halo_depth, shifts[0], fractions[0], tables)
    sheared = [jnp.swapaxes(moved, 1, 2)]
    return jnp.stack(sheared)


def shear_rows_pass(stacked, shifts, fractions, tables):
    halo_depth = SHIFT_Y + MARGIN
    row_devices = lax.axis_size("row")
    share = stacked.shape[3] // row_devices
    offset = lax.axis_index("row") * share
    spread = lax.all_to_all(stacked, "row", split_axis=3, concat_axis=2, tiled=True)
    padded = jnp.pad(spread, ((0, 0), (0, 0), (halo_depth, halo_depth), (0, 0)))
    column_shifts = lax.dynamic_slice_in_dim(shifts, offset, share, 1)
    column_fractions = lax.dynamic_slice_in_dim(fractions, offset, share, 1)
    sheared = shear_along_first(padded, halo_depth, column_shifts, column_fractions, tables)
    return lax.all_to_all(sheared, "row", split_axis=2, concat_axis=3, tiled=True)


def travel_local(extended, distance, tables):
    ramp_real, ramp_imaginary = travel_ramp(distance, tables[2])
    halfway = line_pass(extended, MARGIN, None, ramp_real, ramp_imaginary, tables)
    flipped = jnp.swapaxes(halfway, 1, 2)
    finished = line_pass(flipped, MARGIN, None, ramp_real, ramp_imaginary, tables)
    return jnp.swapaxes(finished, 1, 2)


def transmit(rotated, wave):
    phase_part = rotated[0].astype(jnp.float32)
    absorb_part = rotated[1].astype(jnp.float32)
    amplitude = jnp.exp(-ABSORB * absorb_part)
    through_real = amplitude * jnp.cos(phase_part)
    through_imaginary = amplitude * jnp.sin(phase_part)
    wave_real = wave[0].astype(jnp.float32)
    wave_imaginary = wave[1].astype(jnp.float32)
    return jnp.stack(
        [
            wave_real * through_real - wave_imaginary * through_imaginary,
            wave_real * through_imaginary + wave_imaginary * through_real,
        ]
    ).astype(jnp.bfloat16)


def general_on_device(
    volume_plane,
    wave_a,
    wave_b,
    shift_rows,
    fraction_rows,
    shift_columns,
    fraction_columns,
    travel_distance,
):
    tables = fourier_tables(BLOCK, MARGIN)
    source = volume_plane[None]
    results = []
    for member in range(2):
        stacked = general_shear_columns(
            source,
            shift_rows[member : member + 1, 0],
            fraction_rows[member : member + 1, 0],
            tables,
        )
        stacked = shear_rows_pass(
            stacked,
            shift_columns[member : member + 1],
            fraction_columns[member : member + 1],
            tables,
        )
        stacked = general_shear_columns(
            stacked,
            shift_rows[member : member + 1, 1],
            fraction_rows[member : member + 1, 1],
            tables,
        )
        results.append(stacked[0])
    view_one = results[0]
    view_two = results[1]
    turned = jnp.swapaxes(jnp.flip(view_two, 2), 1, 2)
    for bit_number in range(lax.axis_size("col").bit_length() - 1):
        turned = swapped(turned, "col", bit_number)
    product_a = transmit(view_one, wave_a)
    extended_a = padded_2(product_a, (("row", 1), ("col", 2)), MARGIN)
    exit_a = travel_local(extended_a, travel_distance[0], tables)
    product_b = transmit(turned, wave_b)
    extended_b = padded_2(product_b, (("row", 2), ("col", 1)), MARGIN)
    exit_b = travel_local(extended_b, travel_distance[1], tables)
    return (exit_a, exit_b)


def solution(mesh):
    def either(volume_plane, *rest):
        rows, width = volume_plane.shape[1:]
        fits = (
            rows == BLOCK * lax.axis_size("col")
            and width == BLOCK * lax.axis_size("row")
            and width >= -(-(SHIFT_X + MARGIN) // BLOCK) * BLOCK >= rows
        )
        chosen = on_device if fits else general_on_device
        return chosen(volume_plane, *rest)

    return jax.shard_map(
        either,
        mesh=mesh,
        in_specs=(
            P(None, "row", "col"),
            P(None, "row", "col"),
            P(None, "col", "row"),
            P(None, None, "row"),
            P(None, None, "row"),
            P(None, "col"),
            P(None, "col"),
            P(),
        ),
        out_specs=(P(None, "row", "col"), P(None, "col", "row")),
        check_vma=False,
    )
```

```python
import functools

import jax
import jax.numpy as jnp
import numpy as np
from jax import lax
from jax.experimental import pallas as pl
from jax.experimental.pallas import tpu as pltpu
from jax.sharding import PartitionSpec as P

BLOCK = 128
MARGIN = 32
SHIFT_X = 864
SHIFT_Y = 1728


ABSORB = 0.25

WINDOW = BLOCK + 2 * MARGIN
BINS = WINDOW // 2
GROUP = 16
PARTS = 2
ROWS = 256
STEPS = 2
VMEM_LIMIT = 56 * 1024 * 1024


def angle_table(rows, columns):
    return 2.0 * np.pi * (np.outer(rows, columns) % WINDOW) / WINDOW


def real_tables():
    position = np.arange(WINDOW)
    bins = np.arange(BINS + 1)
    target = np.arange(BLOCK) + MARGIN
    forward = np.zeros((2 * BLOCK, 2 * BLOCK), np.float32)
    forward[:WINDOW, : BINS + 1] = np.cos(angle_table(position, bins))
    forward[:WINDOW, BLOCK + 1 : BLOCK + BINS] = -np.sin(angle_table(position, bins[1:BINS]))
    weight = np.where((bins == 0) | (bins == BINS), 1.0, 2.0) / WINDOW
    inverse = np.zeros((2 * BLOCK, BLOCK), np.float32)
    inverse[: BINS + 1] = np.cos(angle_table(bins, target)) * weight[:, None]
    inverse[BLOCK + 1 : BLOCK + BINS] = (
        -np.sin(angle_table(bins[1:BINS], target)) * weight[1:BINS, None]
    )
    return forward, inverse


def travel_matrices(distance, forward, inverse):
    frequency = jnp.arange(BLOCK, dtype=jnp.float32)
    phases = -2.0 * jnp.pi / (WINDOW * WINDOW) * distance[:, None] * frequency * frequency
    ramps = jnp.stack([jnp.cos(phases), jnp.sin(phases)], 1)
    ramps = jnp.concatenate([ramps, ramps], 2)
    scaled = ramps[..., None] * jnp.asarray(inverse)
    matrices = jnp.einsum(
        "pq,vrqu->vrpu",
        jnp.asarray(forward[:WINDOW]),
        scaled,
        precision=lax.Precision.HIGHEST,
    )
    return matrices


def lane_iota(rows):
    return lax.broadcasted_iota(jnp.int32, (rows, BLOCK), 1)


def shift_lines(strip, shifted, base, base_offset, spare, windows, chunk_offset, rows):
    def one_group(group, carry):
        first = pl.multiple_of(group * GROUP, GROUP)
        lines = pl.ds(first, GROUP)
        start = base[base_offset + group] + chunk_offset
        offset = spare[lines, :]
        later = offset >= BLOCK
        lane = lane_iota(GROUP) + (offset & (BLOCK - 1))
        wraps = lane >= BLOCK
        index = lane & (BLOCK - 1)
        for part in range(2):
            here = strip[start, part, lines, :].astype(jnp.float32)
            before = None
            for i in range(windows + 2):
                following = strip[start + i + 1, part, lines, :].astype(jnp.float32)
                turned = jnp.take_along_axis(jnp.where(later, following, here), index, axis=1)
                if before is not None:
                    shifted[i - 1, part, lines, :] = jnp.where(wraps, turned, before).astype(
                        jnp.bfloat16
                    )
                before = turned
                here = following
        return carry

    lax.fori_loop(0, rows // GROUP, one_group, 0, unroll=4)


def ramped_lines(shifted, windows, rows, cosine, sine, forward):
    count = len(windows)
    lower = jnp.concatenate([shifted[m].reshape(2 * rows, BLOCK) for m in windows], 0)
    upper = jnp.concatenate([shifted[m + 1].reshape(2 * rows, BLOCK) for m in windows], 0)
    spectrum = jnp.dot(
        jnp.concatenate([lower, upper], 1), forward[...], preferred_element_type=jnp.float32
    )
    real = spectrum[:, :BLOCK].reshape(count * 2, rows, BLOCK)
    imaginary = spectrum[:, BLOCK:].reshape(count * 2, rows, BLOCK)
    ramp_real = cosine[...][None]
    ramp_imaginary = sine[...][None]
    ramped = jnp.concatenate(
        [
            (real * ramp_real - imaginary * ramp_imaginary).astype(jnp.bfloat16),
            (real * ramp_imaginary + imaginary * ramp_real).astype(jnp.bfloat16),
        ],
        2,
    )
    return ramped.reshape(count * 2 * rows, 2 * BLOCK)


def down_lines(vector):
    return jnp.broadcast_to(vector, (BLOCK, vector.shape[1])).T


def line_ramps(fractions, cosine, sine):
    bins = lane_iota(fractions.shape[1]).astype(jnp.float32)
    sine[...], cosine[...] = sine_cosine(down_lines(fractions) * bins * (-2.0 * np.pi / WINDOW))


def shear_tile_kernel(halo, tiles, rows, batch, wide, parts, sent, base, rank, *refs):
    lefts, rights, refs = refs[:parts], refs[parts : 2 * parts], refs[2 * parts :]
    waves, refs = refs[: int(sent)], refs[int(sent) :]
    own, offsets, fractions, forward, inverse, out = refs[:6]
    strip, shifted, spare, cosine, sine = refs[6:]
    step = pl.program_id(0)
    groups = rows // GROUP
    end = halo + tiles + halo

    @pl.when(step == 0)
    def _():
        strip[end : end + 2] = jnp.zeros((2, 2, rows, BLOCK), jnp.bfloat16)

    def fill(piece, first, count):
        for i in range(count):
            if wide:
                strip[first + i] = piece[:, :, i * BLOCK : (i + 1) * BLOCK]
            else:
                strip[first + i] = piece[i]

    share = pl.num_programs(0) // parts
    for part in range(parts):

        @pl.when(step // share == part)
        def _():
            fill(lefts[part], 0, halo)
            fill(rights[part], halo + tiles, halo)

    fill(own, halo, tiles)
    spare[...] = down_lines(offsets[0]).astype(jnp.int32)
    line_ramps(fractions[0], cosine, sine)
    shift_lines(strip, shifted, base, step * groups, spare, tiles, 0, rows)
    for first in range(0, tiles, batch):
        windows = [slot if sent else slot ^ rank[0] for slot in range(first, first + batch)]
        ramped = ramped_lines(shifted, windows, rows, cosine, sine, forward)
        result = jnp.dot(ramped, inverse[...], preferred_element_type=jnp.float32)
        result = result.astype(jnp.bfloat16).reshape(batch, 2, rows, BLOCK)
        if sent:
            for i, window in enumerate(windows):
                wave = waves[0][:, :, window * BLOCK : (window + 1) * BLOCK]
                for part, value in enumerate(transmitted(result[i], wave)):
                    out[window, part] = value
        else:
            out[first : first + batch] = result


def shear_tile(own, lefts, rights, first, lines, halo, base, rank, spare, fractions, tables, *waves):
    wide = own.ndim == 3
    parts = len(lefts)
    line_count = lines
    part_lines = line_count // parts
    tiles = own.shape[2] // BLOCK if wide else own.shape[0]
    rows = min(part_lines, ROWS)
    share = part_lines // rows
    offset = first // rows
    forward, inverse = tables

    def piece_spec(piece, place):
        if wide:
            return pl.BlockSpec((2, rows, piece.shape[2]), lambda i, *_: (0, place(i), 0))
        return pl.BlockSpec((piece.shape[0], 2, rows, BLOCK), lambda i, *_: (0, 0, place(i), 0))

    halo_specs = [
        piece_spec(x, lambda i, part=part: jnp.clip(i - part * share, 0, share - 1))
        for x in (lefts[0], rights[0])
        for part in range(parts)
    ]
    line_spec = pl.BlockSpec((1, 1, rows), lambda i, *_: (i + offset, 0, 0))
    along = lambda x: x.astype(jnp.float32).reshape(-1, 1, rows)
    out_shape = jax.ShapeDtypeStruct((tiles, 2, line_count, BLOCK), jnp.bfloat16)
    out_spec = pl.BlockSpec((tiles, 2, rows, BLOCK), lambda i, *_: (0, 0, i, 0))
    groups = rows // GROUP
    kernel = functools.partial(
        shear_tile_kernel,
        halo,
        tiles,
        rows,
        tiles // 4 if tiles % 4 == 0 else tiles,
        wide,
        parts,
        len(waves) > 0,
    )
    return pl.pallas_call(
        kernel,
        grid_spec=pltpu.PrefetchScalarGridSpec(
            num_scalar_prefetch=2,
            grid=(line_count // rows,),
            in_specs=halo_specs
            + [pl.BlockSpec((2, rows, x.shape[2]), lambda i, *_: (0, i + offset, 0)) for x in waves]
            + [piece_spec(own, lambda i: i + offset)]
            + [line_spec] * 2
            + [
                pl.BlockSpec(forward.shape, lambda i, *_: (0, 0)),
                pl.BlockSpec(inverse.shape, lambda i, *_: (0, 0)),
            ],
            out_specs=out_spec,
            scratch_shapes=[
                pltpu.VMEM((halo + tiles + halo + 2, 2, rows, BLOCK), jnp.bfloat16),
                pltpu.VMEM((tiles + 1, 2, rows, BLOCK), jnp.bfloat16),
                pltpu.VMEM((rows, BLOCK), jnp.int32),
                pltpu.VMEM((rows, BLOCK), jnp.float32),
                pltpu.VMEM((rows, BLOCK), jnp.float32),
            ],
        ),
        out_shape=out_shape,
        compiler_params=pltpu.CompilerParams(vmem_limit_bytes=VMEM_LIMIT),
        name="shear_tile",
    )(
        lax.slice_in_dim(base, offset * groups, offset * groups + line_count // GROUP),
        rank,
        *lefts,
        *rights,
        *waves,
        own,
        along(spare),
        along(fractions),
        forward,
        inverse,
    )


def shear_whole_kernel(
    halo,
    devices,
    tiles,
    rows,
    base,
    own,
    offsets,
    fractions,
    forward,
    flipped,
    out,
    strip,
    shifted,
    spare,
    cosine,
    sine,
):
    step = pl.program_id(0)
    chunks = devices * tiles
    length = tiles * BLOCK

    @pl.when(step == 0)
    def _():
        strip[0:halo] = jnp.zeros((halo, 2, rows, BLOCK), jnp.bfloat16)
        strip[halo + chunks :] = jnp.zeros((halo + 2, 2, rows, BLOCK), jnp.bfloat16)
        for chunk in range(chunks):
            strip[halo + chunk] = own[chunk % tiles, chunk // tiles]
        out[0, :, 0:MARGIN, :] = jnp.zeros((2, MARGIN, rows), jnp.bfloat16)
        out[devices - 1, :, MARGIN + length :, :] = jnp.zeros((2, MARGIN, rows), jnp.bfloat16)
        spare[...] = down_lines(offsets[...]).astype(jnp.int32)
        line_ramps(fractions[...], cosine, sine)

    shift_lines(strip, shifted, base, 0, spare, tiles, step * tiles, rows)
    ramped = ramped_lines(shifted, range(tiles), rows, cosine, sine, forward)
    target = devices - 1 - step
    result = lax.dot_general(
        flipped[...], ramped, (((1,), (1,)), ((), ())), preferred_element_type=jnp.float32
    ).astype(jnp.bfloat16)
    for window in range(tiles):
        block = tiles - 1 - window
        low = MARGIN + block * BLOCK
        for part in range(2):
            lanes = (2 * window + part) * rows
            piece = result[:, lanes : lanes + rows]
            out[target, part, low : low + BLOCK, :] = piece
            if block == 0:

                @pl.when(target > 0)
                def _():
                    out[target - 1, part, MARGIN + length :, :] = piece[:MARGIN]

            if block == tiles - 1:

                @pl.when(target < devices - 1)
                def _():
                    out[target + 1, part, 0:MARGIN, :] = piece[BLOCK - MARGIN :]


def shear_whole(own, halo, base, spare, fractions, tables):
    tiles, devices, _, rows, _ = own.shape
    forward, flipped = tables
    operands = (
        own,
        spare.astype(jnp.float32).reshape(1, rows),
        fractions.reshape(1, rows),
        forward,
        flipped,
    )
    full = lambda shape: pl.BlockSpec(shape, lambda i, *_: (0,) * len(shape))
    out = (devices, 2, tiles * BLOCK + 2 * MARGIN, rows)
    return pl.pallas_call(
        functools.partial(shear_whole_kernel, halo, devices, tiles, rows),
        grid_spec=pltpu.PrefetchScalarGridSpec(
            num_scalar_prefetch=1,
            grid=(devices,),
            in_specs=[full(x.shape) for x in operands],
            out_specs=full(out),
            scratch_shapes=[
                pltpu.VMEM((2 * halo + devices * tiles + 2, 2, rows, BLOCK), jnp.bfloat16),
                pltpu.VMEM((tiles + 1, 2, rows, BLOCK), jnp.bfloat16),
                pltpu.VMEM((rows, BLOCK), jnp.int32),
                pltpu.VMEM((rows, BLOCK), jnp.float32),
                pltpu.VMEM((rows, BLOCK), jnp.float32),
            ],
        ),
        out_shape=jax.ShapeDtypeStruct(out, jnp.bfloat16),
        compiler_params=pltpu.CompilerParams(vmem_limit_bytes=VMEM_LIMIT),
        name="shear_whole",
    )(base, *operands)


def shear_columns_kernel(front, blocks, length, rows_out, place, base, rank, *refs):
    owns, refs = refs[: len(place)], refs[len(place) :]
    offsets, fractions, forward, inverse, out, strip, shifted, cosine, sine = refs
    step = pl.program_id(0)
    per_step = length // BLOCK
    per_grid = blocks // pl.num_programs(0)
    total = strip.shape[1]

    @pl.when(step == 0)
    def _():
        strip[:, 0:front, :] = jnp.zeros((2, front, BLOCK), jnp.bfloat16)
        back = front + blocks * length
        strip[:, back:, :] = jnp.zeros((2, total - back, BLOCK), jnp.bfloat16)
        for own, slots in zip(owns, place):
            count = own.shape[2]
            for i, (slot, within) in enumerate(slots):
                first = front + slot * length + within
                for part in range(2):
                    strip[part, first : first + count, :] = own[i, part]
        bins = lax.broadcasted_iota(jnp.int32, (BLOCK, BLOCK), 0).astype(jnp.float32)
        sine[...], cosine[...] = sine_cosine(bins * fractions[...] * (-2.0 * np.pi / WINDOW))

    offset = jnp.broadcast_to(offsets[...], (8, BLOCK))
    row = lax.broadcasted_iota(jnp.int32, (8, BLOCK), 0) + (offset & 7)
    wraps = row >= 8
    index = row & 7

    def one_chunk(block_rows, chunk):
        begin = pl.multiple_of(base[0] + block_rows + chunk * BLOCK, GROUP)
        for part in range(2):
            value = strip[part, pl.ds(begin, 2 * BLOCK), :].astype(jnp.float32)
            value = value.reshape(2 * BLOCK // 8, 8, BLOCK)
            for bit in (64, 32, 16, 8):
                taken = ((offset & bit) != 0)[None]
                value = jnp.where(taken, value[bit // 8 :], value[: -(bit // 8)])
            pieces = [
                jnp.take_along_axis(value[i], index, axis=0) for i in range(BLOCK // 8 + 1)
            ]
            moved = [
                jnp.where(wraps, pieces[i + 1], pieces[i]) for i in range(BLOCK // 8)
            ]
            shifted[chunk * BLOCK : (chunk + 1) * BLOCK, part * BLOCK : (part + 1) * BLOCK] = (
                jnp.concatenate(moved, 0).astype(jnp.bfloat16)
            )

    def one_block(local, carry):
        block_rows = ((step * per_grid + local) ^ rank[0]) * length
        for chunk in range(per_step + 1):
            one_chunk(block_rows, chunk)
        windows = [shifted[m * BLOCK : (m + 2) * BLOCK, :] for m in range(per_step)]
        spectrum = jnp.dot(
            forward[...], jnp.concatenate(windows, 1), preferred_element_type=jnp.float32
        )
        ramp_real = jnp.concatenate([cosine[...]] * (2 * per_step), 1)
        ramp_imaginary = jnp.concatenate([sine[...]] * (2 * per_step), 1)
        real, imaginary = spectrum[:BLOCK], spectrum[BLOCK:]
        ramped = jnp.concatenate(
            [
                (real * ramp_real - imaginary * ramp_imaginary).astype(jnp.bfloat16),
                (real * ramp_imaginary + imaginary * ramp_real).astype(jnp.bfloat16),
            ],
            0,
        )
        result = jnp.dot(inverse[...], ramped, preferred_element_type=jnp.float32)
        result = result.astype(jnp.bfloat16)
        for window in range(per_step):
            piece, within = window * BLOCK // rows_out, window * BLOCK % rows_out
            for part in range(2):
                lanes = (2 * window + part) * BLOCK
                out[local * (length // rows_out) + piece, part, within : within + BLOCK, :] = (
                    result[:, lanes : lanes + BLOCK]
                )
        return carry

    lax.fori_loop(0, per_grid, one_block, 0)


def shear_columns(owns, place, blocks, front, back, base, rank, spare, fractions, tables, rows_out):
    length = sum(own.shape[0] * own.shape[2] for own in owns) // blocks
    forward, inverse = tables
    operands = (
        *owns,
        spare.astype(jnp.int32).reshape(1, BLOCK),
        fractions.reshape(1, BLOCK),
        forward,
        inverse,
    )
    full = lambda shape: pl.BlockSpec(shape, lambda i, *_: (0,) * len(shape))
    pieces = blocks * length // rows_out
    steps = STEPS if blocks % STEPS == 0 else 1
    return pl.pallas_call(
        functools.partial(shear_columns_kernel, front, blocks, length, rows_out, place),
        grid_spec=pltpu.PrefetchScalarGridSpec(
            num_scalar_prefetch=2,
            grid=(steps,),
            in_specs=[full(x.shape) for x in operands],
            out_specs=pl.BlockSpec(
                (pieces // steps, 2, rows_out, BLOCK), lambda i, *_: (i, 0, 0, 0)
            ),
            scratch_shapes=[
                pltpu.VMEM((2, front + blocks * length + back, BLOCK), jnp.bfloat16),
                pltpu.VMEM((length + BLOCK, 2 * BLOCK), jnp.bfloat16),
                pltpu.VMEM((BLOCK, BLOCK), jnp.float32),
                pltpu.VMEM((BLOCK, BLOCK), jnp.float32),
            ],
        ),
        out_shape=jax.ShapeDtypeStruct((pieces, 2, rows_out, BLOCK), jnp.bfloat16),
        compiler_params=pltpu.CompilerParams(vmem_limit_bytes=VMEM_LIMIT),
        name="shear_columns",
    )(base, rank, *operands)


def sine_cosine(angle):
    turns = jnp.round(angle * (2.0 / np.pi))
    rest = angle - turns * 1.5703125
    rest = rest - turns * 4.837512969970703125e-4
    rest = rest - turns * 7.549789954891882e-8
    square = rest * rest
    sine = rest + rest * square * (
        -1.6666654611e-1 + square * (8.3321608736e-3 - square * 1.9515295891e-4)
    )
    cosine = (
        1.0
        - 0.5 * square
        + square
        * square
        * (4.166664568298827e-2 + square * (-1.388731625493765e-3 + square * 2.443315711809948e-5))
    )
    quadrant = turns.astype(jnp.int32)
    odd = (quadrant & 1) != 0
    sine_out = jnp.where(odd, cosine, sine)
    cosine_out = jnp.where(odd, sine, cosine)
    sine_out = jnp.where((quadrant & 2) != 0, -sine_out, sine_out)
    cosine_out = jnp.where(((quadrant + 1) & 2) != 0, -cosine_out, cosine_out)
    return sine_out, cosine_out


def transmitted(rotated, wave):
    sine, cosine = sine_cosine(rotated[0].astype(jnp.float32))
    amplitude = jnp.exp(-ABSORB * rotated[1].astype(jnp.float32))
    through_real = amplitude * cosine
    through_imaginary = amplitude * sine
    wave_real = wave[0].astype(jnp.float32)
    wave_imaginary = wave[1].astype(jnp.float32)
    return (
        (wave_real * through_real - wave_imaginary * through_imaginary).astype(jnp.bfloat16),
        (wave_real * through_imaginary + wave_imaginary * through_real).astype(jnp.bfloat16),
    )


def travel_first_kernel(length, count, sent, *refs):
    if sent:
        body, top, bottom, matrix, out, field = refs
        for chunk in range(count):
            across = slice(chunk * BLOCK, (chunk + 1) * BLOCK)
            for part in range(2):
                field[part, 0:MARGIN, across] = top[chunk, part]
                field[part, MARGIN : MARGIN + length, across] = body[chunk, part]
                field[part, MARGIN + length :, across] = bottom[chunk, part]
    else:
        body, wave, wave_top, wave_bottom, matrix, out, field = refs
        pieces = [(0, MARGIN, wave_top, 0)]
        pieces += [(MARGIN + first, BLOCK, wave, first) for first in range(0, length, BLOCK)]
        pieces += [(MARGIN + length, MARGIN, wave_bottom, 0)]
        for chunk in range(count):
            across = slice(chunk * BLOCK, (chunk + 1) * BLOCK)
            for place, height, waves, first in pieces:
                parts = transmitted(
                    [body[chunk, p, place : place + height, :] for p in range(2)],
                    [waves[p, first : first + height, across] for p in range(2)],
                )
                for part in range(2):
                    field[part, place : place + height, across] = parts[part]
    for m in range(0, length, BLOCK):
        window = jnp.concatenate([field[0, m : m + WINDOW, :], field[1, m : m + WINDOW, :]], 0)
        result = jnp.dot(matrix[...], window, preferred_element_type=jnp.float32)
        result = result.astype(jnp.bfloat16)
        for chunk in range(count):
            across = slice(chunk * BLOCK, (chunk + 1) * BLOCK)
            for part in range(2):
                out[chunk, part, m : m + BLOCK, :] = result[
                    part * BLOCK : (part + 1) * BLOCK, across
                ]


def travel_first(body, halos, waves, matrix):
    chunks = body.shape[0]
    count = chunks // STEPS if chunks % STEPS == 0 else chunks
    length = body.shape[2] if len(halos) > 0 else body.shape[2] - 2 * MARGIN
    chunk_spec = lambda x: pl.BlockSpec((count, 2, x.shape[2], BLOCK), lambda i: (i, 0, 0, 0))
    wide_spec = lambda x: pl.BlockSpec((2, x.shape[1], count * BLOCK), lambda i: (0, 0, i))
    return pl.pallas_call(
        functools.partial(travel_first_kernel, length, count, len(halos) > 0),
        grid=(chunks // count,),
        in_specs=[chunk_spec(x) for x in (body, *halos)]
        + [wide_spec(x) for x in waves]
        + [pl.BlockSpec(matrix.shape, lambda i: (0, 0))],
        out_specs=pl.BlockSpec((count, 2, length, BLOCK), lambda i: (i, 0, 0, 0)),
        out_shape=jax.ShapeDtypeStruct((chunks, 2, length, BLOCK), jnp.bfloat16),
        scratch_shapes=[pltpu.VMEM((2, length + 2 * MARGIN, count * BLOCK), jnp.bfloat16)],
        compiler_params=pltpu.CompilerParams(vmem_limit_bytes=VMEM_LIMIT),
        name="travel_first",
    )(body, *halos, *waves, matrix)


def travel_second_kernel(chunks, rows, left, body, right, matrix, out):
    parts = [[left[0, p]] + [body[m, p] for m in range(chunks)] + [right[0, p]] for p in range(2)]
    windows = [
        jnp.concatenate(parts[0][m : m + 3] + parts[1][m : m + 3], 1) for m in range(chunks)
    ]
    result = jnp.dot(
        jnp.concatenate(windows, 0), matrix[...], preferred_element_type=jnp.float32
    ).astype(jnp.bfloat16)
    for m in range(chunks):
        for part in range(2):
            out[part, :, m * BLOCK : (m + 1) * BLOCK] = result[
                m * rows : (m + 1) * rows, part * BLOCK : (part + 1) * BLOCK
            ]


def travel_second(left, body, right, matrix):
    chunks, _, length, _ = body.shape
    rows = length // STEPS if length % (STEPS * BLOCK) == 0 else length
    edge = pl.BlockSpec((1, 2, rows, BLOCK), lambda i: (0, 0, i, 0))
    return pl.pallas_call(
        functools.partial(travel_second_kernel, chunks, rows),
        grid=(length // rows,),
        in_specs=[
            edge,
            pl.BlockSpec((chunks, 2, rows, BLOCK), lambda i: (0, 0, i, 0)),
            edge,
            pl.BlockSpec(matrix.shape, lambda i: (0, 0)),
        ],
        out_specs=pl.BlockSpec((2, rows, chunks * BLOCK), lambda i: (0, i, 0)),
        out_shape=jax.ShapeDtypeStruct((2, length, chunks * BLOCK), jnp.bfloat16),
        compiler_params=pltpu.CompilerParams(vmem_limit_bytes=VMEM_LIMIT),
        name="travel_second",
    )(left, body, right, matrix)


def from_both_sides(first, last, axis):
    devices = lax.axis_size(axis)
    up = [(i, i + 1) for i in range(devices - 1)]
    down = [(j, i) for i, j in up]
    return lax.ppermute(last, axis, up), lax.ppermute(first, axis, down)


def after(value, *others):
    return lax.optimization_barrier((value, others))[0]


def ordered_kernel(halo, rank, *refs):
    pieces, (out, first, last) = refs[:-3], refs[-3:]
    count = len(pieces)
    for s, piece in enumerate(pieces):
        place = s ^ rank[0]
        out[place] = piece[0]

        @pl.when(place < halo)
        def _():
            first[place] = piece[0]

        @pl.when(place >= count - halo)
        def _():
            last[place - (count - halo)] = piece[0]


def ordered(pieces, halo, rank):
    count = len(pieces)
    block = pieces[0].shape
    shapes = [(n, *block[1:]) for n in (count, halo, halo)]
    full = lambda shape: pl.BlockSpec(shape, lambda i, *_: (0,) * len(shape))
    return pl.pallas_call(
        functools.partial(ordered_kernel, halo),
        grid_spec=pltpu.PrefetchScalarGridSpec(
            num_scalar_prefetch=1,
            grid=(1,),
            in_specs=[full(block)] * count,
            out_specs=[full(shape) for shape in shapes],
        ),
        out_shape=[jax.ShapeDtypeStruct(shape, pieces[0].dtype) for shape in shapes],
        compiler_params=pltpu.CompilerParams(vmem_limit_bytes=VMEM_LIMIT),
        name="ordered",
    )(rank, *pieces)


def swapped_shares(slots):
    devices = lax.axis_size("row")
    return [slots[0]] + [
        lax.ppermute(slots[s], "row", [(i, i ^ s) for i in range(devices)])
        for s in range(1, devices)
    ]


def group_starts(starts, group, unit):
    lines = starts.shape[-1]
    grouped = starts.reshape(*starts.shape[:-1], lines // group, group)
    base = jnp.min(grouped, -1) // unit
    spare = grouped - base[..., None] * unit
    return base.astype(jnp.int32), spare.reshape(starts.shape)


def on_device(
    volume_plane,
    wave_a,
    wave_b,
    shift_rows,
    fraction_rows,
    shift_columns,
    fraction_columns,
    travel_distance,
):
    _, line_count, width = volume_plane.shape
    row_devices, column_devices = lax.axis_size("row"), lax.axis_size("col")
    row_index, column_index = lax.axis_index("row"), lax.axis_index("col")
    tiles = width // BLOCK
    halo = -(-(SHIFT_X + MARGIN) // BLOCK)
    reach = halo * BLOCK

    forward, inverse = real_tables()
    half = lambda x: jnp.asarray(x, jnp.bfloat16)
    row_tables = (half(forward), half(inverse))
    column_tables = (half(forward.T), half(inverse.T))
    turned_tables = (half(forward), half(inverse[:, ::-1].T))
    in_order = jnp.zeros((1,), jnp.int32)
    by_rank = row_index.astype(jnp.int32).reshape(1)

    part_lines = line_count // PARTS
    lefts, rights, edges = [], [], ()
    for part in range(PARTS):
        lines = after(volume_plane, edges)[:, part * part_lines : (part + 1) * part_lines]
        edges = (lines[:, :, :reach], lines[:, :, width - reach :])
        if part == PARTS - 1:
            fill = ((0, 0), (0, 0), (0, reach - line_count))
            margins = (wave_b[:, :MARGIN], wave_b[:, -MARGIN:])
            edges = [
                jnp.concatenate([edge, jnp.pad(margin, fill)], 1)
                for edge, margin in zip(edges, margins)
            ]
        left, right = from_both_sides(*edges, "col")
        lefts.append(left)
        rights.append(right)
    wave_b_halos = [x[-1][:, part_lines:, :line_count] for x in (lefts, rights)]

    base_rows, spare_rows = group_starts(reach - MARGIN - shift_rows, GROUP, BLOCK)

    front = -(-(SHIFT_Y + MARGIN) // GROUP) * GROUP
    back = front + 3 * BLOCK
    mine = lambda x: lax.dynamic_slice_in_dim(x, row_index * BLOCK, BLOCK, 1)
    base_columns, spare_columns = group_starts(front - MARGIN - mine(shift_columns), BLOCK, GROUP)
    column_fractions = mine(fraction_columns)

    def first(view, begin, lefts, rights, rank):
        return shear_tile(
            volume_plane,
            lefts,
            rights,
            begin,
            len(lefts) * part_lines,
            halo,
            base_rows[view, 0],
            rank,
            spare_rows[view, 0],
            fraction_rows[view, 0],
            row_tables,
        )

    def second(view, pieces, place, rank, rows_out):
        return shear_columns(
            pieces,
            place,
            row_devices,
            front,
            back,
            base_columns[view] * GROUP,
            rank,
            spare_columns[view],
            column_fractions[view],
            column_tables,
            rows_out,
        )

    matrices = travel_matrices(travel_distance, forward, inverse)
    real, imaginary = matrices[:, 0], matrices[:, 1]
    along_rows = jnp.concatenate(
        [
            jnp.concatenate([real, -imaginary], 1),
            jnp.concatenate([imaginary, real], 1),
        ],
        2,
    )
    along_rows = jnp.swapaxes(along_rows, 1, 2).astype(jnp.bfloat16)
    spaced = jnp.pad(matrices, ((0, 0), (0, 0), (BLOCK - MARGIN, BLOCK - MARGIN), (0, 0)))
    real, imaginary = spaced[:, 0], spaced[:, 1]
    along_columns = jnp.concatenate(
        [
            jnp.concatenate([real, -imaginary], 1),
            jnp.concatenate([imaginary, real], 1),
        ],
        2,
    ).astype(jnp.bfloat16)

    across_rows = lambda x: lax.all_to_all(x, "row", split_axis=0, concat_axis=0, tiled=True)

    spread_a, sheared = [], ()
    for part in range(PARTS):
        left, right = after((lefts[part], rights[part]), sheared)
        sheared = first(0, part * part_lines, [left], [right], in_order)
        spread_a.append(across_rows(sheared))
    lefts, rights = after((lefts, rights), sheared)
    sheared_b = after(first(1, 0, lefts, rights, in_order), spread_a)
    spread_b = across_rows(sheared_b)

    spread_a = after(spread_a, sheared_b)
    place = [[(b, part * part_lines) for b in range(row_devices)] for part in range(PARTS)]
    moved_a = second(0, spread_a, place, by_rank, line_count)
    pieces = swapped_shares([moved_a[s : s + 1] for s in range(row_devices)])
    spread_b, early = lax.optimization_barrier((spread_b, pieces[1:5]))
    pieces[1:5] = early
    place = [[(b, 0) for b in range(row_devices)]]
    moved_b = second(1, [spread_b], place, in_order, BLOCK)
    whole = lax.all_to_all(moved_b, ("row", "col"), split_axis=0, concat_axis=0, tiled=True)

    tile, low, high = ordered(pieces, halo, by_rank)
    left, right = from_both_sides(low, high, "col")

    whole = whole.reshape(row_devices, column_devices, 2, BLOCK, BLOCK)
    own_lines = lambda x: lax.dynamic_slice_in_dim(x, column_index * BLOCK, BLOCK, 0)
    groups = BLOCK // GROUP
    turned = shear_whole(
        whole,
        halo,
        lax.dynamic_slice_in_dim(base_rows[1, 1], column_index * groups, groups, 0),
        own_lines(spare_rows[1, 1]),
        own_lines(fraction_rows[1, 1]),
        turned_tables,
    )
    turned = lax.all_to_all(turned, "col", split_axis=0, concat_axis=0, tiled=True)

    field_a = shear_tile(
        tile,
        [left],
        [right],
        0,
        line_count,
        halo,
        base_rows[0, 1],
        in_order,
        spare_rows[0, 1],
        fraction_rows[0, 1],
        row_tables,
        wave_a,
    )
    halos = from_both_sides(field_a[:, :, :MARGIN], field_a[:, :, -MARGIN:], "row")
    half_a = travel_first(field_a, halos, (), along_rows[0])
    low, high = from_both_sides(half_a[:1], half_a[-1:], "col")
    exit_a = travel_second(low, half_a, high, along_columns[0])

    turned = after(turned, exit_a)
    half_b = travel_first(turned, (), (wave_b, *wave_b_halos), along_rows[1])
    low, high = from_both_sides(half_b[:1], half_b[-1:], "row")
    exit_b = travel_second(low, half_b, high, along_columns[1])
    return exit_a, exit_b


def swapped(value, axis, bit):
    mask = 2**bit
    pairs = [(source, source ^ mask) for source in range(lax.axis_size(axis))]
    return lax.ppermute(value, axis, pairs)


def padded_2(x, sides, width):
    for axis, dim in sides:
        devices, length = (lax.axis_size(axis), x.shape[dim])
        up = [(i, (i + 1) % devices) for i in range(devices - 1)]
        down = [(j, i) for i, j in up]
        last = lax.slice_in_dim(x, length - width, length, axis=dim)
        first = lax.slice_in_dim(x, 0, width, axis=dim)
        before = lax.ppermute(last, axis, up)
        after = lax.ppermute(first, axis, down)
        x = jnp.concatenate([before, x, after], axis=dim)
    return x


def fourier_tables(block_len, margin):
    window_len = block_len + 2 * margin
    frequency = jnp.arange(window_len, dtype=jnp.int32) - window_len // 2
    position = jnp.arange(window_len, dtype=jnp.int32)
    angles = (
        2.0
        * jnp.pi
        * jnp.mod(position[:, None] * frequency[None, :], window_len).astype(jnp.float32)
        / window_len
    )
    cosine = jnp.cos(angles)
    sines = jnp.sin(angles)
    forward = jnp.concatenate(
        [jnp.concatenate([cosine, -sines], 1), jnp.concatenate([sines, cosine], 1)], 0
    ).astype(jnp.bfloat16)
    target = jnp.arange(block_len, dtype=jnp.int32) + margin
    inverse_angle = (
        2.0
        * jnp.pi
        * jnp.mod(frequency[:, None] * target[None, :], window_len).astype(jnp.float32)
        / window_len
    )
    inverse_cosine = jnp.cos(inverse_angle) / window_len
    inverse_sine = jnp.sin(inverse_angle) / window_len
    inverse = jnp.concatenate(
        [
            jnp.concatenate([inverse_cosine, inverse_sine], 1),
            jnp.concatenate([-inverse_sine, inverse_cosine], 1),
        ],
        0,
    ).astype(jnp.bfloat16)
    return (forward, inverse, frequency.astype(jnp.float32))


def shear_ramp(fractions, frequency):
    window_len = frequency.shape[0]
    phases = -2.0 * jnp.pi / window_len * fractions[:, None] * frequency[None, :]
    nyquist = (jnp.arange(window_len) == 0)[None, :]
    ramp_real = jnp.where(nyquist, jnp.cos(jnp.pi * fractions)[:, None], jnp.cos(phases))
    ramp_imaginary = jnp.where(nyquist, 0.0, jnp.sin(phases))
    return (ramp_real, ramp_imaginary)


def travel_ramp(distance, frequency):
    window_len = frequency.shape[0]
    phases = -2.0 * jnp.pi / (window_len * window_len) * distance * frequency * frequency
    return (jnp.cos(phases)[None, :], jnp.sin(phases)[None, :])


def select_window(padded, starts, out_len):
    total_len = padded.shape[2]
    offset_range = total_len - out_len
    bit_count = max(offset_range, 1).bit_length()
    current = jnp.pad(padded, ((0, 0), (0, 0), (0, out_len + 2**bit_count - 1 - total_len)))
    for bit_number in reversed(range(bit_count)):
        stride = 2**bit_number
        kept_len = current.shape[2] - stride
        chosen = (starts // stride % 2 == 1)[None, :, None]
        current = jnp.where(
            chosen, current[:, :, stride : stride + kept_len], current[:, :, :kept_len]
        )
    return current


def line_pass(padded, extent, shifts, ramp_real, ramp_imaginary, tables):
    forward, inverse = (tables[0], tables[1])
    window_len = BLOCK + 2 * MARGIN
    line_count = padded.shape[1]
    blocks = (padded.shape[2] - 2 * extent) // BLOCK
    reach_len = blocks * BLOCK + 2 * MARGIN
    if shifts is None:
        shifted = padded
    else:
        starts = extent - MARGIN - shifts
        shifted = select_window(padded, starts, reach_len)
    middle = shifted[:, :, MARGIN : MARGIN + blocks * BLOCK].reshape(2, line_count, blocks, BLOCK)
    left_rim = shifted[:, :, : blocks * BLOCK].reshape(2, line_count, blocks, BLOCK)[..., :MARGIN]
    right_rim = shifted[:, :, 2 * MARGIN : 2 * MARGIN + blocks * BLOCK].reshape(
        2, line_count, blocks, BLOCK
    )[..., BLOCK - MARGIN :]
    windows = jnp.concatenate([left_rim, middle, right_rim], 3)
    spectrum = jnp.einsum(
        "cpms,cst->pmt",
        windows,
        forward.reshape(2, window_len, 2 * window_len),
        preferred_element_type=jnp.float32,
    )
    spec_real = spectrum[..., :window_len]
    spec_imaginary = spectrum[..., window_len:]
    factor_real = ramp_real[:, None, :]
    factor_imaginary = ramp_imaginary[:, None, :]
    ramped = jnp.concatenate(
        [
            spec_real * factor_real - spec_imaginary * factor_imaginary,
            spec_real * factor_imaginary + spec_imaginary * factor_real,
        ],
        -1,
    ).astype(jnp.bfloat16)
    result = jnp.einsum(
        "pms,scb->cpmb",
        ramped,
        inverse.reshape(2 * window_len, 2, BLOCK),
        preferred_element_type=jnp.float32,
    )
    return result.reshape(2, line_count, blocks * BLOCK).astype(jnp.bfloat16)


def single_pass(padded, extent, shifts, fractions, tables):
    ramp_real, ramp_imaginary = shear_ramp(fractions, tables[2])
    return line_pass(padded, extent, shifts, ramp_real, ramp_imaginary, tables)


def general_shear_columns(stacked, shifts, fractions, tables):
    halo_depth = SHIFT_X + MARGIN
    inputs = stacked.shape[0]
    column_devices = lax.axis_size("col")
    share = stacked.shape[2] // column_devices
    offset = lax.axis_index("col") * share
    spread = lax.all_to_all(stacked, "col", split_axis=2, concat_axis=3, tiled=True)
    padded = jnp.pad(spread, ((0, 0), (0, 0), (0, 0), (halo_depth, halo_depth)))
    row_shifts = lax.dynamic_slice_in_dim(shifts, offset, share, 1)
    row_fractions = lax.dynamic_slice_in_dim(fractions, offset, share, 1)
    sheared = jnp.stack(
        [
            single_pass(
                padded[min(0, inputs - 1)], halo_depth, row_shifts[0], row_fractions[0], tables
            )
        ]
    )
    return lax.all_to_all(sheared, "col", split_axis=3, concat_axis=2, tiled=True)


def shear_along_first(padded_lines, halo_depth, shifts, fractions, tables):
    flipped = jnp.swapaxes(padded_lines[0], 1, 2)
    moved = single_pass(flipped, halo_depth, shifts[0], fractions[0], tables)
    sheared = [jnp.swapaxes(moved, 1, 2)]
    return jnp.stack(sheared)


def shear_rows_pass(stacked, shifts, fractions, tables):
    halo_depth = SHIFT_Y + MARGIN
    row_devices = lax.axis_size("row")
    share = stacked.shape[3] // row_devices
    offset = lax.axis_index("row") * share
    spread = lax.all_to_all(stacked, "row", split_axis=3, concat_axis=2, tiled=True)
    padded = jnp.pad(spread, ((0, 0), (0, 0), (halo_depth, halo_depth), (0, 0)))
    column_shifts = lax.dynamic_slice_in_dim(shifts, offset, share, 1)
    column_fractions = lax.dynamic_slice_in_dim(fractions, offset, share, 1)
    sheared = shear_along_first(padded, halo_depth, column_shifts, column_fractions, tables)
    return lax.all_to_all(sheared, "row", split_axis=2, concat_axis=3, tiled=True)


def travel_local(extended, distance, tables):
    ramp_real, ramp_imaginary = travel_ramp(distance, tables[2])
    halfway = line_pass(extended, MARGIN, None, ramp_real, ramp_imaginary, tables)
    flipped = jnp.swapaxes(halfway, 1, 2)
    finished = line_pass(flipped, MARGIN, None, ramp_real, ramp_imaginary, tables)
    return jnp.swapaxes(finished, 1, 2)


def transmit(rotated, wave):
    phase_part = rotated[0].astype(jnp.float32)
    absorb_part = rotated[1].astype(jnp.float32)
    amplitude = jnp.exp(-ABSORB * absorb_part)
    through_real = amplitude * jnp.cos(phase_part)
    through_imaginary = amplitude * jnp.sin(phase_part)
    wave_real = wave[0].astype(jnp.float32)
    wave_imaginary = wave[1].astype(jnp.float32)
    return jnp.stack(
        [
            wave_real * through_real - wave_imaginary * through_imaginary,
            wave_real * through_imaginary + wave_imaginary * through_real,
        ]
    ).astype(jnp.bfloat16)


def general_on_device(
    volume_plane,
    wave_a,
    wave_b,
    shift_rows,
    fraction_rows,
    shift_columns,
    fraction_columns,
    travel_distance,
):
    tables = fourier_tables(BLOCK, MARGIN)
    source = volume_plane[None]
    results = []
    for member in range(2):
        stacked = general_shear_columns(
            source,
            shift_rows[member : member + 1, 0],
            fraction_rows[member : member + 1, 0],
            tables,
        )
        stacked = shear_rows_pass(
            stacked,
            shift_columns[member : member + 1],
            fraction_columns[member : member + 1],
            tables,
        )
        stacked = general_shear_columns(
            stacked,
            shift_rows[member : member + 1, 1],
            fraction_rows[member : member + 1, 1],
            tables,
        )
        results.append(stacked[0])
    view_one = results[0]
    view_two = results[1]
    turned = jnp.swapaxes(jnp.flip(view_two, 2), 1, 2)
    for bit_number in range(lax.axis_size("col").bit_length() - 1):
        turned = swapped(turned, "col", bit_number)
    product_a = transmit(view_one, wave_a)
    extended_a = padded_2(product_a, (("row", 1), ("col", 2)), MARGIN)
    exit_a = travel_local(extended_a, travel_distance[0], tables)
    product_b = transmit(turned, wave_b)
    extended_b = padded_2(product_b, (("row", 2), ("col", 1)), MARGIN)
    exit_b = travel_local(extended_b, travel_distance[1], tables)
    return (exit_a, exit_b)


def solution(mesh):
    def either(volume_plane, *rest):
        rows, width = volume_plane.shape[1:]
        fits = (
            rows == BLOCK * lax.axis_size("col")
            and width == BLOCK * lax.axis_size("row")
            and width >= -(-(SHIFT_X + MARGIN) // BLOCK) * BLOCK >= rows
        )
        chosen = on_device if fits else general_on_device
        return chosen(volume_plane, *rest)

    return jax.shard_map(
        either,
        mesh=mesh,
        in_specs=(
            P(None, "row", "col"),
            P(None, "row", "col"),
            P(None, "col", "row"),
            P(None, None, "row"),
            P(None, None, "row"),
            P(None, "col"),
            P(None, "col"),
            P(),
        ),
        out_specs=(P(None, "row", "col"), P(None, "col", "row")),
        check_vma=False,
    )
```

```python
import functools

import jax
import jax.numpy as jnp
import numpy as np
from jax import lax
from jax.experimental import pallas as pl
from jax.experimental.pallas import tpu as pltpu
from jax.sharding import PartitionSpec as P

BLOCK = 128
MARGIN = 32
SHIFT_X = 864
SHIFT_Y = 1728


ABSORB = 0.25

WINDOW = BLOCK + 2 * MARGIN
BINS = WINDOW // 2
GROUP = 16
PARTS = 2
ROWS = 256
STEPS = 2
VMEM_LIMIT = 56 * 1024 * 1024


def angle_table(rows, columns):
    return 2.0 * np.pi * (np.outer(rows, columns) % WINDOW) / WINDOW


def real_tables():
    position = np.arange(WINDOW)
    bins = np.arange(BINS + 1)
    target = np.arange(BLOCK) + MARGIN
    forward = np.zeros((2 * BLOCK, 2 * BLOCK), np.float32)
    forward[:WINDOW, : BINS + 1] = np.cos(angle_table(position, bins))
    forward[:WINDOW, BLOCK + 1 : BLOCK + BINS] = -np.sin(angle_table(position, bins[1:BINS]))
    weight = np.where((bins == 0) | (bins == BINS), 1.0, 2.0) / WINDOW
    inverse = np.zeros((2 * BLOCK, BLOCK), np.float32)
    inverse[: BINS + 1] = np.cos(angle_table(bins, target)) * weight[:, None]
    inverse[BLOCK + 1 : BLOCK + BINS] = (
        -np.sin(angle_table(bins[1:BINS], target)) * weight[1:BINS, None]
    )
    return forward, inverse


def travel_matrices(distance, forward, inverse):
    frequency = jnp.arange(BLOCK, dtype=jnp.float32)
    phases = -2.0 * jnp.pi / (WINDOW * WINDOW) * distance[:, None] * frequency * frequency
    ramps = jnp.stack([jnp.cos(phases), jnp.sin(phases)], 1)
    ramps = jnp.concatenate([ramps, ramps], 2)
    scaled = ramps[..., None] * jnp.asarray(inverse)
    matrices = jnp.einsum(
        "pq,vrqu->vrpu",
        jnp.asarray(forward[:WINDOW]),
        scaled,
        precision=lax.Precision.HIGHEST,
    )
    return matrices


def lane_iota(rows):
    return lax.broadcasted_iota(jnp.int32, (rows, BLOCK), 1)


def shift_lines(strip, shifted, base, base_offset, spare, windows, chunk_offset, rows):
    def one_group(group, carry):
        first = pl.multiple_of(group * GROUP, GROUP)
        lines = pl.ds(first, GROUP)
        start = base[base_offset + group] + chunk_offset
        offset = spare[lines, :]
        later = offset >= BLOCK
        lane = lane_iota(GROUP) + (offset & (BLOCK - 1))
        wraps = lane >= BLOCK
        index = lane & (BLOCK - 1)
        for part in range(2):
            here = strip[start, part, lines, :].astype(jnp.float32)
            before = None
            for i in range(windows + 2):
                following = strip[start + i + 1, part, lines, :].astype(jnp.float32)
                turned = jnp.take_along_axis(jnp.where(later, following, here), index, axis=1)
                if before is not None:
                    shifted[i - 1, part, lines, :] = jnp.where(wraps, turned, before).astype(
                        jnp.bfloat16
                    )
                before = turned
                here = following
        return carry

    lax.fori_loop(0, rows // GROUP, one_group, 0, unroll=4)


def ramped_lines(shifted, windows, rows, cosine, sine, forward):
    count = len(windows)
    lower = jnp.concatenate([shifted[m].reshape(2 * rows, BLOCK) for m in windows], 0)
    upper = jnp.concatenate([shifted[m + 1].reshape(2 * rows, BLOCK) for m in windows], 0)
    spectrum = jnp.dot(
        jnp.concatenate([lower, upper], 1), forward[...], preferred_element_type=jnp.float32
    )
    real = spectrum[:, :BLOCK].reshape(count * 2, rows, BLOCK)
    imaginary = spectrum[:, BLOCK:].reshape(count * 2, rows, BLOCK)
    ramp_real = cosine[...][None]
    ramp_imaginary = sine[...][None]
    ramped = jnp.concatenate(
        [
            (real * ramp_real - imaginary * ramp_imaginary).astype(jnp.bfloat16),
            (real * ramp_imaginary + imaginary * ramp_real).astype(jnp.bfloat16),
        ],
        2,
    )
    return ramped.reshape(count * 2 * rows, 2 * BLOCK)


def down_lines(vector):
    return jnp.broadcast_to(vector, (BLOCK, vector.shape[1])).T


def line_ramps(fractions, cosine, sine):
    bins = lane_iota(fractions.shape[1]).astype(jnp.float32)
    sine[...], cosine[...] = sine_cosine(down_lines(fractions) * bins * (-2.0 * np.pi / WINDOW))


def shear_tile_kernel(halo, tiles, rows, batch, wide, parts, sent, base, rank, *refs):
    lefts, rights, refs = refs[:parts], refs[parts : 2 * parts], refs[2 * parts :]
    waves, refs = refs[: int(sent)], refs[int(sent) :]
    own, offsets, fractions, forward, inverse, out = refs[:6]
    strip, shifted, spare, cosine, sine = refs[6:]
    step = pl.program_id(0)
    groups = rows // GROUP
    end = halo + tiles + halo

    @pl.when(step == 0)
    def _():
        strip[end : end + 2] = jnp.zeros((2, 2, rows, BLOCK), jnp.bfloat16)

    def fill(piece, first, count):
        for i in range(count):
            if wide:
                strip[first + i] = piece[:, :, i * BLOCK : (i + 1) * BLOCK]
            else:
                strip[first + i] = piece[i]

    share = pl.num_programs(0) // parts
    for part in range(parts):

        @pl.when(step // share == part)
        def _():
            fill(lefts[part], 0, halo)
            fill(rights[part], halo + tiles, halo)

    fill(own, halo, tiles)
    spare[...] = down_lines(offsets[0]).astype(jnp.int32)
    line_ramps(fractions[0], cosine, sine)
    shift_lines(strip, shifted, base, step * groups, spare, tiles, 0, rows)
    for first in range(0, tiles, batch):
        windows = [slot if sent else slot ^ rank[0] for slot in range(first, first + batch)]
        ramped = ramped_lines(shifted, windows, rows, cosine, sine, forward)
        result = jnp.dot(ramped, inverse[...], preferred_element_type=jnp.float32)
        result = result.astype(jnp.bfloat16).reshape(batch, 2, rows, BLOCK)
        if sent:
            for i, window in enumerate(windows):
                wave = waves[0][:, :, window * BLOCK : (window + 1) * BLOCK]
                for part, value in enumerate(transmitted(result[i], wave)):
                    out[window, part] = value
        else:
            out[first : first + batch] = result


def shear_tile(own, lefts, rights, first, lines, halo, base, rank, spare, fractions, tables, *waves):
    wide = own.ndim == 3
    parts = len(lefts)
    line_count = lines
    part_lines = line_count // parts
    tiles = own.shape[2] // BLOCK if wide else own.shape[0]
    rows = min(part_lines, ROWS)
    share = part_lines // rows
    offset = first // rows
    forward, inverse = tables

    def piece_spec(piece, place):
        if wide:
            return pl.BlockSpec((2, rows, piece.shape[2]), lambda i, *_: (0, place(i), 0))
        return pl.BlockSpec((piece.shape[0], 2, rows, BLOCK), lambda i, *_: (0, 0, place(i), 0))

    halo_specs = [
        piece_spec(x, lambda i, part=part: jnp.clip(i - part * share, 0, share - 1))
        for x in (lefts[0], rights[0])
        for part in range(parts)
    ]
    line_spec = pl.BlockSpec((1, 1, rows), lambda i, *_: (i + offset, 0, 0))
    along = lambda x: x.astype(jnp.float32).reshape(-1, 1, rows)
    out_shape = jax.ShapeDtypeStruct((tiles, 2, line_count, BLOCK), jnp.bfloat16)
    out_spec = pl.BlockSpec((tiles, 2, rows, BLOCK), lambda i, *_: (0, 0, i, 0))
    groups = rows // GROUP
    kernel = functools.partial(
        shear_tile_kernel,
        halo,
        tiles,
        rows,
        tiles // 4 if tiles % 4 == 0 else tiles,
        wide,
        parts,
        len(waves) > 0,
    )
    return pl.pallas_call(
        kernel,
        grid_spec=pltpu.PrefetchScalarGridSpec(
            num_scalar_prefetch=2,
            grid=(line_count // rows,),
            in_specs=halo_specs
            + [pl.BlockSpec((2, rows, x.shape[2]), lambda i, *_: (0, i + offset, 0)) for x in waves]
            + [piece_spec(own, lambda i: i + offset)]
            + [line_spec] * 2
            + [
                pl.BlockSpec(forward.shape, lambda i, *_: (0, 0)),
                pl.BlockSpec(inverse.shape, lambda i, *_: (0, 0)),
            ],
            out_specs=out_spec,
            scratch_shapes=[
                pltpu.VMEM((halo + tiles + halo + 2, 2, rows, BLOCK), jnp.bfloat16),
                pltpu.VMEM((tiles + 1, 2, rows, BLOCK), jnp.bfloat16),
                pltpu.VMEM((rows, BLOCK), jnp.int32),
                pltpu.VMEM((rows, BLOCK), jnp.float32),
                pltpu.VMEM((rows, BLOCK), jnp.float32),
            ],
        ),
        out_shape=out_shape,
        compiler_params=pltpu.CompilerParams(vmem_limit_bytes=VMEM_LIMIT),
        name="shear_tile",
    )(
        lax.slice_in_dim(base, offset * groups, offset * groups + line_count // GROUP),
        rank,
        *lefts,
        *rights,
        *waves,
        own,
        along(spare),
        along(fractions),
        forward,
        inverse,
    )


def shear_whole_kernel(
    halo,
    devices,
    tiles,
    rows,
    base,
    own,
    offsets,
    fractions,
    forward,
    flipped,
    out,
    strip,
    shifted,
    spare,
    cosine,
    sine,
):
    step = pl.program_id(0)
    chunks = devices * tiles
    length = tiles * BLOCK

    @pl.when(step == 0)
    def _():
        strip[0:halo] = jnp.zeros((halo, 2, rows, BLOCK), jnp.bfloat16)
        strip[halo + chunks :] = jnp.zeros((halo + 2, 2, rows, BLOCK), jnp.bfloat16)
        for chunk in range(chunks):
            strip[halo + chunk] = own[chunk % tiles, chunk // tiles]
        out[0, :, 0:MARGIN, :] = jnp.zeros((2, MARGIN, rows), jnp.bfloat16)
        out[devices - 1, :, MARGIN + length :, :] = jnp.zeros((2, MARGIN, rows), jnp.bfloat16)
        spare[...] = down_lines(offsets[...]).astype(jnp.int32)
        line_ramps(fractions[...], cosine, sine)

    shift_lines(strip, shifted, base, 0, spare, tiles, step * tiles, rows)
    ramped = ramped_lines(shifted, range(tiles), rows, cosine, sine, forward)
    target = devices - 1 - step
    result = lax.dot_general(
        flipped[...], ramped, (((1,), (1,)), ((), ())), preferred_element_type=jnp.float32
    ).astype(jnp.bfloat16)
    for window in range(tiles):
        block = tiles - 1 - window
        low = MARGIN + block * BLOCK
        for part in range(2):
            lanes = (2 * window + part) * rows
            piece = result[:, lanes : lanes + rows]
            out[target, part, low : low + BLOCK, :] = piece
            if block == 0:

                @pl.when(target > 0)
                def _():
                    out[target - 1, part, MARGIN + length :, :] = piece[:MARGIN]

            if block == tiles - 1:

                @pl.when(target < devices - 1)
                def _():
                    out[target + 1, part, 0:MARGIN, :] = piece[BLOCK - MARGIN :]


def shear_whole(own, halo, base, spare, fractions, tables):
    tiles, devices, _, rows, _ = own.shape
    forward, flipped = tables
    operands = (
        own,
        spare.astype(jnp.float32).reshape(1, rows),
        fractions.reshape(1, rows),
        forward,
        flipped,
    )
    full = lambda shape: pl.BlockSpec(shape, lambda i, *_: (0,) * len(shape))
    out = (devices, 2, tiles * BLOCK + 2 * MARGIN, rows)
    return pl.pallas_call(
        functools.partial(shear_whole_kernel, halo, devices, tiles, rows),
        grid_spec=pltpu.PrefetchScalarGridSpec(
            num_scalar_prefetch=1,
            grid=(devices,),
            in_specs=[full(x.shape) for x in operands],
            out_specs=full(out),
            scratch_shapes=[
                pltpu.VMEM((2 * halo + devices * tiles + 2, 2, rows, BLOCK), jnp.bfloat16),
                pltpu.VMEM((tiles + 1, 2, rows, BLOCK), jnp.bfloat16),
                pltpu.VMEM((rows, BLOCK), jnp.int32),
                pltpu.VMEM((rows, BLOCK), jnp.float32),
                pltpu.VMEM((rows, BLOCK), jnp.float32),
            ],
        ),
        out_shape=jax.ShapeDtypeStruct(out, jnp.bfloat16),
        compiler_params=pltpu.CompilerParams(vmem_limit_bytes=VMEM_LIMIT),
        name="shear_whole",
    )(base, *operands)


def shear_columns_kernel(front, blocks, length, rows_out, place, base, rank, *refs):
    owns, refs = refs[: len(place)], refs[len(place) :]
    offsets, fractions, forward, inverse, out, strip, shifted, cosine, sine = refs
    step = pl.program_id(0)
    per_step = length // BLOCK
    per_grid = blocks // pl.num_programs(0)
    total = strip.shape[1]

    @pl.when(step == 0)
    def _():
        strip[:, 0:front, :] = jnp.zeros((2, front, BLOCK), jnp.bfloat16)
        back = front + blocks * length
        strip[:, back:, :] = jnp.zeros((2, total - back, BLOCK), jnp.bfloat16)
        for own, slots in zip(owns, place):
            count = own.shape[2]
            for i, (slot, within) in enumerate(slots):
                first = pl.multiple_of(front + (slot ^ rank[0]) * length + within, GROUP)
                for part in range(2):
                    strip[part, pl.ds(first, count), :] = own[i, part]
        bins = lax.broadcasted_iota(jnp.int32, (BLOCK, BLOCK), 0).astype(jnp.float32)
        sine[...], cosine[...] = sine_cosine(bins * fractions[...] * (-2.0 * np.pi / WINDOW))

    offset = jnp.broadcast_to(offsets[...], (8, BLOCK))
    row = lax.broadcasted_iota(jnp.int32, (8, BLOCK), 0) + (offset & 7)
    wraps = row >= 8
    index = row & 7

    def one_chunk(block_rows, chunk):
        begin = pl.multiple_of(base[0] + block_rows + chunk * BLOCK, GROUP)
        for part in range(2):
            value = strip[part, pl.ds(begin, 2 * BLOCK), :].astype(jnp.float32)
            value = value.reshape(2 * BLOCK // 8, 8, BLOCK)
            for bit in (64, 32, 16, 8):
                taken = ((offset & bit) != 0)[None]
                value = jnp.where(taken, value[bit // 8 :], value[: -(bit // 8)])
            pieces = [
                jnp.take_along_axis(value[i], index, axis=0) for i in range(BLOCK // 8 + 1)
            ]
            moved = [
                jnp.where(wraps, pieces[i + 1], pieces[i]) for i in range(BLOCK // 8)
            ]
            shifted[chunk * BLOCK : (chunk + 1) * BLOCK, part * BLOCK : (part + 1) * BLOCK] = (
                jnp.concatenate(moved, 0).astype(jnp.bfloat16)
            )

    def one_block(local, carry):
        block_rows = ((step * per_grid + local) ^ rank[0]) * length
        for chunk in range(per_step + 1):
            one_chunk(block_rows, chunk)
        windows = [shifted[m * BLOCK : (m + 2) * BLOCK, :] for m in range(per_step)]
        spectrum = jnp.dot(
            forward[...], jnp.concatenate(windows, 1), preferred_element_type=jnp.float32
        )
        ramp_real = jnp.concatenate([cosine[...]] * (2 * per_step), 1)
        ramp_imaginary = jnp.concatenate([sine[...]] * (2 * per_step), 1)
        real, imaginary = spectrum[:BLOCK], spectrum[BLOCK:]
        ramped = jnp.concatenate(
            [
                (real * ramp_real - imaginary * ramp_imaginary).astype(jnp.bfloat16),
                (real * ramp_imaginary + imaginary * ramp_real).astype(jnp.bfloat16),
            ],
            0,
        )
        result = jnp.dot(inverse[...], ramped, preferred_element_type=jnp.float32)
        result = result.astype(jnp.bfloat16)
        for window in range(per_step):
            piece, within = window * BLOCK // rows_out, window * BLOCK % rows_out
            for part in range(2):
                lanes = (2 * window + part) * BLOCK
                out[local * (length // rows_out) + piece, part, within : within + BLOCK, :] = (
                    result[:, lanes : lanes + BLOCK]
                )
        return carry

    lax.fori_loop(0, per_grid, one_block, 0)


def shear_columns(owns, place, blocks, front, back, base, rank, spare, fractions, tables, rows_out):
    length = sum(own.shape[0] * own.shape[2] for own in owns) // blocks
    forward, inverse = tables
    operands = (
        *owns,
        spare.astype(jnp.int32).reshape(1, BLOCK),
        fractions.reshape(1, BLOCK),
        forward,
        inverse,
    )
    full = lambda shape: pl.BlockSpec(shape, lambda i, *_: (0,) * len(shape))
    pieces = blocks * length // rows_out
    steps = STEPS if blocks % STEPS == 0 else 1
    return pl.pallas_call(
        functools.partial(shear_columns_kernel, front, blocks, length, rows_out, place),
        grid_spec=pltpu.PrefetchScalarGridSpec(
            num_scalar_prefetch=2,
            grid=(steps,),
            in_specs=[full(x.shape) for x in operands],
            out_specs=pl.BlockSpec(
                (pieces // steps, 2, rows_out, BLOCK), lambda i, *_: (i, 0, 0, 0)
            ),
            scratch_shapes=[
                pltpu.VMEM((2, front + blocks * length + back, BLOCK), jnp.bfloat16),
                pltpu.VMEM((length + BLOCK, 2 * BLOCK), jnp.bfloat16),
                pltpu.VMEM((BLOCK, BLOCK), jnp.float32),
                pltpu.VMEM((BLOCK, BLOCK), jnp.float32),
            ],
        ),
        out_shape=jax.ShapeDtypeStruct((pieces, 2, rows_out, BLOCK), jnp.bfloat16),
        compiler_params=pltpu.CompilerParams(vmem_limit_bytes=VMEM_LIMIT),
        name="shear_columns",
    )(base, rank, *operands)


def sine_cosine(angle):
    turns = jnp.round(angle * (2.0 / np.pi))
    rest = angle - turns * 1.5703125
    rest = rest - turns * 4.837512969970703125e-4
    rest = rest - turns * 7.549789954891882e-8
    square = rest * rest
    sine = rest + rest * square * (
        -1.6666654611e-1 + square * (8.3321608736e-3 - square * 1.9515295891e-4)
    )
    cosine = (
        1.0
        - 0.5 * square
        + square
        * square
        * (4.166664568298827e-2 + square * (-1.388731625493765e-3 + square * 2.443315711809948e-5))
    )
    quadrant = turns.astype(jnp.int32)
    odd = (quadrant & 1) != 0
    sine_out = jnp.where(odd, cosine, sine)
    cosine_out = jnp.where(odd, sine, cosine)
    sine_out = jnp.where((quadrant & 2) != 0, -sine_out, sine_out)
    cosine_out = jnp.where(((quadrant + 1) & 2) != 0, -cosine_out, cosine_out)
    return sine_out, cosine_out


def transmitted(rotated, wave):
    sine, cosine = sine_cosine(rotated[0].astype(jnp.float32))
    amplitude = jnp.exp(-ABSORB * rotated[1].astype(jnp.float32))
    through_real = amplitude * cosine
    through_imaginary = amplitude * sine
    wave_real = wave[0].astype(jnp.float32)
    wave_imaginary = wave[1].astype(jnp.float32)
    return (
        (wave_real * through_real - wave_imaginary * through_imaginary).astype(jnp.bfloat16),
        (wave_real * through_imaginary + wave_imaginary * through_real).astype(jnp.bfloat16),
    )


def travel_first_kernel(length, count, sent, *refs):
    if sent:
        body, top, bottom, matrix, out, field = refs
        for chunk in range(count):
            across = slice(chunk * BLOCK, (chunk + 1) * BLOCK)
            for part in range(2):
                field[part, 0:MARGIN, across] = top[chunk, part]
                field[part, MARGIN : MARGIN + length, across] = body[chunk, part]
                field[part, MARGIN + length :, across] = bottom[chunk, part]
    else:
        body, wave, wave_top, wave_bottom, matrix, out, field = refs
        pieces = [(0, MARGIN, wave_top, 0)]
        pieces += [(MARGIN + first, BLOCK, wave, first) for first in range(0, length, BLOCK)]
        pieces += [(MARGIN + length, MARGIN, wave_bottom, 0)]
        for chunk in range(count):
            across = slice(chunk * BLOCK, (chunk + 1) * BLOCK)
            for place, height, waves, first in pieces:
                parts = transmitted(
                    [body[chunk, p, place : place + height, :] for p in range(2)],
                    [waves[p, first : first + height, across] for p in range(2)],
                )
                for part in range(2):
                    field[part, place : place + height, across] = parts[part]
    for m in range(0, length, BLOCK):
        window = jnp.concatenate([field[0, m : m + WINDOW, :], field[1, m : m + WINDOW, :]], 0)
        result = jnp.dot(matrix[...], window, preferred_element_type=jnp.float32)
        result = result.astype(jnp.bfloat16)
        for chunk in range(count):
            across = slice(chunk * BLOCK, (chunk + 1) * BLOCK)
            for part in range(2):
                out[chunk, part, m : m + BLOCK, :] = result[
                    part * BLOCK : (part + 1) * BLOCK, across
                ]


def travel_first(body, halos, waves, matrix):
    chunks = body.shape[0]
    count = chunks // STEPS if chunks % STEPS == 0 else chunks
    length = body.shape[2] if len(halos) > 0 else body.shape[2] - 2 * MARGIN
    chunk_spec = lambda x: pl.BlockSpec((count, 2, x.shape[2], BLOCK), lambda i: (i, 0, 0, 0))
    wide_spec = lambda x: pl.BlockSpec((2, x.shape[1], count * BLOCK), lambda i: (0, 0, i))
    return pl.pallas_call(
        functools.partial(travel_first_kernel, length, count, len(halos) > 0),
        grid=(chunks // count,),
        in_specs=[chunk_spec(x) for x in (body, *halos)]
        + [wide_spec(x) for x in waves]
        + [pl.BlockSpec(matrix.shape, lambda i: (0, 0))],
        out_specs=pl.BlockSpec((count, 2, length, BLOCK), lambda i: (i, 0, 0, 0)),
        out_shape=jax.ShapeDtypeStruct((chunks, 2, length, BLOCK), jnp.bfloat16),
        scratch_shapes=[pltpu.VMEM((2, length + 2 * MARGIN, count * BLOCK), jnp.bfloat16)],
        compiler_params=pltpu.CompilerParams(vmem_limit_bytes=VMEM_LIMIT),
        name="travel_first",
    )(body, *halos, *waves, matrix)


def travel_second_kernel(chunks, rows, left, body, right, matrix, out):
    parts = [[left[0, p]] + [body[m, p] for m in range(chunks)] + [right[0, p]] for p in range(2)]
    windows = [
        jnp.concatenate(parts[0][m : m + 3] + parts[1][m : m + 3], 1) for m in range(chunks)
    ]
    result = jnp.dot(
        jnp.concatenate(windows, 0), matrix[...], preferred_element_type=jnp.float32
    ).astype(jnp.bfloat16)
    for m in range(chunks):
        for part in range(2):
            out[part, :, m * BLOCK : (m + 1) * BLOCK] = result[
                m * rows : (m + 1) * rows, part * BLOCK : (part + 1) * BLOCK
            ]


def travel_second(left, body, right, matrix):
    chunks, _, length, _ = body.shape
    rows = length // STEPS if length % (STEPS * BLOCK) == 0 else length
    edge = pl.BlockSpec((1, 2, rows, BLOCK), lambda i: (0, 0, i, 0))
    return pl.pallas_call(
        functools.partial(travel_second_kernel, chunks, rows),
        grid=(length // rows,),
        in_specs=[
            edge,
            pl.BlockSpec((chunks, 2, rows, BLOCK), lambda i: (0, 0, i, 0)),
            edge,
            pl.BlockSpec(matrix.shape, lambda i: (0, 0)),
        ],
        out_specs=pl.BlockSpec((2, rows, chunks * BLOCK), lambda i: (0, i, 0)),
        out_shape=jax.ShapeDtypeStruct((2, length, chunks * BLOCK), jnp.bfloat16),
        compiler_params=pltpu.CompilerParams(vmem_limit_bytes=VMEM_LIMIT),
        name="travel_second",
    )(left, body, right, matrix)


def from_both_sides(first, last, axis):
    devices = lax.axis_size(axis)
    up = [(i, i + 1) for i in range(devices - 1)]
    down = [(j, i) for i, j in up]
    return lax.ppermute(last, axis, up), lax.ppermute(first, axis, down)


def after(value, *others):
    return lax.optimization_barrier((value, others))[0]


def ordered_kernel(halo, rank, *refs):
    pieces, (out, first, last) = refs[:-3], refs[-3:]
    count = len(pieces)
    for s, piece in enumerate(pieces):
        place = s ^ rank[0]
        out[place] = piece[0]

        @pl.when(place < halo)
        def _():
            first[place] = piece[0]

        @pl.when(place >= count - halo)
        def _():
            last[place - (count - halo)] = piece[0]


def ordered(pieces, halo, rank):
    count = len(pieces)
    block = pieces[0].shape
    shapes = [(n, *block[1:]) for n in (count, halo, halo)]
    full = lambda shape: pl.BlockSpec(shape, lambda i, *_: (0,) * len(shape))
    return pl.pallas_call(
        functools.partial(ordered_kernel, halo),
        grid_spec=pltpu.PrefetchScalarGridSpec(
            num_scalar_prefetch=1,
            grid=(1,),
            in_specs=[full(block)] * count,
            out_specs=[full(shape) for shape in shapes],
        ),
        out_shape=[jax.ShapeDtypeStruct(shape, pieces[0].dtype) for shape in shapes],
        compiler_params=pltpu.CompilerParams(vmem_limit_bytes=VMEM_LIMIT),
        name="ordered",
    )(rank, *pieces)


def swapped_shares(slots):
    devices = lax.axis_size("row")
    return [slots[0]] + [
        lax.ppermute(slots[s], "row", [(i, i ^ s) for i in range(devices)])
        for s in range(1, devices)
    ]


def group_starts(starts, group, unit):
    lines = starts.shape[-1]
    grouped = starts.reshape(*starts.shape[:-1], lines // group, group)
    base = jnp.min(grouped, -1) // unit
    spare = grouped - base[..., None] * unit
    return base.astype(jnp.int32), spare.reshape(starts.shape)


def on_device(
    volume_plane,
    wave_a,
    wave_b,
    shift_rows,
    fraction_rows,
    shift_columns,
    fraction_columns,
    travel_distance,
):
    _, line_count, width = volume_plane.shape
    row_devices, column_devices = lax.axis_size("row"), lax.axis_size("col")
    row_index, column_index = lax.axis_index("row"), lax.axis_index("col")
    tiles = width // BLOCK
    halo = -(-(SHIFT_X + MARGIN) // BLOCK)
    reach = halo * BLOCK

    forward, inverse = real_tables()
    half = lambda x: jnp.asarray(x, jnp.bfloat16)
    row_tables = (half(forward), half(inverse))
    column_tables = (half(forward.T), half(inverse.T))
    turned_tables = (half(forward), half(inverse[:, ::-1].T))
    in_order = jnp.zeros((1,), jnp.int32)
    by_rank = row_index.astype(jnp.int32).reshape(1)

    part_lines = line_count // PARTS
    lefts, rights, edges = [], [], ()
    for part in range(PARTS):
        lines = after(volume_plane, edges)[:, part * part_lines : (part + 1) * part_lines]
        edges = (lines[:, :, :reach], lines[:, :, width - reach :])
        if part == PARTS - 1:
            fill = ((0, 0), (0, 0), (0, reach - line_count))
            margins = (wave_b[:, :MARGIN], wave_b[:, -MARGIN:])
            edges = [
                jnp.concatenate([edge, jnp.pad(margin, fill)], 1)
                for edge, margin in zip(edges, margins)
            ]
        left, right = from_both_sides(*edges, "col")
        lefts.append(left)
        rights.append(right)
    wave_b_halos = [x[-1][:, part_lines:, :line_count] for x in (lefts, rights)]

    base_rows, spare_rows = group_starts(reach - MARGIN - shift_rows, GROUP, BLOCK)

    front = -(-(SHIFT_Y + MARGIN) // GROUP) * GROUP
    back = front + 3 * BLOCK
    mine = lambda x: lax.dynamic_slice_in_dim(x, row_index * BLOCK, BLOCK, 1)
    base_columns, spare_columns = group_starts(front - MARGIN - mine(shift_columns), BLOCK, GROUP)
    column_fractions = mine(fraction_columns)

    def first(view, begin, lefts, rights, rank):
        return shear_tile(
            volume_plane,
            lefts,
            rights,
            begin,
            len(lefts) * part_lines,
            halo,
            base_rows[view, 0],
            rank,
            spare_rows[view, 0],
            fraction_rows[view, 0],
            row_tables,
        )

    def second(view, pieces, place, rank, rows_out):
        return shear_columns(
            pieces,
            place,
            row_devices,
            front,
            back,
            base_columns[view] * GROUP,
            rank,
            spare_columns[view],
            column_fractions[view],
            column_tables,
            rows_out,
        )

    matrices = travel_matrices(travel_distance, forward, inverse)
    real, imaginary = matrices[:, 0], matrices[:, 1]
    along_rows = jnp.concatenate(
        [
            jnp.concatenate([real, -imaginary], 1),
            jnp.concatenate([imaginary, real], 1),
        ],
        2,
    )
    along_rows = jnp.swapaxes(along_rows, 1, 2).astype(jnp.bfloat16)
    spaced = jnp.pad(matrices, ((0, 0), (0, 0), (BLOCK - MARGIN, BLOCK - MARGIN), (0, 0)))
    real, imaginary = spaced[:, 0], spaced[:, 1]
    along_columns = jnp.concatenate(
        [
            jnp.concatenate([real, -imaginary], 1),
            jnp.concatenate([imaginary, real], 1),
        ],
        2,
    ).astype(jnp.bfloat16)

    spread, sheared = [], ()
    for part in range(PARTS):
        left, right = after((lefts[part], rights[part]), sheared)
        sheared = first(1, part * part_lines, [left], [right], in_order)
        spread.append(lax.all_to_all(sheared, "row", split_axis=0, concat_axis=0, tiled=True))
    lefts, rights = after((lefts, rights), sheared)
    slots = first(0, 0, lefts, rights, by_rank)
    shares = [slots[s : s + 1] for s in range(row_devices)]
    spread = after(spread, shares)
    pieces = swapped_shares(shares)

    place = [[(b, part * part_lines) for b in range(row_devices)] for part in range(PARTS)]
    moved_b = second(1, spread, place, in_order, BLOCK)
    whole = lax.all_to_all(moved_b, ("row", "col"), split_axis=0, concat_axis=0, tiled=True)
    whole = after(whole, pieces)
    whole = whole.reshape(row_devices, column_devices, 2, BLOCK, BLOCK)
    own_lines = lambda x: lax.dynamic_slice_in_dim(x, column_index * BLOCK, BLOCK, 0)
    groups = BLOCK // GROUP
    turned = shear_whole(
        whole,
        halo,
        lax.dynamic_slice_in_dim(base_rows[1, 1], column_index * groups, groups, 0),
        own_lines(spare_rows[1, 1]),
        own_lines(fraction_rows[1, 1]),
        turned_tables,
    )

    sent = lax.all_to_all(turned, "col", split_axis=0, concat_axis=0, tiled=True)

    pieces = after(pieces, turned)
    moved_a = second(0, pieces, [[(s, 0)] for s in range(row_devices)], by_rank, line_count)
    pieces = swapped_shares([moved_a[s : s + 1] for s in range(row_devices)])
    tile, low, high = ordered(pieces, halo, by_rank)
    left, right = from_both_sides(low, high, "col")

    half_b = travel_first(sent, (), (wave_b, *wave_b_halos), along_rows[1])
    low, high = from_both_sides(half_b[:1], half_b[-1:], "row")
    exit_b = travel_second(low, half_b, high, along_columns[1])

    left, right = after((left, right), exit_b)
    field_a = shear_tile(
        tile,
        [left],
        [right],
        0,
        line_count,
        halo,
        base_rows[0, 1],
        in_order,
        spare_rows[0, 1],
        fraction_rows[0, 1],
        row_tables,
        wave_a,
    )
    halos = from_both_sides(field_a[:, :, :MARGIN], field_a[:, :, -MARGIN:], "row")
    half_a = travel_first(field_a, halos, (), along_rows[0])
    low, high = from_both_sides(half_a[:1], half_a[-1:], "col")
    exit_a = travel_second(low, half_a, high, along_columns[0])
    return exit_a, exit_b


def swapped(value, axis, bit):
    mask = 2**bit
    pairs = [(source, source ^ mask) for source in range(lax.axis_size(axis))]
    return lax.ppermute(value, axis, pairs)


def padded_2(x, sides, width):
    for axis, dim in sides:
        devices, length = (lax.axis_size(axis), x.shape[dim])
        up = [(i, (i + 1) % devices) for i in range(devices - 1)]
        down = [(j, i) for i, j in up]
        last = lax.slice_in_dim(x, length - width, length, axis=dim)
        first = lax.slice_in_dim(x, 0, width, axis=dim)
        before = lax.ppermute(last, axis, up)
        after = lax.ppermute(first, axis, down)
        x = jnp.concatenate([before, x, after], axis=dim)
    return x


def fourier_tables(block_len, margin):
    window_len = block_len + 2 * margin
    frequency = jnp.arange(window_len, dtype=jnp.int32) - window_len // 2
    position = jnp.arange(window_len, dtype=jnp.int32)
    angles = (
        2.0
        * jnp.pi
        * jnp.mod(position[:, None] * frequency[None, :], window_len).astype(jnp.float32)
        / window_len
    )
    cosine = jnp.cos(angles)
    sines = jnp.sin(angles)
    forward = jnp.concatenate(
        [jnp.concatenate([cosine, -sines], 1), jnp.concatenate([sines, cosine], 1)], 0
    ).astype(jnp.bfloat16)
    target = jnp.arange(block_len, dtype=jnp.int32) + margin
    inverse_angle = (
        2.0
        * jnp.pi
        * jnp.mod(frequency[:, None] * target[None, :], window_len).astype(jnp.float32)
        / window_len
    )
    inverse_cosine = jnp.cos(inverse_angle) / window_len
    inverse_sine = jnp.sin(inverse_angle) / window_len
    inverse = jnp.concatenate(
        [
            jnp.concatenate([inverse_cosine, inverse_sine], 1),
            jnp.concatenate([-inverse_sine, inverse_cosine], 1),
        ],
        0,
    ).astype(jnp.bfloat16)
    return (forward, inverse, frequency.astype(jnp.float32))


def shear_ramp(fractions, frequency):
    window_len = frequency.shape[0]
    phases = -2.0 * jnp.pi / window_len * fractions[:, None] * frequency[None, :]
    nyquist = (jnp.arange(window_len) == 0)[None, :]
    ramp_real = jnp.where(nyquist, jnp.cos(jnp.pi * fractions)[:, None], jnp.cos(phases))
    ramp_imaginary = jnp.where(nyquist, 0.0, jnp.sin(phases))
    return (ramp_real, ramp_imaginary)


def travel_ramp(distance, frequency):
    window_len = frequency.shape[0]
    phases = -2.0 * jnp.pi / (window_len * window_len) * distance * frequency * frequency
    return (jnp.cos(phases)[None, :], jnp.sin(phases)[None, :])


def select_window(padded, starts, out_len):
    total_len = padded.shape[2]
    offset_range = total_len - out_len
    bit_count = max(offset_range, 1).bit_length()
    current = jnp.pad(padded, ((0, 0), (0, 0), (0, out_len + 2**bit_count - 1 - total_len)))
    for bit_number in reversed(range(bit_count)):
        stride = 2**bit_number
        kept_len = current.shape[2] - stride
        chosen = (starts // stride % 2 == 1)[None, :, None]
        current = jnp.where(
            chosen, current[:, :, stride : stride + kept_len], current[:, :, :kept_len]
        )
    return current


def line_pass(padded, extent, shifts, ramp_real, ramp_imaginary, tables):
    forward, inverse = (tables[0], tables[1])
    window_len = BLOCK + 2 * MARGIN
    line_count = padded.shape[1]
    blocks = (padded.shape[2] - 2 * extent) // BLOCK
    reach_len = blocks * BLOCK + 2 * MARGIN
    if shifts is None:
        shifted = padded
    else:
        starts = extent - MARGIN - shifts
        shifted = select_window(padded, starts, reach_len)
    middle = shifted[:, :, MARGIN : MARGIN + blocks * BLOCK].reshape(2, line_count, blocks, BLOCK)
    left_rim = shifted[:, :, : blocks * BLOCK].reshape(2, line_count, blocks, BLOCK)[..., :MARGIN]
    right_rim = shifted[:, :, 2 * MARGIN : 2 * MARGIN + blocks * BLOCK].reshape(
        2, line_count, blocks, BLOCK
    )[..., BLOCK - MARGIN :]
    windows = jnp.concatenate([left_rim, middle, right_rim], 3)
    spectrum = jnp.einsum(
        "cpms,cst->pmt",
        windows,
        forward.reshape(2, window_len, 2 * window_len),
        preferred_element_type=jnp.float32,
    )
    spec_real = spectrum[..., :window_len]
    spec_imaginary = spectrum[..., window_len:]
    factor_real = ramp_real[:, None, :]
    factor_imaginary = ramp_imaginary[:, None, :]
    ramped = jnp.concatenate(
        [
            spec_real * factor_real - spec_imaginary * factor_imaginary,
            spec_real * factor_imaginary + spec_imaginary * factor_real,
        ],
        -1,
    ).astype(jnp.bfloat16)
    result = jnp.einsum(
        "pms,scb->cpmb",
        ramped,
        inverse.reshape(2 * window_len, 2, BLOCK),
        preferred_element_type=jnp.float32,
    )
    return result.reshape(2, line_count, blocks * BLOCK).astype(jnp.bfloat16)


def single_pass(padded, extent, shifts, fractions, tables):
    ramp_real, ramp_imaginary = shear_ramp(fractions, tables[2])
    return line_pass(padded, extent, shifts, ramp_real, ramp_imaginary, tables)


def general_shear_columns(stacked, shifts, fractions, tables):
    halo_depth = SHIFT_X + MARGIN
    inputs = stacked.shape[0]
    column_devices = lax.axis_size("col")
    share = stacked.shape[2] // column_devices
    offset = lax.axis_index("col") * share
    spread = lax.all_to_all(stacked, "col", split_axis=2, concat_axis=3, tiled=True)
    padded = jnp.pad(spread, ((0, 0), (0, 0), (0, 0), (halo_depth, halo_depth)))
    row_shifts = lax.dynamic_slice_in_dim(shifts, offset, share, 1)
    row_fractions = lax.dynamic_slice_in_dim(fractions, offset, share, 1)
    sheared = jnp.stack(
        [
            single_pass(
                padded[min(0, inputs - 1)], halo_depth, row_shifts[0], row_fractions[0], tables
            )
        ]
    )
    return lax.all_to_all(sheared, "col", split_axis=3, concat_axis=2, tiled=True)


def shear_along_first(padded_lines, halo_depth, shifts, fractions, tables):
    flipped = jnp.swapaxes(padded_lines[0], 1, 2)
    moved = single_pass(flipped, halo_depth, shifts[0], fractions[0], tables)
    sheared = [jnp.swapaxes(moved, 1, 2)]
    return jnp.stack(sheared)


def shear_rows_pass(stacked, shifts, fractions, tables):
    halo_depth = SHIFT_Y + MARGIN
    row_devices = lax.axis_size("row")
    share = stacked.shape[3] // row_devices
    offset = lax.axis_index("row") * share
    spread = lax.all_to_all(stacked, "row", split_axis=3, concat_axis=2, tiled=True)
    padded = jnp.pad(spread, ((0, 0), (0, 0), (halo_depth, halo_depth), (0, 0)))
    column_shifts = lax.dynamic_slice_in_dim(shifts, offset, share, 1)
    column_fractions = lax.dynamic_slice_in_dim(fractions, offset, share, 1)
    sheared = shear_along_first(padded, halo_depth, column_shifts, column_fractions, tables)
    return lax.all_to_all(sheared, "row", split_axis=2, concat_axis=3, tiled=True)


def travel_local(extended, distance, tables):
    ramp_real, ramp_imaginary = travel_ramp(distance, tables[2])
    halfway = line_pass(extended, MARGIN, None, ramp_real, ramp_imaginary, tables)
    flipped = jnp.swapaxes(halfway, 1, 2)
    finished = line_pass(flipped, MARGIN, None, ramp_real, ramp_imaginary, tables)
    return jnp.swapaxes(finished, 1, 2)


def transmit(rotated, wave):
    phase_part = rotated[0].astype(jnp.float32)
    absorb_part = rotated[1].astype(jnp.float32)
    amplitude = jnp.exp(-ABSORB * absorb_part)
    through_real = amplitude * jnp.cos(phase_part)
    through_imaginary = amplitude * jnp.sin(phase_part)
    wave_real = wave[0].astype(jnp.float32)
    wave_imaginary = wave[1].astype(jnp.float32)
    return jnp.stack(
        [
            wave_real * through_real - wave_imaginary * through_imaginary,
            wave_real * through_imaginary + wave_imaginary * through_real,
        ]
    ).astype(jnp.bfloat16)


def general_on_device(
    volume_plane,
    wave_a,
    wave_b,
    shift_rows,
    fraction_rows,
    shift_columns,
    fraction_columns,
    travel_distance,
):
    tables = fourier_tables(BLOCK, MARGIN)
    source = volume_plane[None]
    results = []
    for member in range(2):
        stacked = general_shear_columns(
            source,
            shift_rows[member : member + 1, 0],
            fraction_rows[member : member + 1, 0],
            tables,
        )
        stacked = shear_rows_pass(
            stacked,
            shift_columns[member : member + 1],
            fraction_columns[member : member + 1],
            tables,
        )
        stacked = general_shear_columns(
            stacked,
            shift_rows[member : member + 1, 1],
            fraction_rows[member : member + 1, 1],
            tables,
        )
        results.append(stacked[0])
    view_one = results[0]
    view_two = results[1]
    turned = jnp.swapaxes(jnp.flip(view_two, 2), 1, 2)
    for bit_number in range(lax.axis_size("col").bit_length() - 1):
        turned = swapped(turned, "col", bit_number)
    product_a = transmit(view_one, wave_a)
    extended_a = padded_2(product_a, (("row", 1), ("col", 2)), MARGIN)
    exit_a = travel_local(extended_a, travel_distance[0], tables)
    product_b = transmit(turned, wave_b)
    extended_b = padded_2(product_b, (("row", 2), ("col", 1)), MARGIN)
    exit_b = travel_local(extended_b, travel_distance[1], tables)
    return (exit_a, exit_b)


def solution(mesh):
    def either(volume_plane, *rest):
        rows, width = volume_plane.shape[1:]
        fits = (
            rows == BLOCK * lax.axis_size("col")
            and width == BLOCK * lax.axis_size("row")
            and width >= -(-(SHIFT_X + MARGIN) // BLOCK) * BLOCK >= rows
        )
        chosen = on_device if fits else general_on_device
        return chosen(volume_plane, *rest)

    return jax.shard_map(
        either,
        mesh=mesh,
        in_specs=(
            P(None, "row", "col"),
            P(None, "row", "col"),
            P(None, "col", "row"),
            P(None, None, "row"),
            P(None, None, "row"),
            P(None, "col"),
            P(None, "col"),
            P(),
        ),
        out_specs=(P(None, "row", "col"), P(None, "col", "row")),
        check_vma=False,
    )
```

```python
import functools

import jax
import jax.numpy as jnp
import numpy as np
from jax import lax
from jax.experimental import pallas as pl
from jax.experimental.pallas import tpu as pltpu
from jax.sharding import PartitionSpec as P

BLOCK = 128
MARGIN = 32
SHIFT_X = 864
SHIFT_Y = 1728


ABSORB = 0.25

WINDOW = BLOCK + 2 * MARGIN
BINS = WINDOW // 2
GROUP = 16
PARTS = 2
ROWS = 256
STEPS = 2
VMEM_LIMIT = 56 * 1024 * 1024


def angle_table(rows, columns):
    return 2.0 * np.pi * (np.outer(rows, columns) % WINDOW) / WINDOW


def real_tables():
    position = np.arange(WINDOW)
    bins = np.arange(BINS + 1)
    target = np.arange(BLOCK) + MARGIN
    forward = np.zeros((2 * BLOCK, 2 * BLOCK), np.float32)
    forward[:WINDOW, : BINS + 1] = np.cos(angle_table(position, bins))
    forward[:WINDOW, BLOCK + 1 : BLOCK + BINS] = -np.sin(angle_table(position, bins[1:BINS]))
    weight = np.where((bins == 0) | (bins == BINS), 1.0, 2.0) / WINDOW
    inverse = np.zeros((2 * BLOCK, BLOCK), np.float32)
    inverse[: BINS + 1] = np.cos(angle_table(bins, target)) * weight[:, None]
    inverse[BLOCK + 1 : BLOCK + BINS] = (
        -np.sin(angle_table(bins[1:BINS], target)) * weight[1:BINS, None]
    )
    return forward, inverse


def travel_matrices(distance, forward, inverse):
    frequency = jnp.arange(BLOCK, dtype=jnp.float32)
    phases = -2.0 * jnp.pi / (WINDOW * WINDOW) * distance[:, None] * frequency * frequency
    ramps = jnp.stack([jnp.cos(phases), jnp.sin(phases)], 1)
    ramps = jnp.concatenate([ramps, ramps], 2)
    scaled = ramps[..., None] * jnp.asarray(inverse)
    matrices = jnp.einsum(
        "pq,vrqu->vrpu",
        jnp.asarray(forward[:WINDOW]),
        scaled,
        precision=lax.Precision.HIGHEST,
    )
    return matrices


def lane_iota(rows):
    return lax.broadcasted_iota(jnp.int32, (rows, BLOCK), 1)


def shift_lines(strip, shifted, base, base_offset, spare, windows, chunk_offset, rows):
    def one_group(group, carry):
        first = pl.multiple_of(group * GROUP, GROUP)
        lines = pl.ds(first, GROUP)
        start = base[base_offset + group] + chunk_offset
        offset = spare[lines, :]
        later = offset >= BLOCK
        lane = lane_iota(GROUP) + (offset & (BLOCK - 1))
        wraps = lane >= BLOCK
        index = lane & (BLOCK - 1)
        for part in range(2):
            here = strip[start, part, lines, :].astype(jnp.float32)
            before = None
            for i in range(windows + 2):
                following = strip[start + i + 1, part, lines, :].astype(jnp.float32)
                turned = jnp.take_along_axis(jnp.where(later, following, here), index, axis=1)
                if before is not None:
                    shifted[i - 1, part, lines, :] = jnp.where(wraps, turned, before).astype(
                        jnp.bfloat16
                    )
                before = turned
                here = following
        return carry

    lax.fori_loop(0, rows // GROUP, one_group, 0, unroll=4)


def ramped_lines(shifted, windows, rows, cosine, sine, forward):
    count = len(windows)
    lower = jnp.concatenate([shifted[m].reshape(2 * rows, BLOCK) for m in windows], 0)
    upper = jnp.concatenate([shifted[m + 1].reshape(2 * rows, BLOCK) for m in windows], 0)
    spectrum = jnp.dot(
        jnp.concatenate([lower, upper], 1), forward[...], preferred_element_type=jnp.float32
    )
    real = spectrum[:, :BLOCK].reshape(count * 2, rows, BLOCK)
    imaginary = spectrum[:, BLOCK:].reshape(count * 2, rows, BLOCK)
    ramp_real = cosine[...][None]
    ramp_imaginary = sine[...][None]
    ramped = jnp.concatenate(
        [
            (real * ramp_real - imaginary * ramp_imaginary).astype(jnp.bfloat16),
            (real * ramp_imaginary + imaginary * ramp_real).astype(jnp.bfloat16),
        ],
        2,
    )
    return ramped.reshape(count * 2 * rows, 2 * BLOCK)


def down_lines(vector):
    return jnp.broadcast_to(vector, (BLOCK, vector.shape[1])).T


def line_ramps(fractions, cosine, sine):
    bins = lane_iota(fractions.shape[1]).astype(jnp.float32)
    sine[...], cosine[...] = sine_cosine(down_lines(fractions) * bins * (-2.0 * np.pi / WINDOW))


def shear_tile_kernel(halo, tiles, rows, batch, wide, parts, sent, base, rank, *refs):
    lefts, rights, refs = refs[:parts], refs[parts : 2 * parts], refs[2 * parts :]
    waves, refs = refs[: int(sent)], refs[int(sent) :]
    own, offsets, fractions, forward, inverse, out = refs[:6]
    strip, shifted, spare, cosine, sine = refs[6:]
    step = pl.program_id(0)
    groups = rows // GROUP
    end = halo + tiles + halo

    @pl.when(step == 0)
    def _():
        strip[end : end + 2] = jnp.zeros((2, 2, rows, BLOCK), jnp.bfloat16)

    def fill(piece, first, count):
        for i in range(count):
            if wide:
                strip[first + i] = piece[:, :, i * BLOCK : (i + 1) * BLOCK]
            else:
                strip[first + i] = piece[i]

    share = pl.num_programs(0) // parts
    for part in range(parts):

        @pl.when(step // share == part)
        def _():
            fill(lefts[part], 0, halo)
            fill(rights[part], halo + tiles, halo)

    fill(own, halo, tiles)
    spare[...] = down_lines(offsets[0]).astype(jnp.int32)
    line_ramps(fractions[0], cosine, sine)
    shift_lines(strip, shifted, base, step * groups, spare, tiles, 0, rows)
    for first in range(0, tiles, batch):
        windows = [slot if sent else slot ^ rank[0] for slot in range(first, first + batch)]
        ramped = ramped_lines(shifted, windows, rows, cosine, sine, forward)
        result = jnp.dot(ramped, inverse[...], preferred_element_type=jnp.float32)
        result = result.astype(jnp.bfloat16).reshape(batch, 2, rows, BLOCK)
        if sent:
            for i, window in enumerate(windows):
                wave = waves[0][:, :, window * BLOCK : (window + 1) * BLOCK]
                for part, value in enumerate(transmitted(result[i], wave)):
                    out[window, part] = value
        else:
            out[first : first + batch] = result


def shear_tile(own, lefts, rights, first, lines, halo, base, rank, spare, fractions, tables, *waves):
    wide = own.ndim == 3
    parts = len(lefts)
    line_count = lines
    part_lines = line_count // parts
    tiles = own.shape[2] // BLOCK if wide else own.shape[0]
    rows = min(part_lines, ROWS)
    share = part_lines // rows
    offset = first // rows
    forward, inverse = tables

    def piece_spec(piece, place):
        if wide:
            return pl.BlockSpec((2, rows, piece.shape[2]), lambda i, *_: (0, place(i), 0))
        return pl.BlockSpec((piece.shape[0], 2, rows, BLOCK), lambda i, *_: (0, 0, place(i), 0))

    halo_specs = [
        piece_spec(x, lambda i, part=part: jnp.clip(i - part * share, 0, share - 1))
        for x in (lefts[0], rights[0])
        for part in range(parts)
    ]
    line_spec = pl.BlockSpec((1, 1, rows), lambda i, *_: (i + offset, 0, 0))
    along = lambda x: x.astype(jnp.float32).reshape(-1, 1, rows)
    out_shape = jax.ShapeDtypeStruct((tiles, 2, line_count, BLOCK), jnp.bfloat16)
    out_spec = pl.BlockSpec((tiles, 2, rows, BLOCK), lambda i, *_: (0, 0, i, 0))
    groups = rows // GROUP
    kernel = functools.partial(
        shear_tile_kernel,
        halo,
        tiles,
        rows,
        tiles // 4 if tiles % 4 == 0 else tiles,
        wide,
        parts,
        len(waves) > 0,
    )
    return pl.pallas_call(
        kernel,
        grid_spec=pltpu.PrefetchScalarGridSpec(
            num_scalar_prefetch=2,
            grid=(line_count // rows,),
            in_specs=halo_specs
            + [pl.BlockSpec((2, rows, x.shape[2]), lambda i, *_: (0, i + offset, 0)) for x in waves]
            + [piece_spec(own, lambda i: i + offset)]
            + [line_spec] * 2
            + [
                pl.BlockSpec(forward.shape, lambda i, *_: (0, 0)),
                pl.BlockSpec(inverse.shape, lambda i, *_: (0, 0)),
            ],
            out_specs=out_spec,
            scratch_shapes=[
                pltpu.VMEM((halo + tiles + halo + 2, 2, rows, BLOCK), jnp.bfloat16),
                pltpu.VMEM((tiles + 1, 2, rows, BLOCK), jnp.bfloat16),
                pltpu.VMEM((rows, BLOCK), jnp.int32),
                pltpu.VMEM((rows, BLOCK), jnp.float32),
                pltpu.VMEM((rows, BLOCK), jnp.float32),
            ],
        ),
        out_shape=out_shape,
        compiler_params=pltpu.CompilerParams(vmem_limit_bytes=VMEM_LIMIT),
        name="shear_tile",
    )(
        lax.slice_in_dim(base, offset * groups, offset * groups + line_count // GROUP),
        rank,
        *lefts,
        *rights,
        *waves,
        own,
        along(spare),
        along(fractions),
        forward,
        inverse,
    )


def shear_whole_kernel(
    halo,
    devices,
    tiles,
    rows,
    base,
    own,
    offsets,
    fractions,
    forward,
    flipped,
    out,
    strip,
    shifted,
    spare,
    cosine,
    sine,
):
    step = pl.program_id(0)
    chunks = devices * tiles
    length = tiles * BLOCK

    @pl.when(step == 0)
    def _():
        strip[0:halo] = jnp.zeros((halo, 2, rows, BLOCK), jnp.bfloat16)
        strip[halo + chunks :] = jnp.zeros((halo + 2, 2, rows, BLOCK), jnp.bfloat16)
        for chunk in range(chunks):
            strip[halo + chunk] = own[chunk % tiles, chunk // tiles]
        out[0, :, 0:MARGIN, :] = jnp.zeros((2, MARGIN, rows), jnp.bfloat16)
        out[devices - 1, :, MARGIN + length :, :] = jnp.zeros((2, MARGIN, rows), jnp.bfloat16)
        spare[...] = down_lines(offsets[...]).astype(jnp.int32)
        line_ramps(fractions[...], cosine, sine)

    shift_lines(strip, shifted, base, 0, spare, tiles, step * tiles, rows)
    ramped = ramped_lines(shifted, range(tiles), rows, cosine, sine, forward)
    target = devices - 1 - step
    result = lax.dot_general(
        flipped[...], ramped, (((1,), (1,)), ((), ())), preferred_element_type=jnp.float32
    ).astype(jnp.bfloat16)
    for window in range(tiles):
        block = tiles - 1 - window
        low = MARGIN + block * BLOCK
        for part in range(2):
            lanes = (2 * window + part) * rows
            piece = result[:, lanes : lanes + rows]
            out[target, part, low : low + BLOCK, :] = piece
            if block == 0:

                @pl.when(target > 0)
                def _():
                    out[target - 1, part, MARGIN + length :, :] = piece[:MARGIN]

            if block == tiles - 1:

                @pl.when(target < devices - 1)
                def _():
                    out[target + 1, part, 0:MARGIN, :] = piece[BLOCK - MARGIN :]


def shear_whole(own, halo, base, spare, fractions, tables):
    tiles, devices, _, rows, _ = own.shape
    forward, flipped = tables
    operands = (
        own,
        spare.astype(jnp.float32).reshape(1, rows),
        fractions.reshape(1, rows),
        forward,
        flipped,
    )
    full = lambda shape: pl.BlockSpec(shape, lambda i, *_: (0,) * len(shape))
    out = (devices, 2, tiles * BLOCK + 2 * MARGIN, rows)
    return pl.pallas_call(
        functools.partial(shear_whole_kernel, halo, devices, tiles, rows),
        grid_spec=pltpu.PrefetchScalarGridSpec(
            num_scalar_prefetch=1,
            grid=(devices,),
            in_specs=[full(x.shape) for x in operands],
            out_specs=full(out),
            scratch_shapes=[
                pltpu.VMEM((2 * halo + devices * tiles + 2, 2, rows, BLOCK), jnp.bfloat16),
                pltpu.VMEM((tiles + 1, 2, rows, BLOCK), jnp.bfloat16),
                pltpu.VMEM((rows, BLOCK), jnp.int32),
                pltpu.VMEM((rows, BLOCK), jnp.float32),
                pltpu.VMEM((rows, BLOCK), jnp.float32),
            ],
        ),
        out_shape=jax.ShapeDtypeStruct(out, jnp.bfloat16),
        compiler_params=pltpu.CompilerParams(vmem_limit_bytes=VMEM_LIMIT),
        name="shear_whole",
    )(base, *operands)


def shear_columns_kernel(front, blocks, length, rows_out, place, base, rank, *refs):
    owns, refs = refs[: len(place)], refs[len(place) :]
    offsets, fractions, forward, inverse, out, strip, shifted, cosine, sine = refs
    step = pl.program_id(0)
    per_step = length // BLOCK
    per_grid = blocks // pl.num_programs(0)
    total = strip.shape[1]

    @pl.when(step == 0)
    def _():
        strip[:, 0:front, :] = jnp.zeros((2, front, BLOCK), jnp.bfloat16)
        back = front + blocks * length
        strip[:, back:, :] = jnp.zeros((2, total - back, BLOCK), jnp.bfloat16)
        for own, slots in zip(owns, place):
            count = own.shape[2]
            for i, (slot, within) in enumerate(slots):
                first = pl.multiple_of(front + (slot ^ rank[0]) * length + within, GROUP)
                for part in range(2):
                    strip[part, pl.ds(first, count), :] = own[i, part]
        bins = lax.broadcasted_iota(jnp.int32, (BLOCK, BLOCK), 0).astype(jnp.float32)
        sine[...], cosine[...] = sine_cosine(bins * fractions[...] * (-2.0 * np.pi / WINDOW))

    offset = jnp.broadcast_to(offsets[...], (8, BLOCK))
    row = lax.broadcasted_iota(jnp.int32, (8, BLOCK), 0) + (offset & 7)
    wraps = row >= 8
    index = row & 7

    def one_chunk(block_rows, chunk):
        begin = pl.multiple_of(base[0] + block_rows + chunk * BLOCK, GROUP)
        for part in range(2):
            value = strip[part, pl.ds(begin, 2 * BLOCK), :].astype(jnp.float32)
            value = value.reshape(2 * BLOCK // 8, 8, BLOCK)
            for bit in (64, 32, 16, 8):
                taken = ((offset & bit) != 0)[None]
                value = jnp.where(taken, value[bit // 8 :], value[: -(bit // 8)])
            pieces = [
                jnp.take_along_axis(value[i], index, axis=0) for i in range(BLOCK // 8 + 1)
            ]
            moved = [
                jnp.where(wraps, pieces[i + 1], pieces[i]) for i in range(BLOCK // 8)
            ]
            shifted[chunk * BLOCK : (chunk + 1) * BLOCK, part * BLOCK : (part + 1) * BLOCK] = (
                jnp.concatenate(moved, 0).astype(jnp.bfloat16)
            )

    def one_block(local, carry):
        block_rows = ((step * per_grid + local) ^ rank[0]) * length
        for chunk in range(per_step + 1):
            one_chunk(block_rows, chunk)
        windows = [shifted[m * BLOCK : (m + 2) * BLOCK, :] for m in range(per_step)]
        spectrum = jnp.dot(
            forward[...], jnp.concatenate(windows, 1), preferred_element_type=jnp.float32
        )
        ramp_real = jnp.concatenate([cosine[...]] * (2 * per_step), 1)
        ramp_imaginary = jnp.concatenate([sine[...]] * (2 * per_step), 1)
        real, imaginary = spectrum[:BLOCK], spectrum[BLOCK:]
        ramped = jnp.concatenate(
            [
                (real * ramp_real - imaginary * ramp_imaginary).astype(jnp.bfloat16),
                (real * ramp_imaginary + imaginary * ramp_real).astype(jnp.bfloat16),
            ],
            0,
        )
        result = jnp.dot(inverse[...], ramped, preferred_element_type=jnp.float32)
        result = result.astype(jnp.bfloat16)
        for window in range(per_step):
            piece, within = window * BLOCK // rows_out, window * BLOCK % rows_out
            for part in range(2):
                lanes = (2 * window + part) * BLOCK
                out[local * (length // rows_out) + piece, part, within : within + BLOCK, :] = (
                    result[:, lanes : lanes + BLOCK]
                )
        return carry

    lax.fori_loop(0, per_grid, one_block, 0)


def shear_columns(owns, place, blocks, front, back, base, rank, spare, fractions, tables, rows_out):
    length = sum(own.shape[0] * own.shape[2] for own in owns) // blocks
    forward, inverse = tables
    operands = (
        *owns,
        spare.astype(jnp.int32).reshape(1, BLOCK),
        fractions.reshape(1, BLOCK),
        forward,
        inverse,
    )
    full = lambda shape: pl.BlockSpec(shape, lambda i, *_: (0,) * len(shape))
    pieces = blocks * length // rows_out
    steps = STEPS if blocks % STEPS == 0 else 1
    return pl.pallas_call(
        functools.partial(shear_columns_kernel, front, blocks, length, rows_out, place),
        grid_spec=pltpu.PrefetchScalarGridSpec(
            num_scalar_prefetch=2,
            grid=(steps,),
            in_specs=[full(x.shape) for x in operands],
            out_specs=pl.BlockSpec(
                (pieces // steps, 2, rows_out, BLOCK), lambda i, *_: (i, 0, 0, 0)
            ),
            scratch_shapes=[
                pltpu.VMEM((2, front + blocks * length + back, BLOCK), jnp.bfloat16),
                pltpu.VMEM((length + BLOCK, 2 * BLOCK), jnp.bfloat16),
                pltpu.VMEM((BLOCK, BLOCK), jnp.float32),
                pltpu.VMEM((BLOCK, BLOCK), jnp.float32),
            ],
        ),
        out_shape=jax.ShapeDtypeStruct((pieces, 2, rows_out, BLOCK), jnp.bfloat16),
        compiler_params=pltpu.CompilerParams(vmem_limit_bytes=VMEM_LIMIT),
        name="shear_columns",
    )(base, rank, *operands)


def sine_cosine(angle):
    turns = jnp.round(angle * (2.0 / np.pi))
    rest = angle - turns * 1.5703125
    rest = rest - turns * 4.837512969970703125e-4
    rest = rest - turns * 7.549789954891882e-8
    square = rest * rest
    sine = rest + rest * square * (
        -1.6666654611e-1 + square * (8.3321608736e-3 - square * 1.9515295891e-4)
    )
    cosine = (
        1.0
        - 0.5 * square
        + square
        * square
        * (4.166664568298827e-2 + square * (-1.388731625493765e-3 + square * 2.443315711809948e-5))
    )
    quadrant = turns.astype(jnp.int32)
    odd = (quadrant & 1) != 0
    sine_out = jnp.where(odd, cosine, sine)
    cosine_out = jnp.where(odd, sine, cosine)
    sine_out = jnp.where((quadrant & 2) != 0, -sine_out, sine_out)
    cosine_out = jnp.where(((quadrant + 1) & 2) != 0, -cosine_out, cosine_out)
    return sine_out, cosine_out


def transmitted(rotated, wave):
    sine, cosine = sine_cosine(rotated[0].astype(jnp.float32))
    amplitude = jnp.exp(-ABSORB * rotated[1].astype(jnp.float32))
    through_real = amplitude * cosine
    through_imaginary = amplitude * sine
    wave_real = wave[0].astype(jnp.float32)
    wave_imaginary = wave[1].astype(jnp.float32)
    return (
        (wave_real * through_real - wave_imaginary * through_imaginary).astype(jnp.bfloat16),
        (wave_real * through_imaginary + wave_imaginary * through_real).astype(jnp.bfloat16),
    )


def travel_first_kernel(length, count, sent, *refs):
    if sent:
        body, top, bottom, matrix, out, low, high, field = refs
        for chunk in range(count):
            across = slice(chunk * BLOCK, (chunk + 1) * BLOCK)
            for part in range(2):
                field[part, 0:MARGIN, across] = top[chunk, part]
                field[part, MARGIN : MARGIN + length, across] = body[chunk, part]
                field[part, MARGIN + length :, across] = bottom[chunk, part]
    else:
        body, wave, wave_top, wave_bottom, matrix, out, low, high, field = refs
        pieces = [(0, MARGIN, wave_top, 0)]
        pieces += [(MARGIN + first, BLOCK, wave, first) for first in range(0, length, BLOCK)]
        pieces += [(MARGIN + length, MARGIN, wave_bottom, 0)]
        for chunk in range(count):
            across = slice(chunk * BLOCK, (chunk + 1) * BLOCK)
            for place, height, waves, first in pieces:
                parts = transmitted(
                    [body[chunk, p, place : place + height, :] for p in range(2)],
                    [waves[p, first : first + height, across] for p in range(2)],
                )
                for part in range(2):
                    field[part, place : place + height, across] = parts[part]
    for m in range(0, length, BLOCK):
        window = jnp.concatenate([field[0, m : m + WINDOW, :], field[1, m : m + WINDOW, :]], 0)
        result = jnp.dot(matrix[...], window, preferred_element_type=jnp.float32)
        result = result.astype(jnp.bfloat16)
        for chunk in range(count):
            across = slice(chunk * BLOCK, (chunk + 1) * BLOCK)
            for part in range(2):
                out[chunk, part, m : m + BLOCK, :] = result[
                    part * BLOCK : (part + 1) * BLOCK, across
                ]

    def outermost(chunk, edge, first):
        for part in range(2):
            for m in range(0, length, BLOCK):
                turned = out[chunk, part, m : m + BLOCK, :].astype(jnp.float32).T
                edge[part, :, m : m + BLOCK] = turned[first : first + MARGIN].astype(jnp.bfloat16)

    @pl.when(pl.program_id(0) == 0)
    def _():
        outermost(0, low, 0)

    @pl.when(pl.program_id(0) == pl.num_programs(0) - 1)
    def _():
        outermost(count - 1, high, BLOCK - MARGIN)


def travel_first(body, halos, waves, matrix):
    chunks = body.shape[0]
    count = chunks // STEPS if chunks % STEPS == 0 else chunks
    length = body.shape[2] if len(halos) > 0 else body.shape[2] - 2 * MARGIN
    chunk_spec = lambda x: pl.BlockSpec((count, 2, x.shape[2], BLOCK), lambda i: (i, 0, 0, 0))
    wide_spec = lambda x: pl.BlockSpec((2, x.shape[1], count * BLOCK), lambda i: (0, 0, i))
    return pl.pallas_call(
        functools.partial(travel_first_kernel, length, count, len(halos) > 0),
        grid=(chunks // count,),
        in_specs=[chunk_spec(x) for x in (body, *halos)]
        + [wide_spec(x) for x in waves]
        + [pl.BlockSpec(matrix.shape, lambda i: (0, 0))],
        out_specs=[pl.BlockSpec((count, 2, length, BLOCK), lambda i: (i, 0, 0, 0))]
        + [pl.BlockSpec((2, MARGIN, length), lambda i: (0, 0, 0))] * 2,
        out_shape=[jax.ShapeDtypeStruct((chunks, 2, length, BLOCK), jnp.bfloat16)]
        + [jax.ShapeDtypeStruct((2, MARGIN, length), jnp.bfloat16)] * 2,
        scratch_shapes=[pltpu.VMEM((2, length + 2 * MARGIN, count * BLOCK), jnp.bfloat16)],
        compiler_params=pltpu.CompilerParams(vmem_limit_bytes=VMEM_LIMIT),
        name="travel_first",
    )(body, *halos, *waves, matrix)


def travel_second_kernel(chunks, rows, left, body, right, matrix, out):
    empty = jnp.zeros((BLOCK - MARGIN, rows), jnp.float32)
    upright = lambda *pieces: jnp.concatenate(pieces, 0).T.astype(jnp.bfloat16)
    parts = [
        [upright(empty, left[p].astype(jnp.float32))]
        + [body[m, p] for m in range(chunks)]
        + [upright(right[p].astype(jnp.float32), empty)]
        for p in range(2)
    ]
    windows = [
        jnp.concatenate(parts[0][m : m + 3] + parts[1][m : m + 3], 1) for m in range(chunks)
    ]
    result = jnp.dot(
        jnp.concatenate(windows, 0), matrix[...], preferred_element_type=jnp.float32
    ).astype(jnp.bfloat16)
    for m in range(chunks):
        for part in range(2):
            out[part, :, m * BLOCK : (m + 1) * BLOCK] = result[
                m * rows : (m + 1) * rows, part * BLOCK : (part + 1) * BLOCK
            ]


def travel_second(left, body, right, matrix):
    chunks, _, length, _ = body.shape
    rows = length // STEPS if length % (STEPS * BLOCK) == 0 else length
    edge = pl.BlockSpec((2, MARGIN, rows), lambda i: (0, 0, i))
    return pl.pallas_call(
        functools.partial(travel_second_kernel, chunks, rows),
        grid=(length // rows,),
        in_specs=[
            edge,
            pl.BlockSpec((chunks, 2, rows, BLOCK), lambda i: (0, 0, i, 0)),
            edge,
            pl.BlockSpec(matrix.shape, lambda i: (0, 0)),
        ],
        out_specs=pl.BlockSpec((2, rows, chunks * BLOCK), lambda i: (0, i, 0)),
        out_shape=jax.ShapeDtypeStruct((2, length, chunks * BLOCK), jnp.bfloat16),
        compiler_params=pltpu.CompilerParams(vmem_limit_bytes=VMEM_LIMIT),
        name="travel_second",
    )(left, body, right, matrix)


def from_both_sides(first, last, axis):
    devices = lax.axis_size(axis)
    up = [(i, i + 1) for i in range(devices - 1)]
    down = [(j, i) for i, j in up]
    return lax.ppermute(last, axis, up), lax.ppermute(first, axis, down)


def after(value, *others):
    return lax.optimization_barrier((value, others))[0]


def ordered_kernel(halo, rank, *refs):
    pieces, (out, first, last) = refs[:-3], refs[-3:]
    count = len(pieces)
    for s, piece in enumerate(pieces):
        place = s ^ rank[0]
        out[place] = piece[0]

        @pl.when(place < halo)
        def _():
            first[place] = piece[0]

        @pl.when(place >= count - halo)
        def _():
            last[place - (count - halo)] = piece[0]


def ordered(pieces, halo, rank):
    count = len(pieces)
    block = pieces[0].shape
    shapes = [(n, *block[1:]) for n in (count, halo, halo)]
    full = lambda shape: pl.BlockSpec(shape, lambda i, *_: (0,) * len(shape))
    return pl.pallas_call(
        functools.partial(ordered_kernel, halo),
        grid_spec=pltpu.PrefetchScalarGridSpec(
            num_scalar_prefetch=1,
            grid=(1,),
            in_specs=[full(block)] * count,
            out_specs=[full(shape) for shape in shapes],
        ),
        out_shape=[jax.ShapeDtypeStruct(shape, pieces[0].dtype) for shape in shapes],
        compiler_params=pltpu.CompilerParams(vmem_limit_bytes=VMEM_LIMIT),
        name="ordered",
    )(rank, *pieces)


def swapped_shares(slots):
    devices = lax.axis_size("row")
    return [slots[0]] + [
        lax.ppermute(slots[s], "row", [(i, i ^ s) for i in range(devices)])
        for s in range(1, devices)
    ]


def group_starts(starts, group, unit):
    lines = starts.shape[-1]
    grouped = starts.reshape(*starts.shape[:-1], lines // group, group)
    base = jnp.min(grouped, -1) // unit
    spare = grouped - base[..., None] * unit
    return base.astype(jnp.int32), spare.reshape(starts.shape)


def on_device(
    volume_plane,
    wave_a,
    wave_b,
    shift_rows,
    fraction_rows,
    shift_columns,
    fraction_columns,
    travel_distance,
):
    _, line_count, width = volume_plane.shape
    row_devices, column_devices = lax.axis_size("row"), lax.axis_size("col")
    row_index, column_index = lax.axis_index("row"), lax.axis_index("col")
    tiles = width // BLOCK
    halo = -(-(SHIFT_X + MARGIN) // BLOCK)
    reach = halo * BLOCK

    forward, inverse = real_tables()
    half = lambda x: jnp.asarray(x, jnp.bfloat16)
    row_tables = (half(forward), half(inverse))
    column_tables = (half(forward.T), half(inverse.T))
    turned_tables = (half(forward), half(inverse[:, ::-1].T))
    in_order = jnp.zeros((1,), jnp.int32)
    by_rank = row_index.astype(jnp.int32).reshape(1)

    part_lines = line_count // PARTS
    lefts, rights, edges = [], [], ()
    for part in range(PARTS):
        lines = after(volume_plane, edges)[:, part * part_lines : (part + 1) * part_lines]
        edges = (lines[:, :, :reach], lines[:, :, width - reach :])
        if part == PARTS - 1:
            fill = ((0, 0), (0, 0), (0, reach - line_count))
            margins = (wave_b[:, :MARGIN], wave_b[:, -MARGIN:])
            edges = [
                jnp.concatenate([edge, jnp.pad(margin, fill)], 1)
                for edge, margin in zip(edges, margins)
            ]
        left, right = from_both_sides(*edges, "col")
        lefts.append(left)
        rights.append(right)
    wave_b_halos = [x[-1][:, part_lines:, :line_count] for x in (lefts, rights)]

    base_rows, spare_rows = group_starts(reach - MARGIN - shift_rows, GROUP, BLOCK)

    front = -(-(SHIFT_Y + MARGIN) // GROUP) * GROUP
    back = front + 3 * BLOCK
    mine = lambda x: lax.dynamic_slice_in_dim(x, row_index * BLOCK, BLOCK, 1)
    base_columns, spare_columns = group_starts(front - MARGIN - mine(shift_columns), BLOCK, GROUP)
    column_fractions = mine(fraction_columns)

    def first(view, begin, lefts, rights, rank):
        return shear_tile(
            volume_plane,
            lefts,
            rights,
            begin,
            len(lefts) * part_lines,
            halo,
            base_rows[view, 0],
            rank,
            spare_rows[view, 0],
            fraction_rows[view, 0],
            row_tables,
        )

    def second(view, pieces, place, rank, rows_out):
        return shear_columns(
            pieces,
            place,
            row_devices,
            front,
            back,
            base_columns[view] * GROUP,
            rank,
            spare_columns[view],
            column_fractions[view],
            column_tables,
            rows_out,
        )

    matrices = travel_matrices(travel_distance, forward, inverse)
    real, imaginary = matrices[:, 0], matrices[:, 1]
    along_rows = jnp.concatenate(
        [
            jnp.concatenate([real, -imaginary], 1),
            jnp.concatenate([imaginary, real], 1),
        ],
        2,
    )
    along_rows = jnp.swapaxes(along_rows, 1, 2).astype(jnp.bfloat16)
    spaced = jnp.pad(matrices, ((0, 0), (0, 0), (BLOCK - MARGIN, BLOCK - MARGIN), (0, 0)))
    real, imaginary = spaced[:, 0], spaced[:, 1]
    along_columns = jnp.concatenate(
        [
            jnp.concatenate([real, -imaginary], 1),
            jnp.concatenate([imaginary, real], 1),
        ],
        2,
    ).astype(jnp.bfloat16)

    spread, sheared = [], ()
    for part in range(PARTS):
        left, right = after((lefts[part], rights[part]), sheared)
        sheared = first(1, part * part_lines, [left], [right], in_order)
        spread.append(lax.all_to_all(sheared, "row", split_axis=0, concat_axis=0, tiled=True))
    lefts, rights = after((lefts, rights), sheared)
    slots = first(0, 0, lefts, rights, by_rank)
    shares = [slots[s : s + 1] for s in range(row_devices)]
    spread = after(spread, shares)
    pieces = swapped_shares(shares)

    place = [[(b, part * part_lines) for b in range(row_devices)] for part in range(PARTS)]
    moved_b = second(1, spread, place, in_order, BLOCK)
    whole = lax.all_to_all(moved_b, ("row", "col"), split_axis=0, concat_axis=0, tiled=True)
    whole = after(whole, pieces)
    whole = whole.reshape(row_devices, column_devices, 2, BLOCK, BLOCK)
    own_lines = lambda x: lax.dynamic_slice_in_dim(x, column_index * BLOCK, BLOCK, 0)
    groups = BLOCK // GROUP
    turned = shear_whole(
        whole,
        halo,
        lax.dynamic_slice_in_dim(base_rows[1, 1], column_index * groups, groups, 0),
        own_lines(spare_rows[1, 1]),
        own_lines(fraction_rows[1, 1]),
        turned_tables,
    )

    sent = lax.all_to_all(turned, "col", split_axis=0, concat_axis=0, tiled=True)

    pieces = after(pieces, turned)
    moved_a = second(0, pieces, [[(s, 0)] for s in range(row_devices)], by_rank, line_count)
    pieces = swapped_shares([moved_a[s : s + 1] for s in range(row_devices)])
    tile, low, high = ordered(pieces, halo, by_rank)
    left, right = from_both_sides(low, high, "col")

    half_b, low, high = travel_first(sent, (), (wave_b, *wave_b_halos), along_rows[1])
    low, high = from_both_sides(low, high, "row")
    exit_b = travel_second(low, half_b, high, along_columns[1])

    left, right = after((left, right), exit_b)
    field_a = shear_tile(
        tile,
        [left],
        [right],
        0,
        line_count,
        halo,
        base_rows[0, 1],
        in_order,
        spare_rows[0, 1],
        fraction_rows[0, 1],
        row_tables,
        wave_a,
    )
    halos = from_both_sides(field_a[:, :, :MARGIN], field_a[:, :, -MARGIN:], "row")
    half_a, low, high = travel_first(field_a, halos, (), along_rows[0])
    low, high = from_both_sides(low, high, "col")
    exit_a = travel_second(low, half_a, high, along_columns[0])
    return exit_a, exit_b


def swapped(value, axis, bit):
    mask = 2**bit
    pairs = [(source, source ^ mask) for source in range(lax.axis_size(axis))]
    return lax.ppermute(value, axis, pairs)


def padded_2(x, sides, width):
    for axis, dim in sides:
        devices, length = (lax.axis_size(axis), x.shape[dim])
        up = [(i, (i + 1) % devices) for i in range(devices - 1)]
        down = [(j, i) for i, j in up]
        last = lax.slice_in_dim(x, length - width, length, axis=dim)
        first = lax.slice_in_dim(x, 0, width, axis=dim)
        before = lax.ppermute(last, axis, up)
        after = lax.ppermute(first, axis, down)
        x = jnp.concatenate([before, x, after], axis=dim)
    return x


def fourier_tables(block_len, margin):
    window_len = block_len + 2 * margin
    frequency = jnp.arange(window_len, dtype=jnp.int32) - window_len // 2
    position = jnp.arange(window_len, dtype=jnp.int32)
    angles = (
        2.0
        * jnp.pi
        * jnp.mod(position[:, None] * frequency[None, :], window_len).astype(jnp.float32)
        / window_len
    )
    cosine = jnp.cos(angles)
    sines = jnp.sin(angles)
    forward = jnp.concatenate(
        [jnp.concatenate([cosine, -sines], 1), jnp.concatenate([sines, cosine], 1)], 0
    ).astype(jnp.bfloat16)
    target = jnp.arange(block_len, dtype=jnp.int32) + margin
    inverse_angle = (
        2.0
        * jnp.pi
        * jnp.mod(frequency[:, None] * target[None, :], window_len).astype(jnp.float32)
        / window_len
    )
    inverse_cosine = jnp.cos(inverse_angle) / window_len
    inverse_sine = jnp.sin(inverse_angle) / window_len
    inverse = jnp.concatenate(
        [
            jnp.concatenate([inverse_cosine, inverse_sine], 1),
            jnp.concatenate([-inverse_sine, inverse_cosine], 1),
        ],
        0,
    ).astype(jnp.bfloat16)
    return (forward, inverse, frequency.astype(jnp.float32))


def shear_ramp(fractions, frequency):
    window_len = frequency.shape[0]
    phases = -2.0 * jnp.pi / window_len * fractions[:, None] * frequency[None, :]
    nyquist = (jnp.arange(window_len) == 0)[None, :]
    ramp_real = jnp.where(nyquist, jnp.cos(jnp.pi * fractions)[:, None], jnp.cos(phases))
    ramp_imaginary = jnp.where(nyquist, 0.0, jnp.sin(phases))
    return (ramp_real, ramp_imaginary)


def travel_ramp(distance, frequency):
    window_len = frequency.shape[0]
    phases = -2.0 * jnp.pi / (window_len * window_len) * distance * frequency * frequency
    return (jnp.cos(phases)[None, :], jnp.sin(phases)[None, :])


def select_window(padded, starts, out_len):
    total_len = padded.shape[2]
    offset_range = total_len - out_len
    bit_count = max(offset_range, 1).bit_length()
    current = jnp.pad(padded, ((0, 0), (0, 0), (0, out_len + 2**bit_count - 1 - total_len)))
    for bit_number in reversed(range(bit_count)):
        stride = 2**bit_number
        kept_len = current.shape[2] - stride
        chosen = (starts // stride % 2 == 1)[None, :, None]
        current = jnp.where(
            chosen, current[:, :, stride : stride + kept_len], current[:, :, :kept_len]
        )
    return current


def line_pass(padded, extent, shifts, ramp_real, ramp_imaginary, tables):
    forward, inverse = (tables[0], tables[1])
    window_len = BLOCK + 2 * MARGIN
    line_count = padded.shape[1]
    blocks = (padded.shape[2] - 2 * extent) // BLOCK
    reach_len = blocks * BLOCK + 2 * MARGIN
    if shifts is None:
        shifted = padded
    else:
        starts = extent - MARGIN - shifts
        shifted = select_window(padded, starts, reach_len)
    middle = shifted[:, :, MARGIN : MARGIN + blocks * BLOCK].reshape(2, line_count, blocks, BLOCK)
    left_rim = shifted[:, :, : blocks * BLOCK].reshape(2, line_count, blocks, BLOCK)[..., :MARGIN]
    right_rim = shifted[:, :, 2 * MARGIN : 2 * MARGIN + blocks * BLOCK].reshape(
        2, line_count, blocks, BLOCK
    )[..., BLOCK - MARGIN :]
    windows = jnp.concatenate([left_rim, middle, right_rim], 3)
    spectrum = jnp.einsum(
        "cpms,cst->pmt",
        windows,
        forward.reshape(2, window_len, 2 * window_len),
        preferred_element_type=jnp.float32,
    )
    spec_real = spectrum[..., :window_len]
    spec_imaginary = spectrum[..., window_len:]
    factor_real = ramp_real[:, None, :]
    factor_imaginary = ramp_imaginary[:, None, :]
    ramped = jnp.concatenate(
        [
            spec_real * factor_real - spec_imaginary * factor_imaginary,
            spec_real * factor_imaginary + spec_imaginary * factor_real,
        ],
        -1,
    ).astype(jnp.bfloat16)
    result = jnp.einsum(
        "pms,scb->cpmb",
        ramped,
        inverse.reshape(2 * window_len, 2, BLOCK),
        preferred_element_type=jnp.float32,
    )
    return result.reshape(2, line_count, blocks * BLOCK).astype(jnp.bfloat16)


def single_pass(padded, extent, shifts, fractions, tables):
    ramp_real, ramp_imaginary = shear_ramp(fractions, tables[2])
    return line_pass(padded, extent, shifts, ramp_real, ramp_imaginary, tables)


def general_shear_columns(stacked, shifts, fractions, tables):
    halo_depth = SHIFT_X + MARGIN
    inputs = stacked.shape[0]
    column_devices = lax.axis_size("col")
    share = stacked.shape[2] // column_devices
    offset = lax.axis_index("col") * share
    spread = lax.all_to_all(stacked, "col", split_axis=2, concat_axis=3, tiled=True)
    padded = jnp.pad(spread, ((0, 0), (0, 0), (0, 0), (halo_depth, halo_depth)))
    row_shifts = lax.dynamic_slice_in_dim(shifts, offset, share, 1)
    row_fractions = lax.dynamic_slice_in_dim(fractions, offset, share, 1)
    sheared = jnp.stack(
        [
            single_pass(
                padded[min(0, inputs - 1)], halo_depth, row_shifts[0], row_fractions[0], tables
            )
        ]
    )
    return lax.all_to_all(sheared, "col", split_axis=3, concat_axis=2, tiled=True)


def shear_along_first(padded_lines, halo_depth, shifts, fractions, tables):
    flipped = jnp.swapaxes(padded_lines[0], 1, 2)
    moved = single_pass(flipped, halo_depth, shifts[0], fractions[0], tables)
    sheared = [jnp.swapaxes(moved, 1, 2)]
    return jnp.stack(sheared)


def shear_rows_pass(stacked, shifts, fractions, tables):
    halo_depth = SHIFT_Y + MARGIN
    row_devices = lax.axis_size("row")
    share = stacked.shape[3] // row_devices
    offset = lax.axis_index("row") * share
    spread = lax.all_to_all(stacked, "row", split_axis=3, concat_axis=2, tiled=True)
    padded = jnp.pad(spread, ((0, 0), (0, 0), (halo_depth, halo_depth), (0, 0)))
    column_shifts = lax.dynamic_slice_in_dim(shifts, offset, share, 1)
    column_fractions = lax.dynamic_slice_in_dim(fractions, offset, share, 1)
    sheared = shear_along_first(padded, halo_depth, column_shifts, column_fractions, tables)
    return lax.all_to_all(sheared, "row", split_axis=2, concat_axis=3, tiled=True)


def travel_local(extended, distance, tables):
    ramp_real, ramp_imaginary = travel_ramp(distance, tables[2])
    halfway = line_pass(extended, MARGIN, None, ramp_real, ramp_imaginary, tables)
    flipped = jnp.swapaxes(halfway, 1, 2)
    finished = line_pass(flipped, MARGIN, None, ramp_real, ramp_imaginary, tables)
    return jnp.swapaxes(finished, 1, 2)


def transmit(rotated, wave):
    phase_part = rotated[0].astype(jnp.float32)
    absorb_part = rotated[1].astype(jnp.float32)
    amplitude = jnp.exp(-ABSORB * absorb_part)
    through_real = amplitude * jnp.cos(phase_part)
    through_imaginary = amplitude * jnp.sin(phase_part)
    wave_real = wave[0].astype(jnp.float32)
    wave_imaginary = wave[1].astype(jnp.float32)
    return jnp.stack(
        [
            wave_real * through_real - wave_imaginary * through_imaginary,
            wave_real * through_imaginary + wave_imaginary * through_real,
        ]
    ).astype(jnp.bfloat16)


def general_on_device(
    volume_plane,
    wave_a,
    wave_b,
    shift_rows,
    fraction_rows,
    shift_columns,
    fraction_columns,
    travel_distance,
):
    tables = fourier_tables(BLOCK, MARGIN)
    source = volume_plane[None]
    results = []
    for member in range(2):
        stacked = general_shear_columns(
            source,
            shift_rows[member : member + 1, 0],
            fraction_rows[member : member + 1, 0],
            tables,
        )
        stacked = shear_rows_pass(
            stacked,
            shift_columns[member : member + 1],
            fraction_columns[member : member + 1],
            tables,
        )
        stacked = general_shear_columns(
            stacked,
            shift_rows[member : member + 1, 1],
            fraction_rows[member : member + 1, 1],
            tables,
        )
        results.append(stacked[0])
    view_one = results[0]
    view_two = results[1]
    turned = jnp.swapaxes(jnp.flip(view_two, 2), 1, 2)
    for bit_number in range(lax.axis_size("col").bit_length() - 1):
        turned = swapped(turned, "col", bit_number)
    product_a = transmit(view_one, wave_a)
    extended_a = padded_2(product_a, (("row", 1), ("col", 2)), MARGIN)
    exit_a = travel_local(extended_a, travel_distance[0], tables)
    product_b = transmit(turned, wave_b)
    extended_b = padded_2(product_b, (("row", 2), ("col", 1)), MARGIN)
    exit_b = travel_local(extended_b, travel_distance[1], tables)
    return (exit_a, exit_b)


def solution(mesh):
    def either(volume_plane, *rest):
        rows, width = volume_plane.shape[1:]
        fits = (
            rows == BLOCK * lax.axis_size("col")
            and width == BLOCK * lax.axis_size("row")
            and width >= -(-(SHIFT_X + MARGIN) // BLOCK) * BLOCK >= rows
        )
        chosen = on_device if fits else general_on_device
        return chosen(volume_plane, *rest)

    return jax.shard_map(
        either,
        mesh=mesh,
        in_specs=(
            P(None, "row", "col"),
            P(None, "row", "col"),
            P(None, "col", "row"),
            P(None, None, "row"),
            P(None, None, "row"),
            P(None, "col"),
            P(None, "col"),
            P(),
        ),
        out_specs=(P(None, "row", "col"), P(None, "col", "row")),
        check_vma=False,
    )
```

```python
import functools

import jax
import jax.numpy as jnp
import numpy as np
from jax import lax
from jax.experimental import pallas as pl
from jax.experimental.pallas import tpu as pltpu
from jax.sharding import PartitionSpec as P

BLOCK = 128
MARGIN = 32
SHIFT_X = 864
SHIFT_Y = 1728


ABSORB = 0.25

WINDOW = BLOCK + 2 * MARGIN
BINS = WINDOW // 2
GROUP = 16
PARTS = 2
ROWS = 256
STEPS = 2
VMEM_LIMIT = 56 * 1024 * 1024


def angle_table(rows, columns):
    return 2.0 * np.pi * (np.outer(rows, columns) % WINDOW) / WINDOW


def real_tables():
    position = np.arange(WINDOW)
    bins = np.arange(BINS + 1)
    target = np.arange(BLOCK) + MARGIN
    forward = np.zeros((2 * BLOCK, 2 * BLOCK), np.float32)
    forward[:WINDOW, : BINS + 1] = np.cos(angle_table(position, bins))
    forward[:WINDOW, BLOCK + 1 : BLOCK + BINS] = -np.sin(angle_table(position, bins[1:BINS]))
    weight = np.where((bins == 0) | (bins == BINS), 1.0, 2.0) / WINDOW
    inverse = np.zeros((2 * BLOCK, BLOCK), np.float32)
    inverse[: BINS + 1] = np.cos(angle_table(bins, target)) * weight[:, None]
    inverse[BLOCK + 1 : BLOCK + BINS] = (
        -np.sin(angle_table(bins[1:BINS], target)) * weight[1:BINS, None]
    )
    return forward, inverse


def travel_matrices(distance, forward, inverse):
    frequency = jnp.arange(BLOCK, dtype=jnp.float32)
    phases = -2.0 * jnp.pi / (WINDOW * WINDOW) * distance[:, None] * frequency * frequency
    ramps = jnp.stack([jnp.cos(phases), jnp.sin(phases)], 1)
    ramps = jnp.concatenate([ramps, ramps], 2)
    scaled = ramps[..., None] * jnp.asarray(inverse)
    matrices = jnp.einsum(
        "pq,vrqu->vrpu",
        jnp.asarray(forward[:WINDOW]),
        scaled,
        precision=lax.Precision.HIGHEST,
    )
    return matrices


def lane_iota(rows):
    return lax.broadcasted_iota(jnp.int32, (rows, BLOCK), 1)


def shift_lines(strip, shifted, base, base_offset, spare, windows, chunk_offset, rows):
    def one_group(group, carry):
        first = pl.multiple_of(group * GROUP, GROUP)
        lines = pl.ds(first, GROUP)
        start = base[base_offset + group] + chunk_offset
        offset = spare[lines, :]
        later = offset >= BLOCK
        lane = lane_iota(GROUP) + (offset & (BLOCK - 1))
        wraps = lane >= BLOCK
        index = lane & (BLOCK - 1)
        for part in range(2):
            here = strip[start, part, lines, :].astype(jnp.float32)
            before = None
            for i in range(windows + 2):
                following = strip[start + i + 1, part, lines, :].astype(jnp.float32)
                turned = jnp.take_along_axis(jnp.where(later, following, here), index, axis=1)
                if before is not None:
                    shifted[i - 1, part, lines, :] = jnp.where(wraps, turned, before).astype(
                        jnp.bfloat16
                    )
                before = turned
                here = following
        return carry

    lax.fori_loop(0, rows // GROUP, one_group, 0, unroll=4)


def ramped_lines(shifted, windows, rows, cosine, sine, forward):
    count = len(windows)
    lower = jnp.concatenate([shifted[m].reshape(2 * rows, BLOCK) for m in windows], 0)
    upper = jnp.concatenate([shifted[m + 1].reshape(2 * rows, BLOCK) for m in windows], 0)
    spectrum = jnp.dot(
        jnp.concatenate([lower, upper], 1), forward[...], preferred_element_type=jnp.float32
    )
    real = spectrum[:, :BLOCK].reshape(count * 2, rows, BLOCK)
    imaginary = spectrum[:, BLOCK:].reshape(count * 2, rows, BLOCK)
    ramp_real = cosine[...][None]
    ramp_imaginary = sine[...][None]
    ramped = jnp.concatenate(
        [
            (real * ramp_real - imaginary * ramp_imaginary).astype(jnp.bfloat16),
            (real * ramp_imaginary + imaginary * ramp_real).astype(jnp.bfloat16),
        ],
        2,
    )
    return ramped.reshape(count * 2 * rows, 2 * BLOCK)


def down_lines(vector):
    return jnp.broadcast_to(vector, (BLOCK, vector.shape[1])).T


def line_ramps(fractions, cosine, sine):
    bins = lane_iota(fractions.shape[1]).astype(jnp.float32)
    sine[...], cosine[...] = sine_cosine(down_lines(fractions) * bins * (-2.0 * np.pi / WINDOW))


def shear_tile_kernel(halo, tiles, rows, batch, wide, parts, sent, base, rank, *refs):
    lefts, rights, refs = refs[:parts], refs[parts : 2 * parts], refs[2 * parts :]
    waves, refs = refs[: int(sent)], refs[int(sent) :]
    own, offsets, fractions, forward, inverse, out = refs[:6]
    strip, shifted, spare, cosine, sine = refs[6:]
    step = pl.program_id(0)
    groups = rows // GROUP
    end = halo + tiles + halo

    @pl.when(step == 0)
    def _():
        strip[end : end + 2] = jnp.zeros((2, 2, rows, BLOCK), jnp.bfloat16)

    def fill(piece, first, count):
        for i in range(count):
            if wide:
                strip[first + i] = piece[:, :, i * BLOCK : (i + 1) * BLOCK]
            else:
                strip[first + i] = piece[i]

    share = pl.num_programs(0) // parts
    for part in range(parts):

        @pl.when(step // share == part)
        def _():
            fill(lefts[part], 0, halo)
            fill(rights[part], halo + tiles, halo)

    fill(own, halo, tiles)
    spare[...] = down_lines(offsets[0]).astype(jnp.int32)
    line_ramps(fractions[0], cosine, sine)
    shift_lines(strip, shifted, base, step * groups, spare, tiles, 0, rows)
    for first in range(0, tiles, batch):
        windows = [slot if sent else slot ^ rank[0] for slot in range(first, first + batch)]
        ramped = ramped_lines(shifted, windows, rows, cosine, sine, forward)
        result = jnp.dot(ramped, inverse[...], preferred_element_type=jnp.float32)
        result = result.astype(jnp.bfloat16).reshape(batch, 2, rows, BLOCK)
        if sent:
            for i, window in enumerate(windows):
                wave = waves[0][:, :, window * BLOCK : (window + 1) * BLOCK]
                for part, value in enumerate(transmitted(result[i], wave)):
                    out[window, part] = value
        else:
            out[first : first + batch] = result


def shear_tile(own, lefts, rights, first, lines, halo, base, rank, spare, fractions, tables, *waves):
    wide = own.ndim == 3
    parts = len(lefts)
    line_count = lines
    part_lines = line_count // parts
    tiles = own.shape[2] // BLOCK if wide else own.shape[0]
    rows = min(part_lines, ROWS)
    share = part_lines // rows
    offset = first // rows
    forward, inverse = tables

    def piece_spec(piece, place):
        if wide:
            return pl.BlockSpec((2, rows, piece.shape[2]), lambda i, *_: (0, place(i), 0))
        return pl.BlockSpec((piece.shape[0], 2, rows, BLOCK), lambda i, *_: (0, 0, place(i), 0))

    halo_specs = [
        piece_spec(x, lambda i, part=part: jnp.clip(i - part * share, 0, share - 1))
        for x in (lefts[0], rights[0])
        for part in range(parts)
    ]
    line_spec = pl.BlockSpec((1, 1, rows), lambda i, *_: (i + offset, 0, 0))
    along = lambda x: x.astype(jnp.float32).reshape(-1, 1, rows)
    out_shape = jax.ShapeDtypeStruct((tiles, 2, line_count, BLOCK), jnp.bfloat16)
    out_spec = pl.BlockSpec((tiles, 2, rows, BLOCK), lambda i, *_: (0, 0, i, 0))
    groups = rows // GROUP
    kernel = functools.partial(
        shear_tile_kernel,
        halo,
        tiles,
        rows,
        tiles // 4 if tiles % 4 == 0 else tiles,
        wide,
        parts,
        len(waves) > 0,
    )
    return pl.pallas_call(
        kernel,
        grid_spec=pltpu.PrefetchScalarGridSpec(
            num_scalar_prefetch=2,
            grid=(line_count // rows,),
            in_specs=halo_specs
            + [pl.BlockSpec((2, rows, x.shape[2]), lambda i, *_: (0, i + offset, 0)) for x in waves]
            + [piece_spec(own, lambda i: i + offset)]
            + [line_spec] * 2
            + [
                pl.BlockSpec(forward.shape, lambda i, *_: (0, 0)),
                pl.BlockSpec(inverse.shape, lambda i, *_: (0, 0)),
            ],
            out_specs=out_spec,
            scratch_shapes=[
                pltpu.VMEM((halo + tiles + halo + 2, 2, rows, BLOCK), jnp.bfloat16),
                pltpu.VMEM((tiles + 1, 2, rows, BLOCK), jnp.bfloat16),
                pltpu.VMEM((rows, BLOCK), jnp.int32),
                pltpu.VMEM((rows, BLOCK), jnp.float32),
                pltpu.VMEM((rows, BLOCK), jnp.float32),
            ],
        ),
        out_shape=out_shape,
        compiler_params=pltpu.CompilerParams(vmem_limit_bytes=VMEM_LIMIT),
        name="shear_tile",
    )(
        lax.slice_in_dim(base, offset * groups, offset * groups + line_count // GROUP),
        rank,
        *lefts,
        *rights,
        *waves,
        own,
        along(spare),
        along(fractions),
        forward,
        inverse,
    )


def shear_whole_kernel(
    halo,
    devices,
    tiles,
    rows,
    base,
    own,
    offsets,
    fractions,
    forward,
    flipped,
    out,
    strip,
    shifted,
    spare,
    cosine,
    sine,
):
    step = pl.program_id(0)
    chunks = devices * tiles
    length = tiles * BLOCK

    @pl.when(step == 0)
    def _():
        strip[0:halo] = jnp.zeros((halo, 2, rows, BLOCK), jnp.bfloat16)
        strip[halo + chunks :] = jnp.zeros((halo + 2, 2, rows, BLOCK), jnp.bfloat16)
        for chunk in range(chunks):
            strip[halo + chunk] = own[chunk % tiles, chunk // tiles]
        out[0, :, 0:MARGIN, :] = jnp.zeros((2, MARGIN, rows), jnp.bfloat16)
        out[devices - 1, :, MARGIN + length :, :] = jnp.zeros((2, MARGIN, rows), jnp.bfloat16)
        spare[...] = down_lines(offsets[...]).astype(jnp.int32)
        line_ramps(fractions[...], cosine, sine)

    shift_lines(strip, shifted, base, 0, spare, tiles, step * tiles, rows)
    ramped = ramped_lines(shifted, range(tiles), rows, cosine, sine, forward)
    target = devices - 1 - step
    result = lax.dot_general(
        flipped[...], ramped, (((1,), (1,)), ((), ())), preferred_element_type=jnp.float32
    ).astype(jnp.bfloat16)
    for window in range(tiles):
        block = tiles - 1 - window
        low = MARGIN + block * BLOCK
        for part in range(2):
            lanes = (2 * window + part) * rows
            piece = result[:, lanes : lanes + rows]
            out[target, part, low : low + BLOCK, :] = piece
            if block == 0:

                @pl.when(target > 0)
                def _():
                    out[target - 1, part, MARGIN + length :, :] = piece[:MARGIN]

            if block == tiles - 1:

                @pl.when(target < devices - 1)
                def _():
                    out[target + 1, part, 0:MARGIN, :] = piece[BLOCK - MARGIN :]


def shear_whole(own, halo, base, spare, fractions, tables):
    tiles, devices, _, rows, _ = own.shape
    forward, flipped = tables
    operands = (
        own,
        spare.astype(jnp.float32).reshape(1, rows),
        fractions.reshape(1, rows),
        forward,
        flipped,
    )
    full = lambda shape: pl.BlockSpec(shape, lambda i, *_: (0,) * len(shape))
    out = (devices, 2, tiles * BLOCK + 2 * MARGIN, rows)
    return pl.pallas_call(
        functools.partial(shear_whole_kernel, halo, devices, tiles, rows),
        grid_spec=pltpu.PrefetchScalarGridSpec(
            num_scalar_prefetch=1,
            grid=(devices,),
            in_specs=[full(x.shape) for x in operands],
            out_specs=full(out),
            scratch_shapes=[
                pltpu.VMEM((2 * halo + devices * tiles + 2, 2, rows, BLOCK), jnp.bfloat16),
                pltpu.VMEM((tiles + 1, 2, rows, BLOCK), jnp.bfloat16),
                pltpu.VMEM((rows, BLOCK), jnp.int32),
                pltpu.VMEM((rows, BLOCK), jnp.float32),
                pltpu.VMEM((rows, BLOCK), jnp.float32),
            ],
        ),
        out_shape=jax.ShapeDtypeStruct(out, jnp.bfloat16),
        compiler_params=pltpu.CompilerParams(vmem_limit_bytes=VMEM_LIMIT),
        name="shear_whole",
    )(base, *operands)


def shear_columns_kernel(front, blocks, steps, length, rows_out, place, base, rank, *refs):
    owns, refs = refs[: len(place)], refs[len(place) :]
    offsets, fractions, forward, inverse = refs[:4]
    outs, (strip, shifted, cosine, sine) = refs[4:-4], refs[-4:]
    step = pl.program_id(0)
    per_step = length // BLOCK
    per_grid = blocks // steps
    total = strip.shape[1]

    @pl.when(step == 0)
    def _():
        strip[:, 0:front, :] = jnp.zeros((2, front, BLOCK), jnp.bfloat16)
        back = front + blocks * length
        strip[:, back:, :] = jnp.zeros((2, total - back, BLOCK), jnp.bfloat16)
        for own, slots in zip(owns, place):
            count = own.shape[2]
            for i, (slot, within) in enumerate(slots):
                first = pl.multiple_of(front + (slot ^ rank[0]) * length + within, GROUP)
                for part in range(2):
                    strip[part, pl.ds(first, count), :] = own[i, part]
        bins = lax.broadcasted_iota(jnp.int32, (BLOCK, BLOCK), 0).astype(jnp.float32)
        sine[...], cosine[...] = sine_cosine(bins * fractions[...] * (-2.0 * np.pi / WINDOW))

    offset = jnp.broadcast_to(offsets[...], (8, BLOCK))
    row = lax.broadcasted_iota(jnp.int32, (8, BLOCK), 0) + (offset & 7)
    wraps = row >= 8
    index = row & 7

    def one_chunk(block_rows, chunk):
        begin = pl.multiple_of(base[0] + block_rows + chunk * BLOCK, GROUP)
        for part in range(2):
            value = strip[part, pl.ds(begin, 2 * BLOCK), :].astype(jnp.float32)
            value = value.reshape(2 * BLOCK // 8, 8, BLOCK)
            for bit in (64, 32, 16, 8):
                taken = ((offset & bit) != 0)[None]
                value = jnp.where(taken, value[bit // 8 :], value[: -(bit // 8)])
            pieces = [
                jnp.take_along_axis(value[i], index, axis=0) for i in range(BLOCK // 8 + 1)
            ]
            moved = [
                jnp.where(wraps, pieces[i + 1], pieces[i]) for i in range(BLOCK // 8)
            ]
            shifted[chunk * BLOCK : (chunk + 1) * BLOCK, part * BLOCK : (part + 1) * BLOCK] = (
                jnp.concatenate(moved, 0).astype(jnp.bfloat16)
            )

    def one_block(local):
        block_rows = ((step * per_grid + local) ^ rank[0]) * length
        for chunk in range(per_step + 1):
            one_chunk(block_rows, chunk)
        windows = [shifted[m * BLOCK : (m + 2) * BLOCK, :] for m in range(per_step)]
        spectrum = jnp.dot(
            forward[...], jnp.concatenate(windows, 1), preferred_element_type=jnp.float32
        )
        ramp_real = jnp.concatenate([cosine[...]] * (2 * per_step), 1)
        ramp_imaginary = jnp.concatenate([sine[...]] * (2 * per_step), 1)
        real, imaginary = spectrum[:BLOCK], spectrum[BLOCK:]
        ramped = jnp.concatenate(
            [
                (real * ramp_real - imaginary * ramp_imaginary).astype(jnp.bfloat16),
                (real * ramp_imaginary + imaginary * ramp_real).astype(jnp.bfloat16),
            ],
            0,
        )
        result = jnp.dot(inverse[...], ramped, preferred_element_type=jnp.float32)
        result = result.astype(jnp.bfloat16)
        for window in range(per_step):
            piece, within = window * BLOCK // rows_out, window * BLOCK % rows_out
            for part in range(2):
                lanes = (2 * window + part) * BLOCK
                value = result[:, lanes : lanes + BLOCK]
                if len(outs) > 1:
                    outs[local][piece, part, within : within + BLOCK, :] = value
                else:
                    index = local * (length // rows_out) + piece
                    outs[0][index, part, within : within + BLOCK, :] = value

    for local in range(blocks // steps):
        one_block(local)


def shear_columns(
    owns, place, blocks, front, back, base, rank, spare, fractions, tables, rows_out, split
):
    length = sum(own.shape[0] * own.shape[2] for own in owns) // blocks
    forward, inverse = tables
    operands = (
        *owns,
        spare.astype(jnp.int32).reshape(1, BLOCK),
        fractions.reshape(1, BLOCK),
        forward,
        inverse,
    )
    full = lambda shape: pl.BlockSpec(shape, lambda i, *_: (0,) * len(shape))
    pieces = blocks * length // rows_out
    steps = STEPS if blocks % STEPS == 0 and not split else 1
    parts = blocks if split else 1
    shape = (pieces // parts, 2, rows_out, BLOCK)
    return pl.pallas_call(
        functools.partial(shear_columns_kernel, front, blocks, steps, length, rows_out, place),
        grid_spec=pltpu.PrefetchScalarGridSpec(
            num_scalar_prefetch=2,
            grid=(steps,),
            in_specs=[full(x.shape) for x in operands],
            out_specs=[
                pl.BlockSpec((shape[0] // steps, *shape[1:]), lambda i, *_: (i, 0, 0, 0))
            ]
            * parts,
            scratch_shapes=[
                pltpu.VMEM((2, front + blocks * length + back, BLOCK), jnp.bfloat16),
                pltpu.VMEM((length + BLOCK, 2 * BLOCK), jnp.bfloat16),
                pltpu.VMEM((BLOCK, BLOCK), jnp.float32),
                pltpu.VMEM((BLOCK, BLOCK), jnp.float32),
            ],
        ),
        out_shape=[jax.ShapeDtypeStruct(shape, jnp.bfloat16)] * parts,
        compiler_params=pltpu.CompilerParams(vmem_limit_bytes=VMEM_LIMIT),
        name="shear_columns",
    )(base, rank, *operands)


def sine_cosine(angle):
    turns = jnp.round(angle * (2.0 / np.pi))
    rest = angle - turns * 1.5703125
    rest = rest - turns * 4.837512969970703125e-4
    rest = rest - turns * 7.549789954891882e-8
    square = rest * rest
    sine = rest + rest * square * (
        -1.6666654611e-1 + square * (8.3321608736e-3 - square * 1.9515295891e-4)
    )
    cosine = (
        1.0
        - 0.5 * square
        + square
        * square
        * (4.166664568298827e-2 + square * (-1.388731625493765e-3 + square * 2.443315711809948e-5))
    )
    quadrant = turns.astype(jnp.int32)
    odd = (quadrant & 1) != 0
    sine_out = jnp.where(odd, cosine, sine)
    cosine_out = jnp.where(odd, sine, cosine)
    sine_out = jnp.where((quadrant & 2) != 0, -sine_out, sine_out)
    cosine_out = jnp.where(((quadrant + 1) & 2) != 0, -cosine_out, cosine_out)
    return sine_out, cosine_out


def transmitted(rotated, wave):
    sine, cosine = sine_cosine(rotated[0].astype(jnp.float32))
    amplitude = jnp.exp(-ABSORB * rotated[1].astype(jnp.float32))
    through_real = amplitude * cosine
    through_imaginary = amplitude * sine
    wave_real = wave[0].astype(jnp.float32)
    wave_imaginary = wave[1].astype(jnp.float32)
    return (
        (wave_real * through_real - wave_imaginary * through_imaginary).astype(jnp.bfloat16),
        (wave_real * through_imaginary + wave_imaginary * through_real).astype(jnp.bfloat16),
    )


def travel_first_kernel(length, count, sent, *refs):
    if sent:
        body, top, bottom, matrix, out, low, high, field = refs
        for chunk in range(count):
            across = slice(chunk * BLOCK, (chunk + 1) * BLOCK)
            for part in range(2):
                field[part, 0:MARGIN, across] = top[chunk, part]
                field[part, MARGIN : MARGIN + length, across] = body[chunk, part]
                field[part, MARGIN + length :, across] = bottom[chunk, part]
    else:
        body, wave, wave_top, wave_bottom, matrix, out, low, high, field = refs
        pieces = [(0, MARGIN, wave_top, 0)]
        pieces += [(MARGIN + first, BLOCK, wave, first) for first in range(0, length, BLOCK)]
        pieces += [(MARGIN + length, MARGIN, wave_bottom, 0)]
        for chunk in range(count):
            across = slice(chunk * BLOCK, (chunk + 1) * BLOCK)
            for place, height, waves, first in pieces:
                parts = transmitted(
                    [body[chunk, p, place : place + height, :] for p in range(2)],
                    [waves[p, first : first + height, across] for p in range(2)],
                )
                for part in range(2):
                    field[part, place : place + height, across] = parts[part]
    for m in range(0, length, BLOCK):
        window = jnp.concatenate([field[0, m : m + WINDOW, :], field[1, m : m + WINDOW, :]], 0)
        result = jnp.dot(matrix[...], window, preferred_element_type=jnp.float32)
        result = result.astype(jnp.bfloat16)
        for chunk in range(count):
            across = slice(chunk * BLOCK, (chunk + 1) * BLOCK)
            for part in range(2):
                out[chunk, part, m : m + BLOCK, :] = result[
                    part * BLOCK : (part + 1) * BLOCK, across
                ]

    def outermost(chunk, edge, first):
        for part in range(2):
            for m in range(0, length, BLOCK):
                turned = out[chunk, part, m : m + BLOCK, :].astype(jnp.float32).T
                edge[part, :, m : m + BLOCK] = turned[first : first + MARGIN].astype(jnp.bfloat16)

    @pl.when(pl.program_id(0) == 0)
    def _():
        outermost(0, low, 0)

    @pl.when(pl.program_id(0) == pl.num_programs(0) - 1)
    def _():
        outermost(count - 1, high, BLOCK - MARGIN)


def travel_first(body, halos, waves, matrix):
    chunks = body.shape[0]
    count = chunks // STEPS if chunks % STEPS == 0 else chunks
    length = body.shape[2] if len(halos) > 0 else body.shape[2] - 2 * MARGIN
    chunk_spec = lambda x: pl.BlockSpec((count, 2, x.shape[2], BLOCK), lambda i: (i, 0, 0, 0))
    wide_spec = lambda x: pl.BlockSpec((2, x.shape[1], count * BLOCK), lambda i: (0, 0, i))
    return pl.pallas_call(
        functools.partial(travel_first_kernel, length, count, len(halos) > 0),
        grid=(chunks // count,),
        in_specs=[chunk_spec(x) for x in (body, *halos)]
        + [wide_spec(x) for x in waves]
        + [pl.BlockSpec(matrix.shape, lambda i: (0, 0))],
        out_specs=[pl.BlockSpec((count, 2, length, BLOCK), lambda i: (i, 0, 0, 0))]
        + [pl.BlockSpec((2, MARGIN, length), lambda i: (0, 0, 0))] * 2,
        out_shape=[jax.ShapeDtypeStruct((chunks, 2, length, BLOCK), jnp.bfloat16)]
        + [jax.ShapeDtypeStruct((2, MARGIN, length), jnp.bfloat16)] * 2,
        scratch_shapes=[pltpu.VMEM((2, length + 2 * MARGIN, count * BLOCK), jnp.bfloat16)],
        compiler_params=pltpu.CompilerParams(vmem_limit_bytes=VMEM_LIMIT),
        name="travel_first",
    )(body, *halos, *waves, matrix)


def travel_second_kernel(chunks, rows, left, body, right, matrix, out):
    empty = jnp.zeros((BLOCK - MARGIN, rows), jnp.float32)
    upright = lambda *pieces: jnp.concatenate(pieces, 0).T.astype(jnp.bfloat16)
    parts = [
        [upright(empty, left[p].astype(jnp.float32))]
        + [body[m, p] for m in range(chunks)]
        + [upright(right[p].astype(jnp.float32), empty)]
        for p in range(2)
    ]
    windows = [
        jnp.concatenate(parts[0][m : m + 3] + parts[1][m : m + 3], 1) for m in range(chunks)
    ]
    result = jnp.dot(
        jnp.concatenate(windows, 0), matrix[...], preferred_element_type=jnp.float32
    ).astype(jnp.bfloat16)
    for m in range(chunks):
        for part in range(2):
            out[part, :, m * BLOCK : (m + 1) * BLOCK] = result[
                m * rows : (m + 1) * rows, part * BLOCK : (part + 1) * BLOCK
            ]


def travel_second(left, body, right, matrix):
    chunks, _, length, _ = body.shape
    rows = length // STEPS if length % (STEPS * BLOCK) == 0 else length
    edge = pl.BlockSpec((2, MARGIN, rows), lambda i: (0, 0, i))
    return pl.pallas_call(
        functools.partial(travel_second_kernel, chunks, rows),
        grid=(length // rows,),
        in_specs=[
            edge,
            pl.BlockSpec((chunks, 2, rows, BLOCK), lambda i: (0, 0, i, 0)),
            edge,
            pl.BlockSpec(matrix.shape, lambda i: (0, 0)),
        ],
        out_specs=pl.BlockSpec((2, rows, chunks * BLOCK), lambda i: (0, i, 0)),
        out_shape=jax.ShapeDtypeStruct((2, length, chunks * BLOCK), jnp.bfloat16),
        compiler_params=pltpu.CompilerParams(vmem_limit_bytes=VMEM_LIMIT),
        name="travel_second",
    )(left, body, right, matrix)


def from_both_sides(first, last, axis):
    devices = lax.axis_size(axis)
    up = [(i, i + 1) for i in range(devices - 1)]
    down = [(j, i) for i, j in up]
    return lax.ppermute(last, axis, up), lax.ppermute(first, axis, down)


def after(value, *others):
    return lax.optimization_barrier((value, others))[0]


def ordered_kernel(halo, rank, *refs):
    pieces, (out, first, last) = refs[:-3], refs[-3:]
    count = len(pieces)
    for s, piece in enumerate(pieces):
        place = s ^ rank[0]
        out[place] = piece[0]

        @pl.when(place < halo)
        def _():
            first[place] = piece[0]

        @pl.when(place >= count - halo)
        def _():
            last[place - (count - halo)] = piece[0]


def ordered(pieces, halo, rank):
    count = len(pieces)
    block = pieces[0].shape
    shapes = [(n, *block[1:]) for n in (count, halo, halo)]
    full = lambda shape: pl.BlockSpec(shape, lambda i, *_: (0,) * len(shape))
    return pl.pallas_call(
        functools.partial(ordered_kernel, halo),
        grid_spec=pltpu.PrefetchScalarGridSpec(
            num_scalar_prefetch=1,
            grid=(1,),
            in_specs=[full(block)] * count,
            out_specs=[full(shape) for shape in shapes],
        ),
        out_shape=[jax.ShapeDtypeStruct(shape, pieces[0].dtype) for shape in shapes],
        compiler_params=pltpu.CompilerParams(vmem_limit_bytes=VMEM_LIMIT),
        name="ordered",
    )(rank, *pieces)


def swapped_shares(slots):
    devices = lax.axis_size("row")
    return [slots[0]] + [
        lax.ppermute(slots[s], "row", [(i, i ^ s) for i in range(devices)])
        for s in range(1, devices)
    ]


def group_starts(starts, group, unit):
    lines = starts.shape[-1]
    grouped = starts.reshape(*starts.shape[:-1], lines // group, group)
    base = jnp.min(grouped, -1) // unit
    spare = grouped - base[..., None] * unit
    return base.astype(jnp.int32), spare.reshape(starts.shape)


def on_device(
    volume_plane,
    wave_a,
    wave_b,
    shift_rows,
    fraction_rows,
    shift_columns,
    fraction_columns,
    travel_distance,
):
    _, line_count, width = volume_plane.shape
    row_devices, column_devices = lax.axis_size("row"), lax.axis_size("col")
    row_index, column_index = lax.axis_index("row"), lax.axis_index("col")
    tiles = width // BLOCK
    halo = -(-(SHIFT_X + MARGIN) // BLOCK)
    reach = halo * BLOCK

    forward, inverse = real_tables()
    half = lambda x: jnp.asarray(x, jnp.bfloat16)
    row_tables = (half(forward), half(inverse))
    column_tables = (half(forward.T), half(inverse.T))
    turned_tables = (half(forward), half(inverse[:, ::-1].T))
    in_order = jnp.zeros((1,), jnp.int32)
    by_rank = row_index.astype(jnp.int32).reshape(1)

    part_lines = line_count // PARTS
    lefts, rights, edges = [], [], ()
    for part in range(PARTS):
        lines = after(volume_plane, edges)[:, part * part_lines : (part + 1) * part_lines]
        edges = (lines[:, :, :reach], lines[:, :, width - reach :])
        if part == PARTS - 1:
            fill = ((0, 0), (0, 0), (0, reach - line_count))
            margins = (wave_b[:, :MARGIN], wave_b[:, -MARGIN:])
            edges = [
                jnp.concatenate([edge, jnp.pad(margin, fill)], 1)
                for edge, margin in zip(edges, margins)
            ]
        left, right = from_both_sides(*edges, "col")
        lefts.append(left)
        rights.append(right)
    wave_b_halos = [x[-1][:, part_lines:, :line_count] for x in (lefts, rights)]

    base_rows, spare_rows = group_starts(reach - MARGIN - shift_rows, GROUP, BLOCK)

    front = -(-(SHIFT_Y + MARGIN) // GROUP) * GROUP
    back = front + 3 * BLOCK
    mine = lambda x: lax.dynamic_slice_in_dim(x, row_index * BLOCK, BLOCK, 1)
    base_columns, spare_columns = group_starts(front - MARGIN - mine(shift_columns), BLOCK, GROUP)
    column_fractions = mine(fraction_columns)

    def first(view, begin, lefts, rights, rank):
        return shear_tile(
            volume_plane,
            lefts,
            rights,
            begin,
            len(lefts) * part_lines,
            halo,
            base_rows[view, 0],
            rank,
            spare_rows[view, 0],
            fraction_rows[view, 0],
            row_tables,
        )

    def second(view, pieces, place, rank, rows_out, split):
        return shear_columns(
            pieces,
            place,
            row_devices,
            front,
            back,
            base_columns[view] * GROUP,
            rank,
            spare_columns[view],
            column_fractions[view],
            column_tables,
            rows_out,
            split,
        )

    matrices = travel_matrices(travel_distance, forward, inverse)
    real, imaginary = matrices[:, 0], matrices[:, 1]
    along_rows = jnp.concatenate(
        [
            jnp.concatenate([real, -imaginary], 1),
            jnp.concatenate([imaginary, real], 1),
        ],
        2,
    )
    along_rows = jnp.swapaxes(along_rows, 1, 2).astype(jnp.bfloat16)
    spaced = jnp.pad(matrices, ((0, 0), (0, 0), (BLOCK - MARGIN, BLOCK - MARGIN), (0, 0)))
    real, imaginary = spaced[:, 0], spaced[:, 1]
    along_columns = jnp.concatenate(
        [
            jnp.concatenate([real, -imaginary], 1),
            jnp.concatenate([imaginary, real], 1),
        ],
        2,
    ).astype(jnp.bfloat16)

    spread, sheared = [], ()
    for part in range(PARTS):
        left, right = after((lefts[part], rights[part]), sheared)
        sheared = first(1, part * part_lines, [left], [right], in_order)
        spread.append(lax.all_to_all(sheared, "row", split_axis=0, concat_axis=0, tiled=True))
    lefts, rights = after((lefts, rights), sheared)
    slots = first(0, 0, lefts, rights, by_rank)
    shares = [slots[s : s + 1] for s in range(row_devices)]
    spread = after(spread, shares)
    pieces = swapped_shares(shares)

    place = [[(b, part * part_lines) for b in range(row_devices)] for part in range(PARTS)]
    (moved_b,) = second(1, spread, place, in_order, BLOCK, False)
    whole = lax.all_to_all(moved_b, ("row", "col"), split_axis=0, concat_axis=0, tiled=True)
    whole = after(whole, pieces)
    whole = whole.reshape(row_devices, column_devices, 2, BLOCK, BLOCK)
    own_lines = lambda x: lax.dynamic_slice_in_dim(x, column_index * BLOCK, BLOCK, 0)
    groups = BLOCK // GROUP
    turned = shear_whole(
        whole,
        halo,
        lax.dynamic_slice_in_dim(base_rows[1, 1], column_index * groups, groups, 0),
        own_lines(spare_rows[1, 1]),
        own_lines(fraction_rows[1, 1]),
        turned_tables,
    )

    sent = lax.all_to_all(turned, "col", split_axis=0, concat_axis=0, tiled=True)

    pieces = after(pieces, turned)
    place = [[(s, 0)] for s in range(row_devices)]
    pieces = swapped_shares(second(0, pieces, place, by_rank, line_count, True))
    tile, low, high = ordered(pieces, halo, by_rank)
    left, right = from_both_sides(low, high, "col")

    half_b, low, high = travel_first(sent, (), (wave_b, *wave_b_halos), along_rows[1])
    low, high = from_both_sides(low, high, "row")
    exit_b = travel_second(low, half_b, high, along_columns[1])

    left, right = after((left, right), exit_b)
    field_a = shear_tile(
        tile,
        [left],
        [right],
        0,
        line_count,
        halo,
        base_rows[0, 1],
        in_order,
        spare_rows[0, 1],
        fraction_rows[0, 1],
        row_tables,
        wave_a,
    )
    halos = from_both_sides(field_a[:, :, :MARGIN], field_a[:, :, -MARGIN:], "row")
    half_a, low, high = travel_first(field_a, halos, (), along_rows[0])
    low, high = from_both_sides(low, high, "col")
    exit_a = travel_second(low, half_a, high, along_columns[0])
    return exit_a, exit_b


def swapped(value, axis, bit):
    mask = 2**bit
    pairs = [(source, source ^ mask) for source in range(lax.axis_size(axis))]
    return lax.ppermute(value, axis, pairs)


def padded_2(x, sides, width):
    for axis, dim in sides:
        devices, length = (lax.axis_size(axis), x.shape[dim])
        up = [(i, (i + 1) % devices) for i in range(devices - 1)]
        down = [(j, i) for i, j in up]
        last = lax.slice_in_dim(x, length - width, length, axis=dim)
        first = lax.slice_in_dim(x, 0, width, axis=dim)
        before = lax.ppermute(last, axis, up)
        after = lax.ppermute(first, axis, down)
        x = jnp.concatenate([before, x, after], axis=dim)
    return x


def fourier_tables(block_len, margin):
    window_len = block_len + 2 * margin
    frequency = jnp.arange(window_len, dtype=jnp.int32) - window_len // 2
    position = jnp.arange(window_len, dtype=jnp.int32)
    angles = (
        2.0
        * jnp.pi
        * jnp.mod(position[:, None] * frequency[None, :], window_len).astype(jnp.float32)
        / window_len
    )
    cosine = jnp.cos(angles)
    sines = jnp.sin(angles)
    forward = jnp.concatenate(
        [jnp.concatenate([cosine, -sines], 1), jnp.concatenate([sines, cosine], 1)], 0
    ).astype(jnp.bfloat16)
    target = jnp.arange(block_len, dtype=jnp.int32) + margin
    inverse_angle = (
        2.0
        * jnp.pi
        * jnp.mod(frequency[:, None] * target[None, :], window_len).astype(jnp.float32)
        / window_len
    )
    inverse_cosine = jnp.cos(inverse_angle) / window_len
    inverse_sine = jnp.sin(inverse_angle) / window_len
    inverse = jnp.concatenate(
        [
            jnp.concatenate([inverse_cosine, inverse_sine], 1),
            jnp.concatenate([-inverse_sine, inverse_cosine], 1),
        ],
        0,
    ).astype(jnp.bfloat16)
    return (forward, inverse, frequency.astype(jnp.float32))


def shear_ramp(fractions, frequency):
    window_len = frequency.shape[0]
    phases = -2.0 * jnp.pi / window_len * fractions[:, None] * frequency[None, :]
    nyquist = (jnp.arange(window_len) == 0)[None, :]
    ramp_real = jnp.where(nyquist, jnp.cos(jnp.pi * fractions)[:, None], jnp.cos(phases))
    ramp_imaginary = jnp.where(nyquist, 0.0, jnp.sin(phases))
    return (ramp_real, ramp_imaginary)


def travel_ramp(distance, frequency):
    window_len = frequency.shape[0]
    phases = -2.0 * jnp.pi / (window_len * window_len) * distance * frequency * frequency
    return (jnp.cos(phases)[None, :], jnp.sin(phases)[None, :])


def select_window(padded, starts, out_len):
    total_len = padded.shape[2]
    offset_range = total_len - out_len
    bit_count = max(offset_range, 1).bit_length()
    current = jnp.pad(padded, ((0, 0), (0, 0), (0, out_len + 2**bit_count - 1 - total_len)))
    for bit_number in reversed(range(bit_count)):
        stride = 2**bit_number
        kept_len = current.shape[2] - stride
        chosen = (starts // stride % 2 == 1)[None, :, None]
        current = jnp.where(
            chosen, current[:, :, stride : stride + kept_len], current[:, :, :kept_len]
        )
    return current


def line_pass(padded, extent, shifts, ramp_real, ramp_imaginary, tables):
    forward, inverse = (tables[0], tables[1])
    window_len = BLOCK + 2 * MARGIN
    line_count = padded.shape[1]
    blocks = (padded.shape[2] - 2 * extent) // BLOCK
    reach_len = blocks * BLOCK + 2 * MARGIN
    if shifts is None:
        shifted = padded
    else:
        starts = extent - MARGIN - shifts
        shifted = select_window(padded, starts, reach_len)
    middle = shifted[:, :, MARGIN : MARGIN + blocks * BLOCK].reshape(2, line_count, blocks, BLOCK)
    left_rim = shifted[:, :, : blocks * BLOCK].reshape(2, line_count, blocks, BLOCK)[..., :MARGIN]
    right_rim = shifted[:, :, 2 * MARGIN : 2 * MARGIN + blocks * BLOCK].reshape(
        2, line_count, blocks, BLOCK
    )[..., BLOCK - MARGIN :]
    windows = jnp.concatenate([left_rim, middle, right_rim], 3)
    spectrum = jnp.einsum(
        "cpms,cst->pmt",
        windows,
        forward.reshape(2, window_len, 2 * window_len),
        preferred_element_type=jnp.float32,
    )
    spec_real = spectrum[..., :window_len]
    spec_imaginary = spectrum[..., window_len:]
    factor_real = ramp_real[:, None, :]
    factor_imaginary = ramp_imaginary[:, None, :]
    ramped = jnp.concatenate(
        [
            spec_real * factor_real - spec_imaginary * factor_imaginary,
            spec_real * factor_imaginary + spec_imaginary * factor_real,
        ],
        -1,
    ).astype(jnp.bfloat16)
    result = jnp.einsum(
        "pms,scb->cpmb",
        ramped,
        inverse.reshape(2 * window_len, 2, BLOCK),
        preferred_element_type=jnp.float32,
    )
    return result.reshape(2, line_count, blocks * BLOCK).astype(jnp.bfloat16)


def single_pass(padded, extent, shifts, fractions, tables):
    ramp_real, ramp_imaginary = shear_ramp(fractions, tables[2])
    return line_pass(padded, extent, shifts, ramp_real, ramp_imaginary, tables)


def general_shear_columns(stacked, shifts, fractions, tables):
    halo_depth = SHIFT_X + MARGIN
    inputs = stacked.shape[0]
    column_devices = lax.axis_size("col")
    share = stacked.shape[2] // column_devices
    offset = lax.axis_index("col") * share
    spread = lax.all_to_all(stacked, "col", split_axis=2, concat_axis=3, tiled=True)
    padded = jnp.pad(spread, ((0, 0), (0, 0), (0, 0), (halo_depth, halo_depth)))
    row_shifts = lax.dynamic_slice_in_dim(shifts, offset, share, 1)
    row_fractions = lax.dynamic_slice_in_dim(fractions, offset, share, 1)
    sheared = jnp.stack(
        [
            single_pass(
                padded[min(0, inputs - 1)], halo_depth, row_shifts[0], row_fractions[0], tables
            )
        ]
    )
    return lax.all_to_all(sheared, "col", split_axis=3, concat_axis=2, tiled=True)


def shear_along_first(padded_lines, halo_depth, shifts, fractions, tables):
    flipped = jnp.swapaxes(padded_lines[0], 1, 2)
    moved = single_pass(flipped, halo_depth, shifts[0], fractions[0], tables)
    sheared = [jnp.swapaxes(moved, 1, 2)]
    return jnp.stack(sheared)


def shear_rows_pass(stacked, shifts, fractions, tables):
    halo_depth = SHIFT_Y + MARGIN
    row_devices = lax.axis_size("row")
    share = stacked.shape[3] // row_devices
    offset = lax.axis_index("row") * share
    spread = lax.all_to_all(stacked, "row", split_axis=3, concat_axis=2, tiled=True)
    padded = jnp.pad(spread, ((0, 0), (0, 0), (halo_depth, halo_depth), (0, 0)))
    column_shifts = lax.dynamic_slice_in_dim(shifts, offset, share, 1)
    column_fractions = lax.dynamic_slice_in_dim(fractions, offset, share, 1)
    sheared = shear_along_first(padded, halo_depth, column_shifts, column_fractions, tables)
    return lax.all_to_all(sheared, "row", split_axis=2, concat_axis=3, tiled=True)


def travel_local(extended, distance, tables):
    ramp_real, ramp_imaginary = travel_ramp(distance, tables[2])
    halfway = line_pass(extended, MARGIN, None, ramp_real, ramp_imaginary, tables)
    flipped = jnp.swapaxes(halfway, 1, 2)
    finished = line_pass(flipped, MARGIN, None, ramp_real, ramp_imaginary, tables)
    return jnp.swapaxes(finished, 1, 2)


def transmit(rotated, wave):
    phase_part = rotated[0].astype(jnp.float32)
    absorb_part = rotated[1].astype(jnp.float32)
    amplitude = jnp.exp(-ABSORB * absorb_part)
    through_real = amplitude * jnp.cos(phase_part)
    through_imaginary = amplitude * jnp.sin(phase_part)
    wave_real = wave[0].astype(jnp.float32)
    wave_imaginary = wave[1].astype(jnp.float32)
    return jnp.stack(
        [
            wave_real * through_real - wave_imaginary * through_imaginary,
            wave_real * through_imaginary + wave_imaginary * through_real,
        ]
    ).astype(jnp.bfloat16)


def general_on_device(
    volume_plane,
    wave_a,
    wave_b,
    shift_rows,
    fraction_rows,
    shift_columns,
    fraction_columns,
    travel_distance,
):
    tables = fourier_tables(BLOCK, MARGIN)
    source = volume_plane[None]
    results = []
    for member in range(2):
        stacked = general_shear_columns(
            source,
            shift_rows[member : member + 1, 0],
            fraction_rows[member : member + 1, 0],
            tables,
        )
        stacked = shear_rows_pass(
            stacked,
            shift_columns[member : member + 1],
            fraction_columns[member : member + 1],
            tables,
        )
        stacked = general_shear_columns(
            stacked,
            shift_rows[member : member + 1, 1],
            fraction_rows[member : member + 1, 1],
            tables,
        )
        results.append(stacked[0])
    view_one = results[0]
    view_two = results[1]
    turned = jnp.swapaxes(jnp.flip(view_two, 2), 1, 2)
    for bit_number in range(lax.axis_size("col").bit_length() - 1):
        turned = swapped(turned, "col", bit_number)
    product_a = transmit(view_one, wave_a)
    extended_a = padded_2(product_a, (("row", 1), ("col", 2)), MARGIN)
    exit_a = travel_local(extended_a, travel_distance[0], tables)
    product_b = transmit(turned, wave_b)
    extended_b = padded_2(product_b, (("row", 2), ("col", 1)), MARGIN)
    exit_b = travel_local(extended_b, travel_distance[1], tables)
    return (exit_a, exit_b)


def solution(mesh):
    def either(volume_plane, *rest):
        rows, width = volume_plane.shape[1:]
        fits = (
            rows == BLOCK * lax.axis_size("col")
            and width == BLOCK * lax.axis_size("row")
            and width >= -(-(SHIFT_X + MARGIN) // BLOCK) * BLOCK >= rows
        )
        chosen = on_device if fits else general_on_device
        return chosen(volume_plane, *rest)

    return jax.shard_map(
        either,
        mesh=mesh,
        in_specs=(
            P(None, "row", "col"),
            P(None, "row", "col"),
            P(None, "col", "row"),
            P(None, None, "row"),
            P(None, None, "row"),
            P(None, "col"),
            P(None, "col"),
            P(),
        ),
        out_specs=(P(None, "row", "col"), P(None, "col", "row")),
        check_vma=False,
    )
```
